32 devices in a mesh: gz: 2 (over core), gy: 16 (over z, y, x).
Axes of the slice: x: 2, y: 2, z: 4, core: 2. Of those that a mesh axis runs over, the one named last changes fastest.
Arguments:
- data: bfloat16 [2, 64, 2048, 128], P('gz', 'gy'), may hold values from -6 to 6
- band_offset: int32 [4096], replicated, may hold values from -1 to 0
- interp_weight: float32 [2, 4096], replicated, may hold values from 0.3 to 1
Outputs:
- volume: float32 [2, 2048, 4096], P('gz', 'gy')
- residual: float32 [2, 64, 2048, 128], P('gz', 'gy')
The draws below stay inside these ranges and needn't reach their ends.
All inputs are finite; a program needn't handle non-finite values.
Results may differ from the reference program's by a relative error of at most 0.0003.
Values sent between devices are 32-bit elements; how exact they have to be, the bound alone decides.
No kernel may reach another device: no remote copies, remote signals or barrier semaphores. Data moves between devices by JAX's collectives and lax.ppermute only.
A program may use at most 192 MiB of HBM per device.

```python
import math
import jax
import jax.numpy as jnp
from jax import lax

NX = 4096
NY = 2048
XB = 64
ITERS = 2
XA = 64
NZ = 2


def with_ends(drawn, rng, smallest, top_value):
    index_at = [jax.random.randint(jax.random.fold_in(rng, axis), (), 0, length) for axis, length in enumerate(drawn.shape)]
    widest = drawn.shape.index(max(drawn.shape))
    neighbour = index_at[:widest] + [(index_at[widest] + 1) % drawn.shape[widest]] + index_at[widest + 1:]
    return drawn.at[tuple(index_at)].set(smallest).at[tuple(neighbour)].set(top_value)


def block_levels(rng, dims, split, smallest, high):
    def one(axis_at, blocks):
        draws = jax.random.uniform(jax.random.fold_in(jax.random.fold_in(rng, 6), axis_at), (blocks,), jnp.float32, smallest / len(split), high / len(split))
        return jnp.repeat(jnp.exp(draws), dims[axis_at] // blocks).reshape((-1,) + (1,) * (len(dims) - axis_at - 1))

    loudness = one(*split[0])
    for cut in split[1:]:
        loudness = loudness * one(*cut)
    return loudness


def gaussian(own_key, extent, width, bound, cuts=(), held_as=jnp.bfloat16):
    array = jax.random.normal(own_key, extent, jnp.float32) * width
    if len(cuts) > 0:
        array = block_levels(own_key, extent, cuts, -0.22, 0.18) * array
    return jnp.clip(array, min=-bound, max=bound).astype(held_as)


def setup_inputs(seed: int = 0) -> dict:
    streams_of = jax.random.split(jax.random.key(seed), 4)
    return {
        "data": gaussian(streams_of[0], (NZ, XB, NY, 2 * XA), 1.0, 6.0, ((0, 2), (1, 16))),
        "band_offset": with_ends(jax.random.randint(streams_of[1], (NX,), -1, 1), jax.random.fold_in(streams_of[1], 1), -1, 0).astype(jnp.int32),
        "interp_weight": jnp.clip(jnp.exp(jax.random.uniform(streams_of[2], (2, NX), jnp.float32, math.log(0.3), math.log(1.0))), 0.3, 1.0),
    }


PENALTY = 0.5
TV_WEIGHT = 0.25


def pack_parts(spectrum):
    slices = spectrum.shape[0]
    grid_view = spectrum.reshape(slices, NY, XB, XA)
    joined = jnp.concatenate([jnp.real(grid_view), jnp.imag(grid_view)], axis=-1)
    return jnp.transpose(joined, (0, 2, 1, 3))


def unpack_parts(packed):
    slices = packed.shape[0]
    ordered = jnp.transpose(packed, (0, 2, 1, 3))
    joined = lax.complex(ordered[..., :XA], ordered[..., XA:])
    return joined.reshape(slices, NY, NX)


def tilt_slices(field_in, band_offset, interp_weight, adjoint):
    padded = jnp.pad(field_in, ((1, 1), (0, 0), (0, 0)))
    below_rim = padded[:-2]
    middle = padded[1:-1]
    above_rim = padded[2:]
    lower_tap = band_offset < 0
    first_weight = interp_weight[0]
    second_weight = interp_weight[1]
    if adjoint:
        return jnp.where(lower_tap, first_weight * above_rim + second_weight * middle,
                         first_weight * middle + second_weight * below_rim)
    return jnp.where(lower_tap, first_weight * below_rim + second_weight * middle,
                     first_weight * middle + second_weight * above_rim)


def project(volume, band_offset, interp_weight):
    spectrum = jnp.fft.fft2(volume, axes=(1, 2), norm="ortho")
    return pack_parts(tilt_slices(spectrum, band_offset, interp_weight, False))


def back_project(packed, band_offset, interp_weight):
    spectrum = tilt_slices(unpack_parts(packed), band_offset, interp_weight, True)
    return jnp.real(jnp.fft.ifft2(spectrum, axes=(1, 2), norm="ortho")).astype(packed.dtype)


def forward_diff(field_in):
    parts_list = []
    for dim_index in range(3):
        count = field_in.shape[dim_index]
        upper = lax.slice_in_dim(field_in, 1, count, axis=dim_index)
        lower = lax.slice_in_dim(field_in, 0, count - 1, axis=dim_index)
        zero_slab = jnp.zeros_like(lax.slice_in_dim(field_in, 0, 1, axis=dim_index))
        parts_list.append(jnp.concatenate([upper - lower, zero_slab], axis=dim_index))
    return jnp.stack(parts_list)


def transpose_diff(components):
    result = jnp.zeros_like(components[0])
    for dim_index in range(3):
        component = components[dim_index]
        count = component.shape[dim_index]
        kept_part = lax.slice_in_dim(component, 0, count - 1, axis=dim_index)
        zero_slab = jnp.zeros_like(lax.slice_in_dim(component, 0, 1, axis=dim_index))
        previous = jnp.concatenate([zero_slab, kept_part], axis=dim_index)
        current = jnp.concatenate([kept_part, zero_slab], axis=dim_index)
        result = result + previous - current
    return result


def reference(data, band_offset, interp_weight):
    measured = data.astype(jnp.float32)
    volume = jnp.zeros((NZ, NY, NX), jnp.float32)
    split_var = jnp.zeros((3, NZ, NY, NX), jnp.float32)
    dual_var = jnp.zeros((3, NZ, NY, NX), jnp.float32)
    residual = -measured
    for iteration in range(ITERS):
        tv_gap = forward_diff(volume) - split_var + dual_var / PENALTY
        descent = back_project(residual, band_offset, interp_weight) + PENALTY * transpose_diff(tv_gap)
        projected = project(descent, band_offset, interp_weight)
        slope_field = forward_diff(descent)
        step_length = jnp.sum(descent * descent) / (
            jnp.sum(projected * projected) + PENALTY * jnp.sum(slope_field * slope_field))
        volume = volume - step_length * descent
        residual = residual - step_length * projected
        grad_volume = forward_diff(volume)
        shifted = grad_volume + dual_var / PENALTY
        split_var = shifted - jnp.clip(shifted, -TV_WEIGHT / PENALTY, TV_WEIGHT / PENALTY)
        dual_var = dual_var + PENALTY * (grad_volume - split_var)
    return volume, residual
```

```python
import functools

import jax
import jax.numpy as jnp
import numpy as np
from jax import lax
from jax.experimental import pallas as pl
from jax.experimental.pallas import tpu as pltpu
from jax.sharding import PartitionSpec as P

PENALTY = 0.5
TV_WEIGHT = 0.25
CLIP = TV_WEIGHT / PENALTY
HALF = 64
YR = 8
LANES = 128
F32 = jnp.float32
BF16 = jnp.bfloat16
VMEM_LIMIT = 48 * 1024 * 1024


def dft_parts(length, scale):
    index = np.arange(length)
    angles = 2.0 * np.pi / length * (index[:, None] * index[None, :] % length)
    return np.cos(angles) * scale, np.sin(angles) * scale


def two_parts(table):
    table = jnp.asarray(table.astype(np.float32))
    high = table.astype(BF16)
    low = (table - high.astype(F32)).astype(BF16)
    return high, low


def host_parts(table):
    table = table.astype(np.float32)
    high = table.astype(BF16)
    low = (table - high.astype(np.float32)).astype(BF16)
    return high, low


def y_matrix(ny, forward, sign):
    n = ny // YR
    cos, sin = dft_parts(n, sign * ny**-0.5)
    if forward:
        table = np.block([[cos, sin], [-sin, cos]])
    else:
        table = np.block([[cos, -sin], [sin, cos]])
    return jnp.asarray(np.concatenate(host_parts(table), axis=0))


def y_twiddle(ny):
    n = ny // YR
    angles = 2.0 * np.pi / ny * (np.arange(YR)[:, None] * np.arange(n)[None, :])
    table = np.stack([np.cos(angles), np.sin(angles)]).astype(np.float32)
    return jnp.asarray(np.ascontiguousarray(np.broadcast_to(table[..., None], (2, YR, n, LANES))))


def x_inverse_matrix(nx, ka):
    cos, sin = dft_parts(ka, nx**-0.5)
    return jnp.asarray(np.concatenate(host_parts(np.concatenate([cos, -sin], axis=0)), axis=1))


def x_forward_matrix(nx, ka):
    cos, sin = dft_parts(ka, nx**-0.5)
    return jnp.asarray(np.concatenate(host_parts(np.concatenate([cos, -sin], axis=1)), axis=1))


def x_twiddle(nx, ka):
    kb = nx // ka
    angles = 2.0 * np.pi / nx * (np.arange(kb)[:, None] * np.arange(ka)[None, :])
    table = np.stack([np.cos(angles), np.sin(angles)]).astype(np.float32)
    return jnp.asarray(np.ascontiguousarray(np.broadcast_to(table[:, :, None], (2, kb, 8, ka))))


def short_fft(planes, sign):
    n = len(planes)
    if n == 1:
        return planes
    even = short_fft(planes[0::2], sign)
    odd = short_fft(planes[1::2], sign)
    half = n // 2
    out = [None] * n
    for k in range(half):
        er, ei = even[k]
        tr, ti = odd[k]
        if 4 * k == n:
            if sign > 0:
                out[k] = (er - ti, ei + tr)
                out[k + half] = (er + ti, ei - tr)
            else:
                out[k] = (er + ti, ei - tr)
                out[k + half] = (er - ti, ei + tr)
            continue
        if k > 0:
            c = float(np.cos(2.0 * np.pi * k / n))
            s = float(sign * np.sin(2.0 * np.pi * k / n))
            if 8 * k == n:
                tr, ti = (tr - ti, ti + tr) if sign > 0 else (tr + ti, ti - tr)
                tr, ti = tr * c, ti * c
            elif 8 * k == 3 * n:
                m = float(np.sin(2.0 * np.pi * k / n))
                tr, ti = (-(tr + ti), tr - ti) if sign > 0 else (ti - tr, -(tr + ti))
                tr, ti = tr * m, ti * m
            else:
                tr, ti = tr * c - ti * s, ti * c + tr * s
        out[k] = (er + tr, ei + ti)
        out[k + half] = (er - tr, ei - ti)
    return out


def split2(x):
    high = x.astype(BF16)
    return high, (x - high.astype(F32)).astype(BF16)


def dot(a, b):
    return jnp.dot(a, b, preferred_element_type=F32)


def fold(x):
    rows, lanes = x.shape
    x = jnp.sum(x.reshape(rows // 8, 8, lanes), axis=0)
    total = x[:, :LANES]
    for i in range(1, lanes // LANES):
        total = total + x[:, i * LANES : (i + 1) * LANES]
    return total


def full_sum(x):
    return jnp.sum(jnp.sum(x, axis=0, keepdims=True), axis=1, keepdims=True)


def step_of(sums_ref):
    total = jnp.sum(sums_ref[...], axis=0)
    parts = jnp.sum(total, axis=1, keepdims=True)
    return parts[0:1] / (parts[1:2] + PENALTY * parts[2:3])


def put_sums(out_ref, values):
    rows = [jnp.sum(v, axis=0, keepdims=True) for v in values]
    index = lax.broadcasted_iota(jnp.int32, (8, LANES), 0)
    block = jnp.zeros((8, LANES), F32)
    for i, row in enumerate(rows):
        block = jnp.where(index == i, jnp.broadcast_to(row, (8, LANES)), block)
    for i in range(out_ref.shape[0]):
        out_ref[i] = block


def mix_adjoint(coef, planes):
    own, below, above = coef
    out = []
    for z in range(len(planes)):
        value = own * planes[z]
        if z + 1 < len(planes):
            value = value + below * planes[z + 1]
        if z > 0:
            value = value + above * planes[z - 1]
        out.append(value)
    return out


def mix(coef, planes):
    own, below, above = coef
    out = []
    for z in range(len(planes)):
        value = own * planes[z]
        if z > 0:
            value = value + below * planes[z - 1]
        if z + 1 < len(planes):
            value = value + above * planes[z + 1]
        out.append(value)
    return out


def y_inverse_kernel(rows, gz, data_ref, table_ref, tw_ref, out_ref, re_s, im_s, mix_s):
    ny = data_ref.shape[1]
    n = ny // YR
    gy = out_ref.shape[0] // gz
    lane = lax.broadcasted_iota(jnp.int32, (n, LANES), 1)

    def unpack(i, carry):
        part = pl.ds(pl.multiple_of(i * n, n), n)
        first = data_ref[0, part, :].astype(F32)
        second = data_ref[1, part, :].astype(F32)
        re_s[part, :] = jnp.where(lane < HALF, first, pltpu.roll(second, HALF, 1))
        im_s[part, :] = jnp.where(lane < HALF, pltpu.roll(first, HALF, 1), second)
        return carry

    lax.fori_loop(0, YR, unpack, 0)

    table = table_ref[...]
    for k in range(0, YR, 2):
        pieces = [
            jnp.concatenate([s[pl.ds(k + d, n, stride=YR), :] for d in range(2)], axis=1)
            for s in (re_s, im_s)
        ]
        both = dot(table, jnp.concatenate(pieces, axis=0).astype(BF16))
        both = both[: 2 * n] + both[2 * n :]
        for d in range(2):
            mix_s[k + d] = both[:, d * LANES : (d + 1) * LANES]

    def combine(i, carry):
        start = pl.multiple_of(i * 8, 8)
        part = pl.ds(start, 8)
        planes = []
        for k in range(YR):
            re = mix_s[k, part, :]
            im = mix_s[k, pl.ds(pl.multiple_of(n + i * 8, 8), 8), :]
            if k > 0:
                c = tw_ref[0, k, part, :]
                s = tw_ref[1, k, part, :]
                re, im = re * c - im * s, im * c + re * s
            planes.append((re, im))
        for k, (re, im) in enumerate(short_fft(planes, 1)):
            y = k * n + start
            flat = y // rows
            to = (flat % gz) * gy + flat // gz
            at = pl.ds(pl.multiple_of(y % rows, 8), 8)
            out_ref[to, 0, at, :] = re
            out_ref[to, 1, at, :] = im
        return carry

    lax.fori_loop(0, n // 8, combine, 0, unroll=2)


def y_inverse(data, rows, gz, gy):
    blocks, ny, width = data.shape
    n = ny // YR
    return pl.pallas_call(
        functools.partial(y_inverse_kernel, rows, gz),
        grid=(blocks // 2,),
        in_specs=[
            pl.BlockSpec((2, ny, width), lambda c: (c, 0, 0)),
            pl.BlockSpec((4 * n, 2 * n), lambda c: (0, 0)),
            pl.BlockSpec((2, YR, n, LANES), lambda c: (0, 0, 0, 0)),
        ],
        out_specs=pl.BlockSpec((gz * gy, 2, rows, LANES), lambda c: (0, 0, 0, c)),
        out_shape=jax.ShapeDtypeStruct((gz * gy, 2, rows, blocks * HALF), F32),
        scratch_shapes=[
            pltpu.VMEM((ny, LANES), F32),
            pltpu.VMEM((ny, LANES), F32),
            pltpu.VMEM((YR, 2 * n, LANES), F32),
        ],
        compiler_params=pltpu.CompilerParams(vmem_limit_bytes=VMEM_LIMIT),
        name="y_inverse",
    )(data, y_matrix(ny, False, -1.0), y_twiddle(ny))


def y_forward_kernel(gz, spec_ref, data_ref, table_ref, tw_ref, out_ref, re_s, im_s, mix_s):
    ny = data_ref.shape[1]
    n = ny // YR
    peers, _, rows, _ = spec_ref.shape
    gy = peers // gz

    def unpack(i, carry):
        part = pl.ds(pl.multiple_of(i * rows, rows), rows)
        source = (i % gz) * gy + i // gz
        re_s[part, :] = spec_ref[source, 0]
        im_s[part, :] = spec_ref[source, 1]
        return carry

    lax.fori_loop(0, peers, unpack, 0)

    table = table_ref[...]
    for k in range(0, YR, 2):
        pieces = [
            jnp.concatenate([s[pl.ds(k + d, n, stride=YR), :] for d in range(2)], axis=1)
            for s in (re_s, im_s)
        ]
        high, low = split2(jnp.concatenate(pieces, axis=0))
        both = dot(table, high)
        both = both[: 2 * n] + both[2 * n :] + dot(table[: 2 * n], low)
        for d in range(2):
            mix_s[k + d] = both[:, d * LANES : (d + 1) * LANES]

    lane = lax.broadcasted_iota(jnp.int32, (16, LANES), 1)

    def combine(i, carry):
        start = pl.multiple_of(i * 16, 16)
        part = pl.ds(start, 16)
        planes = []
        for k in range(YR):
            re = mix_s[k, part, :]
            im = mix_s[k, pl.ds(pl.multiple_of(n + i * 16, 16), 16), :]
            if k > 0:
                c = tw_ref[0, k, part, :]
                s = tw_ref[1, k, part, :]
                re, im = re * c + im * s, im * c - re * s
            planes.append((re, im))
        for k, (re, im) in enumerate(short_fft(planes, -1)):
            at = pl.ds(pl.multiple_of(k * n + start, 16), 16)
            first = jnp.where(lane < HALF, re, pltpu.roll(im, HALF, 1))
            second = jnp.where(lane < HALF, pltpu.roll(re, HALF, 1), im)
            out_ref[0, at, :] = first - data_ref[0, at, :].astype(F32)
            out_ref[1, at, :] = second - data_ref[1, at, :].astype(F32)
        return carry

    lax.fori_loop(0, n // 16, combine, 0)


def y_forward(spec, data, gz):
    blocks, ny, width = data.shape
    peers, _, rows, _ = spec.shape
    n = ny // YR
    return pl.pallas_call(
        functools.partial(y_forward_kernel, gz),
        grid=(blocks // 2,),
        in_specs=[
            pl.BlockSpec((peers, 2, rows, LANES), lambda c: (0, 0, 0, c)),
            pl.BlockSpec((2, ny, width), lambda c: (c, 0, 0)),
            pl.BlockSpec((4 * n, 2 * n), lambda c: (0, 0)),
            pl.BlockSpec((2, YR, n, LANES), lambda c: (0, 0, 0, 0)),
        ],
        out_specs=pl.BlockSpec((2, ny, width), lambda c: (c, 0, 0)),
        out_shape=jax.ShapeDtypeStruct((blocks, ny, width), F32),
        scratch_shapes=[
            pltpu.VMEM((ny, LANES), F32),
            pltpu.VMEM((ny, LANES), F32),
            pltpu.VMEM((YR, 2 * n, LANES), F32),
        ],
        compiler_params=pltpu.CompilerParams(vmem_limit_bytes=VMEM_LIMIT),
        name="y_forward",
    )(spec, data, y_matrix(ny, True, 1.0), y_twiddle(ny))


def plane_chunk(planes, rows):
    chunk = max(1, 512 // rows)
    while planes % chunk:
        chunk -= 1
    return chunk


def x_inverse_kernel(zs, spec_ref, coef_ref, tw_ref, table_ref, out_ref, head_ref, tail_ref, re_s, im_s):
    planes, _, rows, ka = spec_ref.shape
    kb = planes // zs

    def columns(i, carry):
        part = pl.ds(pl.multiple_of(i * 8, 8), 8)
        for start in range(0, ka, LANES):
            lanes = slice(start, start + LANES)
            mixed = [[None] * kb for _ in range(zs)]
            for k in range(kb):
                coef = [coef_ref[j, k, :, lanes] for j in range(3)]
                re = mix_adjoint(coef, [spec_ref[z * kb + k, 0, part, lanes] for z in range(zs)])
                im = mix_adjoint(coef, [spec_ref[z * kb + k, 1, part, lanes] for z in range(zs)])
                for z in range(zs):
                    mixed[z][k] = (re[z], im[z])
            for z in range(zs):
                for b, (re, im) in enumerate(short_fft(mixed[z], 1)):
                    if b > 0:
                        c = tw_ref[0, b, :, lanes]
                        s = tw_ref[1, b, :, lanes]
                        re, im = re * c - im * s, im * c + re * s
                    re_s[z * kb + b, part, lanes] = re
                    im_s[z * kb + b, part, lanes] = im
        return carry

    lax.fori_loop(0, rows // 8, columns, 0)

    chunk = plane_chunk(planes, rows)

    def multiply(i, carry):
        part = pl.ds(i * chunk, chunk)
        both = jnp.concatenate(
            [re_s[part].reshape(chunk * rows, ka), im_s[part].reshape(chunk * rows, ka)], axis=1
        )
        high, low = split2(both)
        value = dot(high, table_ref[...])
        value = value[:, :ka] + value[:, ka:] + dot(low, table_ref[:, :ka])
        out_ref[part] = value.reshape(chunk, rows, ka)
        return carry

    lax.fori_loop(0, planes // chunk, multiply, 0)

    for p in range(planes):
        for r in range(head_ref.shape[0]):
            head_ref[r, p : p + 1, :] = out_ref[p, r : r + 1, :]
        tail_ref[p : p + 1, :] = out_ref[p, rows - 1 : rows, :]


def x_inverse(spec, coef, zs, nx):
    planes, _, rows, ka = spec.shape
    vmem = pl.BlockSpec(memory_space=pltpu.VMEM)
    return pl.pallas_call(
        functools.partial(x_inverse_kernel, zs),
        in_specs=[vmem] * 4,
        out_specs=[vmem] * 3,
        out_shape=[
            jax.ShapeDtypeStruct((planes, rows, ka), F32),
            jax.ShapeDtypeStruct((2, planes, ka), F32),
            jax.ShapeDtypeStruct((planes, ka), F32),
        ],
        scratch_shapes=[pltpu.VMEM((planes, rows, ka), F32)] * 2,
        compiler_params=pltpu.CompilerParams(vmem_limit_bytes=VMEM_LIMIT),
        name="x_inverse",
    )(spec, coef, x_twiddle(nx, ka), x_inverse_matrix(nx, ka))


def forward_into(zs, field_ref, coef_ref, tw_ref, table_ref, spec_ref, re_s, im_s):
    planes, rows, ka = field_ref.shape
    kb = planes // zs
    chunk = plane_chunk(planes, rows)

    def multiply(i, carry):
        part = pl.ds(i * chunk, chunk)
        high, low = split2(field_ref[part].reshape(chunk * rows, ka))
        value = dot(high, table_ref[...])
        value = value[:, : 2 * ka] + value[:, 2 * ka :] + dot(low, table_ref[:, : 2 * ka])
        re_s[part] = value[:, :ka].reshape(chunk, rows, ka)
        im_s[part] = value[:, ka:].reshape(chunk, rows, ka)
        return carry

    lax.fori_loop(0, planes // chunk, multiply, 0)

    def columns(i, total):
        part = pl.ds(pl.multiple_of(i * 8, 8), 8)
        for start in range(0, ka, LANES):
            lanes = slice(start, start + LANES)
            spectra = []
            for z in range(zs):
                turned = []
                for b in range(kb):
                    re = re_s[z * kb + b, part, lanes]
                    im = im_s[z * kb + b, part, lanes]
                    if b > 0:
                        c = tw_ref[0, b, :, lanes]
                        s = tw_ref[1, b, :, lanes]
                        re, im = re * c + im * s, im * c - re * s
                    turned.append((re, im))
                spectra.append(short_fft(turned, -1))
            for k in range(kb):
                coef = [coef_ref[j, k, :, lanes] for j in range(3)]
                for p in range(2):
                    for z, value in enumerate(mix(coef, [spectra[z][k][p] for z in range(zs)])):
                        spec_ref[z * kb + k, p, part, lanes] = value
                        total = total + value * value
        return total

    return lax.fori_loop(0, rows // 8, columns, jnp.zeros((8, LANES), F32))


def next_plane(field_ref, p, kb):
    rows, ka = field_ref.shape[1:]
    if (p + 1) % kb:
        return field_ref[p + 1]
    lane = lax.broadcasted_iota(jnp.int32, (rows, ka), 1)
    return jnp.where(lane == ka - 1, field_ref[p], pltpu.roll(field_ref[p + 1 - kb], ka - 1, 1))


def prev_plane(field_ref, p, kb):
    rows, ka = field_ref.shape[1:]
    if p % kb:
        return field_ref[p - 1]
    lane = lax.broadcasted_iota(jnp.int32, (rows, ka), 1)
    return jnp.where(lane == 0, field_ref[p], pltpu.roll(field_ref[p + kb - 1], 1, 1))


def first_kernel(zs, field_ref, coef_ref, tw_ref, table_ref, spec_ref, sums_ref, re_s, im_s):
    planes, rows, ka = field_ref.shape
    kb = planes // zs
    projected = forward_into(zs, field_ref, coef_ref, tw_ref, table_ref, spec_ref, re_s, im_s)
    row = lax.broadcasted_iota(jnp.int32, (rows, ka), 0)
    square = jnp.zeros((8, LANES), F32)
    slope = jnp.zeros((8, LANES), F32)
    for p in range(planes):
        here = field_ref[p]
        square = square + fold(here * here)
        along_x = next_plane(field_ref, p, kb) - here
        along_y = jnp.where(row == rows - 1, 0.0, pltpu.roll(here, rows - 1, 0) - here)
        terms = along_x * along_x + along_y * along_y
        if p + kb < planes:
            along_z = field_ref[p + kb] - here
            terms = terms + along_z * along_z
        slope = slope + fold(terms)
    sums_ref[0] = square
    sums_ref[1] = projected
    sums_ref[2] = slope


def first_projection(field, coef, zs, nx):
    planes, rows, ka = field.shape
    vmem = pl.BlockSpec(memory_space=pltpu.VMEM)
    return pl.pallas_call(
        functools.partial(first_kernel, zs),
        in_specs=[vmem] * 4,
        out_specs=[vmem] * 2,
        out_shape=[
            jax.ShapeDtypeStruct((planes, 2, rows, ka), F32),
            jax.ShapeDtypeStruct((3, 8, LANES), F32),
        ],
        scratch_shapes=[pltpu.VMEM((planes, rows, ka), F32)] * 2,
        compiler_params=pltpu.CompilerParams(vmem_limit_bytes=VMEM_LIMIT),
        name="first_projection",
    )(field, coef, x_twiddle(nx, ka), x_forward_matrix(nx, ka))


def border_kernel(edge_ref, sums_ref, tail_ref, next_ref, out_ref):
    step = (next_ref[0] - tail_ref[...]) * jnp.where(edge_ref[1] > 0, 0.0, 1.0)
    put_sums(out_ref, [sums_ref[0], sums_ref[1], sums_ref[2] + fold(step * step)])


def border_sums(edge, sums, tail, next_head, devices):
    vmem = pl.BlockSpec(memory_space=pltpu.VMEM)
    return pl.pallas_call(
        border_kernel,
        in_specs=[pl.BlockSpec(memory_space=pltpu.SMEM)] + [vmem] * 3,
        out_specs=vmem,
        out_shape=jax.ShapeDtypeStruct((devices, 8, LANES), F32),
        name="border_sums",
    )(edge, sums, tail, next_head)


def second_kernel(
    zs, edge_ref, sums_ref, d0_ref, nd0_ref, tail_ref, prev_ref, next_ref, nnext_ref,
    coef_ref, tw_ref, table_ref, d1_ref, spec_ref, eta_ref, out_ref, re_s, im_s, row_s,
):
    planes, rows, ka = d0_ref.shape
    kb = planes // zs
    eta_here = step_of(sums_ref)
    eta_ref[...] = jnp.broadcast_to(eta_here, (8, LANES))
    eta = jnp.max(eta_here)
    first = edge_ref[0] > 0
    last = edge_ref[1] > 0

    def shrink(difference):
        return jnp.clip(-eta * difference, -CLIP, CLIP)

    lane2 = lax.broadcasted_iota(jnp.int32, (kb, ka), 1)
    row2 = lax.broadcasted_iota(jnp.int32, (kb, ka), 0)
    for z in range(zs):
        part = slice(z * kb, (z + 1) * kb)
        here = next_ref[0, part, :]
        value = here - eta * nnext_ref[0, part, :]
        up = pltpu.roll(here, kb - 1, 0)
        up = jnp.where(
            row2 == kb - 1, jnp.where(lane2 == ka - 1, here, pltpu.roll(up, ka - 1, 1)), up
        )
        down = pltpu.roll(here, 1, 0)
        down = jnp.where(row2 == 0, jnp.where(lane2 == 0, here, pltpu.roll(down, 1, 1)), down)
        value = value + shrink(here - down) - shrink(up - here)
        value = value + shrink(here - tail_ref[part, :]) - shrink(next_ref[1, part, :] - here)
        if z > 0:
            value = value + shrink(here - next_ref[0, (z - 1) * kb : z * kb, :])
        if z + 1 < zs:
            value = value - shrink(next_ref[0, (z + 1) * kb : (z + 2) * kb, :] - here)
        row_s[part, :] = value

    row = lax.broadcasted_iota(jnp.int32, (rows, ka), 0)
    square = jnp.zeros((8, LANES), F32)
    for p in range(planes):
        here = d0_ref[p]
        value = here - eta * nd0_ref[p]
        value = value + shrink(here - prev_plane(d0_ref, p, kb))
        value = value - shrink(next_plane(d0_ref, p, kb) - here)
        below = jnp.where(last, here[rows - 1 :, :], next_ref[0, p : p + 1, :])
        above = jnp.where(first, here[:1, :], prev_ref[p : p + 1, :])
        upper = shrink(jnp.where(row == rows - 1, below, pltpu.roll(here, rows - 1, 0)) - here)
        lower = jnp.where(row == 0, shrink(here[:1, :] - above), pltpu.roll(upper, 1, 0))
        value = value + lower - upper
        if p >= kb:
            value = value + shrink(here - d0_ref[p - kb])
        if p + kb < planes:
            value = value - shrink(d0_ref[p + kb] - here)
        d1_ref[p] = value
        square = square + fold(value * value)

    slope = jnp.zeros((8, LANES), F32)
    for p in range(planes):
        here = d1_ref[p]
        along_x = next_plane(d1_ref, p, kb) - here
        below = jnp.where(last, here[rows - 1 :, :], row_s[p : p + 1, :])
        along_y = jnp.where(row == rows - 1, below, pltpu.roll(here, rows - 1, 0)) - here
        terms = along_x * along_x + along_y * along_y
        if p + kb < planes:
            along_z = d1_ref[p + kb] - here
            terms = terms + along_z * along_z
        slope = slope + fold(terms)

    projected = forward_into(zs, d1_ref, coef_ref, tw_ref, table_ref, spec_ref, re_s, im_s)
    put_sums(out_ref, [square, projected, slope])


def second_descent(edge, sums, d0, nd0, tail, prev_tail, next_head, next_nhead, coef, zs, nx):
    planes, rows, ka = d0.shape
    devices = sums.shape[0]
    vmem = pl.BlockSpec(memory_space=pltpu.VMEM)
    return pl.pallas_call(
        functools.partial(second_kernel, zs),
        in_specs=[pl.BlockSpec(memory_space=pltpu.SMEM)] + [vmem] * 10,
        out_specs=[vmem] * 4,
        out_shape=[
            jax.ShapeDtypeStruct((planes, rows, ka), F32),
            jax.ShapeDtypeStruct((planes, 2, rows, ka), F32),
            jax.ShapeDtypeStruct((8, LANES), F32),
            jax.ShapeDtypeStruct((devices, 8, LANES), F32),
        ],
        scratch_shapes=[
            pltpu.VMEM((planes, rows, ka), F32),
            pltpu.VMEM((planes, rows, ka), F32),
            pltpu.VMEM((planes, ka), F32),
        ],
        compiler_params=pltpu.CompilerParams(vmem_limit_bytes=VMEM_LIMIT),
        name="second_descent",
    )(
        edge, sums, d0, nd0, tail, prev_tail, next_head, next_nhead, coef,
        x_twiddle(nx, ka), x_forward_matrix(nx, ka),
    )


def combine_kernel(sums_ref, eta_ref, first_ref, second_ref, out_ref, steps_ref):
    eta0 = jnp.max(eta_ref[...])
    eta1 = jnp.max(step_of(sums_ref))
    out_ref[...] = -(eta0 * first_ref[...] + eta1 * second_ref[...])
    steps_ref[0] = eta_ref[...]
    steps_ref[1] = jnp.full((8, LANES), eta1, F32)


def combine_spectra(sums, eta, first, second):
    planes, parts, rows, ka = first.shape
    devices = sums.shape[0]
    count = 4 if planes % 4 == 0 else 1
    block = pl.BlockSpec((count, parts, rows, ka), lambda i: (i, 0, 0, 0))
    return pl.pallas_call(
        combine_kernel,
        grid=(planes // count,),
        in_specs=[
            pl.BlockSpec((devices, 8, LANES), lambda i: (0, 0, 0)),
            pl.BlockSpec((8, LANES), lambda i: (0, 0)),
            block,
            block,
        ],
        out_specs=[block, pl.BlockSpec((2, 8, LANES), lambda i: (0, 0, 0))],
        out_shape=[
            jax.ShapeDtypeStruct(first.shape, F32),
            jax.ShapeDtypeStruct((2, 8, LANES), F32),
        ],
        name="combine_spectra",
    )(sums, eta, first, second)


def everywhere(sums):
    return lax.all_to_all(sums, ("gz", "gy"), 0, 0, tiled=True)


def shards(data, band_offset, interp_weight):
    gz = lax.axis_size("gz")
    gy = lax.axis_size("gy")
    devices = gz * gy
    data = data[0]
    blocks, ny, width = data.shape
    rows = ny // devices
    ka = blocks * HALF
    nx = ka * gy

    flat = lax.axis_index("gy") * gz + lax.axis_index("gz")
    edge = jnp.stack([(flat == 0).astype(jnp.int32), (flat == devices - 1).astype(jnp.int32)])
    order = [(i % gz) * gy + i // gz for i in range(devices)]
    up = [(order[i + 1], order[i]) for i in range(devices - 1)]
    down = [(order[i], order[i + 1]) for i in range(devices - 1)]

    lower = band_offset < 0
    weight = interp_weight
    coef = jnp.stack(
        [
            jnp.where(lower, weight[1], weight[0]),
            jnp.where(lower, weight[0], 0.0),
            jnp.where(lower, 0.0, weight[1]),
        ]
    ).reshape(3, gy, 1, ka)
    coef = jnp.broadcast_to(coef, (3, gy, 8, ka))

    spec = y_inverse(data, rows, gz, gy)
    spec = lax.all_to_all(spec, ("gz", "gy"), 0, 0, tiled=True)
    d0, head, tail = x_inverse(spec, coef, gz, nx)
    next_head = lax.ppermute(head, ("gz", "gy"), up)
    prev_tail = lax.ppermute(tail, ("gz", "gy"), down)
    spec0, sums = first_projection(d0, coef, gz, nx)
    sums = everywhere(border_sums(edge, sums, tail, next_head, devices))
    nd0, nhead, _ = x_inverse(spec0, coef, gz, nx)
    next_nhead = lax.ppermute(nhead, ("gz", "gy"), up)
    d1, spec1, eta, sums = second_descent(
        edge, sums, d0, nd0, tail, prev_tail, next_head, next_nhead, coef, gz, nx
    )
    sums = everywhere(sums)
    spec, steps = combine_spectra(sums, eta, spec0, spec1)
    spec = lax.all_to_all(spec, ("gz", "gy"), 0, 0, tiled=True)
    residual = y_forward(spec, data, gz)

    volume = -(steps[0, 0, 0] * d0 + steps[1, 0, 0] * d1)
    volume = volume.reshape(gz, gy, rows, ka).transpose(0, 2, 3, 1).reshape(gz, rows, nx)
    volume = lax.all_to_all(volume, "gz", 0, 1, tiled=True)
    return (volume, residual[None])


NX = 4096
NY = 2048
XB = 64
YB = 64
ITERS = 2
XA = 64
YA = 32
PRECISE = lax.Precision.HIGHEST


def with_halo(block, sides, width):
    for axis, dim in sides:
        count = lax.axis_size(axis)
        forward = [(i, i + 1) for i in range(count - 1)]
        backward = [(target, source) for source, target in forward]
        low = lax.ppermute(
            lax.slice_in_dim(block, block.shape[dim] - width, None, axis=dim), axis, forward
        )
        high = lax.ppermute(lax.slice_in_dim(block, 0, width, axis=dim), axis, backward)
        block = jnp.concatenate([low, block, high], axis=dim)
    return block


def from_behind(block, axis, distance):
    devices = range(lax.axis_size(axis))
    route = [(i - distance, i) for i in devices if i - distance in devices]
    return lax.ppermute(block, axis, route)


def unit_table(length):
    counter = jnp.arange(length, dtype=jnp.int32)
    phase_int = counter[:, None] * counter[None, :] % length
    angles = 2.0 * jnp.pi / length * phase_int.astype(jnp.float32)
    factor = length ** (-0.5)
    return (jnp.cos(angles) * factor, jnp.sin(angles) * factor)


def twiddle_table(row_len, col_len, period):
    phase_int = (
        jnp.arange(row_len, dtype=jnp.int32)[:, None]
        * jnp.arange(col_len, dtype=jnp.int32)[None, :]
        % period
    )
    angles = 2.0 * jnp.pi / period * phase_int.astype(jnp.float32)
    return (jnp.cos(angles), jnp.sin(angles))


def split_parts(packed):
    half_width = packed.shape[-1] // 2
    return (packed[..., :half_width], packed[..., half_width:])


def join_parts(real_part, imag_part):
    return jnp.concatenate([real_part, imag_part], axis=-1)


def complex_contract(packed, cos_table, sin_table, subscripts, conj_sign):
    cos_out = jnp.einsum(subscripts, packed, cos_table, precision=PRECISE)
    sin_out = jnp.einsum(subscripts, packed, sin_table, precision=PRECISE)
    cos_re, cos_im = split_parts(cos_out)
    sin_re, sin_im = split_parts(sin_out)
    return join_parts(cos_re - conj_sign * sin_im, cos_im + conj_sign * sin_re)


def rotate(packed, cos_table, sin_table, conj_sign):
    real_part, imag_part = split_parts(packed)
    return join_parts(
        real_part * cos_table - conj_sign * imag_part * sin_table,
        imag_part * cos_table + conj_sign * real_part * sin_table,
    )


def forward_x(volume):
    slices, row_count = (volume.shape[0], volume.shape[1])
    cos_a, sin_a = unit_table(XA)
    cos_b, sin_b = unit_table(XB)
    first_table = jnp.concatenate([cos_a, -sin_a], axis=1)
    grid_view = volume.reshape(slices, row_count, XA, XB)
    mixing = jnp.einsum("zyab,am->zybm", grid_view, first_table, precision=PRECISE)
    tw_cos, tw_sin = twiddle_table(XB, XA, NX)
    mixing = rotate(mixing, tw_cos, tw_sin, -1.0)
    return complex_contract(mixing, cos_b, sin_b, "zybm,bl->zlym", -1.0)


def inverse_x(packed):
    slices, row_count = (packed.shape[0], packed.shape[2])
    cos_a, sin_a = unit_table(XA)
    cos_b, sin_b = unit_table(XB)
    mixing = complex_contract(packed, cos_b, sin_b, "zlym,lb->zybm", 1.0)
    tw_cos, tw_sin = twiddle_table(XB, XA, NX)
    mixing = rotate(mixing, tw_cos, tw_sin, 1.0)
    last_table = jnp.concatenate([cos_a, -sin_a], axis=0)
    grid_view = jnp.einsum("zybm,ma->zyab", mixing, last_table, precision=PRECISE)
    return grid_view.reshape(slices, row_count, NX)


def forward_y(packed):
    slices, blocks, width = (packed.shape[0], packed.shape[1], packed.shape[3])
    cos_a, sin_a = unit_table(YA)
    cos_b, sin_b = unit_table(YB)
    grid_view = packed.reshape(slices, blocks, YA, YB, width)
    mixing = complex_contract(grid_view, cos_a, sin_a, "zjcdm,ck->zjkdm", -1.0)
    tw_cos, tw_sin = twiddle_table(YA, YB, NY)
    mixing = rotate(mixing, tw_cos[:, :, None], tw_sin[:, :, None], -1.0)
    result = complex_contract(mixing, cos_b, sin_b, "zjkdm,dl->zjlkm", -1.0)
    return result.reshape(slices, blocks, NY, width)


def inverse_y(packed):
    slices, blocks, width = (packed.shape[0], packed.shape[1], packed.shape[3])
    cos_a, sin_a = unit_table(YA)
    cos_b, sin_b = unit_table(YB)
    grid_view = packed.reshape(slices, blocks, YB, YA, width)
    mixing = complex_contract(grid_view, cos_b, sin_b, "zjlkm,ld->zjkdm", 1.0)
    tw_cos, tw_sin = twiddle_table(YA, YB, NY)
    mixing = rotate(mixing, tw_cos[:, :, None], tw_sin[:, :, None], 1.0)
    result = complex_contract(mixing, cos_a, sin_a, "zjkdm,kc->zjcdm", 1.0)
    return result.reshape(slices, blocks, NY, width)


def tilt_coefficients(band_offset, interp_weight, first_block, blocks):
    offsets = lax.dynamic_slice_in_dim(band_offset.reshape(XB, XA), first_block, blocks, 0)
    weights = lax.dynamic_slice_in_dim(interp_weight.reshape(2, XB, XA), first_block, blocks, 1)
    lower_tap = (jnp.concatenate([offsets, offsets], axis=1) < 0)[:, None, :]
    first_weight = jnp.concatenate([weights[0], weights[0]], axis=1)[:, None, :]
    second_weight = jnp.concatenate([weights[1], weights[1]], axis=1)[:, None, :]
    return (lower_tap, first_weight, second_weight)


def tilt(field_in, coefficients, adjoint):
    lower_tap, first_weight, second_weight = coefficients
    padded = with_halo(field_in, (("gz", 0),), 1)
    below_rim = padded[:-2]
    middle = padded[1:-1]
    above_rim = padded[2:]
    if adjoint:
        return jnp.where(
            lower_tap,
            first_weight * above_rim + second_weight * middle,
            first_weight * middle + second_weight * below_rim,
        )
    return jnp.where(
        lower_tap,
        first_weight * below_rim + second_weight * middle,
        first_weight * middle + second_weight * above_rim,
    )


def to_pencil(slab_part):
    return lax.all_to_all(slab_part, "gy", split_axis=1, concat_axis=2, tiled=True)


def to_slab(pencil_part):
    return lax.all_to_all(pencil_part, "gy", split_axis=2, concat_axis=1, tiled=True)


def back_project(packed, pencil_coef):
    return inverse_x(to_slab(inverse_y(tilt(packed, pencil_coef, True))))


def edge_masks(slices, row_count):
    z_global = lax.axis_index("gz") * slices + jnp.arange(slices, dtype=jnp.int32)
    y_global = lax.axis_index("gy") * row_count + jnp.arange(row_count, dtype=jnp.int32)
    keep_z = (z_global < slices * lax.axis_size("gz") - 1).astype(jnp.float32)[:, None, None]
    keep_y = (y_global < row_count * lax.axis_size("gy") - 1).astype(jnp.float32)[None, :, None]
    return (keep_z, keep_y)


def forward_diff(field_in, keep_z, keep_y):
    slices, row_count = (field_in.shape[0], field_in.shape[1])
    next_z = from_behind(field_in, "gz", -1)
    next_y = from_behind(field_in[:, :1], "gy", -1)
    along_z = (jnp.concatenate([field_in[1:], next_z], axis=0) - field_in) * keep_z
    along_y = (jnp.concatenate([field_in[:, 1:], next_y], axis=1) - field_in) * keep_y
    zero_col = jnp.zeros((slices, row_count, 1), jnp.float32)
    along_x = jnp.concatenate([field_in[:, :, 1:] - field_in[:, :, :-1], zero_col], axis=2)
    return jnp.stack([along_z, along_y, along_x])


def transpose_diff(components, keep_z, keep_y):
    slices, row_count = (components.shape[1], components.shape[2])
    zero_col = jnp.zeros((slices, row_count, 1), jnp.float32)
    comp_z = components[0] * keep_z
    comp_y = components[1] * keep_y
    comp_x = jnp.concatenate([components[2][:, :, :-1], zero_col], axis=2)
    prev_z = from_behind(comp_z, "gz", 1)
    prev_y = from_behind(comp_y[:, -1:], "gy", 1)
    result = jnp.concatenate([prev_z, comp_z[:-1]], axis=0) - comp_z
    result = result + jnp.concatenate([prev_y, comp_y[:, :-1]], axis=1) - comp_y
    result = result + jnp.concatenate([zero_col, comp_x[:, :, :-1]], axis=2) - comp_x
    return result


def plain_shards(data, band_offset, interp_weight):
    slices = data.shape[0]
    blocks = data.shape[1]
    width = data.shape[3]
    row_count = NY // lax.axis_size("gy")
    slab_coef = tilt_coefficients(band_offset, interp_weight, 0, XB)
    pencil_coef = tilt_coefficients(
        band_offset, interp_weight, lax.axis_index("gy") * blocks, blocks
    )
    keep_z, keep_y = edge_masks(slices, row_count)
    measured = data.astype(jnp.float32)
    volume = jnp.zeros((slices, row_count, NX), jnp.float32)
    grad_volume = jnp.zeros((3, slices, row_count, NX), jnp.float32)
    split_var = grad_volume
    dual_var = grad_volume
    data_back = back_project(measured, pencil_coef)
    normal_part = jnp.zeros_like(volume)
    tilted = jnp.zeros((slices, XB, row_count, width), jnp.float32)
    for iteration in range(ITERS):
        data_grad = normal_part - data_back
        if iteration > 0:
            tv_gap = grad_volume - split_var + dual_var / PENALTY
            descent = data_grad + PENALTY * transpose_diff(tv_gap, keep_z, keep_y)
        else:
            descent = data_grad
        slope_field = forward_diff(descent, keep_z, keep_y)
        projected = tilt(forward_x(descent), slab_coef, False)
        line_totals = lax.psum(
            (
                jnp.sum(descent * descent),
                jnp.sum(projected * projected),
                jnp.sum(slope_field * slope_field),
            ),
            ("gz", "gy"),
        )
        step_length = line_totals[0] / (line_totals[1] + PENALTY * line_totals[2])
        volume = volume - step_length * descent
        grad_volume = grad_volume - step_length * slope_field
        tilted = tilted - step_length * projected
        if iteration + 1 < ITERS:
            normal_part = normal_part - step_length * inverse_x(tilt(projected, slab_coef, True))
        if iteration + 1 < ITERS:
            shifted = grad_volume + dual_var / PENALTY
            split_var = shifted - jnp.clip(shifted, -TV_WEIGHT / PENALTY, TV_WEIGHT / PENALTY)
            dual_var = PENALTY * (grad_volume - split_var)
    residual = forward_y(to_pencil(tilted)) - measured
    return (volume, residual)


def tiles_fit(mesh, ny, blocks):
    rows = ny // (mesh.shape["gz"] * mesh.shape["gy"])
    return rows % 16 == 0 and blocks // mesh.shape["gy"] % 2 == 0


def solution(mesh):
    in_specs = (P("gz", "gy", None, None), P(), P())
    out_specs = (P("gz", "gy", None), P("gz", "gy", None, None))

    def run(data, band_offset, interp_weight):
        body = shards if tiles_fit(mesh, data.shape[2], data.shape[1]) else plain_shards
        call = jax.shard_map(
            body, mesh=mesh, in_specs=in_specs, out_specs=out_specs, check_vma=False
        )
        return call(data, band_offset, interp_weight)

    return run
```

```python
import functools

import jax
import jax.numpy as jnp
import numpy as np
from jax import lax
from jax.experimental import pallas as pl
from jax.experimental.pallas import tpu as pltpu
from jax.sharding import PartitionSpec as P

PENALTY = 0.5
TV_WEIGHT = 0.25
CLIP = TV_WEIGHT / PENALTY
HALF = 64
YR = 8
LANES = 128
F32 = jnp.float32
BF16 = jnp.bfloat16
VMEM_LIMIT = 48 * 1024 * 1024


def dft_parts(length, scale):
    index = np.arange(length)
    angles = 2.0 * np.pi / length * (index[:, None] * index[None, :] % length)
    return np.cos(angles) * scale, np.sin(angles) * scale


def two_parts(table):
    table = jnp.asarray(table.astype(np.float32))
    high = table.astype(BF16)
    low = (table - high.astype(F32)).astype(BF16)
    return high, low


def host_parts(table):
    table = table.astype(np.float32)
    high = table.astype(BF16)
    low = (table - high.astype(np.float32)).astype(BF16)
    return high, low


def y_matrix(ny, forward, sign):
    n = ny // YR
    cos, sin = dft_parts(n, sign * ny**-0.5)
    if forward:
        table = np.block([[cos, sin], [-sin, cos]])
    else:
        table = np.block([[cos, -sin], [sin, cos]])
    return jnp.asarray(np.concatenate(host_parts(table), axis=0))


def y_twiddle(ny):
    n = ny // YR
    angles = 2.0 * np.pi / ny * (np.arange(YR)[:, None] * np.arange(n)[None, :])
    table = np.stack([np.cos(angles), np.sin(angles)]).astype(np.float32)
    return jnp.asarray(np.ascontiguousarray(np.broadcast_to(table[..., None], (2, YR, n, LANES))))


def x_inverse_matrix(nx, ka):
    cos, sin = dft_parts(ka, nx**-0.5)
    return np.concatenate(host_parts(np.concatenate([cos, -sin], axis=0)), axis=1)


def x_forward_matrix(nx, ka):
    cos, sin = dft_parts(ka, nx**-0.5)
    return jnp.asarray(np.concatenate(host_parts(np.concatenate([cos, -sin], axis=1)), axis=1))


def x_twiddle(nx, ka):
    kb = nx // ka
    angles = 2.0 * np.pi / nx * (np.arange(kb)[:, None] * np.arange(ka)[None, :])
    table = np.stack([np.cos(angles), np.sin(angles)]).astype(np.float32)
    return jnp.asarray(np.ascontiguousarray(np.broadcast_to(table[:, :, None], (2, kb, 8, ka))))


def short_fft(planes, sign):
    n = len(planes)
    if n == 1:
        return planes
    even = short_fft(planes[0::2], sign)
    odd = short_fft(planes[1::2], sign)
    half = n // 2
    out = [None] * n
    for k in range(half):
        er, ei = even[k]
        tr, ti = odd[k]
        if 4 * k == n:
            if sign > 0:
                out[k] = (er - ti, ei + tr)
                out[k + half] = (er + ti, ei - tr)
            else:
                out[k] = (er + ti, ei - tr)
                out[k + half] = (er - ti, ei + tr)
            continue
        if k > 0:
            c = float(np.cos(2.0 * np.pi * k / n))
            s = float(sign * np.sin(2.0 * np.pi * k / n))
            if 8 * k == n:
                tr, ti = (tr - ti, ti + tr) if sign > 0 else (tr + ti, ti - tr)
                tr, ti = tr * c, ti * c
            elif 8 * k == 3 * n:
                m = float(np.sin(2.0 * np.pi * k / n))
                tr, ti = (-(tr + ti), tr - ti) if sign > 0 else (ti - tr, -(tr + ti))
                tr, ti = tr * m, ti * m
            else:
                tr, ti = tr * c - ti * s, ti * c + tr * s
        out[k] = (er + tr, ei + ti)
        out[k + half] = (er - tr, ei - ti)
    return out


def split2(x):
    high = x.astype(BF16)
    return high, (x - high.astype(F32)).astype(BF16)


def dot(a, b):
    return jnp.dot(a, b, preferred_element_type=F32)


def fold(x):
    rows, lanes = x.shape
    x = jnp.sum(x.reshape(rows // 8, 8, lanes), axis=0)
    total = x[:, :LANES]
    for i in range(1, lanes // LANES):
        total = total + x[:, i * LANES : (i + 1) * LANES]
    return total


def full_sum(x):
    return jnp.sum(jnp.sum(x, axis=0, keepdims=True), axis=1, keepdims=True)


def step_of(sums_ref):
    total = jnp.sum(sums_ref[...], axis=0)
    parts = jnp.sum(total, axis=1, keepdims=True)
    return parts[0:1] / (parts[1:2] + PENALTY * parts[2:3])


def put_sums(out_ref, values):
    rows = [jnp.sum(v, axis=0, keepdims=True) for v in values]
    index = lax.broadcasted_iota(jnp.int32, (8, LANES), 0)
    block = jnp.zeros((8, LANES), F32)
    for i, row in enumerate(rows):
        block = jnp.where(index == i, jnp.broadcast_to(row, (8, LANES)), block)
    for i in range(out_ref.shape[0]):
        out_ref[i] = block


def mix_adjoint(coef, planes):
    own, below, above = coef
    out = []
    for z in range(len(planes)):
        value = own * planes[z]
        if z + 1 < len(planes):
            value = value + below * planes[z + 1]
        if z > 0:
            value = value + above * planes[z - 1]
        out.append(value)
    return out


def mix(coef, planes):
    own, below, above = coef
    out = []
    for z in range(len(planes)):
        value = own * planes[z]
        if z > 0:
            value = value + below * planes[z - 1]
        if z + 1 < len(planes):
            value = value + above * planes[z + 1]
        out.append(value)
    return out


def y_inverse_kernel(gz, edge_ref, data_ref, table_ref, tw_ref, *refs):
    out_refs, (re_s, im_s, mix_s) = refs[:gz], refs[gz:]
    ny = data_ref.shape[1]
    n = ny // YR
    rows = out_refs[0].shape[2]
    lane = lax.broadcasted_iota(jnp.int32, (n, LANES), 1)

    def unpack(i, carry):
        part = pl.ds(pl.multiple_of(i * n, n), n)
        first = data_ref[0, part, :].astype(F32)
        second = data_ref[1, part, :].astype(F32)
        re_s[part, :] = jnp.where(lane < HALF, first, pltpu.roll(second, HALF, 1))
        im_s[part, :] = jnp.where(lane < HALF, pltpu.roll(first, HALF, 1), second)
        return carry

    lax.fori_loop(0, YR, unpack, 0)

    table = table_ref[...]
    for k in range(0, YR, 2):
        pieces = [
            jnp.concatenate([s[pl.ds(k + d, n, stride=YR), :] for d in range(2)], axis=1)
            for s in (re_s, im_s)
        ]
        both = dot(table, jnp.concatenate(pieces, axis=0).astype(BF16))
        both = both[: 2 * n] + both[2 * n :]
        for d in range(2):
            mix_s[k + d] = both[:, d * LANES : (d + 1) * LANES]

    steps = rows // 8
    for r in range(gz):
        core = lax.rem(edge_ref[2] + r, gz)

        def combine(i, carry):
            y2 = ((i // steps) * gz + core) * rows + lax.rem(i, steps) * 8
            part = pl.ds(pl.multiple_of(y2, 8), 8)
            planes = []
            for k in range(YR):
                re = mix_s[k, part, :]
                im = mix_s[k, pl.ds(pl.multiple_of(n + y2, 8), 8), :]
                if k > 0:
                    c = tw_ref[0, k, part, :]
                    s = tw_ref[1, k, part, :]
                    re, im = re * c - im * s, im * c + re * s
                planes.append((re, im))
            at = pl.ds(pl.multiple_of(lax.rem(i, steps) * 8, 8), 8)
            for k, (re, im) in enumerate(short_fft(planes, 1)):
                to = k * (n // (gz * rows)) + i // steps
                out_refs[r][to, 0, at, :] = re
                out_refs[r][to, 1, at, :] = im
            return carry

        lax.fori_loop(0, n // gz // 8, combine, 0, unroll=2)


def y_inverse(edge, data, c, rows, gz, gy):
    _, ny, width = data.shape
    n = ny // YR
    piece = (gy, 2, rows, LANES)
    return pl.pallas_call(
        functools.partial(y_inverse_kernel, gz),
        grid=(1,),
        in_specs=[
            pl.BlockSpec(memory_space=pltpu.SMEM),
            pl.BlockSpec((2, ny, width), lambda i: (c, 0, 0)),
            pl.BlockSpec((4 * n, 2 * n), lambda i: (0, 0)),
            pl.BlockSpec((2, YR, n, LANES), lambda i: (0, 0, 0, 0)),
        ],
        out_specs=[pl.BlockSpec(piece, lambda i: (0, 0, 0, 0))] * gz,
        out_shape=[jax.ShapeDtypeStruct(piece, F32)] * gz,
        scratch_shapes=[
            pltpu.VMEM((ny, LANES), F32),
            pltpu.VMEM((ny, LANES), F32),
            pltpu.VMEM((YR, 2 * n, LANES), F32),
        ],
        compiler_params=pltpu.CompilerParams(vmem_limit_bytes=VMEM_LIMIT),
        cost_estimate=pl.CostEstimate(
            flops=16 * n * n * YR * LANES, bytes_accessed=8 * ny * LANES, transcendentals=0
        ),
        name="y_inverse",
    )(edge, data, y_matrix(ny, False, -1.0), y_twiddle(ny))


def y_forward_kernel(gz, edge_ref, *refs):
    spec_refs, refs = refs[:gz], refs[gz:]
    data_ref, table_ref, tw_ref = refs[:3]
    out_ref, re_s, im_s, mix_s = refs[-4:]
    ny = data_ref.shape[1]
    n = ny // YR
    gy, _, rows, _ = spec_refs[0].shape

    for r in range(gz):
        core = lax.rem(edge_ref[2] + gz - r, gz)

        def unpack(i, carry):
            part = pl.ds(pl.multiple_of((i * gz + core) * rows, rows), rows)
            re_s[part, :] = spec_refs[r][i, 0]
            im_s[part, :] = spec_refs[r][i, 1]
            return carry

        lax.fori_loop(0, gy, unpack, 0)

    table = table_ref[...]
    for k in range(0, YR, 2):
        pieces = [
            jnp.concatenate([s[pl.ds(k + d, n, stride=YR), :] for d in range(2)], axis=1)
            for s in (re_s, im_s)
        ]
        high, low = split2(jnp.concatenate(pieces, axis=0))
        both = dot(table, high)
        both = both[: 2 * n] + both[2 * n :] + dot(table[: 2 * n], low)
        for d in range(2):
            mix_s[k + d] = both[:, d * LANES : (d + 1) * LANES]

    lane = lax.broadcasted_iota(jnp.int32, (16, LANES), 1)

    def combine(i, carry):
        start = pl.multiple_of(i * 16, 16)
        part = pl.ds(start, 16)
        planes = []
        for k in range(YR):
            re = mix_s[k, part, :]
            im = mix_s[k, pl.ds(pl.multiple_of(n + i * 16, 16), 16), :]
            if k > 0:
                c = tw_ref[0, k, part, :]
                s = tw_ref[1, k, part, :]
                re, im = re * c + im * s, im * c - re * s
            planes.append((re, im))
        for k, (re, im) in enumerate(short_fft(planes, -1)):
            at = pl.ds(pl.multiple_of(k * n + start, 16), 16)
            first = jnp.where(lane < HALF, re, pltpu.roll(im, HALF, 1))
            second = jnp.where(lane < HALF, pltpu.roll(re, HALF, 1), im)
            out_ref[0, at, :] = first - data_ref[0, at, :].astype(F32)
            out_ref[1, at, :] = second - data_ref[1, at, :].astype(F32)
        return carry

    lax.fori_loop(0, n // 16, combine, 0)


def y_forward(edge, spec, data, c, so_far):
    gz = len(spec)
    blocks, ny, width = data.shape
    n = ny // YR
    piece = spec[0].shape
    before = [] if so_far is None else [so_far]
    return pl.pallas_call(
        functools.partial(y_forward_kernel, gz),
        grid=(1,),
        in_specs=[pl.BlockSpec(memory_space=pltpu.SMEM)]
        + [pl.BlockSpec(piece, lambda i: (0, 0, 0, 0))] * gz
        + [
            pl.BlockSpec((2, ny, width), lambda i: (c, 0, 0)),
            pl.BlockSpec((4 * n, 2 * n), lambda i: (0, 0)),
            pl.BlockSpec((2, YR, n, LANES), lambda i: (0, 0, 0, 0)),
        ]
        + [pl.BlockSpec(memory_space=pl.ANY)] * len(before),
        out_specs=pl.BlockSpec((2, ny, width), lambda i: (c, 0, 0)),
        out_shape=jax.ShapeDtypeStruct((blocks, ny, width), F32),
        scratch_shapes=[
            pltpu.VMEM((ny, LANES), F32),
            pltpu.VMEM((ny, LANES), F32),
            pltpu.VMEM((YR, 2 * n, LANES), F32),
        ],
        input_output_aliases={gz + 4: 0} if before else {},
        compiler_params=pltpu.CompilerParams(vmem_limit_bytes=VMEM_LIMIT),
        cost_estimate=pl.CostEstimate(
            flops=24 * n * n * YR * LANES, bytes_accessed=16 * ny * LANES, transcendentals=0
        ),
        name="y_forward",
    )(edge, *spec, data, y_matrix(ny, True, 1.0), y_twiddle(ny), *before)


def plane_chunk(planes, rows):
    chunk = max(1, 512 // rows)
    while planes % chunk:
        chunk -= 1
    return chunk


def for_core(edge_ref, gz, body):
    for core in range(gz):
        pl.when(edge_ref[2] == core)(functools.partial(body, core))


def x_inverse_kernel(gz, chunks, way, partial, borders, edge_ref, *refs):
    count = len(chunks) * gz
    spec_refs, refs = refs[:count], refs[count:]
    coef_ref, tw_ref, table_ref = refs[:3]
    refs = refs[3:]
    if partial:
        so_far_ref, refs = refs[0], refs[1:]
    out_ref, refs = refs[0], refs[1:]
    if borders:
        head_ref, tail_ref = refs[:2]
    re_s, im_s = refs[-2:]
    kb, _, rows, width = spec_refs[0].shape
    planes, _, ka = out_ref.shape

    def transform(core):
        def columns(i, carry):
            part = pl.ds(pl.multiple_of(i * 8, 8), 8)
            for at, chunk in enumerate(chunks):
                lanes = slice(chunk * width, (chunk + 1) * width)
                to = slice(at * width, (at + 1) * width)
                slices = [spec_refs[at * gz + (way * (z - core)) % gz] for z in range(gz)]
                mixed = [[None] * kb for _ in range(gz)]
                for k in range(kb):
                    coef = [coef_ref[j, k, :, lanes] for j in range(3)]
                    re = mix_adjoint(coef, [s[k, 0, part, :] for s in slices])
                    im = mix_adjoint(coef, [s[k, 1, part, :] for s in slices])
                    for z in range(gz):
                        mixed[z][k] = (re[z], im[z])
                for z in range(gz):
                    for b, (re, im) in enumerate(short_fft(mixed[z], 1)):
                        if b > 0:
                            c = tw_ref[0, b, :, lanes]
                            s = tw_ref[1, b, :, lanes]
                            re, im = re * c - im * s, im * c + re * s
                        re_s[z * kb + b, part, to] = re
                        im_s[z * kb + b, part, to] = im
            return carry

        lax.fori_loop(0, rows // 8, columns, 0)

    for_core(edge_ref, gz, transform)

    step = plane_chunk(planes, rows)
    depth = len(chunks) * width

    def multiply(i, carry):
        part = pl.ds(i * step, step)
        both = jnp.concatenate(
            [re_s[part].reshape(step * rows, depth), im_s[part].reshape(step * rows, depth)], axis=1
        )
        high, low = split2(both)
        value = dot(high, table_ref[...])
        value = value[:, :ka] + value[:, ka:] + dot(low, table_ref[:, :ka])
        value = value.reshape(step, rows, ka)
        out_ref[part] = value + so_far_ref[part] if partial else value
        return carry

    lax.fori_loop(0, planes // step, multiply, 0)

    if borders:
        for p in range(planes):
            for r in range(head_ref.shape[0]):
                head_ref[r, p : p + 1, :] = out_ref[p, r : r + 1, :]
            tail_ref[p : p + 1, :] = out_ref[p, rows - 1 : rows, :]


def x_inverse(edge, spec, chunks, way, coef, nx, so_far=None, borders=True):
    gz = len(spec[0])
    kb, _, rows, width = spec[0][0].shape
    planes, ka = gz * kb, coef.shape[-1]
    depth = len(chunks) * width
    table = x_inverse_matrix(nx, ka)
    if depth < ka:
        keep = [slice(c * width, (c + 1) * width) for c in chunks]
        table = np.concatenate([table[s] for s in keep] + [table[ka:][s] for s in keep], axis=0)
    vmem = pl.BlockSpec(memory_space=pltpu.VMEM)
    arrays = [piece for pieces in spec for piece in pieces]
    before = [] if so_far is None else [so_far]
    out_shape = [jax.ShapeDtypeStruct((planes, rows, ka), F32)]
    if borders:
        out_shape.append(jax.ShapeDtypeStruct((2, planes, ka), F32))
        out_shape.append(jax.ShapeDtypeStruct((planes, ka), F32))
    return pl.pallas_call(
        functools.partial(x_inverse_kernel, gz, chunks, way, bool(before), borders),
        in_specs=[pl.BlockSpec(memory_space=pltpu.SMEM)]
        + [vmem] * (len(arrays) + 3 + len(before)),
        out_specs=[vmem] * len(out_shape),
        out_shape=out_shape,
        scratch_shapes=[pltpu.VMEM((planes, rows, depth), F32)] * 2,
        compiler_params=pltpu.CompilerParams(vmem_limit_bytes=VMEM_LIMIT),
        cost_estimate=pl.CostEstimate(
            flops=12 * planes * rows * depth * ka,
            bytes_accessed=4 * planes * rows * (2 * depth + ka),
            transcendentals=0,
        ),
        name="x_inverse",
    )(edge, *arrays, coef, x_twiddle(nx, ka), jnp.asarray(table), *before)


def forward_into(gz, edge_ref, field_ref, coef_ref, tw_ref, table_ref, spec_refs, sum_s, re_s, im_s):
    planes, rows, ka = field_ref.shape
    kb = planes // gz
    width = spec_refs[0].shape[3]
    step = plane_chunk(planes, rows)

    def multiply(i, carry):
        part = pl.ds(i * step, step)
        high, low = split2(field_ref[part].reshape(step * rows, ka))
        value = dot(high, table_ref[...])
        value = value[:, : 2 * ka] + value[:, 2 * ka :] + dot(low, table_ref[:, : 2 * ka])
        re_s[part] = value[:, :ka].reshape(step, rows, ka)
        im_s[part] = value[:, ka:].reshape(step, rows, ka)
        return carry

    lax.fori_loop(0, planes // step, multiply, 0)

    def transform(core):
        def columns(i, total):
            part = pl.ds(pl.multiple_of(i * 8, 8), 8)
            for chunk in range(ka // width):
                lanes = slice(chunk * width, (chunk + 1) * width)
                spectra = []
                for z in range(gz):
                    turned = []
                    for b in range(kb):
                        re = re_s[z * kb + b, part, lanes]
                        im = im_s[z * kb + b, part, lanes]
                        if b > 0:
                            c = tw_ref[0, b, :, lanes]
                            s = tw_ref[1, b, :, lanes]
                            re, im = re * c + im * s, im * c - re * s
                        turned.append((re, im))
                    spectra.append(short_fft(turned, -1))
                for k in range(kb):
                    coef = [coef_ref[j, k, :, lanes] for j in range(3)]
                    for p in range(2):
                        for z, value in enumerate(mix(coef, [spectra[z][k][p] for z in range(gz)])):
                            spec_refs[chunk * gz + (z - core) % gz][k, p, part, :] = value
                            total = total + value * value
            return total

        sum_s[...] = lax.fori_loop(0, rows // 8, columns, jnp.zeros((8, LANES), F32))

    for_core(edge_ref, gz, transform)


def next_plane(field_ref, p, kb):
    rows, ka = field_ref.shape[1:]
    if (p + 1) % kb:
        return field_ref[p + 1]
    lane = lax.broadcasted_iota(jnp.int32, (rows, ka), 1)
    return jnp.where(lane == ka - 1, field_ref[p], pltpu.roll(field_ref[p + 1 - kb], ka - 1, 1))


def prev_plane(field_ref, p, kb):
    rows, ka = field_ref.shape[1:]
    if p % kb:
        return field_ref[p - 1]
    lane = lax.broadcasted_iota(jnp.int32, (rows, ka), 1)
    return jnp.where(lane == 0, field_ref[p], pltpu.roll(field_ref[p + kb - 1], 1, 1))


def spec_shapes(gz, field):
    planes, rows, ka = field.shape
    piece = jax.ShapeDtypeStruct((planes // gz, 2, rows, LANES), F32)
    return [piece] * (gz * (ka // LANES))


def by_chunk(gz, pieces):
    return [list(pieces[at : at + gz]) for at in range(0, len(pieces), gz)]


def first_kernel(gz, edge_ref, field_ref, coef_ref, tw_ref, table_ref, sums_ref, *refs):
    spec_refs, (sum_s, re_s, im_s) = refs[:-3], refs[-3:]
    planes, rows, ka = field_ref.shape
    kb = planes // gz
    forward_into(gz, edge_ref, field_ref, coef_ref, tw_ref, table_ref, spec_refs, sum_s, re_s, im_s)
    row = lax.broadcasted_iota(jnp.int32, (rows, ka), 0)
    square = jnp.zeros((8, LANES), F32)
    slope = jnp.zeros((8, LANES), F32)
    for p in range(planes):
        here = field_ref[p]
        square = square + fold(here * here)
        along_x = next_plane(field_ref, p, kb) - here
        along_y = jnp.where(row == rows - 1, 0.0, pltpu.roll(here, rows - 1, 0) - here)
        terms = along_x * along_x + along_y * along_y
        if p + kb < planes:
            along_z = field_ref[p + kb] - here
            terms = terms + along_z * along_z
        slope = slope + fold(terms)
    sums_ref[0] = square
    sums_ref[1] = sum_s[...]
    sums_ref[2] = slope


def first_projection(edge, field, coef, gz, nx):
    planes, rows, ka = field.shape
    vmem = pl.BlockSpec(memory_space=pltpu.VMEM)
    pieces = spec_shapes(gz, field)
    sums, *spec = pl.pallas_call(
        functools.partial(first_kernel, gz),
        in_specs=[pl.BlockSpec(memory_space=pltpu.SMEM)] + [vmem] * 4,
        out_specs=[vmem] * (1 + len(pieces)),
        out_shape=[jax.ShapeDtypeStruct((3, 8, LANES), F32)] + pieces,
        scratch_shapes=[pltpu.VMEM((8, LANES), F32)] + [pltpu.VMEM((planes, rows, ka), F32)] * 2,
        compiler_params=pltpu.CompilerParams(vmem_limit_bytes=VMEM_LIMIT),
        cost_estimate=pl.CostEstimate(
            flops=12 * planes * rows * ka * ka, bytes_accessed=12 * planes * rows * ka, transcendentals=0
        ),
        name="first_projection",
    )(edge, field, coef, x_twiddle(nx, ka), x_forward_matrix(nx, ka))
    return by_chunk(gz, spec), sums


def border_kernel(edge_ref, sums_ref, tail_ref, next_ref, out_ref):
    step = (next_ref[0] - tail_ref[...]) * jnp.where(edge_ref[1] > 0, 0.0, 1.0)
    put_sums(out_ref, [sums_ref[0], sums_ref[1], sums_ref[2] + fold(step * step)])


def border_sums(edge, sums, tail, next_head, devices):
    vmem = pl.BlockSpec(memory_space=pltpu.VMEM)
    return pl.pallas_call(
        border_kernel,
        in_specs=[pl.BlockSpec(memory_space=pltpu.SMEM)] + [vmem] * 3,
        out_specs=vmem,
        out_shape=jax.ShapeDtypeStruct((devices, 8, LANES), F32),
        name="border_sums",
    )(edge, sums, tail, next_head)


def second_kernel(
    gz, edge_ref, sums_ref, d0_ref, nd0_ref, tail_ref, prev_ref, next_ref, nnext_ref,
    coef_ref, tw_ref, table_ref, d1_ref, eta_ref, out_ref, *refs,
):
    spec_refs, (sum_s, re_s, im_s, row_s) = refs[:-4], refs[-4:]
    planes, rows, ka = d0_ref.shape
    kb = planes // gz
    eta_here = step_of(sums_ref)
    eta_ref[...] = jnp.broadcast_to(eta_here, (8, LANES))
    eta = jnp.max(eta_here)
    first = edge_ref[0] > 0
    last = edge_ref[1] > 0

    def shrink(difference):
        return jnp.clip(-eta * difference, -CLIP, CLIP)

    lane2 = lax.broadcasted_iota(jnp.int32, (kb, ka), 1)
    row2 = lax.broadcasted_iota(jnp.int32, (kb, ka), 0)
    for z in range(gz):
        part = slice(z * kb, (z + 1) * kb)
        here = next_ref[0, part, :]
        value = here - eta * nnext_ref[0, part, :]
        up = pltpu.roll(here, kb - 1, 0)
        up = jnp.where(
            row2 == kb - 1, jnp.where(lane2 == ka - 1, here, pltpu.roll(up, ka - 1, 1)), up
        )
        down = pltpu.roll(here, 1, 0)
        down = jnp.where(row2 == 0, jnp.where(lane2 == 0, here, pltpu.roll(down, 1, 1)), down)
        value = value + shrink(here - down) - shrink(up - here)
        value = value + shrink(here - tail_ref[part, :]) - shrink(next_ref[1, part, :] - here)
        if z > 0:
            value = value + shrink(here - next_ref[0, (z - 1) * kb : z * kb, :])
        if z + 1 < gz:
            value = value - shrink(next_ref[0, (z + 1) * kb : (z + 2) * kb, :] - here)
        row_s[part, :] = value

    row = lax.broadcasted_iota(jnp.int32, (rows, ka), 0)
    square = jnp.zeros((8, LANES), F32)
    for p in range(planes):
        here = d0_ref[p]
        value = here - eta * nd0_ref[p]
        value = value + shrink(here - prev_plane(d0_ref, p, kb))
        value = value - shrink(next_plane(d0_ref, p, kb) - here)
        below = jnp.where(last, here[rows - 1 :, :], next_ref[0, p : p + 1, :])
        above = jnp.where(first, here[:1, :], prev_ref[p : p + 1, :])
        upper = shrink(jnp.where(row == rows - 1, below, pltpu.roll(here, rows - 1, 0)) - here)
        lower = jnp.where(row == 0, shrink(here[:1, :] - above), pltpu.roll(upper, 1, 0))
        value = value + lower - upper
        if p >= kb:
            value = value + shrink(here - d0_ref[p - kb])
        if p + kb < planes:
            value = value - shrink(d0_ref[p + kb] - here)
        d1_ref[p] = value
        square = square + fold(value * value)

    slope = jnp.zeros((8, LANES), F32)
    for p in range(planes):
        here = d1_ref[p]
        along_x = next_plane(d1_ref, p, kb) - here
        below = jnp.where(last, here[rows - 1 :, :], row_s[p : p + 1, :])
        along_y = jnp.where(row == rows - 1, below, pltpu.roll(here, rows - 1, 0)) - here
        terms = along_x * along_x + along_y * along_y
        if p + kb < planes:
            along_z = d1_ref[p + kb] - here
            terms = terms + along_z * along_z
        slope = slope + fold(terms)

    forward_into(gz, edge_ref, d1_ref, coef_ref, tw_ref, table_ref, spec_refs, sum_s, re_s, im_s)
    put_sums(out_ref, [square, sum_s[...], slope])


def second_descent(edge, sums, d0, nd0, tail, prev_tail, next_head, next_nhead, coef, gz, nx):
    planes, rows, ka = d0.shape
    devices = sums.shape[0]
    vmem = pl.BlockSpec(memory_space=pltpu.VMEM)
    pieces = spec_shapes(gz, d0)
    d1, eta, out, *spec = pl.pallas_call(
        functools.partial(second_kernel, gz),
        in_specs=[pl.BlockSpec(memory_space=pltpu.SMEM)] + [vmem] * 10,
        out_specs=[vmem] * (3 + len(pieces)),
        out_shape=[
            jax.ShapeDtypeStruct((planes, rows, ka), F32),
            jax.ShapeDtypeStruct((8, LANES), F32),
            jax.ShapeDtypeStruct((devices, 8, LANES), F32),
        ]
        + pieces,
        scratch_shapes=[
            pltpu.VMEM((8, LANES), F32),
            pltpu.VMEM((planes, rows, ka), F32),
            pltpu.VMEM((planes, rows, ka), F32),
            pltpu.VMEM((planes, ka), F32),
        ],
        compiler_params=pltpu.CompilerParams(vmem_limit_bytes=VMEM_LIMIT),
        cost_estimate=pl.CostEstimate(
            flops=12 * planes * rows * ka * ka, bytes_accessed=20 * planes * rows * ka, transcendentals=0
        ),
        name="second_descent",
    )(
        edge, sums, d0, nd0, tail, prev_tail, next_head, next_nhead, coef,
        x_twiddle(nx, ka), x_forward_matrix(nx, ka),
    )
    return d1, by_chunk(gz, spec), eta, out


def combine_kernel(sums_ref, eta_ref, *refs):
    count = (len(refs) - 1) // 3
    first_refs, second_refs, out_refs = refs[:count], refs[count : 2 * count], refs[2 * count : -1]
    eta0 = jnp.max(eta_ref[...])
    eta1 = jnp.max(step_of(sums_ref))
    refs[-1][0] = eta_ref[...]
    refs[-1][1] = jnp.full((8, LANES), eta1, F32)
    for first, second, out in zip(first_refs, second_refs, out_refs):

        def one(i, carry):
            out[i] = -(eta0 * first[i] + eta1 * second[i])
            return carry

        lax.fori_loop(0, out.shape[0], one, 0)


def combine_spectra(sums, eta, first, second):
    gz = len(first[0])
    first = [piece for pieces in first for piece in pieces]
    second = [piece for pieces in second for piece in pieces]
    vmem = pl.BlockSpec(memory_space=pltpu.VMEM)
    *spec, steps = pl.pallas_call(
        combine_kernel,
        in_specs=[vmem] * (2 + 2 * len(first)),
        out_specs=[vmem] * (1 + len(first)),
        out_shape=[jax.ShapeDtypeStruct(piece.shape, F32) for piece in first]
        + [jax.ShapeDtypeStruct((2, 8, LANES), F32)],
        compiler_params=pltpu.CompilerParams(vmem_limit_bytes=VMEM_LIMIT),
        name="combine_spectra",
    )(sums, eta, *first, *second)
    return by_chunk(gz, spec), steps


def everywhere(sums):
    return lax.all_to_all(sums, ("gz", "gy"), 0, 0, tiled=True)


def to_core(piece, r):
    gz = lax.axis_size("gz")
    return lax.ppermute(piece, "gz", [(i, (i + r) % gz) for i in range(gz)]) if r else piece


def transpose(pieces):
    return [
        lax.all_to_all(to_core(piece, r), "gy", 0, 0, tiled=True) for r, piece in enumerate(pieces)
    ]


def shards(data, band_offset, interp_weight):
    gz = lax.axis_size("gz")
    gy = lax.axis_size("gy")
    devices = gz * gy
    data = data[0]
    blocks, ny, width = data.shape
    rows = ny // devices
    ka = blocks * HALF
    nx = ka * gy
    chunks = blocks // 2

    core = lax.axis_index("gz")
    flat = lax.axis_index("gy") * gz + core
    edge = jnp.stack([flat == 0, flat == devices - 1, core]).astype(jnp.int32)
    order = [(i % gz) * gy + i // gz for i in range(devices)]
    up = [(order[i + 1], order[i]) for i in range(devices - 1)]
    down = [(order[i], order[i + 1]) for i in range(devices - 1)]

    lower = band_offset < 0
    weight = interp_weight
    coef = jnp.stack(
        [
            jnp.where(lower, weight[1], weight[0]),
            jnp.where(lower, weight[0], 0.0),
            jnp.where(lower, 0.0, weight[1]),
        ]
    ).reshape(3, gy, 1, ka)
    coef = jnp.broadcast_to(coef, (3, gy, 8, ka))

    d0 = None
    for c in range(chunks):
        spec = transpose(y_inverse(edge, data, c, rows, gz, gy))
        final = c + 1 == chunks
        out = x_inverse(edge, [spec], [c], -1, coef, nx, d0, final)
        d0 = out[0]
    head, tail = out[1:]
    next_head = lax.ppermute(head, ("gz", "gy"), up)
    prev_tail = lax.ppermute(tail, ("gz", "gy"), down)
    spec0, sums = first_projection(edge, d0, coef, gz, nx)
    sums = everywhere(border_sums(edge, sums, tail, next_head, devices))
    nd0, nhead, _ = x_inverse(edge, spec0, list(range(chunks)), 1, coef, nx)
    next_nhead = lax.ppermute(nhead, ("gz", "gy"), up)
    d1, spec1, eta, sums = second_descent(
        edge, sums, d0, nd0, tail, prev_tail, next_head, next_nhead, coef, gz, nx
    )
    sums = everywhere(sums)
    spec, steps = combine_spectra(sums, eta, spec0, spec1)
    residual = None
    for c in range(chunks):
        residual = y_forward(edge, transpose(spec[c]), data, c, residual)

    volume = -(steps[0, 0, 0] * d0 + steps[1, 0, 0] * d1)
    volume = volume.reshape(gz, gy, rows, ka).transpose(0, 2, 3, 1).reshape(gz, rows, nx)
    parts = [
        to_core(lax.dynamic_index_in_dim(volume, lax.rem(core + r, gz), 0, False), r)
        for r in range(gz)
    ]
    volume = jnp.zeros((gz, rows, nx), F32)
    for r, part in enumerate(parts):
        volume = lax.dynamic_update_index_in_dim(volume, part, lax.rem(core + gz - r, gz), 0)
    return (volume.reshape(1, gz * rows, nx), residual[None])


NX = 4096
NY = 2048
XB = 64
YB = 64
ITERS = 2
XA = 64
YA = 32
PRECISE = lax.Precision.HIGHEST


def with_halo(block, sides, width):
    for axis, dim in sides:
        count = lax.axis_size(axis)
        forward = [(i, i + 1) for i in range(count - 1)]
        backward = [(target, source) for source, target in forward]
        low = lax.ppermute(
            lax.slice_in_dim(block, block.shape[dim] - width, None, axis=dim), axis, forward
        )
        high = lax.ppermute(lax.slice_in_dim(block, 0, width, axis=dim), axis, backward)
        block = jnp.concatenate([low, block, high], axis=dim)
    return block


def from_behind(block, axis, distance):
    devices = range(lax.axis_size(axis))
    route = [(i - distance, i) for i in devices if i - distance in devices]
    return lax.ppermute(block, axis, route)


def unit_table(length):
    counter = jnp.arange(length, dtype=jnp.int32)
    phase_int = counter[:, None] * counter[None, :] % length
    angles = 2.0 * jnp.pi / length * phase_int.astype(jnp.float32)
    factor = length ** (-0.5)
    return (jnp.cos(angles) * factor, jnp.sin(angles) * factor)


def twiddle_table(row_len, col_len, period):
    phase_int = (
        jnp.arange(row_len, dtype=jnp.int32)[:, None]
        * jnp.arange(col_len, dtype=jnp.int32)[None, :]
        % period
    )
    angles = 2.0 * jnp.pi / period * phase_int.astype(jnp.float32)
    return (jnp.cos(angles), jnp.sin(angles))


def split_parts(packed):
    half_width = packed.shape[-1] // 2
    return (packed[..., :half_width], packed[..., half_width:])


def join_parts(real_part, imag_part):
    return jnp.concatenate([real_part, imag_part], axis=-1)


def complex_contract(packed, cos_table, sin_table, subscripts, conj_sign):
    cos_out = jnp.einsum(subscripts, packed, cos_table, precision=PRECISE)
    sin_out = jnp.einsum(subscripts, packed, sin_table, precision=PRECISE)
    cos_re, cos_im = split_parts(cos_out)
    sin_re, sin_im = split_parts(sin_out)
    return join_parts(cos_re - conj_sign * sin_im, cos_im + conj_sign * sin_re)


def rotate(packed, cos_table, sin_table, conj_sign):
    real_part, imag_part = split_parts(packed)
    return join_parts(
        real_part * cos_table - conj_sign * imag_part * sin_table,
        imag_part * cos_table + conj_sign * real_part * sin_table,
    )


def forward_x(volume):
    slices, row_count = (volume.shape[0], volume.shape[1])
    cos_a, sin_a = unit_table(XA)
    cos_b, sin_b = unit_table(XB)
    first_table = jnp.concatenate([cos_a, -sin_a], axis=1)
    grid_view = volume.reshape(slices, row_count, XA, XB)
    mixing = jnp.einsum("zyab,am->zybm", grid_view, first_table, precision=PRECISE)
    tw_cos, tw_sin = twiddle_table(XB, XA, NX)
    mixing = rotate(mixing, tw_cos, tw_sin, -1.0)
    return complex_contract(mixing, cos_b, sin_b, "zybm,bl->zlym", -1.0)


def inverse_x(packed):
    slices, row_count = (packed.shape[0], packed.shape[2])
    cos_a, sin_a = unit_table(XA)
    cos_b, sin_b = unit_table(XB)
    mixing = complex_contract(packed, cos_b, sin_b, "zlym,lb->zybm", 1.0)
    tw_cos, tw_sin = twiddle_table(XB, XA, NX)
    mixing = rotate(mixing, tw_cos, tw_sin, 1.0)
    last_table = jnp.concatenate([cos_a, -sin_a], axis=0)
    grid_view = jnp.einsum("zybm,ma->zyab", mixing, last_table, precision=PRECISE)
    return grid_view.reshape(slices, row_count, NX)


def forward_y(packed):
    slices, blocks, width = (packed.shape[0], packed.shape[1], packed.shape[3])
    cos_a, sin_a = unit_table(YA)
    cos_b, sin_b = unit_table(YB)
    grid_view = packed.reshape(slices, blocks, YA, YB, width)
    mixing = complex_contract(grid_view, cos_a, sin_a, "zjcdm,ck->zjkdm", -1.0)
    tw_cos, tw_sin = twiddle_table(YA, YB, NY)
    mixing = rotate(mixing, tw_cos[:, :, None], tw_sin[:, :, None], -1.0)
    result = complex_contract(mixing, cos_b, sin_b, "zjkdm,dl->zjlkm", -1.0)
    return result.reshape(slices, blocks, NY, width)


def inverse_y(packed):
    slices, blocks, width = (packed.shape[0], packed.shape[1], packed.shape[3])
    cos_a, sin_a = unit_table(YA)
    cos_b, sin_b = unit_table(YB)
    grid_view = packed.reshape(slices, blocks, YB, YA, width)
    mixing = complex_contract(grid_view, cos_b, sin_b, "zjlkm,ld->zjkdm", 1.0)
    tw_cos, tw_sin = twiddle_table(YA, YB, NY)
    mixing = rotate(mixing, tw_cos[:, :, None], tw_sin[:, :, None], 1.0)
    result = complex_contract(mixing, cos_a, sin_a, "zjkdm,kc->zjcdm", 1.0)
    return result.reshape(slices, blocks, NY, width)


def tilt_coefficients(band_offset, interp_weight, first_block, blocks):
    offsets = lax.dynamic_slice_in_dim(band_offset.reshape(XB, XA), first_block, blocks, 0)
    weights = lax.dynamic_slice_in_dim(interp_weight.reshape(2, XB, XA), first_block, blocks, 1)
    lower_tap = (jnp.concatenate([offsets, offsets], axis=1) < 0)[:, None, :]
    first_weight = jnp.concatenate([weights[0], weights[0]], axis=1)[:, None, :]
    second_weight = jnp.concatenate([weights[1], weights[1]], axis=1)[:, None, :]
    return (lower_tap, first_weight, second_weight)


def tilt(field_in, coefficients, adjoint):
    lower_tap, first_weight, second_weight = coefficients
    padded = with_halo(field_in, (("gz", 0),), 1)
    below_rim = padded[:-2]
    middle = padded[1:-1]
    above_rim = padded[2:]
    if adjoint:
        return jnp.where(
            lower_tap,
            first_weight * above_rim + second_weight * middle,
            first_weight * middle + second_weight * below_rim,
        )
    return jnp.where(
        lower_tap,
        first_weight * below_rim + second_weight * middle,
        first_weight * middle + second_weight * above_rim,
    )


def to_pencil(slab_part):
    return lax.all_to_all(slab_part, "gy", split_axis=1, concat_axis=2, tiled=True)


def to_slab(pencil_part):
    return lax.all_to_all(pencil_part, "gy", split_axis=2, concat_axis=1, tiled=True)


def back_project(packed, pencil_coef):
    return inverse_x(to_slab(inverse_y(tilt(packed, pencil_coef, True))))


def edge_masks(slices, row_count):
    z_global = lax.axis_index("gz") * slices + jnp.arange(slices, dtype=jnp.int32)
    y_global = lax.axis_index("gy") * row_count + jnp.arange(row_count, dtype=jnp.int32)
    keep_z = (z_global < slices * lax.axis_size("gz") - 1).astype(jnp.float32)[:, None, None]
    keep_y = (y_global < row_count * lax.axis_size("gy") - 1).astype(jnp.float32)[None, :, None]
    return (keep_z, keep_y)


def forward_diff(field_in, keep_z, keep_y):
    slices, row_count = (field_in.shape[0], field_in.shape[1])
    next_z = from_behind(field_in, "gz", -1)
    next_y = from_behind(field_in[:, :1], "gy", -1)
    along_z = (jnp.concatenate([field_in[1:], next_z], axis=0) - field_in) * keep_z
    along_y = (jnp.concatenate([field_in[:, 1:], next_y], axis=1) - field_in) * keep_y
    zero_col = jnp.zeros((slices, row_count, 1), jnp.float32)
    along_x = jnp.concatenate([field_in[:, :, 1:] - field_in[:, :, :-1], zero_col], axis=2)
    return jnp.stack([along_z, along_y, along_x])


def transpose_diff(components, keep_z, keep_y):
    slices, row_count = (components.shape[1], components.shape[2])
    zero_col = jnp.zeros((slices, row_count, 1), jnp.float32)
    comp_z = components[0] * keep_z
    comp_y = components[1] * keep_y
    comp_x = jnp.concatenate([components[2][:, :, :-1], zero_col], axis=2)
    prev_z = from_behind(comp_z, "gz", 1)
    prev_y = from_behind(comp_y[:, -1:], "gy", 1)
    result = jnp.concatenate([prev_z, comp_z[:-1]], axis=0) - comp_z
    result = result + jnp.concatenate([prev_y, comp_y[:, :-1]], axis=1) - comp_y
    result = result + jnp.concatenate([zero_col, comp_x[:, :, :-1]], axis=2) - comp_x
    return result


def plain_shards(data, band_offset, interp_weight):
    slices = data.shape[0]
    blocks = data.shape[1]
    width = data.shape[3]
    row_count = NY // lax.axis_size("gy")
    slab_coef = tilt_coefficients(band_offset, interp_weight, 0, XB)
    pencil_coef = tilt_coefficients(
        band_offset, interp_weight, lax.axis_index("gy") * blocks, blocks
    )
    keep_z, keep_y = edge_masks(slices, row_count)
    measured = data.astype(jnp.float32)
    volume = jnp.zeros((slices, row_count, NX), jnp.float32)
    grad_volume = jnp.zeros((3, slices, row_count, NX), jnp.float32)
    split_var = grad_volume
    dual_var = grad_volume
    data_back = back_project(measured, pencil_coef)
    normal_part = jnp.zeros_like(volume)
    tilted = jnp.zeros((slices, XB, row_count, width), jnp.float32)
    for iteration in range(ITERS):
        data_grad = normal_part - data_back
        if iteration > 0:
            tv_gap = grad_volume - split_var + dual_var / PENALTY
            descent = data_grad + PENALTY * transpose_diff(tv_gap, keep_z, keep_y)
        else:
            descent = data_grad
        slope_field = forward_diff(descent, keep_z, keep_y)
        projected = tilt(forward_x(descent), slab_coef, False)
        line_totals = lax.psum(
            (
                jnp.sum(descent * descent),
                jnp.sum(projected * projected),
                jnp.sum(slope_field * slope_field),
            ),
            ("gz", "gy"),
        )
        step_length = line_totals[0] / (line_totals[1] + PENALTY * line_totals[2])
        volume = volume - step_length * descent
        grad_volume = grad_volume - step_length * slope_field
        tilted = tilted - step_length * projected
        if iteration + 1 < ITERS:
            normal_part = normal_part - step_length * inverse_x(tilt(projected, slab_coef, True))
        if iteration + 1 < ITERS:
            shifted = grad_volume + dual_var / PENALTY
            split_var = shifted - jnp.clip(shifted, -TV_WEIGHT / PENALTY, TV_WEIGHT / PENALTY)
            dual_var = PENALTY * (grad_volume - split_var)
    residual = forward_y(to_pencil(tilted)) - measured
    return (volume, residual)


def tiles_fit(mesh, ny, blocks):
    rows = ny // (mesh.shape["gz"] * mesh.shape["gy"])
    return rows % 16 == 0 and blocks // mesh.shape["gy"] % 2 == 0


NX = 4096
NY = 2048
XB = 64
YB = 64
ITERS = 2
XA = 64
YA = 32
PRECISE = lax.Precision.HIGHEST


def with_halo(block, sides, width):
    for axis, dim in sides:
        count = lax.axis_size(axis)
        forward = [(i, i + 1) for i in range(count - 1)]
        backward = [(target, source) for source, target in forward]
        low = lax.ppermute(
            lax.slice_in_dim(block, block.shape[dim] - width, None, axis=dim), axis, forward
        )
        high = lax.ppermute(lax.slice_in_dim(block, 0, width, axis=dim), axis, backward)
        block = jnp.concatenate([low, block, high], axis=dim)
    return block


def from_behind(block, axis, distance):
    devices = range(lax.axis_size(axis))
    route = [(i - distance, i) for i in devices if i - distance in devices]
    return lax.ppermute(block, axis, route)


def unit_table(length):
    counter = jnp.arange(length, dtype=jnp.int32)
    phase_int = counter[:, None] * counter[None, :] % length
    angles = 2.0 * jnp.pi / length * phase_int.astype(jnp.float32)
    factor = length ** (-0.5)
    return (jnp.cos(angles) * factor, jnp.sin(angles) * factor)


def twiddle_table(row_len, col_len, period):
    phase_int = (
        jnp.arange(row_len, dtype=jnp.int32)[:, None]
        * jnp.arange(col_len, dtype=jnp.int32)[None, :]
        % period
    )
    angles = 2.0 * jnp.pi / period * phase_int.astype(jnp.float32)
    return (jnp.cos(angles), jnp.sin(angles))


def split_parts(packed):
    half_width = packed.shape[-1] // 2
    return (packed[..., :half_width], packed[..., half_width:])


def join_parts(real_part, imag_part):
    return jnp.concatenate([real_part, imag_part], axis=-1)


def complex_contract(packed, cos_table, sin_table, subscripts, conj_sign):
    cos_out = jnp.einsum(subscripts, packed, cos_table, precision=PRECISE)
    sin_out = jnp.einsum(subscripts, packed, sin_table, precision=PRECISE)
    cos_re, cos_im = split_parts(cos_out)
    sin_re, sin_im = split_parts(sin_out)
    return join_parts(cos_re - conj_sign * sin_im, cos_im + conj_sign * sin_re)


def rotate(packed, cos_table, sin_table, conj_sign):
    real_part, imag_part = split_parts(packed)
    return join_parts(
        real_part * cos_table - conj_sign * imag_part * sin_table,
        imag_part * cos_table + conj_sign * real_part * sin_table,
    )


def forward_x(volume):
    slices, row_count = (volume.shape[0], volume.shape[1])
    cos_a, sin_a = unit_table(XA)
    cos_b, sin_b = unit_table(XB)
    first_table = jnp.concatenate([cos_a, -sin_a], axis=1)
    grid_view = volume.reshape(slices, row_count, XA, XB)
    mixing = jnp.einsum("zyab,am->zybm", grid_view, first_table, precision=PRECISE)
    tw_cos, tw_sin = twiddle_table(XB, XA, NX)
    mixing = rotate(mixing, tw_cos, tw_sin, -1.0)
    return complex_contract(mixing, cos_b, sin_b, "zybm,bl->zlym", -1.0)


def inverse_x(packed):
    slices, row_count = (packed.shape[0], packed.shape[2])
    cos_a, sin_a = unit_table(XA)
    cos_b, sin_b = unit_table(XB)
    mixing = complex_contract(packed, cos_b, sin_b, "zlym,lb->zybm", 1.0)
    tw_cos, tw_sin = twiddle_table(XB, XA, NX)
    mixing = rotate(mixing, tw_cos, tw_sin, 1.0)
    last_table = jnp.concatenate([cos_a, -sin_a], axis=0)
    grid_view = jnp.einsum("zybm,ma->zyab", mixing, last_table, precision=PRECISE)
    return grid_view.reshape(slices, row_count, NX)


def forward_y(packed):
    slices, blocks, width = (packed.shape[0], packed.shape[1], packed.shape[3])
    cos_a, sin_a = unit_table(YA)
    cos_b, sin_b = unit_table(YB)
    grid_view = packed.reshape(slices, blocks, YA, YB, width)
    mixing = complex_contract(grid_view, cos_a, sin_a, "zjcdm,ck->zjkdm", -1.0)
    tw_cos, tw_sin = twiddle_table(YA, YB, NY)
    mixing = rotate(mixing, tw_cos[:, :, None], tw_sin[:, :, None], -1.0)
    result = complex_contract(mixing, cos_b, sin_b, "zjkdm,dl->zjlkm", -1.0)
    return result.reshape(slices, blocks, NY, width)


def inverse_y(packed):
    slices, blocks, width = (packed.shape[0], packed.shape[1], packed.shape[3])
    cos_a, sin_a = unit_table(YA)
    cos_b, sin_b = unit_table(YB)
    grid_view = packed.reshape(slices, blocks, YB, YA, width)
    mixing = complex_contract(grid_view, cos_b, sin_b, "zjlkm,ld->zjkdm", 1.0)
    tw_cos, tw_sin = twiddle_table(YA, YB, NY)
    mixing = rotate(mixing, tw_cos[:, :, None], tw_sin[:, :, None], 1.0)
    result = complex_contract(mixing, cos_a, sin_a, "zjkdm,kc->zjcdm", 1.0)
    return result.reshape(slices, blocks, NY, width)


def tilt_coefficients(band_offset, interp_weight, first_block, blocks):
    offsets = lax.dynamic_slice_in_dim(band_offset.reshape(XB, XA), first_block, blocks, 0)
    weights = lax.dynamic_slice_in_dim(interp_weight.reshape(2, XB, XA), first_block, blocks, 1)
    lower_tap = (jnp.concatenate([offsets, offsets], axis=1) < 0)[:, None, :]
    first_weight = jnp.concatenate([weights[0], weights[0]], axis=1)[:, None, :]
    second_weight = jnp.concatenate([weights[1], weights[1]], axis=1)[:, None, :]
    return (lower_tap, first_weight, second_weight)


def tilt(field_in, coefficients, adjoint):
    lower_tap, first_weight, second_weight = coefficients
    padded = with_halo(field_in, (("gz", 0),), 1)
    below_rim = padded[:-2]
    middle = padded[1:-1]
    above_rim = padded[2:]
    if adjoint:
        return jnp.where(
            lower_tap,
            first_weight * above_rim + second_weight * middle,
            first_weight * middle + second_weight * below_rim,
        )
    return jnp.where(
        lower_tap,
        first_weight * below_rim + second_weight * middle,
        first_weight * middle + second_weight * above_rim,
    )


def to_pencil(slab_part):
    return lax.all_to_all(slab_part, "gy", split_axis=1, concat_axis=2, tiled=True)


def to_slab(pencil_part):
    return lax.all_to_all(pencil_part, "gy", split_axis=2, concat_axis=1, tiled=True)


def back_project(packed, pencil_coef):
    return inverse_x(to_slab(inverse_y(tilt(packed, pencil_coef, True))))


def edge_masks(slices, row_count):
    z_global = lax.axis_index("gz") * slices + jnp.arange(slices, dtype=jnp.int32)
    y_global = lax.axis_index("gy") * row_count + jnp.arange(row_count, dtype=jnp.int32)
    keep_z = (z_global < slices * lax.axis_size("gz") - 1).astype(jnp.float32)[:, None, None]
    keep_y = (y_global < row_count * lax.axis_size("gy") - 1).astype(jnp.float32)[None, :, None]
    return (keep_z, keep_y)


def forward_diff(field_in, keep_z, keep_y):
    slices, row_count = (field_in.shape[0], field_in.shape[1])
    next_z = from_behind(field_in, "gz", -1)
    next_y = from_behind(field_in[:, :1], "gy", -1)
    along_z = (jnp.concatenate([field_in[1:], next_z], axis=0) - field_in) * keep_z
    along_y = (jnp.concatenate([field_in[:, 1:], next_y], axis=1) - field_in) * keep_y
    zero_col = jnp.zeros((slices, row_count, 1), jnp.float32)
    along_x = jnp.concatenate([field_in[:, :, 1:] - field_in[:, :, :-1], zero_col], axis=2)
    return jnp.stack([along_z, along_y, along_x])


def transpose_diff(components, keep_z, keep_y):
    slices, row_count = (components.shape[1], components.shape[2])
    zero_col = jnp.zeros((slices, row_count, 1), jnp.float32)
    comp_z = components[0] * keep_z
    comp_y = components[1] * keep_y
    comp_x = jnp.concatenate([components[2][:, :, :-1], zero_col], axis=2)
    prev_z = from_behind(comp_z, "gz", 1)
    prev_y = from_behind(comp_y[:, -1:], "gy", 1)
    result = jnp.concatenate([prev_z, comp_z[:-1]], axis=0) - comp_z
    result = result + jnp.concatenate([prev_y, comp_y[:, :-1]], axis=1) - comp_y
    result = result + jnp.concatenate([zero_col, comp_x[:, :, :-1]], axis=2) - comp_x
    return result


def plain_shards(data, band_offset, interp_weight):
    slices = data.shape[0]
    blocks = data.shape[1]
    width = data.shape[3]
    row_count = NY // lax.axis_size("gy")
    slab_coef = tilt_coefficients(band_offset, interp_weight, 0, XB)
    pencil_coef = tilt_coefficients(
        band_offset, interp_weight, lax.axis_index("gy") * blocks, blocks
    )
    keep_z, keep_y = edge_masks(slices, row_count)
    measured = data.astype(jnp.float32)
    volume = jnp.zeros((slices, row_count, NX), jnp.float32)
    grad_volume = jnp.zeros((3, slices, row_count, NX), jnp.float32)
    split_var = grad_volume
    dual_var = grad_volume
    data_back = back_project(measured, pencil_coef)
    normal_part = jnp.zeros_like(volume)
    tilted = jnp.zeros((slices, XB, row_count, width), jnp.float32)
    for iteration in range(ITERS):
        data_grad = normal_part - data_back
        if iteration > 0:
            tv_gap = grad_volume - split_var + dual_var / PENALTY
            descent = data_grad + PENALTY * transpose_diff(tv_gap, keep_z, keep_y)
        else:
            descent = data_grad
        slope_field = forward_diff(descent, keep_z, keep_y)
        projected = tilt(forward_x(descent), slab_coef, False)
        line_totals = lax.psum(
            (
                jnp.sum(descent * descent),
                jnp.sum(projected * projected),
                jnp.sum(slope_field * slope_field),
            ),
            ("gz", "gy"),
        )
        step_length = line_totals[0] / (line_totals[1] + PENALTY * line_totals[2])
        volume = volume - step_length * descent
        grad_volume = grad_volume - step_length * slope_field
        tilted = tilted - step_length * projected
        if iteration + 1 < ITERS:
            normal_part = normal_part - step_length * inverse_x(tilt(projected, slab_coef, True))
        if iteration + 1 < ITERS:
            shifted = grad_volume + dual_var / PENALTY
            split_var = shifted - jnp.clip(shifted, -TV_WEIGHT / PENALTY, TV_WEIGHT / PENALTY)
            dual_var = PENALTY * (grad_volume - split_var)
    residual = forward_y(to_pencil(tilted)) - measured
    return (volume, residual)


def tiles_fit(mesh, ny, blocks):
    rows = ny // (mesh.shape["gz"] * mesh.shape["gy"])
    return rows % 16 == 0 and mesh.shape["gy"] % YR == 0 and blocks // mesh.shape["gy"] % 2 == 0


def solution(mesh):
    in_specs = (P("gz", "gy", None, None), P(), P())
    out_specs = (P("gz", "gy", None), P("gz", "gy", None, None))

    def run(data, band_offset, interp_weight):
        body = shards if tiles_fit(mesh, data.shape[2], data.shape[1]) else plain_shards
        call = jax.shard_map(
            body, mesh=mesh, in_specs=in_specs, out_specs=out_specs, check_vma=False
        )
        return call(data, band_offset, interp_weight)

    return run
```

```python
import functools

import jax
import jax.numpy as jnp
import numpy as np
from jax import lax
from jax.experimental import pallas as pl
from jax.experimental.pallas import tpu as pltpu
from jax.sharding import PartitionSpec as P

PENALTY = 0.5
TV_WEIGHT = 0.25
CLIP = TV_WEIGHT / PENALTY
HALF = 64
YR = 8
LANES = 128
EARLY = []
F32 = jnp.float32
BF16 = jnp.bfloat16
VMEM_LIMIT = 16 * 1024 * 1024


def dft_parts(length, scale):
    index = np.arange(length)
    angles = 2.0 * np.pi / length * (index[:, None] * index[None, :] % length)
    return np.cos(angles) * scale, np.sin(angles) * scale


def two_parts(table):
    table = jnp.asarray(table.astype(np.float32))
    high = table.astype(BF16)
    low = (table - high.astype(F32)).astype(BF16)
    return high, low


def host_parts(table):
    table = table.astype(np.float32)
    high = table.astype(BF16)
    low = (table - high.astype(np.float32)).astype(BF16)
    return high, low


def y_matrix(ny, forward, sign):
    n = ny // YR
    cos, sin = dft_parts(n, sign * ny**-0.5)
    if forward:
        table = np.block([[cos, sin], [-sin, cos]])
    else:
        table = np.block([[cos, -sin], [sin, cos]])
    return jnp.asarray(np.concatenate(host_parts(table), axis=0))


def y_twiddle(ny):
    n = ny // YR
    angles = 2.0 * np.pi / ny * (np.array([1, 2, 4])[:, None] * np.arange(n)[None, :])
    table = np.stack([np.cos(angles), np.sin(angles)]).astype(np.float32)
    return jnp.asarray(np.ascontiguousarray(np.broadcast_to(table[..., None], (2, 3, n, LANES))))


def x_inverse_matrix(nx, ka):
    cos, sin = dft_parts(ka, nx**-0.5)
    return np.concatenate(host_parts(np.concatenate([cos, -sin], axis=0)), axis=1)


def x_forward_matrix(nx, ka):
    cos, sin = dft_parts(ka, nx**-0.5)
    return jnp.asarray(np.concatenate(host_parts(np.concatenate([cos, -sin], axis=1)), axis=1))


def x_twiddle(nx, ka):
    kb = nx // ka
    angles = 2.0 * np.pi / nx * (np.arange(kb)[:, None] * np.arange(ka)[None, :])
    table = np.stack([np.cos(angles), np.sin(angles)]).astype(np.float32)
    return jnp.asarray(np.ascontiguousarray(np.broadcast_to(table[:, :, None], (2, kb, 8, ka))))


def short_fft(planes, sign):
    n = len(planes)
    if n == 1:
        return planes
    even = short_fft(planes[0::2], sign)
    odd = short_fft(planes[1::2], sign)
    half = n // 2
    out = [None] * n
    for k in range(half):
        er, ei = even[k]
        tr, ti = odd[k]
        if 4 * k == n:
            if sign > 0:
                out[k] = (er - ti, ei + tr)
                out[k + half] = (er + ti, ei - tr)
            else:
                out[k] = (er + ti, ei - tr)
                out[k + half] = (er - ti, ei + tr)
            continue
        if k > 0:
            c = float(np.cos(2.0 * np.pi * k / n))
            s = float(sign * np.sin(2.0 * np.pi * k / n))
            if 8 * k == n:
                tr, ti = (tr - ti, ti + tr) if sign > 0 else (tr + ti, ti - tr)
                tr, ti = tr * c, ti * c
            elif 8 * k == 3 * n:
                m = float(np.sin(2.0 * np.pi * k / n))
                tr, ti = (-(tr + ti), tr - ti) if sign > 0 else (ti - tr, -(tr + ti))
                tr, ti = tr * m, ti * m
            else:
                tr, ti = tr * c - ti * s, ti * c + tr * s
        out[k] = (er + tr, ei + ti)
        out[k + half] = (er - tr, ei - ti)
    return out


def split2(x):
    high = x.astype(BF16)
    return high, (x - high.astype(F32)).astype(BF16)


def dot(a, b):
    return jnp.dot(a, b, preferred_element_type=F32)


def fold(x):
    rows, lanes = x.shape
    x = jnp.sum(x.reshape(rows // 8, 8, lanes), axis=0)
    total = x[:, :LANES]
    for i in range(1, lanes // LANES):
        total = total + x[:, i * LANES : (i + 1) * LANES]
    return total


def full_sum(x):
    return jnp.sum(jnp.sum(x, axis=0, keepdims=True), axis=1, keepdims=True)


def step_of(sums_ref):
    total = jnp.sum(sums_ref[...], axis=0)
    parts = jnp.sum(total, axis=1, keepdims=True)
    return parts[0:1] / (parts[1:2] + PENALTY * parts[2:3])


def put_sums(out_ref, values):
    rows = [jnp.sum(v, axis=0, keepdims=True) for v in values]
    index = lax.broadcasted_iota(jnp.int32, (8, LANES), 0)
    block = jnp.zeros((8, LANES), F32)
    for i, row in enumerate(rows):
        block = jnp.where(index == i, jnp.broadcast_to(row, (8, LANES)), block)
    for i in range(out_ref.shape[0]):
        out_ref[i] = block


def mix_adjoint(coef, planes):
    own, below, above = coef
    out = []
    for z in range(len(planes)):
        value = own * planes[z]
        if z + 1 < len(planes):
            value = value + below * planes[z + 1]
        if z > 0:
            value = value + above * planes[z - 1]
        out.append(value)
    return out


def mix(coef, planes):
    own, below, above = coef
    out = []
    for z in range(len(planes)):
        value = own * planes[z]
        if z > 0:
            value = value + below * planes[z - 1]
        if z + 1 < len(planes):
            value = value + above * planes[z + 1]
        out.append(value)
    return out


def steps_of(gz, gy):
    return [(r, s) for s in reversed(range(gy)) for r in range(gz)]


def send(piece, step):
    r, s = step
    if r == 0 and s == 0:
        return piece
    gz, gy = lax.axis_size("gz"), lax.axis_size("gy")
    route = [
        (g * gy + c, (g + r) % gz * gy + (c ^ s)) for g in range(gz) for c in range(gy)
    ]
    return lax.ppermute(piece, ("gz", "gy"), route)


def towards(edge_ref, gz, step):
    r, s = step
    return lax.rem(edge_ref[2] + r, gz), edge_ref[3] ^ s


def source(edge_ref, gz, step):
    r, s = step
    return lax.rem(edge_ref[2] + gz - r, gz), edge_ref[3] ^ s


def y_turns(tw_ref, part):
    one, two, four = [(tw_ref[0, i, part, :], tw_ref[1, i, part, :]) for i in range(3)]

    def both(a, b):
        return a[0] * b[0] - a[1] * b[1], a[1] * b[0] + a[0] * b[1]

    three = both(one, two)
    return [one, two, three, four, both(one, four), both(two, four), both(three, four)]


def y_inverse_kernel(gz, steps, edge_ref, data_ref, table_ref, tw_ref, *refs):
    out_refs, (re_s, im_s, mix_s, part_s) = refs[: len(steps)], refs[len(steps) :]
    blocks, ny, _ = data_ref.shape
    n = ny // YR
    gy, _, rows, _ = part_s.shape
    lane = lax.broadcasted_iota(jnp.int32, (n, LANES), 1)
    table = table_ref[...]

    for chunk in range(blocks // 2):
        lanes = slice(chunk * LANES, (chunk + 1) * LANES)

        def unpack(i, carry):
            part = pl.ds(pl.multiple_of(i * n, n), n)
            first = data_ref[2 * chunk, part, :].astype(F32)
            second = data_ref[2 * chunk + 1, part, :].astype(F32)
            re_s[part, :] = jnp.where(lane < HALF, first, pltpu.roll(second, HALF, 1))
            im_s[part, :] = jnp.where(lane < HALF, pltpu.roll(first, HALF, 1), second)
            return carry

        lax.fori_loop(0, YR, unpack, 0)

        for k in range(0, YR, 2):
            pieces = [
                jnp.concatenate([s[pl.ds(k + d, n, stride=YR), :] for d in range(2)], axis=1)
                for s in (re_s, im_s)
            ]
            both = dot(table, jnp.concatenate(pieces, axis=0).astype(BF16))
            both = both[: 2 * n] + both[2 * n :]
            for d in range(2):
                mix_s[k + d] = both[:, d * LANES : (d + 1) * LANES]

        tiles = rows // 8
        for r in range(gz):
            core = lax.rem(edge_ref[2] + r, gz)

            def combine(i, carry):
                y2 = ((i // tiles) * gz + core) * rows + lax.rem(i, tiles) * 8
                part = pl.ds(pl.multiple_of(y2, 8), 8)
                turns = [None] + y_turns(tw_ref, part)
                planes = []
                for k in range(YR):
                    re = mix_s[k, part, :]
                    im = mix_s[k, pl.ds(pl.multiple_of(n + y2, 8), 8), :]
                    if k > 0:
                        c, s = turns[k]
                        re, im = re * c - im * s, im * c + re * s
                    planes.append((re, im))
                at = pl.ds(pl.multiple_of(lax.rem(i, tiles) * 8, 8), 8)
                for k, (re, im) in enumerate(short_fft(planes, 1)):
                    to = (k * (n // (gz * rows)) + i // tiles) ^ edge_ref[3]
                    part_s[to, 0, at, :] = re
                    part_s[to, 1, at, :] = im
                return carry

            lax.fori_loop(0, n // gz // 8, combine, 0, unroll=2)
            for step, out_ref in zip(steps, out_refs):
                if step[0] == r:
                    out_ref[:, :, lanes] = part_s[step[1]]


def y_inverse(edge, data, steps, rows, gz, gy):
    blocks, ny, width = data.shape
    n = ny // YR
    vmem = pl.BlockSpec(memory_space=pltpu.VMEM)
    piece = jax.ShapeDtypeStruct((2, rows, blocks * HALF), F32)
    return pl.pallas_call(
        functools.partial(y_inverse_kernel, gz, steps),
        in_specs=[pl.BlockSpec(memory_space=pltpu.SMEM)] + [vmem] * 3,
        out_specs=[vmem] * len(steps),
        out_shape=[piece] * len(steps),
        scratch_shapes=[
            pltpu.VMEM((ny, LANES), F32),
            pltpu.VMEM((ny, LANES), F32),
            pltpu.VMEM((YR, 2 * n, LANES), F32),
            pltpu.VMEM((gy, 2, rows, LANES), F32),
        ],
        compiler_params=pltpu.CompilerParams(vmem_limit_bytes=VMEM_LIMIT),
        name="y_inverse",
    )(edge, data, y_matrix(ny, False, -1.0), y_twiddle(ny))


def y_forward_kernel(gz, early, steps, edge_ref, eta_ref, *refs):
    count = len(early)
    first_refs, second_refs = refs[:count], refs[count : 2 * count]
    spec_refs, refs = refs[2 * count : 2 * count + len(steps)], refs[2 * count + len(steps) :]
    data_ref, table_ref, tw_ref, out_ref, re_s, im_s, mix_s = refs
    ny = data_ref.shape[1]
    n = ny // YR
    rows = spec_refs[0].shape[1]
    chunk = pl.program_id(0)
    lanes = pl.ds(pl.multiple_of(chunk * LANES, LANES), LANES)
    eta0 = jnp.max(eta_ref[0])
    eta1 = jnp.max(eta_ref[1])

    def place(step):
        core, chip = source(edge_ref, gz, step)
        return pl.ds(pl.multiple_of((chip * gz + core) * rows, rows), rows)

    for step, first_ref, second_ref in zip(early, first_refs, second_refs):
        for p, s in enumerate((re_s, im_s)):
            s[place(step), :] = -(eta0 * first_ref[p, :, lanes] + eta1 * second_ref[p, :, lanes])
    for step, spec_ref in zip(steps, spec_refs):
        for p, s in enumerate((re_s, im_s)):
            s[place(step), :] = spec_ref[p, :, lanes]

    table = table_ref[...]
    for k in range(0, YR, 2):
        pieces = [
            jnp.concatenate([s[pl.ds(k + d, n, stride=YR), :] for d in range(2)], axis=1)
            for s in (re_s, im_s)
        ]
        high, low = split2(jnp.concatenate(pieces, axis=0))
        both = dot(table, high)
        both = both[: 2 * n] + both[2 * n :] + dot(table[: 2 * n], low)
        for d in range(2):
            mix_s[k + d] = both[:, d * LANES : (d + 1) * LANES]

    lane = lax.broadcasted_iota(jnp.int32, (16, LANES), 1)

    def combine(i, carry):
        start = pl.multiple_of(i * 16, 16)
        part = pl.ds(start, 16)
        turns = [None] + y_turns(tw_ref, part)
        planes = []
        for k in range(YR):
            re = mix_s[k, part, :]
            im = mix_s[k, pl.ds(pl.multiple_of(n + i * 16, 16), 16), :]
            if k > 0:
                c, s = turns[k]
                re, im = re * c + im * s, im * c - re * s
            planes.append((re, im))
        for k, (re, im) in enumerate(short_fft(planes, -1)):
            at = pl.ds(pl.multiple_of(k * n + start, 16), 16)
            first = jnp.where(lane < HALF, re, pltpu.roll(im, HALF, 1))
            second = jnp.where(lane < HALF, pltpu.roll(re, HALF, 1), im)
            out_ref[0, at, :] = first - data_ref[2 * chunk, at, :].astype(F32)
            out_ref[1, at, :] = second - data_ref[2 * chunk + 1, at, :].astype(F32)
        return carry

    lax.fori_loop(0, n // 16, combine, 0)


def y_forward(edge, etas, early, first, second, steps, spec, data, gz):
    blocks, ny, width = data.shape
    n = ny // YR
    vmem = pl.BlockSpec(memory_space=pltpu.VMEM)
    arrays = [etas, *first, *second, *spec, data, y_matrix(ny, True, 1.0), y_twiddle(ny)]
    return pl.pallas_call(
        functools.partial(y_forward_kernel, gz, early, steps),
        grid=(blocks // 2,),
        in_specs=[pl.BlockSpec(memory_space=pltpu.SMEM)] + [vmem] * len(arrays),
        out_specs=pl.BlockSpec((2, ny, width), lambda i: (i, 0, 0)),
        out_shape=jax.ShapeDtypeStruct((blocks, ny, width), F32),
        scratch_shapes=[
            pltpu.VMEM((ny, LANES), F32),
            pltpu.VMEM((ny, LANES), F32),
            pltpu.VMEM((YR, 2 * n, LANES), F32),
        ],
        compiler_params=pltpu.CompilerParams(vmem_limit_bytes=VMEM_LIMIT),
        name="y_forward",
    )(edge, *arrays)


def plane_chunk(planes, rows):
    chunk = max(1, 512 // rows)
    while planes % chunk:
        chunk -= 1
    return chunk


def x_inverse_kernel(gz, steps, edge_ref, *refs):
    count = max(1, len(steps))
    spec_refs, refs = refs[:count], refs[count:]
    coef_ref, tw_ref, table_ref, out_ref, head_ref, tail_ref, re_s, im_s = refs[:8]
    planes, rows, ka = out_ref.shape
    kb = planes // gz

    spec_ref = spec_refs[0]
    if steps:
        spec_ref = refs[8]
        for step, piece_ref in zip(steps, spec_refs):
            core, chip = source(edge_ref, gz, step)
            spec_ref[core * kb + chip] = piece_ref[...]

    def columns(i, carry):
        part = pl.ds(pl.multiple_of(i * 8, 8), 8)
        for start in range(0, ka, LANES):
            lanes = slice(start, start + LANES)
            mixed = [[None] * kb for _ in range(gz)]
            for k in range(kb):
                coef = [coef_ref[j, k, :, lanes] for j in range(3)]
                re = mix_adjoint(coef, [spec_ref[z * kb + k, 0, part, lanes] for z in range(gz)])
                im = mix_adjoint(coef, [spec_ref[z * kb + k, 1, part, lanes] for z in range(gz)])
                for z in range(gz):
                    mixed[z][k] = (re[z], im[z])
            for z in range(gz):
                for b, (re, im) in enumerate(short_fft(mixed[z], 1)):
                    if b > 0:
                        c = tw_ref[0, b, :, lanes]
                        s = tw_ref[1, b, :, lanes]
                        re, im = re * c - im * s, im * c + re * s
                    re_s[z * kb + b, part, lanes] = re
                    im_s[z * kb + b, part, lanes] = im
        return carry

    lax.fori_loop(0, rows // 8, columns, 0)

    step = plane_chunk(planes, rows)

    def multiply(i, carry):
        part = pl.ds(i * step, step)
        both = jnp.concatenate(
            [re_s[part].reshape(step * rows, ka), im_s[part].reshape(step * rows, ka)], axis=1
        )
        high, low = split2(both)
        value = dot(high, table_ref[...])
        value = value[:, :ka] + value[:, ka:] + dot(low, table_ref[:, :ka])
        out_ref[part] = value.reshape(step, rows, ka)
        return carry

    lax.fori_loop(0, planes // step, multiply, 0)

    for p in range(planes):
        for r in range(head_ref.shape[0]):
            head_ref[r, p : p + 1, :] = out_ref[p, r : r + 1, :]
        tail_ref[p : p + 1, :] = out_ref[p, rows - 1 : rows, :]


def x_inverse(edge, spec, steps, coef, gz, nx):
    kb, ka = coef.shape[1], coef.shape[-1]
    planes, rows = gz * kb, spec[0].shape[-2]
    vmem = pl.BlockSpec(memory_space=pltpu.VMEM)
    scratch = [pltpu.VMEM((planes, rows, ka), F32)] * 2
    if steps:
        scratch = scratch + [pltpu.VMEM((planes, 2, rows, ka), F32)]
    return pl.pallas_call(
        functools.partial(x_inverse_kernel, gz, steps),
        in_specs=[pl.BlockSpec(memory_space=pltpu.SMEM)] + [vmem] * (len(spec) + 3),
        out_specs=[vmem] * 3,
        out_shape=[
            jax.ShapeDtypeStruct((planes, rows, ka), F32),
            jax.ShapeDtypeStruct((2, planes, ka), F32),
            jax.ShapeDtypeStruct((planes, ka), F32),
        ],
        scratch_shapes=scratch,
        compiler_params=pltpu.CompilerParams(vmem_limit_bytes=VMEM_LIMIT),
        name="x_inverse",
    )(edge, *spec, coef, x_twiddle(nx, ka), jnp.asarray(x_inverse_matrix(nx, ka)))


def forward_into(gz, field_ref, coef_ref, tw_ref, table_ref, spec_ref, re_s, im_s):
    planes, rows, ka = field_ref.shape
    kb = planes // gz
    step = plane_chunk(planes, rows)

    def multiply(i, carry):
        part = pl.ds(i * step, step)
        high, low = split2(field_ref[part].reshape(step * rows, ka))
        value = dot(high, table_ref[...])
        value = value[:, : 2 * ka] + value[:, 2 * ka :] + dot(low, table_ref[:, : 2 * ka])
        re_s[part] = value[:, :ka].reshape(step, rows, ka)
        im_s[part] = value[:, ka:].reshape(step, rows, ka)
        return carry

    lax.fori_loop(0, planes // step, multiply, 0)

    def columns(i, total):
        part = pl.ds(pl.multiple_of(i * 8, 8), 8)
        for start in range(0, ka, LANES):
            lanes = slice(start, start + LANES)
            spectra = []
            for z in range(gz):
                turned = []
                for b in range(kb):
                    re = re_s[z * kb + b, part, lanes]
                    im = im_s[z * kb + b, part, lanes]
                    if b > 0:
                        c = tw_ref[0, b, :, lanes]
                        s = tw_ref[1, b, :, lanes]
                        re, im = re * c + im * s, im * c - re * s
                    turned.append((re, im))
                spectra.append(short_fft(turned, -1))
            for k in range(kb):
                coef = [coef_ref[j, k, :, lanes] for j in range(3)]
                for p in range(2):
                    for z, value in enumerate(mix(coef, [spectra[z][k][p] for z in range(gz)])):
                        spec_ref[z * kb + k, p, part, lanes] = value
                        total = total + value * value
        return total

    return lax.fori_loop(0, rows // 8, columns, jnp.zeros((8, LANES), F32))


def cut(gz, steps, edge_ref, spec_ref, piece_refs):
    kb = spec_ref.shape[0] // gz
    for step, piece_ref in zip(steps, piece_refs):
        core, chip = towards(edge_ref, gz, step)
        piece_ref[...] = spec_ref[core * kb + chip]


def next_plane(field_ref, p, kb):
    rows, ka = field_ref.shape[1:]
    if (p + 1) % kb:
        return field_ref[p + 1]
    lane = lax.broadcasted_iota(jnp.int32, (rows, ka), 1)
    return jnp.where(lane == ka - 1, field_ref[p], pltpu.roll(field_ref[p + 1 - kb], ka - 1, 1))


def prev_plane(field_ref, p, kb):
    rows, ka = field_ref.shape[1:]
    if p % kb:
        return field_ref[p - 1]
    lane = lax.broadcasted_iota(jnp.int32, (rows, ka), 1)
    return jnp.where(lane == 0, field_ref[p], pltpu.roll(field_ref[p + kb - 1], 1, 1))


def first_kernel(
    gz, early, edge_ref, field_ref, coef_ref, tw_ref, table_ref, sums_ref, spec_ref, *refs
):
    piece_refs, (re_s, im_s) = refs[:-2], refs[-2:]
    planes, rows, ka = field_ref.shape
    kb = planes // gz
    projected = forward_into(gz, field_ref, coef_ref, tw_ref, table_ref, spec_ref, re_s, im_s)
    cut(gz, early, edge_ref, spec_ref, piece_refs)
    row = lax.broadcasted_iota(jnp.int32, (rows, ka), 0)
    square = jnp.zeros((8, LANES), F32)
    slope = jnp.zeros((8, LANES), F32)
    for p in range(planes):
        here = field_ref[p]
        square = square + fold(here * here)
        along_x = next_plane(field_ref, p, kb) - here
        along_y = jnp.where(row == rows - 1, 0.0, pltpu.roll(here, rows - 1, 0) - here)
        terms = along_x * along_x + along_y * along_y
        if p + kb < planes:
            along_z = field_ref[p + kb] - here
            terms = terms + along_z * along_z
        slope = slope + fold(terms)
    sums_ref[0] = square
    sums_ref[1] = projected
    sums_ref[2] = slope


def first_projection(edge, field, early, coef, gz, nx):
    planes, rows, ka = field.shape
    vmem = pl.BlockSpec(memory_space=pltpu.VMEM)
    sums, spec, *pieces = pl.pallas_call(
        functools.partial(first_kernel, gz, early),
        in_specs=[pl.BlockSpec(memory_space=pltpu.SMEM)] + [vmem] * 4,
        out_specs=[vmem] * (2 + len(early)),
        out_shape=[
            jax.ShapeDtypeStruct((3, 8, LANES), F32),
            jax.ShapeDtypeStruct((planes, 2, rows, ka), F32),
        ]
        + [jax.ShapeDtypeStruct((2, rows, ka), F32)] * len(early),
        scratch_shapes=[pltpu.VMEM((planes, rows, ka), F32)] * 2,
        compiler_params=pltpu.CompilerParams(vmem_limit_bytes=VMEM_LIMIT),
        name="first_projection",
    )(edge, field, coef, x_twiddle(nx, ka), x_forward_matrix(nx, ka))
    return spec, pieces, sums


def border_kernel(edge_ref, sums_ref, tail_ref, next_ref, out_ref):
    step = (next_ref[0] - tail_ref[...]) * jnp.where(edge_ref[1] > 0, 0.0, 1.0)
    put_sums(out_ref, [sums_ref[0], sums_ref[1], sums_ref[2] + fold(step * step)])


def border_sums(edge, sums, tail, next_head, devices):
    vmem = pl.BlockSpec(memory_space=pltpu.VMEM)
    return pl.pallas_call(
        border_kernel,
        in_specs=[pl.BlockSpec(memory_space=pltpu.SMEM)] + [vmem] * 3,
        out_specs=vmem,
        out_shape=jax.ShapeDtypeStruct((devices, 8, LANES), F32),
        name="border_sums",
    )(edge, sums, tail, next_head)


def second_kernel(
    gz, early, edge_ref, sums_ref, d0_ref, nd0_ref, tail_ref, prev_ref, next_ref, nnext_ref,
    coef_ref, tw_ref, table_ref, d1_ref, eta_ref, out_ref, spec_ref, *refs,
):
    piece_refs, (re_s, im_s, row_s) = refs[:-3], refs[-3:]
    planes, rows, ka = d0_ref.shape
    kb = planes // gz
    eta_here = step_of(sums_ref)
    eta_ref[...] = jnp.broadcast_to(eta_here, (8, LANES))
    eta = jnp.max(eta_here)
    first = edge_ref[0] > 0
    last = edge_ref[1] > 0

    def shrink(difference):
        return jnp.clip(-eta * difference, -CLIP, CLIP)

    lane2 = lax.broadcasted_iota(jnp.int32, (kb, ka), 1)
    row2 = lax.broadcasted_iota(jnp.int32, (kb, ka), 0)
    for z in range(gz):
        part = slice(z * kb, (z + 1) * kb)
        here = next_ref[0, part, :]
        value = here - eta * nnext_ref[0, part, :]
        up = pltpu.roll(here, kb - 1, 0)
        up = jnp.where(
            row2 == kb - 1, jnp.where(lane2 == ka - 1, here, pltpu.roll(up, ka - 1, 1)), up
        )
        down = pltpu.roll(here, 1, 0)
        down = jnp.where(row2 == 0, jnp.where(lane2 == 0, here, pltpu.roll(down, 1, 1)), down)
        value = value + shrink(here - down) - shrink(up - here)
        value = value + shrink(here - tail_ref[part, :]) - shrink(next_ref[1, part, :] - here)
        if z > 0:
            value = value + shrink(here - next_ref[0, (z - 1) * kb : z * kb, :])
        if z + 1 < gz:
            value = value - shrink(next_ref[0, (z + 1) * kb : (z + 2) * kb, :] - here)
        row_s[part, :] = value

    row = lax.broadcasted_iota(jnp.int32, (rows, ka), 0)
    square = jnp.zeros((8, LANES), F32)
    for p in range(planes):
        here = d0_ref[p]
        value = here - eta * nd0_ref[p]
        value = value + shrink(here - prev_plane(d0_ref, p, kb))
        value = value - shrink(next_plane(d0_ref, p, kb) - here)
        below = jnp.where(last, here[rows - 1 :, :], next_ref[0, p : p + 1, :])
        above = jnp.where(first, here[:1, :], prev_ref[p : p + 1, :])
        upper = shrink(jnp.where(row == rows - 1, below, pltpu.roll(here, rows - 1, 0)) - here)
        lower = jnp.where(row == 0, shrink(here[:1, :] - above), pltpu.roll(upper, 1, 0))
        value = value + lower - upper
        if p >= kb:
            value = value + shrink(here - d0_ref[p - kb])
        if p + kb < planes:
            value = value - shrink(d0_ref[p + kb] - here)
        d1_ref[p] = value
        square = square + fold(value * value)

    slope = jnp.zeros((8, LANES), F32)
    for p in range(planes):
        here = d1_ref[p]
        along_x = next_plane(d1_ref, p, kb) - here
        below = jnp.where(last, here[rows - 1 :, :], row_s[p : p + 1, :])
        along_y = jnp.where(row == rows - 1, below, pltpu.roll(here, rows - 1, 0)) - here
        terms = along_x * along_x + along_y * along_y
        if p + kb < planes:
            along_z = d1_ref[p + kb] - here
            terms = terms + along_z * along_z
        slope = slope + fold(terms)

    projected = forward_into(gz, d1_ref, coef_ref, tw_ref, table_ref, spec_ref, re_s, im_s)
    cut(gz, early, edge_ref, spec_ref, piece_refs)
    put_sums(out_ref, [square, projected, slope])


def second_descent(edge, sums, d0, nd0, tail, prev_tail, next_head, next_nhead, early, coef, gz, nx):
    planes, rows, ka = d0.shape
    devices = sums.shape[0]
    vmem = pl.BlockSpec(memory_space=pltpu.VMEM)
    d1, eta, out, spec, *pieces = pl.pallas_call(
        functools.partial(second_kernel, gz, early),
        in_specs=[pl.BlockSpec(memory_space=pltpu.SMEM)] + [vmem] * 10,
        out_specs=[vmem] * (4 + len(early)),
        out_shape=[
            jax.ShapeDtypeStruct((planes, rows, ka), F32),
            jax.ShapeDtypeStruct((8, LANES), F32),
            jax.ShapeDtypeStruct((devices, 8, LANES), F32),
            jax.ShapeDtypeStruct((planes, 2, rows, ka), F32),
        ]
        + [jax.ShapeDtypeStruct((2, rows, ka), F32)] * len(early),
        scratch_shapes=[
            pltpu.VMEM((planes, rows, ka), F32),
            pltpu.VMEM((planes, rows, ka), F32),
            pltpu.VMEM((planes, ka), F32),
        ],
        compiler_params=pltpu.CompilerParams(vmem_limit_bytes=VMEM_LIMIT),
        name="second_descent",
    )(
        edge, sums, d0, nd0, tail, prev_tail, next_head, next_nhead, coef,
        x_twiddle(nx, ka), x_forward_matrix(nx, ka),
    )
    return d1, spec, pieces, eta, out


def combine_kernel(gz, steps, edge_ref, sums_ref, eta_ref, first_ref, second_ref, steps_ref, *piece_refs):
    kb = first_ref.shape[0] // gz
    eta0 = jnp.max(eta_ref[...])
    eta1 = jnp.max(step_of(sums_ref))
    steps_ref[0] = eta_ref[...]
    steps_ref[1] = jnp.full((8, LANES), eta1, F32)
    for step, piece_ref in zip(steps, piece_refs):
        core, chip = towards(edge_ref, gz, step)
        at = core * kb + chip
        piece_ref[...] = -(eta0 * first_ref[at] + eta1 * second_ref[at])


def combine_spectra(edge, sums, eta, first, second, steps, gz):
    vmem = pl.BlockSpec(memory_space=pltpu.VMEM)
    etas, *pieces = pl.pallas_call(
        functools.partial(combine_kernel, gz, steps),
        in_specs=[pl.BlockSpec(memory_space=pltpu.SMEM)] + [vmem] * 4,
        out_specs=[vmem] * (1 + len(steps)),
        out_shape=[jax.ShapeDtypeStruct((2, 8, LANES), F32)]
        + [jax.ShapeDtypeStruct(first.shape[1:], F32)] * len(steps),
        compiler_params=pltpu.CompilerParams(vmem_limit_bytes=VMEM_LIMIT),
        name="combine_spectra",
    )(edge, sums, eta, first, second)
    return pieces, etas


def everywhere(sums):
    return lax.all_to_all(sums, ("gz", "gy"), 0, 0, tiled=True)


def shards(data, band_offset, interp_weight):
    gz = lax.axis_size("gz")
    gy = lax.axis_size("gy")
    devices = gz * gy
    data = data[0]
    blocks, ny, width = data.shape
    rows = ny // devices
    ka = blocks * HALF
    nx = ka * gy

    core = lax.axis_index("gz")
    flat = lax.axis_index("gy") * gz + core
    edge = jnp.stack([flat == 0, flat == devices - 1, core, lax.axis_index("gy")]).astype(jnp.int32)
    steps = steps_of(gz, gy)
    early = [step for step in steps if step in EARLY]
    late = [step for step in steps if step not in EARLY]
    order = [(i % gz) * gy + i // gz for i in range(devices)]
    up = [(order[i + 1], order[i]) for i in range(devices - 1)]
    down = [(order[i], order[i + 1]) for i in range(devices - 1)]

    lower = band_offset < 0
    weight = interp_weight
    coef = jnp.stack(
        [
            jnp.where(lower, weight[1], weight[0]),
            jnp.where(lower, weight[0], 0.0),
            jnp.where(lower, 0.0, weight[1]),
        ]
    ).reshape(3, gy, 1, ka)
    coef = jnp.broadcast_to(coef, (3, gy, 8, ka))

    pieces = y_inverse(edge, data, steps, rows, gz, gy)
    pieces = [send(piece, step) for piece, step in zip(pieces, steps)]
    d0, head, tail = x_inverse(edge, pieces, steps, coef, gz, nx)
    next_head = lax.ppermute(head, ("gz", "gy"), up)
    prev_tail = lax.ppermute(tail, ("gz", "gy"), down)
    spec0, first, sums = first_projection(edge, d0, early, coef, gz, nx)
    sums = everywhere(border_sums(edge, sums, tail, next_head, devices))
    first = [send(piece, step) for piece, step in zip(first, early)]
    nd0, nhead, _ = x_inverse(edge, [spec0], [], coef, gz, nx)
    next_nhead = lax.ppermute(nhead, ("gz", "gy"), up)
    d1, spec1, second, eta, sums = second_descent(
        edge, sums, d0, nd0, tail, prev_tail, next_head, next_nhead, early, coef, gz, nx
    )
    second = [send(piece, step) for piece, step in zip(second, early)]
    sums = everywhere(sums)
    pieces, etas = combine_spectra(edge, sums, eta, spec0, spec1, late, gz)
    pieces = [send(piece, step) for piece, step in zip(pieces, late)]
    residual = y_forward(edge, etas, early, first, second, late, pieces, data, gz)

    volume = -(etas[0, 0, 0] * d0 + etas[1, 0, 0] * d1)
    volume = volume.reshape(gz, gy, rows, ka).transpose(0, 2, 3, 1).reshape(gz, rows, nx)
    parts = [
        send(lax.dynamic_index_in_dim(volume, lax.rem(core + r, gz), 0, False), (r, 0))
        for r in range(gz)
    ]
    volume = jnp.zeros((gz, rows, nx), F32)
    for r, part in enumerate(parts):
        volume = lax.dynamic_update_index_in_dim(volume, part, lax.rem(core + gz - r, gz), 0)
    return (volume.reshape(1, gz * rows, nx), residual[None])


NX = 4096
NY = 2048
XB = 64
YB = 64
ITERS = 2
XA = 64
YA = 32
PRECISE = lax.Precision.HIGHEST


def with_halo(block, sides, width):
    for axis, dim in sides:
        count = lax.axis_size(axis)
        forward = [(i, i + 1) for i in range(count - 1)]
        backward = [(target, source) for source, target in forward]
        low = lax.ppermute(
            lax.slice_in_dim(block, block.shape[dim] - width, None, axis=dim), axis, forward
        )
        high = lax.ppermute(lax.slice_in_dim(block, 0, width, axis=dim), axis, backward)
        block = jnp.concatenate([low, block, high], axis=dim)
    return block


def from_behind(block, axis, distance):
    devices = range(lax.axis_size(axis))
    route = [(i - distance, i) for i in devices if i - distance in devices]
    return lax.ppermute(block, axis, route)


def unit_table(length):
    counter = jnp.arange(length, dtype=jnp.int32)
    phase_int = counter[:, None] * counter[None, :] % length
    angles = 2.0 * jnp.pi / length * phase_int.astype(jnp.float32)
    factor = length ** (-0.5)
    return (jnp.cos(angles) * factor, jnp.sin(angles) * factor)


def twiddle_table(row_len, col_len, period):
    phase_int = (
        jnp.arange(row_len, dtype=jnp.int32)[:, None]
        * jnp.arange(col_len, dtype=jnp.int32)[None, :]
        % period
    )
    angles = 2.0 * jnp.pi / period * phase_int.astype(jnp.float32)
    return (jnp.cos(angles), jnp.sin(angles))


def split_parts(packed):
    half_width = packed.shape[-1] // 2
    return (packed[..., :half_width], packed[..., half_width:])


def join_parts(real_part, imag_part):
    return jnp.concatenate([real_part, imag_part], axis=-1)


def complex_contract(packed, cos_table, sin_table, subscripts, conj_sign):
    cos_out = jnp.einsum(subscripts, packed, cos_table, precision=PRECISE)
    sin_out = jnp.einsum(subscripts, packed, sin_table, precision=PRECISE)
    cos_re, cos_im = split_parts(cos_out)
    sin_re, sin_im = split_parts(sin_out)
    return join_parts(cos_re - conj_sign * sin_im, cos_im + conj_sign * sin_re)


def rotate(packed, cos_table, sin_table, conj_sign):
    real_part, imag_part = split_parts(packed)
    return join_parts(
        real_part * cos_table - conj_sign * imag_part * sin_table,
        imag_part * cos_table + conj_sign * real_part * sin_table,
    )


def forward_x(volume):
    slices, row_count = (volume.shape[0], volume.shape[1])
    cos_a, sin_a = unit_table(XA)
    cos_b, sin_b = unit_table(XB)
    first_table = jnp.concatenate([cos_a, -sin_a], axis=1)
    grid_view = volume.reshape(slices, row_count, XA, XB)
    mixing = jnp.einsum("zyab,am->zybm", grid_view, first_table, precision=PRECISE)
    tw_cos, tw_sin = twiddle_table(XB, XA, NX)
    mixing = rotate(mixing, tw_cos, tw_sin, -1.0)
    return complex_contract(mixing, cos_b, sin_b, "zybm,bl->zlym", -1.0)


def inverse_x(packed):
    slices, row_count = (packed.shape[0], packed.shape[2])
    cos_a, sin_a = unit_table(XA)
    cos_b, sin_b = unit_table(XB)
    mixing = complex_contract(packed, cos_b, sin_b, "zlym,lb->zybm", 1.0)
    tw_cos, tw_sin = twiddle_table(XB, XA, NX)
    mixing = rotate(mixing, tw_cos, tw_sin, 1.0)
    last_table = jnp.concatenate([cos_a, -sin_a], axis=0)
    grid_view = jnp.einsum("zybm,ma->zyab", mixing, last_table, precision=PRECISE)
    return grid_view.reshape(slices, row_count, NX)


def forward_y(packed):
    slices, blocks, width = (packed.shape[0], packed.shape[1], packed.shape[3])
    cos_a, sin_a = unit_table(YA)
    cos_b, sin_b = unit_table(YB)
    grid_view = packed.reshape(slices, blocks, YA, YB, width)
    mixing = complex_contract(grid_view, cos_a, sin_a, "zjcdm,ck->zjkdm", -1.0)
    tw_cos, tw_sin = twiddle_table(YA, YB, NY)
    mixing = rotate(mixing, tw_cos[:, :, None], tw_sin[:, :, None], -1.0)
    result = complex_contract(mixing, cos_b, sin_b, "zjkdm,dl->zjlkm", -1.0)
    return result.reshape(slices, blocks, NY, width)


def inverse_y(packed):
    slices, blocks, width = (packed.shape[0], packed.shape[1], packed.shape[3])
    cos_a, sin_a = unit_table(YA)
    cos_b, sin_b = unit_table(YB)
    grid_view = packed.reshape(slices, blocks, YB, YA, width)
    mixing = complex_contract(grid_view, cos_b, sin_b, "zjlkm,ld->zjkdm", 1.0)
    tw_cos, tw_sin = twiddle_table(YA, YB, NY)
    mixing = rotate(mixing, tw_cos[:, :, None], tw_sin[:, :, None], 1.0)
    result = complex_contract(mixing, cos_a, sin_a, "zjkdm,kc->zjcdm", 1.0)
    return result.reshape(slices, blocks, NY, width)


def tilt_coefficients(band_offset, interp_weight, first_block, blocks):
    offsets = lax.dynamic_slice_in_dim(band_offset.reshape(XB, XA), first_block, blocks, 0)
    weights = lax.dynamic_slice_in_dim(interp_weight.reshape(2, XB, XA), first_block, blocks, 1)
    lower_tap = (jnp.concatenate([offsets, offsets], axis=1) < 0)[:, None, :]
    first_weight = jnp.concatenate([weights[0], weights[0]], axis=1)[:, None, :]
    second_weight = jnp.concatenate([weights[1], weights[1]], axis=1)[:, None, :]
    return (lower_tap, first_weight, second_weight)


def tilt(field_in, coefficients, adjoint):
    lower_tap, first_weight, second_weight = coefficients
    padded = with_halo(field_in, (("gz", 0),), 1)
    below_rim = padded[:-2]
    middle = padded[1:-1]
    above_rim = padded[2:]
    if adjoint:
        return jnp.where(
            lower_tap,
            first_weight * above_rim + second_weight * middle,
            first_weight * middle + second_weight * below_rim,
        )
    return jnp.where(
        lower_tap,
        first_weight * below_rim + second_weight * middle,
        first_weight * middle + second_weight * above_rim,
    )


def to_pencil(slab_part):
    return lax.all_to_all(slab_part, "gy", split_axis=1, concat_axis=2, tiled=True)


def to_slab(pencil_part):
    return lax.all_to_all(pencil_part, "gy", split_axis=2, concat_axis=1, tiled=True)


def back_project(packed, pencil_coef):
    return inverse_x(to_slab(inverse_y(tilt(packed, pencil_coef, True))))


def edge_masks(slices, row_count):
    z_global = lax.axis_index("gz") * slices + jnp.arange(slices, dtype=jnp.int32)
    y_global = lax.axis_index("gy") * row_count + jnp.arange(row_count, dtype=jnp.int32)
    keep_z = (z_global < slices * lax.axis_size("gz") - 1).astype(jnp.float32)[:, None, None]
    keep_y = (y_global < row_count * lax.axis_size("gy") - 1).astype(jnp.float32)[None, :, None]
    return (keep_z, keep_y)


def forward_diff(field_in, keep_z, keep_y):
    slices, row_count = (field_in.shape[0], field_in.shape[1])
    next_z = from_behind(field_in, "gz", -1)
    next_y = from_behind(field_in[:, :1], "gy", -1)
    along_z = (jnp.concatenate([field_in[1:], next_z], axis=0) - field_in) * keep_z
    along_y = (jnp.concatenate([field_in[:, 1:], next_y], axis=1) - field_in) * keep_y
    zero_col = jnp.zeros((slices, row_count, 1), jnp.float32)
    along_x = jnp.concatenate([field_in[:, :, 1:] - field_in[:, :, :-1], zero_col], axis=2)
    return jnp.stack([along_z, along_y, along_x])


def transpose_diff(components, keep_z, keep_y):
    slices, row_count = (components.shape[1], components.shape[2])
    zero_col = jnp.zeros((slices, row_count, 1), jnp.float32)
    comp_z = components[0] * keep_z
    comp_y = components[1] * keep_y
    comp_x = jnp.concatenate([components[2][:, :, :-1], zero_col], axis=2)
    prev_z = from_behind(comp_z, "gz", 1)
    prev_y = from_behind(comp_y[:, -1:], "gy", 1)
    result = jnp.concatenate([prev_z, comp_z[:-1]], axis=0) - comp_z
    result = result + jnp.concatenate([prev_y, comp_y[:, :-1]], axis=1) - comp_y
    result = result + jnp.concatenate([zero_col, comp_x[:, :, :-1]], axis=2) - comp_x
    return result


def plain_shards(data, band_offset, interp_weight):
    slices = data.shape[0]
    blocks = data.shape[1]
    width = data.shape[3]
    row_count = NY // lax.axis_size("gy")
    slab_coef = tilt_coefficients(band_offset, interp_weight, 0, XB)
    pencil_coef = tilt_coefficients(
        band_offset, interp_weight, lax.axis_index("gy") * blocks, blocks
    )
    keep_z, keep_y = edge_masks(slices, row_count)
    measured = data.astype(jnp.float32)
    volume = jnp.zeros((slices, row_count, NX), jnp.float32)
    grad_volume = jnp.zeros((3, slices, row_count, NX), jnp.float32)
    split_var = grad_volume
    dual_var = grad_volume
    data_back = back_project(measured, pencil_coef)
    normal_part = jnp.zeros_like(volume)
    tilted = jnp.zeros((slices, XB, row_count, width), jnp.float32)
    for iteration in range(ITERS):
        data_grad = normal_part - data_back
        if iteration > 0:
            tv_gap = grad_volume - split_var + dual_var / PENALTY
            descent = data_grad + PENALTY * transpose_diff(tv_gap, keep_z, keep_y)
        else:
            descent = data_grad
        slope_field = forward_diff(descent, keep_z, keep_y)
        projected = tilt(forward_x(descent), slab_coef, False)
        line_totals = lax.psum(
            (
                jnp.sum(descent * descent),
                jnp.sum(projected * projected),
                jnp.sum(slope_field * slope_field),
            ),
            ("gz", "gy"),
        )
        step_length = line_totals[0] / (line_totals[1] + PENALTY * line_totals[2])
        volume = volume - step_length * descent
        grad_volume = grad_volume - step_length * slope_field
        tilted = tilted - step_length * projected
        if iteration + 1 < ITERS:
            normal_part = normal_part - step_length * inverse_x(tilt(projected, slab_coef, True))
        if iteration + 1 < ITERS:
            shifted = grad_volume + dual_var / PENALTY
            split_var = shifted - jnp.clip(shifted, -TV_WEIGHT / PENALTY, TV_WEIGHT / PENALTY)
            dual_var = PENALTY * (grad_volume - split_var)
    residual = forward_y(to_pencil(tilted)) - measured
    return (volume, residual)


def tiles_fit(mesh, ny, blocks):
    rows = ny // (mesh.shape["gz"] * mesh.shape["gy"])
    return rows % 16 == 0 and mesh.shape["gy"] % YR == 0 and blocks // mesh.shape["gy"] % 2 == 0


def solution(mesh):
    in_specs = (P("gz", "gy", None, None), P(), P())
    out_specs = (P("gz", "gy", None), P("gz", "gy", None, None))

    def run(data, band_offset, interp_weight):
        body = shards if tiles_fit(mesh, data.shape[2], data.shape[1]) else plain_shards
        call = jax.shard_map(
            body, mesh=mesh, in_specs=in_specs, out_specs=out_specs, check_vma=False
        )
        return call(data, band_offset, interp_weight)

    return run
```

```python
import functools

import jax
import jax.numpy as jnp
import numpy as np
from jax import lax
from jax.experimental import pallas as pl
from jax.experimental.pallas import tpu as pltpu
from jax.sharding import PartitionSpec as P

PENALTY = 0.5
TV_WEIGHT = 0.25
CLIP = TV_WEIGHT / PENALTY
HALF = 64
YR = 8
LANES = 128
F32 = jnp.float32
BF16 = jnp.bfloat16
MIB = 1024 * 1024
Y_GRANT = 16 * MIB
X_GRANT = 16 * MIB


def dft_parts(length, scale):
    index = np.arange(length)
    angles = 2.0 * np.pi / length * (index[:, None] * index[None, :] % length)
    return np.cos(angles) * scale, np.sin(angles) * scale


def two_parts(table):
    table = jnp.asarray(table.astype(np.float32))
    high = table.astype(BF16)
    low = (table - high.astype(F32)).astype(BF16)
    return high, low


def host_parts(table):
    table = table.astype(np.float32)
    high = table.astype(BF16)
    low = (table - high.astype(np.float32)).astype(BF16)
    return high, low


def y_matrix(ny, forward, sign):
    n = ny // YR
    cos, sin = dft_parts(n, sign * ny**-0.5)
    if forward:
        table = np.block([[cos, sin], [-sin, cos]])
    else:
        table = np.block([[cos, -sin], [sin, cos]])
    return jnp.asarray(np.concatenate(host_parts(table), axis=0))


def y_twiddle(ny):
    n = ny // YR
    angles = 2.0 * np.pi / ny * (np.array([1, 2, 4])[:, None] * np.arange(n)[None, :])
    table = np.stack([np.cos(angles), np.sin(angles)]).astype(np.float32)
    return jnp.asarray(np.ascontiguousarray(np.broadcast_to(table[..., None], (2, 3, n, LANES))))


def x_inverse_matrix(nx, ka):
    cos, sin = dft_parts(ka, nx**-0.5)
    return np.concatenate(host_parts(np.concatenate([cos, -sin], axis=0)), axis=1)


def x_forward_matrix(nx, ka):
    cos, sin = dft_parts(ka, nx**-0.5)
    return jnp.asarray(np.concatenate(host_parts(np.concatenate([cos, -sin], axis=1)), axis=1))


def x_twiddle(nx, ka):
    kb = nx // ka
    angles = 2.0 * np.pi / nx * (np.arange(kb)[:, None] * np.arange(ka)[None, :])
    table = np.stack([np.cos(angles), np.sin(angles)]).astype(np.float32)
    return jnp.asarray(np.ascontiguousarray(np.broadcast_to(table[:, :, None], (2, kb, 8, ka))))


def short_fft(planes, sign):
    n = len(planes)
    if n == 1:
        return planes
    even = short_fft(planes[0::2], sign)
    odd = short_fft(planes[1::2], sign)
    half = n // 2
    out = [None] * n
    for k in range(half):
        er, ei = even[k]
        tr, ti = odd[k]
        if 4 * k == n:
            if sign > 0:
                out[k] = (er - ti, ei + tr)
                out[k + half] = (er + ti, ei - tr)
            else:
                out[k] = (er + ti, ei - tr)
                out[k + half] = (er - ti, ei + tr)
            continue
        if k > 0:
            c = float(np.cos(2.0 * np.pi * k / n))
            s = float(sign * np.sin(2.0 * np.pi * k / n))
            if 8 * k == n:
                tr, ti = (tr - ti, ti + tr) if sign > 0 else (tr + ti, ti - tr)
                tr, ti = tr * c, ti * c
            elif 8 * k == 3 * n:
                m = float(np.sin(2.0 * np.pi * k / n))
                tr, ti = (-(tr + ti), tr - ti) if sign > 0 else (ti - tr, -(tr + ti))
                tr, ti = tr * m, ti * m
            else:
                tr, ti = tr * c - ti * s, ti * c + tr * s
        out[k] = (er + tr, ei + ti)
        out[k + half] = (er - tr, ei - ti)
    return out


def split2(x):
    high = x.astype(BF16)
    return high, (x - high.astype(F32)).astype(BF16)


def dot(a, b):
    return jnp.dot(a, b, preferred_element_type=F32)


def fold(x):
    rows, lanes = x.shape
    x = jnp.sum(x.reshape(rows // 8, 8, lanes), axis=0)
    total = x[:, :LANES]
    for i in range(1, lanes // LANES):
        total = total + x[:, i * LANES : (i + 1) * LANES]
    return total


def full_sum(x):
    return jnp.sum(jnp.sum(x, axis=0, keepdims=True), axis=1, keepdims=True)


def step_of(sums_refs):
    total = sum(jnp.sum(sums_ref[...], axis=0) for sums_ref in sums_refs)
    parts = jnp.sum(total, axis=1, keepdims=True)
    return parts[0:1] / (parts[1:2] + PENALTY * parts[2:3])


def put_sums(out_ref, values):
    rows = [jnp.sum(v, axis=0, keepdims=True) for v in values]
    index = lax.broadcasted_iota(jnp.int32, (8, LANES), 0)
    block = jnp.zeros((8, LANES), F32)
    for i, row in enumerate(rows):
        block = jnp.where(index == i, jnp.broadcast_to(row, (8, LANES)), block)
    for i in range(out_ref.shape[0]):
        out_ref[i] = block


def mix_adjoint(coef, planes):
    own, below, above = coef
    out = []
    for z in range(len(planes)):
        value = own * planes[z]
        if z + 1 < len(planes):
            value = value + below * planes[z + 1]
        if z > 0:
            value = value + above * planes[z - 1]
        out.append(value)
    return out


def mix(coef, planes):
    own, below, above = coef
    out = []
    for z in range(len(planes)):
        value = own * planes[z]
        if z > 0:
            value = value + below * planes[z - 1]
        if z + 1 < len(planes):
            value = value + above * planes[z + 1]
        out.append(value)
    return out


def core_on(edge_ref, gz, r):
    return lax.rem(edge_ref[2] + gz + r, gz)


def y_turns(tw_ref, part):
    one, two, four = [(tw_ref[0, i, part, :], tw_ref[1, i, part, :]) for i in range(3)]

    def both(a, b):
        return a[0] * b[0] - a[1] * b[1], a[1] * b[0] + a[0] * b[1]

    three = both(one, two)
    return [one, two, three, four, both(one, four), both(two, four), both(three, four)]


def y_inverse_kernel(gz, edge_ref, data_ref, table_ref, tw_ref, *refs):
    out_refs, (re_s, im_s, mix_s) = refs[:gz], refs[gz:]
    blocks, ny, _ = data_ref.shape
    n = ny // YR
    rows = out_refs[0].shape[2]
    lane = lax.broadcasted_iota(jnp.int32, (n, LANES), 1)
    table = table_ref[...]

    for chunk in range(blocks // 2):
        lanes = slice(chunk * LANES, (chunk + 1) * LANES)

        def unpack(i, carry):
            part = pl.ds(pl.multiple_of(i * n, n), n)
            first = data_ref[2 * chunk, part, :].astype(F32)
            second = data_ref[2 * chunk + 1, part, :].astype(F32)
            re_s[part, :] = jnp.where(lane < HALF, first, pltpu.roll(second, HALF, 1))
            im_s[part, :] = jnp.where(lane < HALF, pltpu.roll(first, HALF, 1), second)
            return carry

        lax.fori_loop(0, YR, unpack, 0)

        for k in range(0, YR, 2):
            pieces = [
                jnp.concatenate([s[pl.ds(k + d, n, stride=YR), :] for d in range(2)], axis=1)
                for s in (re_s, im_s)
            ]
            both = dot(table, jnp.concatenate(pieces, axis=0).astype(BF16))
            both = both[: 2 * n] + both[2 * n :]
            for d in range(2):
                mix_s[k + d] = both[:, d * LANES : (d + 1) * LANES]

        tiles = rows // 8
        for r in range(gz):
            core = core_on(edge_ref, gz, r)

            def combine(i, carry):
                y2 = ((i // tiles) * gz + core) * rows + lax.rem(i, tiles) * 8
                part = pl.ds(pl.multiple_of(y2, 8), 8)
                turns = [None] + y_turns(tw_ref, part)
                planes = []
                for k in range(YR):
                    re = mix_s[k, part, :]
                    im = mix_s[k, pl.ds(pl.multiple_of(n + y2, 8), 8), :]
                    if k > 0:
                        c, s = turns[k]
                        re, im = re * c - im * s, im * c + re * s
                    planes.append((re, im))
                at = pl.ds(pl.multiple_of(lax.rem(i, tiles) * 8, 8), 8)
                for k, (re, im) in enumerate(short_fft(planes, 1)):
                    to = k * (n // (gz * rows)) + i // tiles
                    out_refs[r][to, 0, at, lanes] = re
                    out_refs[r][to, 1, at, lanes] = im
                return carry

            lax.fori_loop(0, n // gz // 8, combine, 0, unroll=2)


def y_inverse(edge, data, rows, gz, gy):
    blocks, ny, width = data.shape
    n = ny // YR
    vmem = pl.BlockSpec(memory_space=pltpu.VMEM)
    return pl.pallas_call(
        functools.partial(y_inverse_kernel, gz),
        in_specs=[pl.BlockSpec(memory_space=pltpu.SMEM)] + [vmem] * 3,
        out_specs=[vmem] * gz,
        out_shape=[jax.ShapeDtypeStruct((gy, 2, rows, blocks * HALF), F32)] * gz,
        scratch_shapes=[
            pltpu.VMEM((ny, LANES), F32),
            pltpu.VMEM((ny, LANES), F32),
            pltpu.VMEM((YR, 2 * n, LANES), F32),
        ],
        compiler_params=pltpu.CompilerParams(vmem_limit_bytes=Y_GRANT),
        name="y_inverse",
    )(edge, data, y_matrix(ny, False, -1.0), y_twiddle(ny))


def merge_kernel(gz, edge_ref, *refs):
    out_ref = refs[-1]
    for r in range(gz):
        core = core_on(edge_ref, gz, -r)

        def one(i, carry):
            out_ref[i, core] = refs[r][i]
            return carry

        lax.fori_loop(0, out_ref.shape[0], one, 0)


def merge(edge, pieces):
    gz = len(pieces)
    vmem = pl.BlockSpec(memory_space=pltpu.VMEM)
    gy, *rest = pieces[0].shape
    return pl.pallas_call(
        functools.partial(merge_kernel, gz),
        in_specs=[pl.BlockSpec(memory_space=pltpu.SMEM)] + [vmem] * gz,
        out_specs=vmem,
        out_shape=jax.ShapeDtypeStruct((gy, gz, *rest), F32),
        compiler_params=pltpu.CompilerParams(vmem_limit_bytes=2 * MIB),
        name="merge",
    )(edge, *pieces)


def y_forward_kernel(spec_ref, data_ref, table_ref, tw_ref, out_ref, re_s, im_s, mix_s):
    ny = data_ref.shape[1]
    n = ny // YR
    gy, gz, _, rows, _ = spec_ref.shape
    chunk = pl.program_id(0)

    def unpack(i, carry):
        for core in range(gz):
            part = pl.ds(pl.multiple_of((i * gz + core) * rows, rows), rows)
            re_s[part, :] = spec_ref[i, core, 0]
            im_s[part, :] = spec_ref[i, core, 1]
        return carry

    lax.fori_loop(0, gy, unpack, 0)

    table = table_ref[...]
    for k in range(0, YR, 2):
        pieces = [
            jnp.concatenate([s[pl.ds(k + d, n, stride=YR), :] for d in range(2)], axis=1)
            for s in (re_s, im_s)
        ]
        high, low = split2(jnp.concatenate(pieces, axis=0))
        both = dot(table, high)
        both = both[: 2 * n] + both[2 * n :] + dot(table[: 2 * n], low)
        for d in range(2):
            mix_s[k + d] = both[:, d * LANES : (d + 1) * LANES]

    lane = lax.broadcasted_iota(jnp.int32, (16, LANES), 1)

    def combine(i, carry):
        start = pl.multiple_of(i * 16, 16)
        part = pl.ds(start, 16)
        turns = [None] + y_turns(tw_ref, part)
        planes = []
        for k in range(YR):
            re = mix_s[k, part, :]
            im = mix_s[k, pl.ds(pl.multiple_of(n + i * 16, 16), 16), :]
            if k > 0:
                c, s = turns[k]
                re, im = re * c + im * s, im * c - re * s
            planes.append((re, im))
        for k, (re, im) in enumerate(short_fft(planes, -1)):
            at = pl.ds(pl.multiple_of(k * n + start, 16), 16)
            first = jnp.where(lane < HALF, re, pltpu.roll(im, HALF, 1))
            second = jnp.where(lane < HALF, pltpu.roll(re, HALF, 1), im)
            out_ref[0, at, :] = first - data_ref[2 * chunk, at, :].astype(F32)
            out_ref[1, at, :] = second - data_ref[2 * chunk + 1, at, :].astype(F32)
        return carry

    lax.fori_loop(0, n // 16, combine, 0)


def y_forward(spec, data):
    blocks, ny, width = data.shape
    gy, gz, _, rows, _ = spec.shape
    n = ny // YR
    vmem = pl.BlockSpec(memory_space=pltpu.VMEM)
    return pl.pallas_call(
        y_forward_kernel,
        grid=(blocks // 2,),
        in_specs=[pl.BlockSpec((gy, gz, 2, rows, LANES), lambda i: (0, 0, 0, 0, i))] + [vmem] * 3,
        out_specs=pl.BlockSpec((2, ny, width), lambda i: (i, 0, 0)),
        out_shape=jax.ShapeDtypeStruct((blocks, ny, width), F32),
        scratch_shapes=[
            pltpu.VMEM((ny, LANES), F32),
            pltpu.VMEM((ny, LANES), F32),
            pltpu.VMEM((YR, 2 * n, LANES), F32),
        ],
        compiler_params=pltpu.CompilerParams(vmem_limit_bytes=Y_GRANT + 8 * MIB),
        name="y_forward",
    )(spec, data, y_matrix(ny, True, 1.0), y_twiddle(ny))


def plane_chunk(planes, rows):
    chunk = max(1, 512 // rows)
    while planes % chunk:
        chunk -= 1
    return chunk


def x_inverse_kernel(
    spec_ref, coef_ref, tw_ref, table_ref, out_ref, head_ref, tail_ref, re_s, im_s
):
    kb, gz, _, rows, ka = spec_ref.shape
    planes = gz * kb

    def columns(i, carry):
        part = pl.ds(pl.multiple_of(i * 8, 8), 8)
        for start in range(0, ka, LANES):
            lanes = slice(start, start + LANES)
            mixed = [[None] * kb for _ in range(gz)]
            for k in range(kb):
                coef = [coef_ref[j, k, :, lanes] for j in range(3)]
                re = mix_adjoint(coef, [spec_ref[k, z, 0, part, lanes] for z in range(gz)])
                im = mix_adjoint(coef, [spec_ref[k, z, 1, part, lanes] for z in range(gz)])
                for z in range(gz):
                    mixed[z][k] = (re[z], im[z])
            for z in range(gz):
                for b, (re, im) in enumerate(short_fft(mixed[z], 1)):
                    if b > 0:
                        c = tw_ref[0, b, :, lanes]
                        s = tw_ref[1, b, :, lanes]
                        re, im = re * c - im * s, im * c + re * s
                    re_s[z * kb + b, part, lanes] = re
                    im_s[z * kb + b, part, lanes] = im
        return carry

    lax.fori_loop(0, rows // 8, columns, 0)

    step = plane_chunk(planes, rows)

    def multiply(i, carry):
        part = pl.ds(i * step, step)
        both = jnp.concatenate(
            [re_s[part].reshape(step * rows, ka), im_s[part].reshape(step * rows, ka)], axis=1
        )
        high, low = split2(both)
        value = dot(high, table_ref[...])
        value = value[:, :ka] + value[:, ka:] + dot(low, table_ref[:, :ka])
        out_ref[part] = value.reshape(step, rows, ka)
        return carry

    lax.fori_loop(0, planes // step, multiply, 0)

    for p in range(planes):
        for r in range(head_ref.shape[0]):
            head_ref[r, p : p + 1, :] = out_ref[p, r : r + 1, :]
        tail_ref[p : p + 1, :] = out_ref[p, rows - 1 : rows, :]


def x_inverse(spec, coef, nx):
    kb, gz, _, rows, ka = spec.shape
    planes = gz * kb
    vmem = pl.BlockSpec(memory_space=pltpu.VMEM)
    return pl.pallas_call(
        x_inverse_kernel,
        in_specs=[vmem] * 4,
        out_specs=[vmem] * 3,
        out_shape=[
            jax.ShapeDtypeStruct((planes, rows, ka), F32),
            jax.ShapeDtypeStruct((2, planes, ka), F32),
            jax.ShapeDtypeStruct((planes, ka), F32),
        ],
        scratch_shapes=[pltpu.VMEM((planes, rows, ka), F32)] * 2,
        compiler_params=pltpu.CompilerParams(vmem_limit_bytes=X_GRANT),
        name="x_inverse",
    )(spec, coef, x_twiddle(nx, ka), jnp.asarray(x_inverse_matrix(nx, ka)))


def forward_into(gz, field_ref, coef_ref, tw_ref, table_ref, spec_ref, re_s, im_s):
    planes, rows, ka = field_ref.shape
    kb = planes // gz
    step = plane_chunk(planes, rows)

    def multiply(i, carry):
        part = pl.ds(i * step, step)
        high, low = split2(field_ref[part].reshape(step * rows, ka))
        value = dot(high, table_ref[...])
        value = value[:, : 2 * ka] + value[:, 2 * ka :] + dot(low, table_ref[:, : 2 * ka])
        re_s[part] = value[:, :ka].reshape(step, rows, ka)
        im_s[part] = value[:, ka:].reshape(step, rows, ka)
        return carry

    lax.fori_loop(0, planes // step, multiply, 0)

    def columns(i, total):
        part = pl.ds(pl.multiple_of(i * 8, 8), 8)
        for start in range(0, ka, LANES):
            lanes = slice(start, start + LANES)
            spectra = []
            for z in range(gz):
                turned = []
                for b in range(kb):
                    re = re_s[z * kb + b, part, lanes]
                    im = im_s[z * kb + b, part, lanes]
                    if b > 0:
                        c = tw_ref[0, b, :, lanes]
                        s = tw_ref[1, b, :, lanes]
                        re, im = re * c + im * s, im * c - re * s
                    turned.append((re, im))
                spectra.append(short_fft(turned, -1))
            for k in range(kb):
                coef = [coef_ref[j, k, :, lanes] for j in range(3)]
                for p in range(2):
                    for z, value in enumerate(mix(coef, [spectra[z][k][p] for z in range(gz)])):
                        spec_ref[k, z, p, part, lanes] = value
                        total = total + value * value
        return total

    return lax.fori_loop(0, rows // 8, columns, jnp.zeros((8, LANES), F32))


def cut(gz, edge_ref, spec_ref, piece_refs):
    for r, piece_ref in enumerate(piece_refs):
        core = core_on(edge_ref, gz, r + 1)

        def one(i, carry):
            piece_ref[i] = spec_ref[i, core]
            return carry

        lax.fori_loop(0, spec_ref.shape[0], one, 0)


def next_plane(field_ref, p, kb):
    rows, ka = field_ref.shape[1:]
    if (p + 1) % kb:
        return field_ref[p + 1]
    lane = lax.broadcasted_iota(jnp.int32, (rows, ka), 1)
    return jnp.where(lane == ka - 1, field_ref[p], pltpu.roll(field_ref[p + 1 - kb], ka - 1, 1))


def prev_plane(field_ref, p, kb):
    rows, ka = field_ref.shape[1:]
    if p % kb:
        return field_ref[p - 1]
    lane = lax.broadcasted_iota(jnp.int32, (rows, ka), 1)
    return jnp.where(lane == 0, field_ref[p], pltpu.roll(field_ref[p + kb - 1], 1, 1))


def first_kernel(
    gz, edge_ref, field_ref, coef_ref, tw_ref, table_ref, sums_ref, spec_ref, *refs
):
    piece_refs, (re_s, im_s) = refs[:-2], refs[-2:]
    planes, rows, ka = field_ref.shape
    kb = planes // gz
    projected = forward_into(gz, field_ref, coef_ref, tw_ref, table_ref, spec_ref, re_s, im_s)
    cut(gz, edge_ref, spec_ref, piece_refs)
    row = lax.broadcasted_iota(jnp.int32, (rows, ka), 0)
    square = jnp.zeros((8, LANES), F32)
    slope = jnp.zeros((8, LANES), F32)
    for p in range(planes):
        here = field_ref[p]
        square = square + fold(here * here)
        along_x = next_plane(field_ref, p, kb) - here
        along_y = jnp.where(row == rows - 1, 0.0, pltpu.roll(here, rows - 1, 0) - here)
        terms = along_x * along_x + along_y * along_y
        if p + kb < planes:
            along_z = field_ref[p + kb] - here
            terms = terms + along_z * along_z
        slope = slope + fold(terms)
    sums_ref[0] = square
    sums_ref[1] = projected
    sums_ref[2] = slope


def spec_shapes(gz, field):
    planes, rows, ka = field.shape
    kb = planes // gz
    whole = jax.ShapeDtypeStruct((kb, gz, 2, rows, ka), F32)
    return [whole] + [jax.ShapeDtypeStruct((kb, 2, rows, ka), F32)] * (gz - 1)


def first_projection(edge, field, coef, gz, nx):
    planes, rows, ka = field.shape
    vmem = pl.BlockSpec(memory_space=pltpu.VMEM)
    shapes = spec_shapes(gz, field)
    sums, spec, *pieces = pl.pallas_call(
        functools.partial(first_kernel, gz),
        in_specs=[pl.BlockSpec(memory_space=pltpu.SMEM)] + [vmem] * 4,
        out_specs=[vmem] * (1 + len(shapes)),
        out_shape=[jax.ShapeDtypeStruct((3, 8, LANES), F32)] + shapes,
        scratch_shapes=[pltpu.VMEM((planes, rows, ka), F32)] * 2,
        compiler_params=pltpu.CompilerParams(vmem_limit_bytes=X_GRANT),
        name="first_projection",
    )(edge, field, coef, x_twiddle(nx, ka), x_forward_matrix(nx, ka))
    return spec, pieces, sums


def border_kernel(edge_ref, sums_ref, tail_ref, next_ref, out_ref):
    step = (next_ref[0] - tail_ref[...]) * jnp.where(edge_ref[1] > 0, 0.0, 1.0)
    put_sums(out_ref, [sums_ref[0], sums_ref[1], sums_ref[2] + fold(step * step)])


def border_sums(edge, sums, tail, next_head, copies):
    vmem = pl.BlockSpec(memory_space=pltpu.VMEM)
    return pl.pallas_call(
        border_kernel,
        in_specs=[pl.BlockSpec(memory_space=pltpu.SMEM)] + [vmem] * 3,
        out_specs=vmem,
        out_shape=jax.ShapeDtypeStruct((copies, 8, LANES), F32),
        compiler_params=pltpu.CompilerParams(vmem_limit_bytes=2 * MIB),
        name="border_sums",
    )(edge, sums, tail, next_head)


def second_kernel(
    gz, edge_ref, d0_ref, nd0_ref, tail_ref, prev_ref, next_ref, nnext_ref,
    coef_ref, tw_ref, table_ref, *refs,
):
    sums_refs, (d1_ref, eta_ref, out_ref, spec_ref, *refs) = refs[:gz], refs[gz:]
    piece_refs, (re_s, im_s, row_s) = refs[:-3], refs[-3:]
    planes, rows, ka = d0_ref.shape
    kb = planes // gz
    eta_here = step_of(sums_refs)
    eta_ref[...] = jnp.broadcast_to(eta_here, (8, LANES))
    eta = jnp.max(eta_here)
    first = edge_ref[0] > 0
    last = edge_ref[1] > 0

    def shrink(difference):
        return jnp.clip(-eta * difference, -CLIP, CLIP)

    lane2 = lax.broadcasted_iota(jnp.int32, (kb, ka), 1)
    row2 = lax.broadcasted_iota(jnp.int32, (kb, ka), 0)
    for z in range(gz):
        part = slice(z * kb, (z + 1) * kb)
        here = next_ref[0, part, :]
        value = here - eta * nnext_ref[0, part, :]
        up = pltpu.roll(here, kb - 1, 0)
        up = jnp.where(
            row2 == kb - 1, jnp.where(lane2 == ka - 1, here, pltpu.roll(up, ka - 1, 1)), up
        )
        down = pltpu.roll(here, 1, 0)
        down = jnp.where(row2 == 0, jnp.where(lane2 == 0, here, pltpu.roll(down, 1, 1)), down)
        value = value + shrink(here - down) - shrink(up - here)
        value = value + shrink(here - tail_ref[part, :]) - shrink(next_ref[1, part, :] - here)
        if z > 0:
            value = value + shrink(here - next_ref[0, (z - 1) * kb : z * kb, :])
        if z + 1 < gz:
            value = value - shrink(next_ref[0, (z + 1) * kb : (z + 2) * kb, :] - here)
        row_s[part, :] = value

    row = lax.broadcasted_iota(jnp.int32, (rows, ka), 0)
    square = jnp.zeros((8, LANES), F32)
    for p in range(planes):
        here = d0_ref[p]
        value = here - eta * nd0_ref[p]
        value = value + shrink(here - prev_plane(d0_ref, p, kb))
        value = value - shrink(next_plane(d0_ref, p, kb) - here)
        below = jnp.where(last, here[rows - 1 :, :], next_ref[0, p : p + 1, :])
        above = jnp.where(first, here[:1, :], prev_ref[p : p + 1, :])
        upper = shrink(jnp.where(row == rows - 1, below, pltpu.roll(here, rows - 1, 0)) - here)
        lower = jnp.where(row == 0, shrink(here[:1, :] - above), pltpu.roll(upper, 1, 0))
        value = value + lower - upper
        if p >= kb:
            value = value + shrink(here - d0_ref[p - kb])
        if p + kb < planes:
            value = value - shrink(d0_ref[p + kb] - here)
        d1_ref[p] = value
        square = square + fold(value * value)

    slope = jnp.zeros((8, LANES), F32)
    for p in range(planes):
        here = d1_ref[p]
        along_x = next_plane(d1_ref, p, kb) - here
        below = jnp.where(last, here[rows - 1 :, :], row_s[p : p + 1, :])
        along_y = jnp.where(row == rows - 1, below, pltpu.roll(here, rows - 1, 0)) - here
        terms = along_x * along_x + along_y * along_y
        if p + kb < planes:
            along_z = d1_ref[p + kb] - here
            terms = terms + along_z * along_z
        slope = slope + fold(terms)

    projected = forward_into(gz, d1_ref, coef_ref, tw_ref, table_ref, spec_ref, re_s, im_s)
    cut(gz, edge_ref, spec_ref, piece_refs)
    put_sums(out_ref, [square, projected, slope])


def second_descent(edge, sums, d0, nd0, tail, prev_tail, next_head, next_nhead, coef, gz, nx):
    planes, rows, ka = d0.shape
    vmem = pl.BlockSpec(memory_space=pltpu.VMEM)
    shapes = spec_shapes(gz, d0)
    d1, eta, out, spec, *pieces = pl.pallas_call(
        functools.partial(second_kernel, gz),
        in_specs=[pl.BlockSpec(memory_space=pltpu.SMEM)] + [vmem] * (9 + gz),
        out_specs=[vmem] * (3 + len(shapes)),
        out_shape=[
            jax.ShapeDtypeStruct((planes, rows, ka), F32),
            jax.ShapeDtypeStruct((8, LANES), F32),
            jax.ShapeDtypeStruct(sums[0].shape, F32),
        ]
        + shapes,
        scratch_shapes=[
            pltpu.VMEM((planes, rows, ka), F32),
            pltpu.VMEM((planes, rows, ka), F32),
            pltpu.VMEM((planes, ka), F32),
        ],
        compiler_params=pltpu.CompilerParams(vmem_limit_bytes=X_GRANT),
        name="second_descent",
    )(
        edge, d0, nd0, tail, prev_tail, next_head, next_nhead, coef,
        x_twiddle(nx, ka), x_forward_matrix(nx, ka), *sums,
    )
    return d1, spec, pieces, eta, out


def combine_kernel(gz, edge_ref, eta_ref, *refs):
    sums_refs, refs = refs[:gz], refs[gz:]
    first_refs, second_refs, (out_ref, steps_ref) = refs[:gz], refs[gz : 2 * gz], refs[2 * gz :]
    eta0 = jnp.max(eta_ref[...])
    eta1 = jnp.max(step_of(sums_refs))
    steps_ref[0] = eta_ref[...]
    steps_ref[1] = jnp.full((8, LANES), eta1, F32)
    for r in range(gz):
        core = core_on(edge_ref, gz, -r)

        def one(i, carry):
            at = i if r else (i, core)
            out_ref[i, core] = -(eta0 * first_refs[r][at] + eta1 * second_refs[r][at])
            return carry

        lax.fori_loop(0, out_ref.shape[0], one, 0)


def combine_spectra(edge, eta, sums, first, second):
    gz = len(sums)
    vmem = pl.BlockSpec(memory_space=pltpu.VMEM)
    return pl.pallas_call(
        functools.partial(combine_kernel, gz),
        in_specs=[pl.BlockSpec(memory_space=pltpu.SMEM)] + [vmem] * (1 + 3 * gz),
        out_specs=[vmem] * 2,
        out_shape=[
            jax.ShapeDtypeStruct(first[0].shape, F32),
            jax.ShapeDtypeStruct((2, 8, LANES), F32),
        ],
        compiler_params=pltpu.CompilerParams(vmem_limit_bytes=2 * MIB),
        name="combine_spectra",
    )(edge, eta, *sums, *first, *second)


def to_core(piece, r):
    gz = lax.axis_size("gz")
    return lax.ppermute(piece, "gz", [(i, (i + r) % gz) for i in range(gz)]) if r else piece


def from_cores(pieces):
    return [to_core(piece, r + 1) for r, piece in enumerate(pieces)]


def to_chips(parts):
    return lax.all_to_all(parts, "gy", 0, 0, tiled=True)


def everywhere(sums):
    sums = to_chips(sums)
    return [to_core(sums, r) for r in range(lax.axis_size("gz"))]


def shards(data, band_offset, interp_weight):
    gz = lax.axis_size("gz")
    gy = lax.axis_size("gy")
    devices = gz * gy
    data = data[0]
    blocks, ny, width = data.shape
    rows = ny // devices
    ka = blocks * HALF
    nx = ka * gy

    core = lax.axis_index("gz")
    flat = lax.axis_index("gy") * gz + core
    edge = jnp.stack([flat == 0, flat == devices - 1, core]).astype(jnp.int32)
    order = [(i % gz) * gy + i // gz for i in range(devices)]
    up = [(order[i + 1], order[i]) for i in range(devices - 1)]
    down = [(order[i], order[i + 1]) for i in range(devices - 1)]

    lower = band_offset < 0
    weight = interp_weight
    coef = jnp.stack(
        [
            jnp.where(lower, weight[1], weight[0]),
            jnp.where(lower, weight[0], 0.0),
            jnp.where(lower, 0.0, weight[1]),
        ]
    ).reshape(3, gy, 1, ka)
    coef = jnp.broadcast_to(coef, (3, gy, 8, ka))

    own, *others = y_inverse(edge, data, rows, gz, gy)
    spec = to_chips(merge(edge, [own] + from_cores(others)))
    d0, head, tail = x_inverse(spec, coef, nx)
    next_head = lax.ppermute(head, ("gz", "gy"), up)
    prev_tail = lax.ppermute(tail, ("gz", "gy"), down)
    spec0, others0, sums = first_projection(edge, d0, coef, gz, nx)
    sums = everywhere(border_sums(edge, sums, tail, next_head, gy))
    others0 = from_cores(others0)
    nd0, nhead, _ = x_inverse(spec0, coef, nx)
    next_nhead = lax.ppermute(nhead, ("gz", "gy"), up)
    d1, spec1, others1, eta, sums = second_descent(
        edge, sums, d0, nd0, tail, prev_tail, next_head, next_nhead, coef, gz, nx
    )
    sums = everywhere(sums)
    others1 = from_cores(others1)
    spec, etas = combine_spectra(edge, eta, sums, [spec0] + others0, [spec1] + others1)
    residual = y_forward(to_chips(spec), data)

    volume = -(etas[0, 0, 0] * d0 + etas[1, 0, 0] * d1)
    volume = volume.reshape(gz, gy, rows, ka).transpose(0, 2, 3, 1).reshape(gz, rows, nx)
    parts = [
        to_core(lax.dynamic_index_in_dim(volume, lax.rem(core + r, gz), 0, False), r)
        for r in range(gz)
    ]
    volume = jnp.zeros((gz, rows, nx), F32)
    for r, part in enumerate(parts):
        volume = lax.dynamic_update_index_in_dim(volume, part, lax.rem(core + gz - r, gz), 0)
    return (volume.reshape(1, gz * rows, nx), residual[None])


NX = 4096
NY = 2048
XB = 64
YB = 64
ITERS = 2
XA = 64
YA = 32
PRECISE = lax.Precision.HIGHEST


def with_halo(block, sides, width):
    for axis, dim in sides:
        count = lax.axis_size(axis)
        forward = [(i, i + 1) for i in range(count - 1)]
        backward = [(target, source) for source, target in forward]
        low = lax.ppermute(
            lax.slice_in_dim(block, block.shape[dim] - width, None, axis=dim), axis, forward
        )
        high = lax.ppermute(lax.slice_in_dim(block, 0, width, axis=dim), axis, backward)
        block = jnp.concatenate([low, block, high], axis=dim)
    return block


def from_behind(block, axis, distance):
    devices = range(lax.axis_size(axis))
    route = [(i - distance, i) for i in devices if i - distance in devices]
    return lax.ppermute(block, axis, route)


def unit_table(length):
    counter = jnp.arange(length, dtype=jnp.int32)
    phase_int = counter[:, None] * counter[None, :] % length
    angles = 2.0 * jnp.pi / length * phase_int.astype(jnp.float32)
    factor = length ** (-0.5)
    return (jnp.cos(angles) * factor, jnp.sin(angles) * factor)


def twiddle_table(row_len, col_len, period):
    phase_int = (
        jnp.arange(row_len, dtype=jnp.int32)[:, None]
        * jnp.arange(col_len, dtype=jnp.int32)[None, :]
        % period
    )
    angles = 2.0 * jnp.pi / period * phase_int.astype(jnp.float32)
    return (jnp.cos(angles), jnp.sin(angles))


def split_parts(packed):
    half_width = packed.shape[-1] // 2
    return (packed[..., :half_width], packed[..., half_width:])


def join_parts(real_part, imag_part):
    return jnp.concatenate([real_part, imag_part], axis=-1)


def complex_contract(packed, cos_table, sin_table, subscripts, conj_sign):
    cos_out = jnp.einsum(subscripts, packed, cos_table, precision=PRECISE)
    sin_out = jnp.einsum(subscripts, packed, sin_table, precision=PRECISE)
    cos_re, cos_im = split_parts(cos_out)
    sin_re, sin_im = split_parts(sin_out)
    return join_parts(cos_re - conj_sign * sin_im, cos_im + conj_sign * sin_re)


def rotate(packed, cos_table, sin_table, conj_sign):
    real_part, imag_part = split_parts(packed)
    return join_parts(
        real_part * cos_table - conj_sign * imag_part * sin_table,
        imag_part * cos_table + conj_sign * real_part * sin_table,
    )


def forward_x(volume):
    slices, row_count = (volume.shape[0], volume.shape[1])
    cos_a, sin_a = unit_table(XA)
    cos_b, sin_b = unit_table(XB)
    first_table = jnp.concatenate([cos_a, -sin_a], axis=1)
    grid_view = volume.reshape(slices, row_count, XA, XB)
    mixing = jnp.einsum("zyab,am->zybm", grid_view, first_table, precision=PRECISE)
    tw_cos, tw_sin = twiddle_table(XB, XA, NX)
    mixing = rotate(mixing, tw_cos, tw_sin, -1.0)
    return complex_contract(mixing, cos_b, sin_b, "zybm,bl->zlym", -1.0)


def inverse_x(packed):
    slices, row_count = (packed.shape[0], packed.shape[2])
    cos_a, sin_a = unit_table(XA)
    cos_b, sin_b = unit_table(XB)
    mixing = complex_contract(packed, cos_b, sin_b, "zlym,lb->zybm", 1.0)
    tw_cos, tw_sin = twiddle_table(XB, XA, NX)
    mixing = rotate(mixing, tw_cos, tw_sin, 1.0)
    last_table = jnp.concatenate([cos_a, -sin_a], axis=0)
    grid_view = jnp.einsum("zybm,ma->zyab", mixing, last_table, precision=PRECISE)
    return grid_view.reshape(slices, row_count, NX)


def forward_y(packed):
    slices, blocks, width = (packed.shape[0], packed.shape[1], packed.shape[3])
    cos_a, sin_a = unit_table(YA)
    cos_b, sin_b = unit_table(YB)
    grid_view = packed.reshape(slices, blocks, YA, YB, width)
    mixing = complex_contract(grid_view, cos_a, sin_a, "zjcdm,ck->zjkdm", -1.0)
    tw_cos, tw_sin = twiddle_table(YA, YB, NY)
    mixing = rotate(mixing, tw_cos[:, :, None], tw_sin[:, :, None], -1.0)
    result = complex_contract(mixing, cos_b, sin_b, "zjkdm,dl->zjlkm", -1.0)
    return result.reshape(slices, blocks, NY, width)


def inverse_y(packed):
    slices, blocks, width = (packed.shape[0], packed.shape[1], packed.shape[3])
    cos_a, sin_a = unit_table(YA)
    cos_b, sin_b = unit_table(YB)
    grid_view = packed.reshape(slices, blocks, YB, YA, width)
    mixing = complex_contract(grid_view, cos_b, sin_b, "zjlkm,ld->zjkdm", 1.0)
    tw_cos, tw_sin = twiddle_table(YA, YB, NY)
    mixing = rotate(mixing, tw_cos[:, :, None], tw_sin[:, :, None], 1.0)
    result = complex_contract(mixing, cos_a, sin_a, "zjkdm,kc->zjcdm", 1.0)
    return result.reshape(slices, blocks, NY, width)


def tilt_coefficients(band_offset, interp_weight, first_block, blocks):
    offsets = lax.dynamic_slice_in_dim(band_offset.reshape(XB, XA), first_block, blocks, 0)
    weights = lax.dynamic_slice_in_dim(interp_weight.reshape(2, XB, XA), first_block, blocks, 1)
    lower_tap = (jnp.concatenate([offsets, offsets], axis=1) < 0)[:, None, :]
    first_weight = jnp.concatenate([weights[0], weights[0]], axis=1)[:, None, :]
    second_weight = jnp.concatenate([weights[1], weights[1]], axis=1)[:, None, :]
    return (lower_tap, first_weight, second_weight)


def tilt(field_in, coefficients, adjoint):
    lower_tap, first_weight, second_weight = coefficients
    padded = with_halo(field_in, (("gz", 0),), 1)
    below_rim = padded[:-2]
    middle = padded[1:-1]
    above_rim = padded[2:]
    if adjoint:
        return jnp.where(
            lower_tap,
            first_weight * above_rim + second_weight * middle,
            first_weight * middle + second_weight * below_rim,
        )
    return jnp.where(
        lower_tap,
        first_weight * below_rim + second_weight * middle,
        first_weight * middle + second_weight * above_rim,
    )


def to_pencil(slab_part):
    return lax.all_to_all(slab_part, "gy", split_axis=1, concat_axis=2, tiled=True)


def to_slab(pencil_part):
    return lax.all_to_all(pencil_part, "gy", split_axis=2, concat_axis=1, tiled=True)


def back_project(packed, pencil_coef):
    return inverse_x(to_slab(inverse_y(tilt(packed, pencil_coef, True))))


def edge_masks(slices, row_count):
    z_global = lax.axis_index("gz") * slices + jnp.arange(slices, dtype=jnp.int32)
    y_global = lax.axis_index("gy") * row_count + jnp.arange(row_count, dtype=jnp.int32)
    keep_z = (z_global < slices * lax.axis_size("gz") - 1).astype(jnp.float32)[:, None, None]
    keep_y = (y_global < row_count * lax.axis_size("gy") - 1).astype(jnp.float32)[None, :, None]
    return (keep_z, keep_y)


def forward_diff(field_in, keep_z, keep_y):
    slices, row_count = (field_in.shape[0], field_in.shape[1])
    next_z = from_behind(field_in, "gz", -1)
    next_y = from_behind(field_in[:, :1], "gy", -1)
    along_z = (jnp.concatenate([field_in[1:], next_z], axis=0) - field_in) * keep_z
    along_y = (jnp.concatenate([field_in[:, 1:], next_y], axis=1) - field_in) * keep_y
    zero_col = jnp.zeros((slices, row_count, 1), jnp.float32)
    along_x = jnp.concatenate([field_in[:, :, 1:] - field_in[:, :, :-1], zero_col], axis=2)
    return jnp.stack([along_z, along_y, along_x])


def transpose_diff(components, keep_z, keep_y):
    slices, row_count = (components.shape[1], components.shape[2])
    zero_col = jnp.zeros((slices, row_count, 1), jnp.float32)
    comp_z = components[0] * keep_z
    comp_y = components[1] * keep_y
    comp_x = jnp.concatenate([components[2][:, :, :-1], zero_col], axis=2)
    prev_z = from_behind(comp_z, "gz", 1)
    prev_y = from_behind(comp_y[:, -1:], "gy", 1)
    result = jnp.concatenate([prev_z, comp_z[:-1]], axis=0) - comp_z
    result = result + jnp.concatenate([prev_y, comp_y[:, :-1]], axis=1) - comp_y
    result = result + jnp.concatenate([zero_col, comp_x[:, :, :-1]], axis=2) - comp_x
    return result


def plain_shards(data, band_offset, interp_weight):
    slices = data.shape[0]
    blocks = data.shape[1]
    width = data.shape[3]
    row_count = NY // lax.axis_size("gy")
    slab_coef = tilt_coefficients(band_offset, interp_weight, 0, XB)
    pencil_coef = tilt_coefficients(
        band_offset, interp_weight, lax.axis_index("gy") * blocks, blocks
    )
    keep_z, keep_y = edge_masks(slices, row_count)
    measured = data.astype(jnp.float32)
    volume = jnp.zeros((slices, row_count, NX), jnp.float32)
    grad_volume = jnp.zeros((3, slices, row_count, NX), jnp.float32)
    split_var = grad_volume
    dual_var = grad_volume
    data_back = back_project(measured, pencil_coef)
    normal_part = jnp.zeros_like(volume)
    tilted = jnp.zeros((slices, XB, row_count, width), jnp.float32)
    for iteration in range(ITERS):
        data_grad = normal_part - data_back
        if iteration > 0:
            tv_gap = grad_volume - split_var + dual_var / PENALTY
            descent = data_grad + PENALTY * transpose_diff(tv_gap, keep_z, keep_y)
        else:
            descent = data_grad
        slope_field = forward_diff(descent, keep_z, keep_y)
        projected = tilt(forward_x(descent), slab_coef, False)
        line_totals = lax.psum(
            (
                jnp.sum(descent * descent),
                jnp.sum(projected * projected),
                jnp.sum(slope_field * slope_field),
            ),
            ("gz", "gy"),
        )
        step_length = line_totals[0] / (line_totals[1] + PENALTY * line_totals[2])
        volume = volume - step_length * descent
        grad_volume = grad_volume - step_length * slope_field
        tilted = tilted - step_length * projected
        if iteration + 1 < ITERS:
            normal_part = normal_part - step_length * inverse_x(tilt(projected, slab_coef, True))
        if iteration + 1 < ITERS:
            shifted = grad_volume + dual_var / PENALTY
            split_var = shifted - jnp.clip(shifted, -TV_WEIGHT / PENALTY, TV_WEIGHT / PENALTY)
            dual_var = PENALTY * (grad_volume - split_var)
    residual = forward_y(to_pencil(tilted)) - measured
    return (volume, residual)


def tiles_fit(mesh, ny, blocks):
    rows = ny // (mesh.shape["gz"] * mesh.shape["gy"])
    return rows % 16 == 0 and mesh.shape["gy"] % YR == 0 and blocks // mesh.shape["gy"] % 2 == 0


def solution(mesh):
    in_specs = (P("gz", "gy", None, None), P(), P())
    out_specs = (P("gz", "gy", None), P("gz", "gy", None, None))

    def run(data, band_offset, interp_weight):
        body = shards if tiles_fit(mesh, data.shape[2], data.shape[1]) else plain_shards
        call = jax.shard_map(
            body, mesh=mesh, in_specs=in_specs, out_specs=out_specs, check_vma=False
        )
        return call(data, band_offset, interp_weight)

    return run
```

```python
import functools

import jax
import jax.numpy as jnp
import numpy as np
from jax import lax
from jax.experimental import pallas as pl
from jax.experimental.pallas import tpu as pltpu
from jax.sharding import PartitionSpec as P

PENALTY = 0.5
TV_WEIGHT = 0.25
CLIP = TV_WEIGHT / PENALTY
HALF = 64
YR = 8
LANES = 128
F32 = jnp.float32
BF16 = jnp.bfloat16
MIB = 1024 * 1024
Y_GRANT = 16 * MIB
X_GRANT = 16 * MIB


def dft_parts(length, scale):
    index = np.arange(length)
    angles = 2.0 * np.pi / length * (index[:, None] * index[None, :] % length)
    return np.cos(angles) * scale, np.sin(angles) * scale


def two_parts(table):
    table = jnp.asarray(table.astype(np.float32))
    high = table.astype(BF16)
    low = (table - high.astype(F32)).astype(BF16)
    return high, low


def host_parts(table):
    table = table.astype(np.float32)
    high = table.astype(BF16)
    low = (table - high.astype(np.float32)).astype(BF16)
    return high, low


def y_matrix(ny, forward, sign):
    n = ny // YR
    cos, sin = dft_parts(n, sign * ny**-0.5)
    if forward:
        table = np.block([[cos, sin], [-sin, cos]])
    else:
        table = np.block([[cos, -sin], [sin, cos]])
    return jnp.asarray(np.concatenate(host_parts(table), axis=0))


def y_twiddle(ny):
    n = ny // YR
    angles = 2.0 * np.pi / ny * (np.array([1, 2, 4])[:, None] * np.arange(n)[None, :])
    table = np.stack([np.cos(angles), np.sin(angles)]).astype(np.float32)
    return jnp.asarray(np.ascontiguousarray(np.broadcast_to(table[..., None], (2, 3, n, LANES))))


def x_inverse_matrix(nx, ka):
    cos, sin = dft_parts(ka, nx**-0.5)
    return np.concatenate(host_parts(np.concatenate([cos, -sin], axis=0)), axis=1)


def x_forward_matrix(nx, ka):
    cos, sin = dft_parts(ka, nx**-0.5)
    return jnp.asarray(np.concatenate(host_parts(np.concatenate([cos, -sin], axis=1)), axis=1))


def x_twiddle(nx, ka):
    kb = nx // ka
    angles = 2.0 * np.pi / nx * (np.arange(kb)[:, None] * np.arange(ka)[None, :])
    table = np.stack([np.cos(angles), np.sin(angles)]).astype(np.float32)
    return jnp.asarray(np.ascontiguousarray(np.broadcast_to(table[:, :, None], (2, kb, 8, ka))))


def short_fft(planes, sign):
    n = len(planes)
    if n == 1:
        return planes
    even = short_fft(planes[0::2], sign)
    odd = short_fft(planes[1::2], sign)
    half = n // 2
    out = [None] * n
    for k in range(half):
        er, ei = even[k]
        tr, ti = odd[k]
        if 4 * k == n:
            if sign > 0:
                out[k] = (er - ti, ei + tr)
                out[k + half] = (er + ti, ei - tr)
            else:
                out[k] = (er + ti, ei - tr)
                out[k + half] = (er - ti, ei + tr)
            continue
        if k > 0:
            c = float(np.cos(2.0 * np.pi * k / n))
            s = float(sign * np.sin(2.0 * np.pi * k / n))
            if 8 * k == n:
                tr, ti = (tr - ti, ti + tr) if sign > 0 else (tr + ti, ti - tr)
                tr, ti = tr * c, ti * c
            elif 8 * k == 3 * n:
                m = float(np.sin(2.0 * np.pi * k / n))
                tr, ti = (-(tr + ti), tr - ti) if sign > 0 else (ti - tr, -(tr + ti))
                tr, ti = tr * m, ti * m
            else:
                tr, ti = tr * c - ti * s, ti * c + tr * s
        out[k] = (er + tr, ei + ti)
        out[k + half] = (er - tr, ei - ti)
    return out


def split2(x):
    high = x.astype(BF16)
    return high, (x - high.astype(F32)).astype(BF16)


def dot(a, b):
    return jnp.dot(a, b, preferred_element_type=F32)


def fold(x):
    rows, lanes = x.shape
    x = jnp.sum(x.reshape(rows // 8, 8, lanes), axis=0)
    total = x[:, :LANES]
    for i in range(1, lanes // LANES):
        total = total + x[:, i * LANES : (i + 1) * LANES]
    return total


def full_sum(x):
    return jnp.sum(jnp.sum(x, axis=0, keepdims=True), axis=1, keepdims=True)


def step_of(sums_refs):
    total = sum(jnp.sum(sums_ref[...], axis=0) for sums_ref in sums_refs)
    parts = jnp.sum(total, axis=1, keepdims=True)
    return parts[0:1] / (parts[1:2] + PENALTY * parts[2:3])


def put_sums(out_ref, values):
    rows = [jnp.sum(v, axis=0, keepdims=True) for v in values]
    index = lax.broadcasted_iota(jnp.int32, (8, LANES), 0)
    block = jnp.zeros((8, LANES), F32)
    for i, row in enumerate(rows):
        block = jnp.where(index == i, jnp.broadcast_to(row, (8, LANES)), block)
    for i in range(out_ref.shape[0]):
        out_ref[i] = block


def mix_adjoint(coef, planes):
    own, below, above = coef
    out = []
    for z in range(len(planes)):
        value = own * planes[z]
        if z + 1 < len(planes):
            value = value + below * planes[z + 1]
        if z > 0:
            value = value + above * planes[z - 1]
        out.append(value)
    return out


def mix(coef, planes):
    own, below, above = coef
    out = []
    for z in range(len(planes)):
        value = own * planes[z]
        if z > 0:
            value = value + below * planes[z - 1]
        if z + 1 < len(planes):
            value = value + above * planes[z + 1]
        out.append(value)
    return out


def core_on(edge_ref, gz, r):
    return lax.rem(edge_ref[2] + gz + r, gz)


def y_turns(tw_ref, part):
    one, two, four = [(tw_ref[0, i, part, :], tw_ref[1, i, part, :]) for i in range(3)]

    def both(a, b):
        return a[0] * b[0] - a[1] * b[1], a[1] * b[0] + a[0] * b[1]

    three = both(one, two)
    return [one, two, three, four, both(one, four), both(two, four), both(three, four)]


def y_inverse_kernel(gz, edge_ref, data_hbm, table_hbm, tw_hbm, out_hbm, *refs):
    other_refs, refs = refs[: gz - 1], refs[gz - 1 :]
    data_ref, table_ref, tw_ref, own_s, re_s, im_s, mix_s, sems, out_sems = refs
    blocks, ny, _ = data_ref.shape
    n = ny // YR
    rows = own_s.shape[2]
    lane = lax.broadcasted_iota(jnp.int32, (n, LANES), 1)
    pairs = blocks // 2

    def fetch(chunk):
        part = pl.ds(2 * chunk, 2)
        return pltpu.make_async_copy(data_hbm.at[part], data_ref.at[part], sems.at[2 + chunk])

    fetch_table = pltpu.make_async_copy(table_hbm, table_ref, sems.at[0])
    fetch_tw = pltpu.make_async_copy(tw_hbm, tw_ref, sems.at[1])
    fetch(0).start()
    fetch_table.start()
    fetch_tw.start()
    for chunk in range(1, pairs):
        fetch(chunk).start()

    for chunk in range(pairs):
        lanes = slice(chunk * LANES, (chunk + 1) * LANES)
        fetch(chunk).wait()

        def unpack(i, carry):
            part = pl.ds(pl.multiple_of(i * n, n), n)
            first = data_ref[2 * chunk, part, :].astype(F32)
            second = data_ref[2 * chunk + 1, part, :].astype(F32)
            re_s[part, :] = jnp.where(lane < HALF, first, pltpu.roll(second, HALF, 1))
            im_s[part, :] = jnp.where(lane < HALF, pltpu.roll(first, HALF, 1), second)
            return carry

        lax.fori_loop(0, YR, unpack, 0)
        if chunk == 0:
            fetch_table.wait()
            fetch_tw.wait()

        for k in range(0, YR, 2):
            pieces = [
                jnp.concatenate([s[pl.ds(k + d, n, stride=YR), :] for d in range(2)], axis=1)
                for s in (re_s, im_s)
            ]
            both = dot(table_ref[...], jnp.concatenate(pieces, axis=0).astype(BF16))
            both = both[: 2 * n] + both[2 * n :]
            for d in range(2):
                mix_s[k + d] = both[:, d * LANES : (d + 1) * LANES]

        tiles = rows // 8
        for r in range(gz):
            core = core_on(edge_ref, gz, r)
            target = other_refs[r - 1] if r else own_s

            def combine(i, carry):
                y2 = ((i // tiles) * gz + core) * rows + lax.rem(i, tiles) * 8
                part = pl.ds(pl.multiple_of(y2, 8), 8)
                turns = [None] + y_turns(tw_ref, part)
                planes = []
                for k in range(YR):
                    re = mix_s[k, part, :]
                    im = mix_s[k, pl.ds(pl.multiple_of(n + y2, 8), 8), :]
                    if k > 0:
                        c, s = turns[k]
                        re, im = re * c - im * s, im * c + re * s
                    planes.append((re, im))
                at = pl.ds(pl.multiple_of(lax.rem(i, tiles) * 8, 8), 8)
                for k, (re, im) in enumerate(short_fft(planes, 1)):
                    to = k * (n // (gz * rows)) + i // tiles
                    target[to, 0, at, lanes] = re
                    target[to, 1, at, lanes] = im
                return carry

            lax.fori_loop(0, n // gz // 8, combine, 0, unroll=2)

    give = pltpu.make_async_copy(own_s, out_hbm.at[:, edge_ref[2]], out_sems.at[0])
    give.start()
    give.wait()


def y_inverse(edge, data, rows, gz, gy):
    blocks, ny, width = data.shape
    n = ny // YR
    ka = blocks * HALF
    vmem = pl.BlockSpec(memory_space=pltpu.VMEM)
    hbm = pl.BlockSpec(memory_space=pltpu.HBM)
    piece = jax.ShapeDtypeStruct((gy, 2, rows, ka), F32)
    whole, *others = pl.pallas_call(
        functools.partial(y_inverse_kernel, gz),
        in_specs=[pl.BlockSpec(memory_space=pltpu.SMEM)] + [hbm] * 3,
        out_specs=[hbm] + [vmem] * (gz - 1),
        out_shape=[jax.ShapeDtypeStruct((gy, gz, 2, rows, ka), F32)] + [piece] * (gz - 1),
        scratch_shapes=[
            pltpu.VMEM((blocks, ny, width), BF16),
            pltpu.VMEM((4 * n, 2 * n), BF16),
            pltpu.VMEM((2, 3, n, LANES), F32),
            pltpu.VMEM((gy, 2, rows, ka), F32),
            pltpu.VMEM((ny, LANES), F32),
            pltpu.VMEM((ny, LANES), F32),
            pltpu.VMEM((YR, 2 * n, LANES), F32),
            pltpu.SemaphoreType.DMA((2 + blocks // 2,)),
            pltpu.SemaphoreType.DMA((1,)),
        ],
        compiler_params=pltpu.CompilerParams(vmem_limit_bytes=Y_GRANT + 4 * MIB),
        name="y_inverse",
    )(edge, data, y_matrix(ny, False, -1.0), y_twiddle(ny))
    return whole, others


def merge_kernel(gz, edge_ref, *refs):
    pieces, (_, out_hbm, sems) = refs[: gz - 1], refs[gz - 1 :]
    copies = [
        pltpu.make_async_copy(piece, out_hbm.at[:, core_on(edge_ref, gz, -r - 1)], sems.at[r])
        for r, piece in enumerate(pieces)
    ]
    for copy in copies:
        copy.start()
    for copy in copies:
        copy.wait()


def merge(edge, whole, pieces):
    gz = whole.shape[1]
    hbm = pl.BlockSpec(memory_space=pltpu.HBM)
    return pl.pallas_call(
        functools.partial(merge_kernel, gz),
        in_specs=[pl.BlockSpec(memory_space=pltpu.SMEM)]
        + [pl.BlockSpec(memory_space=pl.ANY)] * (gz - 1)
        + [hbm],
        out_specs=hbm,
        out_shape=jax.ShapeDtypeStruct(whole.shape, F32),
        scratch_shapes=[pltpu.SemaphoreType.DMA((gz - 1,))],
        input_output_aliases={gz: 0},
        compiler_params=pltpu.CompilerParams(vmem_limit_bytes=MIB),
        name="merge",
    )(edge, *pieces, whole)


def y_forward_kernel(spec_ref, data_ref, table_ref, tw_ref, out_ref, re_s, im_s, mix_s):
    ny = data_ref.shape[1]
    n = ny // YR
    gy, gz, _, rows, _ = spec_ref.shape
    chunk = pl.program_id(0)

    def unpack(i, carry):
        for core in range(gz):
            part = pl.ds(pl.multiple_of((i * gz + core) * rows, rows), rows)
            re_s[part, :] = spec_ref[i, core, 0]
            im_s[part, :] = spec_ref[i, core, 1]
        return carry

    lax.fori_loop(0, gy, unpack, 0)

    table = table_ref[...]
    for k in range(0, YR, 2):
        pieces = [
            jnp.concatenate([s[pl.ds(k + d, n, stride=YR), :] for d in range(2)], axis=1)
            for s in (re_s, im_s)
        ]
        high, low = split2(jnp.concatenate(pieces, axis=0))
        both = dot(table, high)
        both = both[: 2 * n] + both[2 * n :] + dot(table[: 2 * n], low)
        for d in range(2):
            mix_s[k + d] = both[:, d * LANES : (d + 1) * LANES]

    lane = lax.broadcasted_iota(jnp.int32, (16, LANES), 1)

    def combine(i, carry):
        start = pl.multiple_of(i * 16, 16)
        part = pl.ds(start, 16)
        turns = [None] + y_turns(tw_ref, part)
        planes = []
        for k in range(YR):
            re = mix_s[k, part, :]
            im = mix_s[k, pl.ds(pl.multiple_of(n + i * 16, 16), 16), :]
            if k > 0:
                c, s = turns[k]
                re, im = re * c + im * s, im * c - re * s
            planes.append((re, im))
        for k, (re, im) in enumerate(short_fft(planes, -1)):
            at = pl.ds(pl.multiple_of(k * n + start, 16), 16)
            first = jnp.where(lane < HALF, re, pltpu.roll(im, HALF, 1))
            second = jnp.where(lane < HALF, pltpu.roll(re, HALF, 1), im)
            out_ref[0, at, :] = first - data_ref[2 * chunk, at, :].astype(F32)
            out_ref[1, at, :] = second - data_ref[2 * chunk + 1, at, :].astype(F32)
        return carry

    lax.fori_loop(0, n // 16, combine, 0)


def y_forward(spec, data):
    blocks, ny, width = data.shape
    gy, gz, _, rows, _ = spec.shape
    n = ny // YR
    vmem = pl.BlockSpec(memory_space=pltpu.VMEM)
    return pl.pallas_call(
        y_forward_kernel,
        grid=(blocks // 2,),
        in_specs=[pl.BlockSpec((gy, gz, 2, rows, LANES), lambda i: (0, 0, 0, 0, i))] + [vmem] * 3,
        out_specs=pl.BlockSpec((2, ny, width), lambda i: (i, 0, 0)),
        out_shape=jax.ShapeDtypeStruct((blocks, ny, width), F32),
        scratch_shapes=[
            pltpu.VMEM((ny, LANES), F32),
            pltpu.VMEM((ny, LANES), F32),
            pltpu.VMEM((YR, 2 * n, LANES), F32),
        ],
        compiler_params=pltpu.CompilerParams(vmem_limit_bytes=Y_GRANT + 8 * MIB),
        name="y_forward",
    )(spec, data, y_matrix(ny, True, 1.0), y_twiddle(ny))


def plane_chunk(planes, rows):
    chunk = max(1, 512 // rows)
    while planes % chunk:
        chunk -= 1
    return chunk


def turn_rows(kb, planes_of, tw_ref, lanes, sign):
    out = []
    for b in range(kb):
        re, im = planes_of(b)
        if b > 0:
            c = tw_ref[0, b, :, lanes]
            s = tw_ref[1, b, :, lanes]
            if sign > 0:
                re, im = re * c - im * s, im * c + re * s
            else:
                re, im = re * c + im * s, im * c - re * s
        out.append((re, im))
    return out


def inverse_columns(gz, kb, spectra, coef_ref, tw_ref, lanes, part, re_s, im_s):
    mixed = [[None] * kb for _ in range(gz)]
    for k in range(kb):
        coef = [coef_ref[j, k, :, lanes] for j in range(3)]
        re = mix_adjoint(coef, [spectra[z][k][0] for z in range(gz)])
        im = mix_adjoint(coef, [spectra[z][k][1] for z in range(gz)])
        for z in range(gz):
            mixed[z][k] = (re[z], im[z])
    for z in range(gz):
        short = short_fft(mixed[z], 1)
        for b, (re, im) in enumerate(turn_rows(kb, lambda b: short[b], tw_ref, lanes, 1)):
            re_s[z * kb + b, part, lanes] = re
            im_s[z * kb + b, part, lanes] = im


def forward_columns(gz, kb, coef_ref, tw_ref, lanes, part, re_s, im_s):
    spectra = []
    for z in range(gz):
        rows_of = lambda b: (re_s[z * kb + b, part, lanes], im_s[z * kb + b, part, lanes])
        spectra.append(short_fft(turn_rows(kb, rows_of, tw_ref, lanes, -1), -1))
    out = [[None] * kb for _ in range(gz)]
    for k in range(kb):
        coef = [coef_ref[j, k, :, lanes] for j in range(3)]
        re = mix(coef, [spectra[z][k][0] for z in range(gz)])
        im = mix(coef, [spectra[z][k][1] for z in range(gz)])
        for z in range(gz):
            out[z][k] = (re[z], im[z])
    return out


def inverse_product(re, im, table_ref):
    ka = re.shape[1]
    high, low = split2(jnp.concatenate([re, im], axis=1))
    value = dot(high, table_ref[...])
    return value[:, :ka] + value[:, ka:] + dot(low, table_ref[:, :ka])


def forward_product(field, table_ref):
    ka = field.shape[1]
    high, low = split2(field)
    value = dot(high, table_ref[...])
    value = value[:, : 2 * ka] + value[:, 2 * ka :] + dot(low, table_ref[:, : 2 * ka])
    return value[:, :ka], value[:, ka:]


def next_plane(field_ref, p, kb):
    rows, ka = field_ref.shape[1:]
    if (p + 1) % kb:
        return field_ref[p + 1]
    lane = lax.broadcasted_iota(jnp.int32, (rows, ka), 1)
    return jnp.where(lane == ka - 1, field_ref[p], pltpu.roll(field_ref[p + 1 - kb], ka - 1, 1))


def prev_plane(field_ref, p, kb):
    rows, ka = field_ref.shape[1:]
    if p % kb:
        return field_ref[p - 1]
    lane = lax.broadcasted_iota(jnp.int32, (rows, ka), 1)
    return jnp.where(lane == 0, field_ref[p], pltpu.roll(field_ref[p + kb - 1], 1, 1))


def first_kernel(
    gz, edge_ref, field_ref, coef_ref, tw_ref, table_ref, sums_ref, spec_ref, *refs
):
    piece_refs, (re_s, im_s) = refs[:-2], refs[-2:]
    planes, rows, ka = field_ref.shape
    kb = planes // gz
    projected = forward_into(gz, field_ref, coef_ref, tw_ref, table_ref, spec_ref, re_s, im_s)
    cut(gz, edge_ref, spec_ref, piece_refs)
    row = lax.broadcasted_iota(jnp.int32, (rows, ka), 0)
    square = jnp.zeros((8, LANES), F32)
    slope = jnp.zeros((8, LANES), F32)
    for p in range(planes):
        here = field_ref[p]
        square = square + fold(here * here)
        along_x = next_plane(field_ref, p, kb) - here
        along_y = jnp.where(row == rows - 1, 0.0, pltpu.roll(here, rows - 1, 0) - here)
        terms = along_x * along_x + along_y * along_y
        if p + kb < planes:
            along_z = field_ref[p + kb] - here
            terms = terms + along_z * along_z
        slope = slope + fold(terms)
    sums_ref[0] = square
    sums_ref[1] = projected
    sums_ref[2] = slope


def middle_kernel(
    gz, edge_ref, spec_hbm, coef_ref, tw_ref, inverse_ref, forward_ref,
    d0_ref, nd0_ref, head_ref, tail_ref, sums_ref, *refs,
):
    give_hbm, (spec_s, re_s, im_s, sems, out_sems) = refs[:gz], refs[gz:]
    kb, _, _, rows, ka = spec_s.shape
    planes = gz * kb
    lane_parts = [slice(start, start + LANES) for start in range(0, ka, LANES)]
    cuts = sems.shape[0]
    cut = rows // cuts

    def fetch(i):
        part = pl.ds(i * cut, cut)
        return pltpu.make_async_copy(
            spec_hbm.at[:, :, :, part], spec_s.at[:, :, :, part], sems.at[i]
        )

    for i in range(cuts):
        fetch(i).start()
    for i in range(cuts):
        fetch(i).wait()

        def first_columns(j, carry):
            part = pl.ds(pl.multiple_of(i * cut + j * 8, 8), 8)
            for lanes in lane_parts:
                spectra = [
                    [(spec_s[k, z, 0, part, lanes], spec_s[k, z, 1, part, lanes]) for k in range(kb)]
                    for z in range(gz)
                ]
                inverse_columns(gz, kb, spectra, coef_ref, tw_ref, lanes, part, re_s, im_s)
            return carry

        lax.fori_loop(0, cut // 8, first_columns, 0)

    step = plane_chunk(planes, rows)
    shape2, shape3 = (step * rows, ka), (step, rows, ka)

    def there_and_back(i, carry):
        part = pl.ds(i * step, step)
        field = inverse_product(re_s[part].reshape(shape2), im_s[part].reshape(shape2), inverse_ref)
        d0_ref[part] = field.reshape(shape3)
        re, im = forward_product(field, forward_ref)
        re_s[part] = re.reshape(shape3)
        im_s[part] = im.reshape(shape3)
        return carry

    lax.fori_loop(0, planes // step, there_and_back, 0)

    def second_columns(j, total):
        part = pl.ds(pl.multiple_of(j * 8, 8), 8)
        for lanes in lane_parts:
            spectra = forward_columns(gz, kb, coef_ref, tw_ref, lanes, part, re_s, im_s)
            for z in range(gz):
                for k in range(kb):
                    for p in range(2):
                        value = spectra[z][k][p]
                        spec_s[k, z, p, part, lanes] = value
                        total = total + value * value
            inverse_columns(gz, kb, spectra, coef_ref, tw_ref, lanes, part, re_s, im_s)
        return total

    projected = lax.fori_loop(0, rows // 8, second_columns, jnp.zeros((8, LANES), F32))
    gives = [
        pltpu.make_async_copy(spec_s.at[:, core_on(edge_ref, gz, r)], give_hbm[r], out_sems.at[r])
        for r in range(gz)
    ]
    for give in gives:
        give.start()

    def back(i, carry):
        part = pl.ds(i * step, step)
        field = inverse_product(re_s[part].reshape(shape2), im_s[part].reshape(shape2), inverse_ref)
        nd0_ref[part] = field.reshape(shape3)
        return carry

    lax.fori_loop(0, planes // step, back, 0)

    for p in range(planes):
        head_ref[0, p : p + 1, :] = d0_ref[p, :1, :]
        head_ref[1, p : p + 1, :] = d0_ref[p, 1:2, :]
        head_ref[2, p : p + 1, :] = nd0_ref[p, :1, :]
        tail_ref[p : p + 1, :] = d0_ref[p, rows - 1 : rows, :]

    row = lax.broadcasted_iota(jnp.int32, (rows, ka), 0)
    square = jnp.zeros((8, LANES), F32)
    slope = jnp.zeros((8, LANES), F32)
    for p in range(planes):
        here = d0_ref[p]
        square = square + fold(here * here)
        along_x = next_plane(d0_ref, p, kb) - here
        along_y = jnp.where(row == rows - 1, 0.0, pltpu.roll(here, rows - 1, 0) - here)
        terms = along_x * along_x + along_y * along_y
        if p + kb < planes:
            along_z = d0_ref[p + kb] - here
            terms = terms + along_z * along_z
        slope = slope + fold(terms)
    sums_ref[0] = square
    sums_ref[1] = projected
    sums_ref[2] = slope
    for give in gives:
        give.wait()


def middle(edge, spec, coef, nx):
    kb, gz, _, rows, ka = spec.shape
    planes = gz * kb
    vmem = pl.BlockSpec(memory_space=pltpu.VMEM)
    hbm = pl.BlockSpec(memory_space=pltpu.HBM)
    field = jax.ShapeDtypeStruct((planes, rows, ka), F32)
    d0, nd0, head, tail, sums, *pieces = pl.pallas_call(
        functools.partial(middle_kernel, gz),
        in_specs=[pl.BlockSpec(memory_space=pltpu.SMEM), hbm] + [vmem] * 4,
        out_specs=[vmem] * 5 + [hbm] * gz,
        out_shape=[
            field,
            field,
            jax.ShapeDtypeStruct((3, planes, ka), F32),
            jax.ShapeDtypeStruct((planes, ka), F32),
            jax.ShapeDtypeStruct((3, 8, LANES), F32),
        ]
        + [jax.ShapeDtypeStruct((kb, 2, rows, ka), F32)] * gz,
        scratch_shapes=[
            pltpu.VMEM((kb, gz, 2, rows, ka), F32),
            pltpu.VMEM((planes, rows, ka), F32),
            pltpu.VMEM((planes, rows, ka), F32),
            pltpu.SemaphoreType.DMA((2 if rows % 16 == 0 else 1,)),
            pltpu.SemaphoreType.DMA((gz,)),
        ],
        compiler_params=pltpu.CompilerParams(vmem_limit_bytes=X_GRANT),
        name="middle",
    )(
        edge, spec, coef, x_twiddle(nx, ka), jnp.asarray(x_inverse_matrix(nx, ka)),
        x_forward_matrix(nx, ka),
    )
    return d0, nd0, head, tail, sums, pieces


def border_kernel(edge_ref, sums_ref, tail_ref, next_ref, out_ref):
    step = (next_ref[0] - tail_ref[...]) * jnp.where(edge_ref[1] > 0, 0.0, 1.0)
    put_sums(out_ref, [sums_ref[0], sums_ref[1], sums_ref[2] + fold(step * step)])


def border_sums(edge, sums, tail, next_head, copies):
    vmem = pl.BlockSpec(memory_space=pltpu.VMEM)
    return pl.pallas_call(
        border_kernel,
        in_specs=[pl.BlockSpec(memory_space=pltpu.SMEM)] + [vmem] * 3,
        out_specs=vmem,
        out_shape=jax.ShapeDtypeStruct((copies, 8, LANES), F32),
        compiler_params=pltpu.CompilerParams(vmem_limit_bytes=2 * MIB),
        name="border_sums",
    )(edge, sums, tail, next_head)


def second_kernel(
    gz, edge_ref, d0_ref, nd0_ref, tail_ref, prev_ref, next_ref,
    coef_ref, tw_ref, table_ref, *refs,
):
    sums_refs, (d1_ref, eta_ref, out_ref, *refs) = refs[:gz], refs[gz:]
    piece_refs, (sum_s, re_s, im_s, row_s) = refs[:gz], refs[gz:]
    planes, rows, ka = d0_ref.shape
    kb = planes // gz
    eta_here = step_of(sums_refs)
    eta_ref[...] = jnp.broadcast_to(eta_here, (8, LANES))
    eta = jnp.max(eta_here)
    first = edge_ref[0] > 0
    last = edge_ref[1] > 0

    def shrink(difference):
        return jnp.clip(-eta * difference, -CLIP, CLIP)

    lane2 = lax.broadcasted_iota(jnp.int32, (kb, ka), 1)
    row2 = lax.broadcasted_iota(jnp.int32, (kb, ka), 0)
    for z in range(gz):
        part = slice(z * kb, (z + 1) * kb)
        here = next_ref[0, part, :]
        value = here - eta * next_ref[2, part, :]
        up = pltpu.roll(here, kb - 1, 0)
        up = jnp.where(
            row2 == kb - 1, jnp.where(lane2 == ka - 1, here, pltpu.roll(up, ka - 1, 1)), up
        )
        down = pltpu.roll(here, 1, 0)
        down = jnp.where(row2 == 0, jnp.where(lane2 == 0, here, pltpu.roll(down, 1, 1)), down)
        value = value + shrink(here - down) - shrink(up - here)
        value = value + shrink(here - tail_ref[part, :]) - shrink(next_ref[1, part, :] - here)
        if z > 0:
            value = value + shrink(here - next_ref[0, (z - 1) * kb : z * kb, :])
        if z + 1 < gz:
            value = value - shrink(next_ref[0, (z + 1) * kb : (z + 2) * kb, :] - here)
        row_s[part, :] = value

    row = lax.broadcasted_iota(jnp.int32, (rows, ka), 0)
    square = jnp.zeros((8, LANES), F32)
    for p in range(planes):
        here = d0_ref[p]
        value = here - eta * nd0_ref[p]
        value = value + shrink(here - prev_plane(d0_ref, p, kb))
        value = value - shrink(next_plane(d0_ref, p, kb) - here)
        below = jnp.where(last, here[rows - 1 :, :], next_ref[0, p : p + 1, :])
        above = jnp.where(first, here[:1, :], prev_ref[p : p + 1, :])
        upper = shrink(jnp.where(row == rows - 1, below, pltpu.roll(here, rows - 1, 0)) - here)
        lower = jnp.where(row == 0, shrink(here[:1, :] - above), pltpu.roll(upper, 1, 0))
        value = value + lower - upper
        if p >= kb:
            value = value + shrink(here - d0_ref[p - kb])
        if p + kb < planes:
            value = value - shrink(d0_ref[p + kb] - here)
        d1_ref[p] = value
        square = square + fold(value * value)

    slope = jnp.zeros((8, LANES), F32)
    for p in range(planes):
        here = d1_ref[p]
        along_x = next_plane(d1_ref, p, kb) - here
        below = jnp.where(last, here[rows - 1 :, :], row_s[p : p + 1, :])
        along_y = jnp.where(row == rows - 1, below, pltpu.roll(here, rows - 1, 0)) - here
        terms = along_x * along_x + along_y * along_y
        if p + kb < planes:
            along_z = d1_ref[p + kb] - here
            terms = terms + along_z * along_z
        slope = slope + fold(terms)

    step = plane_chunk(planes, rows)

    def multiply(i, carry):
        part = pl.ds(i * step, step)
        re, im = forward_product(d1_ref[part].reshape(step * rows, ka), table_ref)
        re_s[part] = re.reshape(step, rows, ka)
        im_s[part] = im.reshape(step, rows, ka)
        return carry

    lax.fori_loop(0, planes // step, multiply, 0)

    def transform(core):
        def columns(j, total):
            part = pl.ds(pl.multiple_of(j * 8, 8), 8)
            for start in range(0, ka, LANES):
                lanes = slice(start, start + LANES)
                spectra = forward_columns(gz, kb, coef_ref, tw_ref, lanes, part, re_s, im_s)
                for z in range(gz):
                    for k in range(kb):
                        for p in range(2):
                            value = spectra[z][k][p]
                            piece_refs[(z - core) % gz][k, p, part, lanes] = value
                            total = total + value * value
            return total

        sum_s[...] = lax.fori_loop(0, rows // 8, columns, jnp.zeros((8, LANES), F32))

    for core in range(gz):
        pl.when(edge_ref[2] == core)(functools.partial(transform, core))
    put_sums(out_ref, [square, sum_s[...], slope])


def second_descent(edge, sums, d0, nd0, tail, prev_tail, next_head, coef, gz, nx):
    planes, rows, ka = d0.shape
    vmem = pl.BlockSpec(memory_space=pltpu.VMEM)
    piece = jax.ShapeDtypeStruct((planes // gz, 2, rows, ka), F32)
    d1, eta, out, *pieces = pl.pallas_call(
        functools.partial(second_kernel, gz),
        in_specs=[pl.BlockSpec(memory_space=pltpu.SMEM)] + [vmem] * (8 + gz),
        out_specs=[vmem] * (3 + gz),
        out_shape=[
            jax.ShapeDtypeStruct((planes, rows, ka), F32),
            jax.ShapeDtypeStruct((8, LANES), F32),
            jax.ShapeDtypeStruct(sums[0].shape, F32),
        ]
        + [piece] * gz,
        scratch_shapes=[
            pltpu.VMEM((8, LANES), F32),
            pltpu.VMEM((planes, rows, ka), F32),
            pltpu.VMEM((planes, rows, ka), F32),
            pltpu.VMEM((planes, ka), F32),
        ],
        compiler_params=pltpu.CompilerParams(vmem_limit_bytes=X_GRANT),
        name="second_descent",
    )(
        edge, d0, nd0, tail, prev_tail, next_head, coef,
        x_twiddle(nx, ka), x_forward_matrix(nx, ka), *sums,
    )
    return d1, pieces, eta, out


def combine_kernel(gz, edge_ref, eta_ref, *refs):
    sums_refs, refs = refs[:gz], refs[gz:]
    first_refs, second_refs, (out_ref, steps_ref) = refs[:gz], refs[gz : 2 * gz], refs[2 * gz :]
    eta0 = jnp.max(eta_ref[...])
    eta1 = jnp.max(step_of(sums_refs))
    steps_ref[0] = eta_ref[...]
    steps_ref[1] = jnp.full((8, LANES), eta1, F32)
    count = out_ref.shape[0]
    start = pl.program_id(0) * count
    for r in range(gz):
        core = core_on(edge_ref, gz, -r)
        for i in range(count):
            out_ref[i, core] = -(eta0 * first_refs[r][start + i] + eta1 * second_refs[r][start + i])


def combine_spectra(edge, eta, sums, first, second):
    gz = len(sums)
    kb, *rest = first[0].shape
    count = 4 if kb % 4 == 0 else 1
    vmem = pl.BlockSpec(memory_space=pltpu.VMEM)
    return pl.pallas_call(
        functools.partial(combine_kernel, gz),
        grid=(kb // count,),
        in_specs=[pl.BlockSpec(memory_space=pltpu.SMEM)] + [vmem] * (1 + 3 * gz),
        out_specs=[
            pl.BlockSpec((count, gz, *rest), lambda i: (i, 0, 0, 0, 0)),
            pl.BlockSpec((2, 8, LANES), lambda i: (0, 0, 0)),
        ],
        out_shape=[
            jax.ShapeDtypeStruct((kb, gz, *rest), F32),
            jax.ShapeDtypeStruct((2, 8, LANES), F32),
        ],
        compiler_params=pltpu.CompilerParams(vmem_limit_bytes=6 * MIB),
        name="combine_spectra",
    )(edge, eta, *sums, *first, *second)


def to_core(piece, r):
    gz = lax.axis_size("gz")
    return lax.ppermute(piece, "gz", [(i, (i + r) % gz) for i in range(gz)]) if r else piece


def from_cores(pieces):
    return [to_core(piece, r + 1) for r, piece in enumerate(pieces)]


def to_chips(parts):
    return lax.all_to_all(parts, "gy", 0, 0, tiled=True)


def everywhere(sums):
    sums = to_chips(sums)
    return [to_core(sums, r) for r in range(lax.axis_size("gz"))]


def shards(data, band_offset, interp_weight):
    gz = lax.axis_size("gz")
    gy = lax.axis_size("gy")
    devices = gz * gy
    data = data[0]
    blocks, ny, width = data.shape
    rows = ny // devices
    ka = blocks * HALF
    nx = ka * gy

    core = lax.axis_index("gz")
    flat = lax.axis_index("gy") * gz + core
    edge = jnp.stack([flat == 0, flat == devices - 1, core]).astype(jnp.int32)
    order = [(i % gz) * gy + i // gz for i in range(devices)]
    up = [(order[i + 1], order[i]) for i in range(devices - 1)]
    down = [(order[i], order[i + 1]) for i in range(devices - 1)]

    lower = band_offset < 0
    weight = interp_weight
    coef = jnp.stack(
        [
            jnp.where(lower, weight[1], weight[0]),
            jnp.where(lower, weight[0], 0.0),
            jnp.where(lower, 0.0, weight[1]),
        ]
    ).reshape(3, gy, 1, ka)
    coef = jnp.broadcast_to(coef, (3, gy, 8, ka))

    whole, others = y_inverse(edge, data, rows, gz, gy)
    spec = to_chips(merge(edge, whole, from_cores(others)))
    d0, nd0, head, tail, sums, first = middle(edge, spec, coef, nx)
    next_head = lax.ppermute(head, ("gz", "gy"), up)
    prev_tail = lax.ppermute(tail, ("gz", "gy"), down)
    sums = everywhere(border_sums(edge, sums, tail, next_head, gy))
    first = first[:1] + from_cores(first[1:])
    d1, second, eta, sums = second_descent(
        edge, sums, d0, nd0, tail, prev_tail, next_head, coef, gz, nx
    )
    sums = everywhere(sums)
    second = second[:1] + from_cores(second[1:])
    spec, etas = combine_spectra(edge, eta, sums, first, second)
    residual = y_forward(to_chips(spec), data)

    volume = -(etas[0, 0, 0] * d0 + etas[1, 0, 0] * d1)
    volume = volume.reshape(gz, gy, rows, ka).transpose(0, 2, 3, 1).reshape(gz, rows, nx)
    parts = [
        to_core(lax.dynamic_index_in_dim(volume, lax.rem(core + r, gz), 0, False), r)
        for r in range(gz)
    ]
    volume = jnp.zeros((gz, rows, nx), F32)
    for r, part in enumerate(parts):
        volume = lax.dynamic_update_index_in_dim(volume, part, lax.rem(core + gz - r, gz), 0)
    return (volume.reshape(1, gz * rows, nx), residual[None])


NX = 4096
NY = 2048
XB = 64
YB = 64
ITERS = 2
XA = 64
YA = 32
PRECISE = lax.Precision.HIGHEST


def with_halo(block, sides, width):
    for axis, dim in sides:
        count = lax.axis_size(axis)
        forward = [(i, i + 1) for i in range(count - 1)]
        backward = [(target, source) for source, target in forward]
        low = lax.ppermute(
            lax.slice_in_dim(block, block.shape[dim] - width, None, axis=dim), axis, forward
        )
        high = lax.ppermute(lax.slice_in_dim(block, 0, width, axis=dim), axis, backward)
        block = jnp.concatenate([low, block, high], axis=dim)
    return block


def from_behind(block, axis, distance):
    devices = range(lax.axis_size(axis))
    route = [(i - distance, i) for i in devices if i - distance in devices]
    return lax.ppermute(block, axis, route)


def unit_table(length):
    counter = jnp.arange(length, dtype=jnp.int32)
    phase_int = counter[:, None] * counter[None, :] % length
    angles = 2.0 * jnp.pi / length * phase_int.astype(jnp.float32)
    factor = length ** (-0.5)
    return (jnp.cos(angles) * factor, jnp.sin(angles) * factor)


def twiddle_table(row_len, col_len, period):
    phase_int = (
        jnp.arange(row_len, dtype=jnp.int32)[:, None]
        * jnp.arange(col_len, dtype=jnp.int32)[None, :]
        % period
    )
    angles = 2.0 * jnp.pi / period * phase_int.astype(jnp.float32)
    return (jnp.cos(angles), jnp.sin(angles))


def split_parts(packed):
    half_width = packed.shape[-1] // 2
    return (packed[..., :half_width], packed[..., half_width:])


def join_parts(real_part, imag_part):
    return jnp.concatenate([real_part, imag_part], axis=-1)


def complex_contract(packed, cos_table, sin_table, subscripts, conj_sign):
    cos_out = jnp.einsum(subscripts, packed, cos_table, precision=PRECISE)
    sin_out = jnp.einsum(subscripts, packed, sin_table, precision=PRECISE)
    cos_re, cos_im = split_parts(cos_out)
    sin_re, sin_im = split_parts(sin_out)
    return join_parts(cos_re - conj_sign * sin_im, cos_im + conj_sign * sin_re)


def rotate(packed, cos_table, sin_table, conj_sign):
    real_part, imag_part = split_parts(packed)
    return join_parts(
        real_part * cos_table - conj_sign * imag_part * sin_table,
        imag_part * cos_table + conj_sign * real_part * sin_table,
    )


def forward_x(volume):
    slices, row_count = (volume.shape[0], volume.shape[1])
    cos_a, sin_a = unit_table(XA)
    cos_b, sin_b = unit_table(XB)
    first_table = jnp.concatenate([cos_a, -sin_a], axis=1)
    grid_view = volume.reshape(slices, row_count, XA, XB)
    mixing = jnp.einsum("zyab,am->zybm", grid_view, first_table, precision=PRECISE)
    tw_cos, tw_sin = twiddle_table(XB, XA, NX)
    mixing = rotate(mixing, tw_cos, tw_sin, -1.0)
    return complex_contract(mixing, cos_b, sin_b, "zybm,bl->zlym", -1.0)


def inverse_x(packed):
    slices, row_count = (packed.shape[0], packed.shape[2])
    cos_a, sin_a = unit_table(XA)
    cos_b, sin_b = unit_table(XB)
    mixing = complex_contract(packed, cos_b, sin_b, "zlym,lb->zybm", 1.0)
    tw_cos, tw_sin = twiddle_table(XB, XA, NX)
    mixing = rotate(mixing, tw_cos, tw_sin, 1.0)
    last_table = jnp.concatenate([cos_a, -sin_a], axis=0)
    grid_view = jnp.einsum("zybm,ma->zyab", mixing, last_table, precision=PRECISE)
    return grid_view.reshape(slices, row_count, NX)


def forward_y(packed):
    slices, blocks, width = (packed.shape[0], packed.shape[1], packed.shape[3])
    cos_a, sin_a = unit_table(YA)
    cos_b, sin_b = unit_table(YB)
    grid_view = packed.reshape(slices, blocks, YA, YB, width)
    mixing = complex_contract(grid_view, cos_a, sin_a, "zjcdm,ck->zjkdm", -1.0)
    tw_cos, tw_sin = twiddle_table(YA, YB, NY)
    mixing = rotate(mixing, tw_cos[:, :, None], tw_sin[:, :, None], -1.0)
    result = complex_contract(mixing, cos_b, sin_b, "zjkdm,dl->zjlkm", -1.0)
    return result.reshape(slices, blocks, NY, width)


def inverse_y(packed):
    slices, blocks, width = (packed.shape[0], packed.shape[1], packed.shape[3])
    cos_a, sin_a = unit_table(YA)
    cos_b, sin_b = unit_table(YB)
    grid_view = packed.reshape(slices, blocks, YB, YA, width)
    mixing = complex_contract(grid_view, cos_b, sin_b, "zjlkm,ld->zjkdm", 1.0)
    tw_cos, tw_sin = twiddle_table(YA, YB, NY)
    mixing = rotate(mixing, tw_cos[:, :, None], tw_sin[:, :, None], 1.0)
    result = complex_contract(mixing, cos_a, sin_a, "zjkdm,kc->zjcdm", 1.0)
    return result.reshape(slices, blocks, NY, width)


def tilt_coefficients(band_offset, interp_weight, first_block, blocks):
    offsets = lax.dynamic_slice_in_dim(band_offset.reshape(XB, XA), first_block, blocks, 0)
    weights = lax.dynamic_slice_in_dim(interp_weight.reshape(2, XB, XA), first_block, blocks, 1)
    lower_tap = (jnp.concatenate([offsets, offsets], axis=1) < 0)[:, None, :]
    first_weight = jnp.concatenate([weights[0], weights[0]], axis=1)[:, None, :]
    second_weight = jnp.concatenate([weights[1], weights[1]], axis=1)[:, None, :]
    return (lower_tap, first_weight, second_weight)


def tilt(field_in, coefficients, adjoint):
    lower_tap, first_weight, second_weight = coefficients
    padded = with_halo(field_in, (("gz", 0),), 1)
    below_rim = padded[:-2]
    middle = padded[1:-1]
    above_rim = padded[2:]
    if adjoint:
        return jnp.where(
            lower_tap,
            first_weight * above_rim + second_weight * middle,
            first_weight * middle + second_weight * below_rim,
        )
    return jnp.where(
        lower_tap,
        first_weight * below_rim + second_weight * middle,
        first_weight * middle + second_weight * above_rim,
    )


def to_pencil(slab_part):
    return lax.all_to_all(slab_part, "gy", split_axis=1, concat_axis=2, tiled=True)


def to_slab(pencil_part):
    return lax.all_to_all(pencil_part, "gy", split_axis=2, concat_axis=1, tiled=True)


def back_project(packed, pencil_coef):
    return inverse_x(to_slab(inverse_y(tilt(packed, pencil_coef, True))))


def edge_masks(slices, row_count):
    z_global = lax.axis_index("gz") * slices + jnp.arange(slices, dtype=jnp.int32)
    y_global = lax.axis_index("gy") * row_count + jnp.arange(row_count, dtype=jnp.int32)
    keep_z = (z_global < slices * lax.axis_size("gz") - 1).astype(jnp.float32)[:, None, None]
    keep_y = (y_global < row_count * lax.axis_size("gy") - 1).astype(jnp.float32)[None, :, None]
    return (keep_z, keep_y)


def forward_diff(field_in, keep_z, keep_y):
    slices, row_count = (field_in.shape[0], field_in.shape[1])
    next_z = from_behind(field_in, "gz", -1)
    next_y = from_behind(field_in[:, :1], "gy", -1)
    along_z = (jnp.concatenate([field_in[1:], next_z], axis=0) - field_in) * keep_z
    along_y = (jnp.concatenate([field_in[:, 1:], next_y], axis=1) - field_in) * keep_y
    zero_col = jnp.zeros((slices, row_count, 1), jnp.float32)
    along_x = jnp.concatenate([field_in[:, :, 1:] - field_in[:, :, :-1], zero_col], axis=2)
    return jnp.stack([along_z, along_y, along_x])


def transpose_diff(components, keep_z, keep_y):
    slices, row_count = (components.shape[1], components.shape[2])
    zero_col = jnp.zeros((slices, row_count, 1), jnp.float32)
    comp_z = components[0] * keep_z
    comp_y = components[1] * keep_y
    comp_x = jnp.concatenate([components[2][:, :, :-1], zero_col], axis=2)
    prev_z = from_behind(comp_z, "gz", 1)
    prev_y = from_behind(comp_y[:, -1:], "gy", 1)
    result = jnp.concatenate([prev_z, comp_z[:-1]], axis=0) - comp_z
    result = result + jnp.concatenate([prev_y, comp_y[:, :-1]], axis=1) - comp_y
    result = result + jnp.concatenate([zero_col, comp_x[:, :, :-1]], axis=2) - comp_x
    return result


def plain_shards(data, band_offset, interp_weight):
    slices = data.shape[0]
    blocks = data.shape[1]
    width = data.shape[3]
    row_count = NY // lax.axis_size("gy")
    slab_coef = tilt_coefficients(band_offset, interp_weight, 0, XB)
    pencil_coef = tilt_coefficients(
        band_offset, interp_weight, lax.axis_index("gy") * blocks, blocks
    )
    keep_z, keep_y = edge_masks(slices, row_count)
    measured = data.astype(jnp.float32)
    volume = jnp.zeros((slices, row_count, NX), jnp.float32)
    grad_volume = jnp.zeros((3, slices, row_count, NX), jnp.float32)
    split_var = grad_volume
    dual_var = grad_volume
    data_back = back_project(measured, pencil_coef)
    normal_part = jnp.zeros_like(volume)
    tilted = jnp.zeros((slices, XB, row_count, width), jnp.float32)
    for iteration in range(ITERS):
        data_grad = normal_part - data_back
        if iteration > 0:
            tv_gap = grad_volume - split_var + dual_var / PENALTY
            descent = data_grad + PENALTY * transpose_diff(tv_gap, keep_z, keep_y)
        else:
            descent = data_grad
        slope_field = forward_diff(descent, keep_z, keep_y)
        projected = tilt(forward_x(descent), slab_coef, False)
        line_totals = lax.psum(
            (
                jnp.sum(descent * descent),
                jnp.sum(projected * projected),
                jnp.sum(slope_field * slope_field),
            ),
            ("gz", "gy"),
        )
        step_length = line_totals[0] / (line_totals[1] + PENALTY * line_totals[2])
        volume = volume - step_length * descent
        grad_volume = grad_volume - step_length * slope_field
        tilted = tilted - step_length * projected
        if iteration + 1 < ITERS:
            normal_part = normal_part - step_length * inverse_x(tilt(projected, slab_coef, True))
        if iteration + 1 < ITERS:
            shifted = grad_volume + dual_var / PENALTY
            split_var = shifted - jnp.clip(shifted, -TV_WEIGHT / PENALTY, TV_WEIGHT / PENALTY)
            dual_var = PENALTY * (grad_volume - split_var)
    residual = forward_y(to_pencil(tilted)) - measured
    return (volume, residual)


def tiles_fit(mesh, ny, blocks):
    rows = ny // (mesh.shape["gz"] * mesh.shape["gy"])
    return rows % 16 == 0 and mesh.shape["gy"] % YR == 0 and blocks // mesh.shape["gy"] % 2 == 0


def solution(mesh):
    in_specs = (P("gz", "gy", None, None), P(), P())
    out_specs = (P("gz", "gy", None), P("gz", "gy", None, None))

    def run(data, band_offset, interp_weight):
        body = shards if tiles_fit(mesh, data.shape[2], data.shape[1]) else plain_shards
        call = jax.shard_map(
            body, mesh=mesh, in_specs=in_specs, out_specs=out_specs, check_vma=False
        )
        return call(data, band_offset, interp_weight)

    return run
```

```python
import functools

import jax
import jax.numpy as jnp
import numpy as np
from jax import lax
from jax.experimental import pallas as pl
from jax.experimental.pallas import tpu as pltpu
from jax.sharding import PartitionSpec as P

PENALTY = 0.5
TV_WEIGHT = 0.25
CLIP = TV_WEIGHT / PENALTY
HALF = 64
YR = 8
LANES = 128
F32 = jnp.float32
BF16 = jnp.bfloat16
MIB = 1024 * 1024
Y_GRANT = 56 * MIB
X_GRANT = 24 * MIB


def dft_parts(length, scale):
    index = np.arange(length)
    angles = 2.0 * np.pi / length * (index[:, None] * index[None, :] % length)
    return np.cos(angles) * scale, np.sin(angles) * scale


def two_parts(table):
    table = jnp.asarray(table.astype(np.float32))
    high = table.astype(BF16)
    low = (table - high.astype(F32)).astype(BF16)
    return high, low


def host_parts(table):
    table = table.astype(np.float32)
    high = table.astype(BF16)
    low = (table - high.astype(np.float32)).astype(BF16)
    return high, low


def y_matrix(ny, forward, sign):
    n = ny // YR
    cos, sin = dft_parts(n, sign * ny**-0.5)
    if forward:
        table = np.block([[cos, sin], [-sin, cos]])
    else:
        table = np.block([[cos, -sin], [sin, cos]])
    return jnp.asarray(np.concatenate(host_parts(table), axis=0))


def y_twiddle(ny):
    n = ny // YR
    angles = 2.0 * np.pi / ny * (np.arange(1, YR)[:, None] * np.arange(n)[None, :])
    table = np.stack([np.cos(angles), np.sin(angles)]).astype(np.float32)
    return jnp.asarray(np.ascontiguousarray(np.broadcast_to(table[..., None], (2, YR - 1, n, LANES))))


def x_inverse_matrix(nx, ka):
    cos, sin = dft_parts(ka, nx**-0.5)
    return np.concatenate(host_parts(np.concatenate([cos, -sin], axis=0)), axis=1)


def x_forward_matrix(nx, ka):
    cos, sin = dft_parts(ka, nx**-0.5)
    return jnp.asarray(np.concatenate(host_parts(np.concatenate([cos, -sin], axis=1)), axis=1))


def x_twiddle(nx, ka):
    kb = nx // ka
    angles = 2.0 * np.pi / nx * (np.arange(kb)[:, None] * np.arange(ka)[None, :])
    table = np.stack([np.cos(angles), np.sin(angles)]).astype(np.float32)
    return jnp.asarray(np.ascontiguousarray(np.broadcast_to(table[:, :, None], (2, kb, 8, ka))))


def short_fft(planes, sign):
    n = len(planes)
    if n == 1:
        return planes
    even = short_fft(planes[0::2], sign)
    odd = short_fft(planes[1::2], sign)
    half = n // 2
    out = [None] * n
    for k in range(half):
        er, ei = even[k]
        tr, ti = odd[k]
        if 4 * k == n:
            if sign > 0:
                out[k] = (er - ti, ei + tr)
                out[k + half] = (er + ti, ei - tr)
            else:
                out[k] = (er + ti, ei - tr)
                out[k + half] = (er - ti, ei + tr)
            continue
        if k > 0:
            c = float(np.cos(2.0 * np.pi * k / n))
            s = float(sign * np.sin(2.0 * np.pi * k / n))
            if 8 * k == n:
                tr, ti = (tr - ti, ti + tr) if sign > 0 else (tr + ti, ti - tr)
                tr, ti = tr * c, ti * c
            elif 8 * k == 3 * n:
                m = float(np.sin(2.0 * np.pi * k / n))
                tr, ti = (-(tr + ti), tr - ti) if sign > 0 else (ti - tr, -(tr + ti))
                tr, ti = tr * m, ti * m
            else:
                tr, ti = tr * c - ti * s, ti * c + tr * s
        out[k] = (er + tr, ei + ti)
        out[k + half] = (er - tr, ei - ti)
    return out


def split2(x):
    high = x.astype(BF16)
    return high, (x - high.astype(F32)).astype(BF16)


def dot(a, b):
    return jnp.dot(a, b, preferred_element_type=F32)


def fold(x):
    rows, lanes = x.shape
    x = jnp.sum(x.reshape(rows // 8, 8, lanes), axis=0)
    total = x[:, :LANES]
    for i in range(1, lanes // LANES):
        total = total + x[:, i * LANES : (i + 1) * LANES]
    return total


def full_sum(x):
    return jnp.sum(jnp.sum(x, axis=0, keepdims=True), axis=1, keepdims=True)


def step_of(sums_refs):
    total = sum(jnp.sum(sums_ref[...], axis=0) for sums_ref in sums_refs)
    parts = jnp.sum(total, axis=1, keepdims=True)
    return parts[0:1] / (parts[1:2] + PENALTY * parts[2:3])


def put_sums(out_ref, values):
    rows = [jnp.sum(v, axis=0, keepdims=True) for v in values]
    index = lax.broadcasted_iota(jnp.int32, (8, LANES), 0)
    block = jnp.zeros((8, LANES), F32)
    for i, row in enumerate(rows):
        block = jnp.where(index == i, jnp.broadcast_to(row, (8, LANES)), block)
    for i in range(out_ref.shape[0]):
        out_ref[i] = block


def mix_adjoint(coef, planes):
    own, below, above = coef
    out = []
    for z in range(len(planes)):
        value = own * planes[z]
        if z + 1 < len(planes):
            value = value + below * planes[z + 1]
        if z > 0:
            value = value + above * planes[z - 1]
        out.append(value)
    return out


def mix(coef, planes):
    own, below, above = coef
    out = []
    for z in range(len(planes)):
        value = own * planes[z]
        if z > 0:
            value = value + below * planes[z - 1]
        if z + 1 < len(planes):
            value = value + above * planes[z + 1]
        out.append(value)
    return out


def core_on(edge_ref, gz, r):
    return lax.rem(edge_ref[2] + gz + r, gz)


def y_inverse_kernel(gz, edge_ref, data_hbm, table_hbm, tw_hbm, out_hbm, *refs):
    other_refs, refs = refs[: gz - 1], refs[gz - 1 :]
    data_ref, table_ref, tw_ref, own_s, re_s, im_s, mix_s, sems, out_sems = refs
    blocks, ny, _ = data_ref.shape
    n = ny // YR
    rows = own_s.shape[2]
    lane = lax.broadcasted_iota(jnp.int32, (n, LANES), 1)
    pairs = blocks // 2

    def fetch(chunk):
        part = pl.ds(2 * chunk, 2)
        return pltpu.make_async_copy(data_hbm.at[part], data_ref.at[part], sems.at[2 + chunk])

    fetch_table = pltpu.make_async_copy(table_hbm, table_ref, sems.at[0])
    fetch_tw = pltpu.make_async_copy(tw_hbm, tw_ref, sems.at[1])
    fetch(0).start()
    fetch_table.start()
    fetch_tw.start()
    for chunk in range(1, pairs):
        fetch(chunk).start()

    for chunk in range(pairs):
        lanes = slice(chunk * LANES, (chunk + 1) * LANES)
        fetch(chunk).wait()

        def unpack(i, carry):
            part = pl.ds(pl.multiple_of(i * n, n), n)
            first = data_ref[2 * chunk, part, :].astype(F32)
            second = data_ref[2 * chunk + 1, part, :].astype(F32)
            re_s[part, :] = jnp.where(lane < HALF, first, pltpu.roll(second, HALF, 1))
            im_s[part, :] = jnp.where(lane < HALF, pltpu.roll(first, HALF, 1), second)
            return carry

        lax.fori_loop(0, YR, unpack, 0)
        if chunk == 0:
            fetch_table.wait()

        for k in range(0, YR, 2):
            pieces = [
                jnp.concatenate([s[pl.ds(k + d, n, stride=YR), :] for d in range(2)], axis=1)
                for s in (re_s, im_s)
            ]
            both = dot(table_ref[...], jnp.concatenate(pieces, axis=0).astype(BF16))
            both = both[: 2 * n] + both[2 * n :]
            for d in range(2):
                mix_s[k + d] = both[:, d * LANES : (d + 1) * LANES]

        if chunk == 0:
            fetch_tw.wait()

        tiles = rows // 8
        for r in range(gz):
            core = core_on(edge_ref, gz, r)
            target = other_refs[r - 1] if r else own_s

            def combine(i, carry):
                y2 = ((i // tiles) * gz + core) * rows + lax.rem(i, tiles) * 8
                part = pl.ds(pl.multiple_of(y2, 8), 8)
                planes = []
                for k in range(YR):
                    re = mix_s[k, part, :]
                    im = mix_s[k, pl.ds(pl.multiple_of(n + y2, 8), 8), :]
                    if k > 0:
                        c = tw_ref[0, k - 1, part, :]
                        s = tw_ref[1, k - 1, part, :]
                        re, im = re * c - im * s, im * c + re * s
                    planes.append((re, im))
                at = pl.ds(pl.multiple_of(lax.rem(i, tiles) * 8, 8), 8)
                for k, (re, im) in enumerate(short_fft(planes, 1)):
                    to = k * (n // (gz * rows)) + i // tiles
                    target[to, 0, at, lanes] = re
                    target[to, 1, at, lanes] = im
                return carry

            lax.fori_loop(0, n // gz // 8, combine, 0, unroll=2)

    give = pltpu.make_async_copy(own_s, out_hbm.at[:, edge_ref[2]], out_sems.at[0])
    give.start()
    give.wait()


def y_inverse(edge, data, rows, gz, gy):
    blocks, ny, width = data.shape
    n = ny // YR
    ka = blocks * HALF
    vmem = pl.BlockSpec(memory_space=pltpu.VMEM)
    hbm = pl.BlockSpec(memory_space=pltpu.HBM)
    piece = jax.ShapeDtypeStruct((gy, 2, rows, ka), F32)
    whole, *others = pl.pallas_call(
        functools.partial(y_inverse_kernel, gz),
        in_specs=[pl.BlockSpec(memory_space=pltpu.SMEM)] + [hbm] * 3,
        out_specs=[hbm] + [vmem] * (gz - 1),
        out_shape=[jax.ShapeDtypeStruct((gy, gz, 2, rows, ka), F32)] + [piece] * (gz - 1),
        scratch_shapes=[
            pltpu.VMEM((blocks, ny, width), BF16),
            pltpu.VMEM((4 * n, 2 * n), BF16),
            pltpu.VMEM((2, YR - 1, n, LANES), F32),
            pltpu.VMEM((gy, 2, rows, ka), F32),
            pltpu.VMEM((ny, LANES), F32),
            pltpu.VMEM((ny, LANES), F32),
            pltpu.VMEM((YR, 2 * n, LANES), F32),
            pltpu.SemaphoreType.DMA((2 + blocks // 2,)),
            pltpu.SemaphoreType.DMA((1,)),
        ],
        compiler_params=pltpu.CompilerParams(vmem_limit_bytes=Y_GRANT),
        name="y_inverse",
    )(edge, data, y_matrix(ny, False, -1.0), y_twiddle(ny))
    return whole, others


def merge_kernel(gz, edge_ref, *refs):
    pieces, (_, out_hbm, sems) = refs[: gz - 1], refs[gz - 1 :]
    copies = [
        pltpu.make_async_copy(piece, out_hbm.at[:, core_on(edge_ref, gz, -r - 1)], sems.at[r])
        for r, piece in enumerate(pieces)
    ]
    for copy in copies:
        copy.start()
    for copy in copies:
        copy.wait()


def merge(edge, whole, pieces):
    gz = whole.shape[1]
    hbm = pl.BlockSpec(memory_space=pltpu.HBM)
    return pl.pallas_call(
        functools.partial(merge_kernel, gz),
        in_specs=[pl.BlockSpec(memory_space=pltpu.SMEM)]
        + [pl.BlockSpec(memory_space=pl.ANY)] * (gz - 1)
        + [hbm],
        out_specs=hbm,
        out_shape=jax.ShapeDtypeStruct(whole.shape, F32),
        scratch_shapes=[pltpu.SemaphoreType.DMA((gz - 1,))],
        input_output_aliases={gz: 0},
        compiler_params=pltpu.CompilerParams(vmem_limit_bytes=Y_GRANT),
        name="merge",
    )(edge, *pieces, whole)


def y_forward_kernel(
    spec_hbm, data_hbm, table_hbm, tw_hbm, out_hbm,
    spec_ref, data_ref, table_ref, tw_ref, out_ref, re_s, im_s, mix_s, sems, spec_sems, out_sems,
):
    blocks, ny, _ = data_ref.shape
    n = ny // YR
    gy, gz, _, rows, _ = spec_ref.shape
    pairs = blocks // 2
    half = n // 2

    def fetch(chunk):
        lanes = pl.ds(chunk * LANES, LANES)
        return pltpu.make_async_copy(
            spec_hbm.at[:, :, :, :, lanes], spec_ref.at[:, :, :, :, lanes], spec_sems.at[chunk]
        )

    def give(chunk, part):
        at = (pl.ds(2 * chunk, 2), slice(None), pl.ds(part * half, half))
        return pltpu.make_async_copy(out_ref.at[at], out_hbm.at[at], out_sems.at[2 * chunk + part])

    fetch_table = pltpu.make_async_copy(table_hbm, table_ref, sems.at[0])
    fetch_tw = pltpu.make_async_copy(tw_hbm, tw_ref, sems.at[1])
    fetch_data = pltpu.make_async_copy(data_hbm, data_ref, sems.at[2])
    fetch(0).start()
    fetch_table.start()
    fetch_tw.start()
    fetch_data.start()
    for chunk in range(1, pairs):
        fetch(chunk).start()

    lane = lax.broadcasted_iota(jnp.int32, (16, LANES), 1)
    for chunk in range(pairs):
        lanes = slice(chunk * LANES, (chunk + 1) * LANES)
        fetch(chunk).wait()

        def unpack(i, carry):
            for core in range(gz):
                part = pl.ds(pl.multiple_of((i * gz + core) * rows, rows), rows)
                re_s[part, :] = spec_ref[i, core, 0, :, lanes]
                im_s[part, :] = spec_ref[i, core, 1, :, lanes]
            return carry

        lax.fori_loop(0, gy, unpack, 0)
        if chunk == 0:
            fetch_table.wait()

        for k in range(0, YR, 2):
            pieces = [
                jnp.concatenate([s[pl.ds(k + d, n, stride=YR), :] for d in range(2)], axis=1)
                for s in (re_s, im_s)
            ]
            high, low = split2(jnp.concatenate(pieces, axis=0))
            both = dot(table_ref[...], high)
            both = both[: 2 * n] + both[2 * n :] + dot(table_ref[: 2 * n], low)
            for d in range(2):
                mix_s[k + d] = both[:, d * LANES : (d + 1) * LANES]
        if chunk == 0:
            fetch_tw.wait()
            fetch_data.wait()

        def combine(i, carry):
            start = pl.multiple_of(i * 16, 16)
            part = pl.ds(start, 16)
            planes = []
            for k in range(YR):
                re = mix_s[k, part, :]
                im = mix_s[k, pl.ds(pl.multiple_of(n + i * 16, 16), 16), :]
                if k > 0:
                    c = tw_ref[0, k - 1, part, :]
                    s = tw_ref[1, k - 1, part, :]
                    re, im = re * c + im * s, im * c - re * s
                planes.append((re, im))
            for k, (re, im) in enumerate(short_fft(planes, -1)):
                at = pl.ds(pl.multiple_of(k * n + start, 16), 16)
                first = jnp.where(lane < HALF, re, pltpu.roll(im, HALF, 1))
                second = jnp.where(lane < HALF, pltpu.roll(re, HALF, 1), im)
                out_ref[2 * chunk, k, part, :] = first - data_ref[2 * chunk, at, :].astype(F32)
                out_ref[2 * chunk + 1, k, part, :] = (
                    second - data_ref[2 * chunk + 1, at, :].astype(F32)
                )
            return carry

        for part in range(2):
            lax.fori_loop(part * half // 16, (part + 1) * half // 16, combine, 0)
            give(chunk, part).start()

    for chunk in range(pairs):
        for part in range(2):
            give(chunk, part).wait()


def y_forward(spec, data):
    blocks, ny, width = data.shape
    n = ny // YR
    hbm = pl.BlockSpec(memory_space=pltpu.HBM)
    out = pl.pallas_call(
        y_forward_kernel,
        in_specs=[hbm] * 4,
        out_specs=hbm,
        out_shape=jax.ShapeDtypeStruct((blocks, YR, n, width), F32),
        scratch_shapes=[
            pltpu.VMEM(spec.shape, F32),
            pltpu.VMEM((blocks, ny, width), BF16),
            pltpu.VMEM((4 * n, 2 * n), BF16),
            pltpu.VMEM((2, YR - 1, n, LANES), F32),
            pltpu.VMEM((blocks, YR, n, width), F32),
            pltpu.VMEM((ny, LANES), F32),
            pltpu.VMEM((ny, LANES), F32),
            pltpu.VMEM((YR, 2 * n, LANES), F32),
            pltpu.SemaphoreType.DMA((3,)),
            pltpu.SemaphoreType.DMA((blocks // 2,)),
            pltpu.SemaphoreType.DMA((blocks,)),
        ],
        compiler_params=pltpu.CompilerParams(vmem_limit_bytes=Y_GRANT),
        name="y_forward",
    )(spec, data, y_matrix(ny, True, 1.0), y_twiddle(ny))
    return out.reshape(blocks, ny, width)


def plane_chunk(planes, rows):
    chunk = max(1, 1024 // rows)
    while planes % chunk:
        chunk -= 1
    return chunk


def turn_rows(kb, planes_of, tw_ref, lanes, sign):
    out = []
    for b in range(kb):
        re, im = planes_of(b)
        if b > 0:
            c = tw_ref[0, b, :, lanes]
            s = tw_ref[1, b, :, lanes]
            if sign > 0:
                re, im = re * c - im * s, im * c + re * s
            else:
                re, im = re * c + im * s, im * c - re * s
        out.append((re, im))
    return out


def inverse_columns(gz, kb, spectra, coef_ref, tw_ref, lanes, part, re_s, im_s):
    mixed = [[None] * kb for _ in range(gz)]
    for k in range(kb):
        coef = [coef_ref[j, k, :, lanes] for j in range(3)]
        re = mix_adjoint(coef, [spectra[z][k][0] for z in range(gz)])
        im = mix_adjoint(coef, [spectra[z][k][1] for z in range(gz)])
        for z in range(gz):
            mixed[z][k] = (re[z], im[z])
    for z in range(gz):
        short = short_fft(mixed[z], 1)
        for b, (re, im) in enumerate(turn_rows(kb, lambda b: short[b], tw_ref, lanes, 1)):
            re_s[z * kb + b, part, lanes] = re
            im_s[z * kb + b, part, lanes] = im


def forward_columns(gz, kb, coef_ref, tw_ref, lanes, part, re_s, im_s):
    spectra = []
    for z in range(gz):
        rows_of = lambda b: (re_s[z * kb + b, part, lanes], im_s[z * kb + b, part, lanes])
        spectra.append(short_fft(turn_rows(kb, rows_of, tw_ref, lanes, -1), -1))
    out = [[None] * kb for _ in range(gz)]
    for k in range(kb):
        coef = [coef_ref[j, k, :, lanes] for j in range(3)]
        re = mix(coef, [spectra[z][k][0] for z in range(gz)])
        im = mix(coef, [spectra[z][k][1] for z in range(gz)])
        for z in range(gz):
            out[z][k] = (re[z], im[z])
    return out


def inverse_product(re, im, table_ref):
    ka = re.shape[1]
    high, low = split2(jnp.concatenate([re, im], axis=1))
    value = dot(high, table_ref[...])
    return value[:, :ka] + value[:, ka:] + dot(low, table_ref[:, :ka])


def forward_product(field, table_ref):
    ka = field.shape[1]
    high, low = split2(field)
    value = dot(high, table_ref[...])
    value = value[:, : 2 * ka] + value[:, 2 * ka :] + dot(low, table_ref[:, : 2 * ka])
    return value[:, :ka], value[:, ka:]


def next_plane(field_ref, p, kb):
    rows, ka = field_ref.shape[1:]
    if (p + 1) % kb:
        return field_ref[p + 1]
    lane = lax.broadcasted_iota(jnp.int32, (rows, ka), 1)
    return jnp.where(lane == ka - 1, field_ref[p], pltpu.roll(field_ref[p + 1 - kb], ka - 1, 1))


def prev_plane(field_ref, p, kb):
    rows, ka = field_ref.shape[1:]
    if p % kb:
        return field_ref[p - 1]
    lane = lax.broadcasted_iota(jnp.int32, (rows, ka), 1)
    return jnp.where(lane == 0, field_ref[p], pltpu.roll(field_ref[p + kb - 1], 1, 1))


def first_kernel(
    gz, edge_ref, field_ref, coef_ref, tw_ref, table_ref, sums_ref, spec_ref, *refs
):
    piece_refs, (re_s, im_s) = refs[:-2], refs[-2:]
    planes, rows, ka = field_ref.shape
    kb = planes // gz
    projected = forward_into(gz, field_ref, coef_ref, tw_ref, table_ref, spec_ref, re_s, im_s)
    cut(gz, edge_ref, spec_ref, piece_refs)
    row = lax.broadcasted_iota(jnp.int32, (rows, ka), 0)
    square = jnp.zeros((8, LANES), F32)
    slope = jnp.zeros((8, LANES), F32)
    for p in range(planes):
        here = field_ref[p]
        square = square + fold(here * here)
        along_x = next_plane(field_ref, p, kb) - here
        along_y = jnp.where(row == rows - 1, 0.0, pltpu.roll(here, rows - 1, 0) - here)
        terms = along_x * along_x + along_y * along_y
        if p + kb < planes:
            along_z = field_ref[p + kb] - here
            terms = terms + along_z * along_z
        slope = slope + fold(terms)
    sums_ref[0] = square
    sums_ref[1] = projected
    sums_ref[2] = slope


def middle_kernel(
    gz, edge_ref, spec_hbm, coef_ref, tw_ref, inverse_ref, forward_ref,
    d0_ref, nd0_ref, head_ref, tail_ref, sums_ref, *refs,
):
    give_hbm, (spec_s, re_s, im_s, sems, out_sems) = refs[:gz], refs[gz:]
    kb, _, _, rows, ka = spec_s.shape
    planes = gz * kb
    lane_parts = [slice(start, start + LANES) for start in range(0, ka, LANES)]
    cuts = sems.shape[0]
    cut = rows // cuts

    def fetch(i):
        part = pl.ds(i * cut, cut)
        return pltpu.make_async_copy(
            spec_hbm.at[:, :, :, part], spec_s.at[:, :, :, part], sems.at[i]
        )

    for i in range(cuts):
        fetch(i).start()
    for i in range(cuts):
        fetch(i).wait()

        def first_columns(j, carry):
            part = pl.ds(pl.multiple_of(i * cut + j * 8, 8), 8)
            for lanes in lane_parts:
                spectra = [
                    [(spec_s[k, z, 0, part, lanes], spec_s[k, z, 1, part, lanes]) for k in range(kb)]
                    for z in range(gz)
                ]
                inverse_columns(gz, kb, spectra, coef_ref, tw_ref, lanes, part, re_s, im_s)
            return carry

        lax.fori_loop(0, cut // 8, first_columns, 0)

    step = plane_chunk(planes, rows)
    shape2, shape3 = (step * rows, ka), (step, rows, ka)

    def there_and_back(i, carry):
        part = pl.ds(i * step, step)
        field = inverse_product(re_s[part].reshape(shape2), im_s[part].reshape(shape2), inverse_ref)
        d0_ref[part] = field.reshape(shape3)
        re, im = forward_product(field, forward_ref)
        re_s[part] = re.reshape(shape3)
        im_s[part] = im.reshape(shape3)
        return carry

    lax.fori_loop(0, planes // step, there_and_back, 0)

    def second_columns(j, total):
        part = pl.ds(pl.multiple_of(j * 8, 8), 8)
        for lanes in lane_parts:
            spectra = forward_columns(gz, kb, coef_ref, tw_ref, lanes, part, re_s, im_s)
            for z in range(gz):
                for k in range(kb):
                    for p in range(2):
                        value = spectra[z][k][p]
                        spec_s[k, z, p, part, lanes] = value
                        total = total + value * value
            inverse_columns(gz, kb, spectra, coef_ref, tw_ref, lanes, part, re_s, im_s)
        return total

    projected = lax.fori_loop(0, rows // 8, second_columns, jnp.zeros((8, LANES), F32))
    gives = [
        pltpu.make_async_copy(spec_s.at[:, core_on(edge_ref, gz, r)], give_hbm[r], out_sems.at[r])
        for r in range(gz)
    ]
    for give in gives:
        give.start()

    def back(i, carry):
        part = pl.ds(i * step, step)
        field = inverse_product(re_s[part].reshape(shape2), im_s[part].reshape(shape2), inverse_ref)
        nd0_ref[part] = field.reshape(shape3)
        return carry

    lax.fori_loop(0, planes // step, back, 0)

    for p in range(planes):
        head_ref[0, p : p + 1, :] = d0_ref[p, :1, :]
        head_ref[1, p : p + 1, :] = d0_ref[p, 1:2, :]
        head_ref[2, p : p + 1, :] = nd0_ref[p, :1, :]
        tail_ref[p : p + 1, :] = d0_ref[p, rows - 1 : rows, :]

    row = lax.broadcasted_iota(jnp.int32, (rows, ka), 0)
    square = jnp.zeros((8, LANES), F32)
    slope = jnp.zeros((8, LANES), F32)
    for p in range(planes):
        here = d0_ref[p]
        square = square + fold(here * here)
        along_x = next_plane(d0_ref, p, kb) - here
        along_y = jnp.where(row == rows - 1, 0.0, pltpu.roll(here, rows - 1, 0) - here)
        terms = along_x * along_x + along_y * along_y
        if p + kb < planes:
            along_z = d0_ref[p + kb] - here
            terms = terms + along_z * along_z
        slope = slope + fold(terms)
    sums_ref[0] = square
    sums_ref[1] = projected
    sums_ref[2] = slope
    for give in gives:
        give.wait()


def middle(edge, spec, coef, nx):
    kb, gz, _, rows, ka = spec.shape
    planes = gz * kb
    vmem = pl.BlockSpec(memory_space=pltpu.VMEM)
    hbm = pl.BlockSpec(memory_space=pltpu.HBM)
    field = jax.ShapeDtypeStruct((planes, rows, ka), F32)
    d0, nd0, head, tail, sums, *pieces = pl.pallas_call(
        functools.partial(middle_kernel, gz),
        in_specs=[pl.BlockSpec(memory_space=pltpu.SMEM), hbm] + [vmem] * 4,
        out_specs=[vmem] * 5 + [hbm] * gz,
        out_shape=[
            field,
            field,
            jax.ShapeDtypeStruct((3, planes, ka), F32),
            jax.ShapeDtypeStruct((planes, ka), F32),
            jax.ShapeDtypeStruct((3, 8, LANES), F32),
        ]
        + [jax.ShapeDtypeStruct((kb, 2, rows, ka), F32)] * gz,
        scratch_shapes=[
            pltpu.VMEM((kb, gz, 2, rows, ka), F32),
            pltpu.VMEM((planes, rows, ka), F32),
            pltpu.VMEM((planes, rows, ka), F32),
            pltpu.SemaphoreType.DMA((2 if rows % 16 == 0 else 1,)),
            pltpu.SemaphoreType.DMA((gz,)),
        ],
        compiler_params=pltpu.CompilerParams(vmem_limit_bytes=X_GRANT),
        name="middle",
    )(
        edge, spec, coef, x_twiddle(nx, ka), jnp.asarray(x_inverse_matrix(nx, ka)),
        x_forward_matrix(nx, ka),
    )
    return d0, nd0, head, tail, sums, pieces


def border_kernel(edge_ref, sums_ref, tail_ref, next_ref, prev_ref, out_ref):
    del prev_ref
    step = (next_ref[0] - tail_ref[...]) * jnp.where(edge_ref[1] > 0, 0.0, 1.0)
    put_sums(out_ref, [sums_ref[0], sums_ref[1], sums_ref[2] + fold(step * step)])


def border_sums(edge, sums, tail, next_head, prev_tail, copies):
    vmem = pl.BlockSpec(memory_space=pltpu.VMEM)
    return pl.pallas_call(
        border_kernel,
        in_specs=[pl.BlockSpec(memory_space=pltpu.SMEM)] + [vmem] * 4,
        out_specs=vmem,
        out_shape=jax.ShapeDtypeStruct((copies, 8, LANES), F32),
        compiler_params=pltpu.CompilerParams(vmem_limit_bytes=2 * MIB),
        name="border_sums",
    )(edge, sums, tail, next_head, prev_tail)


def second_kernel(
    gz, edge_ref, d0_ref, nd0_ref, tail_ref, prev_ref, next_ref,
    coef_ref, tw_ref, table_ref, *refs,
):
    sums_refs, (d1_ref, eta_ref, out_ref, *refs) = refs[:gz], refs[gz:]
    piece_refs, (sum_s, re_s, im_s, row_s) = refs[:gz], refs[gz:]
    planes, rows, ka = d0_ref.shape
    kb = planes // gz
    eta_here = step_of(sums_refs)
    eta_ref[...] = jnp.broadcast_to(eta_here, (8, LANES))
    eta = jnp.max(eta_here)
    first = edge_ref[0] > 0
    last = edge_ref[1] > 0

    def shrink(difference):
        return jnp.clip(-eta * difference, -CLIP, CLIP)

    lane2 = lax.broadcasted_iota(jnp.int32, (kb, ka), 1)
    row2 = lax.broadcasted_iota(jnp.int32, (kb, ka), 0)
    for z in range(gz):
        part = slice(z * kb, (z + 1) * kb)
        here = next_ref[0, part, :]
        value = here - eta * next_ref[2, part, :]
        up = pltpu.roll(here, kb - 1, 0)
        up = jnp.where(
            row2 == kb - 1, jnp.where(lane2 == ka - 1, here, pltpu.roll(up, ka - 1, 1)), up
        )
        down = pltpu.roll(here, 1, 0)
        down = jnp.where(row2 == 0, jnp.where(lane2 == 0, here, pltpu.roll(down, 1, 1)), down)
        value = value + shrink(here - down) - shrink(up - here)
        value = value + shrink(here - tail_ref[part, :]) - shrink(next_ref[1, part, :] - here)
        if z > 0:
            value = value + shrink(here - next_ref[0, (z - 1) * kb : z * kb, :])
        if z + 1 < gz:
            value = value - shrink(next_ref[0, (z + 1) * kb : (z + 2) * kb, :] - here)
        row_s[part, :] = value

    row = lax.broadcasted_iota(jnp.int32, (rows, ka), 0)
    square = jnp.zeros((8, LANES), F32)
    for p in range(planes):
        here = d0_ref[p]
        value = here - eta * nd0_ref[p]
        value = value + shrink(here - prev_plane(d0_ref, p, kb))
        value = value - shrink(next_plane(d0_ref, p, kb) - here)
        below = jnp.where(last, here[rows - 1 :, :], next_ref[0, p : p + 1, :])
        above = jnp.where(first, here[:1, :], prev_ref[p : p + 1, :])
        upper = shrink(jnp.where(row == rows - 1, below, pltpu.roll(here, rows - 1, 0)) - here)
        lower = jnp.where(row == 0, shrink(here[:1, :] - above), pltpu.roll(upper, 1, 0))
        value = value + lower - upper
        if p >= kb:
            value = value + shrink(here - d0_ref[p - kb])
        if p + kb < planes:
            value = value - shrink(d0_ref[p + kb] - here)
        d1_ref[p] = value
        square = square + fold(value * value)

    slope = jnp.zeros((8, LANES), F32)
    for p in range(planes):
        here = d1_ref[p]
        along_x = next_plane(d1_ref, p, kb) - here
        below = jnp.where(last, here[rows - 1 :, :], row_s[p : p + 1, :])
        along_y = jnp.where(row == rows - 1, below, pltpu.roll(here, rows - 1, 0)) - here
        terms = along_x * along_x + along_y * along_y
        if p + kb < planes:
            along_z = d1_ref[p + kb] - here
            terms = terms + along_z * along_z
        slope = slope + fold(terms)

    step = plane_chunk(planes, rows)

    def multiply(i, carry):
        part = pl.ds(i * step, step)
        re, im = forward_product(d1_ref[part].reshape(step * rows, ka), table_ref)
        re_s[part] = re.reshape(step, rows, ka)
        im_s[part] = im.reshape(step, rows, ka)
        return carry

    lax.fori_loop(0, planes // step, multiply, 0)

    def transform(core):
        def columns(j, total):
            part = pl.ds(pl.multiple_of(j * 8, 8), 8)
            for start in range(0, ka, LANES):
                lanes = slice(start, start + LANES)
                spectra = forward_columns(gz, kb, coef_ref, tw_ref, lanes, part, re_s, im_s)
                for z in range(gz):
                    for k in range(kb):
                        for p in range(2):
                            value = spectra[z][k][p]
                            piece_refs[(z - core) % gz][k, p, part, lanes] = value
                            total = total + value * value
            return total

        sum_s[...] = lax.fori_loop(0, rows // 8, columns, jnp.zeros((8, LANES), F32))

    for core in range(gz):
        pl.when(edge_ref[2] == core)(functools.partial(transform, core))
    put_sums(out_ref, [square, sum_s[...], slope])


def second_descent(edge, sums, d0, nd0, tail, prev_tail, next_head, coef, gz, nx):
    planes, rows, ka = d0.shape
    vmem = pl.BlockSpec(memory_space=pltpu.VMEM)
    piece = jax.ShapeDtypeStruct((planes // gz, 2, rows, ka), F32)
    d1, eta, out, *pieces = pl.pallas_call(
        functools.partial(second_kernel, gz),
        in_specs=[pl.BlockSpec(memory_space=pltpu.SMEM)] + [vmem] * (8 + gz),
        out_specs=[vmem] * (3 + gz),
        out_shape=[
            jax.ShapeDtypeStruct((planes, rows, ka), F32),
            jax.ShapeDtypeStruct((8, LANES), F32),
            jax.ShapeDtypeStruct(sums[0].shape, F32),
        ]
        + [piece] * gz,
        scratch_shapes=[
            pltpu.VMEM((8, LANES), F32),
            pltpu.VMEM((planes, rows, ka), F32),
            pltpu.VMEM((planes, rows, ka), F32),
            pltpu.VMEM((planes, ka), F32),
        ],
        compiler_params=pltpu.CompilerParams(vmem_limit_bytes=X_GRANT),
        name="second_descent",
    )(
        edge, d0, nd0, tail, prev_tail, next_head, coef,
        x_twiddle(nx, ka), x_forward_matrix(nx, ka), *sums,
    )
    return d1, pieces, eta, out


def combine_kernel(gz, edge_ref, eta_ref, *refs):
    sums_refs, refs = refs[:gz], refs[gz:]
    first_refs, second_refs, (out_ref, steps_ref) = refs[:gz], refs[gz : 2 * gz], refs[2 * gz :]
    eta0 = jnp.max(eta_ref[...])
    eta1 = jnp.max(step_of(sums_refs))
    steps_ref[0] = eta_ref[...]
    steps_ref[1] = jnp.full((8, LANES), eta1, F32)
    count = out_ref.shape[0]
    start = pl.program_id(0) * count
    for r in range(gz):
        core = core_on(edge_ref, gz, -r)
        for i in range(count):
            out_ref[i, core] = -(eta0 * first_refs[r][start + i] + eta1 * second_refs[r][start + i])


def combine_spectra(edge, eta, sums, first, second):
    gz = len(sums)
    kb, *rest = first[0].shape
    count = 4 if kb % 4 == 0 else 1
    vmem = pl.BlockSpec(memory_space=pltpu.VMEM)
    return pl.pallas_call(
        functools.partial(combine_kernel, gz),
        grid=(kb // count,),
        in_specs=[pl.BlockSpec(memory_space=pltpu.SMEM)] + [vmem] * (1 + 3 * gz),
        out_specs=[
            pl.BlockSpec((count, gz, *rest), lambda i: (i, 0, 0, 0, 0)),
            pl.BlockSpec((2, 8, LANES), lambda i: (0, 0, 0)),
        ],
        out_shape=[
            jax.ShapeDtypeStruct((kb, gz, *rest), F32),
            jax.ShapeDtypeStruct((2, 8, LANES), F32),
        ],
        compiler_params=pltpu.CompilerParams(vmem_limit_bytes=6 * MIB),
        name="combine_spectra",
    )(edge, eta, *sums, *first, *second)


def to_core(piece, r):
    gz = lax.axis_size("gz")
    return lax.ppermute(piece, "gz", [(i, (i + r) % gz) for i in range(gz)]) if r else piece


def from_cores(pieces):
    return [to_core(piece, r + 1) for r, piece in enumerate(pieces)]


def to_chips(parts):
    return lax.all_to_all(parts, "gy", 0, 0, tiled=True)


def everywhere(sums):
    sums = to_chips(sums)
    return [to_core(sums, r) for r in range(lax.axis_size("gz"))]


def shards(data, band_offset, interp_weight):
    gz = lax.axis_size("gz")
    gy = lax.axis_size("gy")
    devices = gz * gy
    data = data[0]
    blocks, ny, width = data.shape
    rows = ny // devices
    ka = blocks * HALF
    nx = ka * gy

    core = lax.axis_index("gz")
    flat = lax.axis_index("gy") * gz + core
    edge = jnp.stack([flat == 0, flat == devices - 1, core]).astype(jnp.int32)
    order = [(i % gz) * gy + i // gz for i in range(devices)]
    up = [(order[i + 1], order[i]) for i in range(devices - 1)]
    down = [(order[i], order[i + 1]) for i in range(devices - 1)]

    lower = band_offset < 0
    weight = interp_weight
    coef = jnp.stack(
        [
            jnp.where(lower, weight[1], weight[0]),
            jnp.where(lower, weight[0], 0.0),
            jnp.where(lower, 0.0, weight[1]),
        ]
    ).reshape(3, gy, 1, ka)
    coef = jnp.broadcast_to(coef, (3, gy, 8, ka))

    whole, others = y_inverse(edge, data, rows, gz, gy)
    spec = to_chips(merge(edge, whole, from_cores(others)))
    d0, nd0, head, tail, sums, first = middle(edge, spec, coef, nx)
    next_head = lax.ppermute(head, ("gz", "gy"), up)
    prev_tail = lax.ppermute(tail, ("gz", "gy"), down)
    sums = everywhere(border_sums(edge, sums, tail, next_head, prev_tail, gy))
    first = first[:1] + from_cores(first[1:])
    d1, second, eta, sums = second_descent(
        edge, sums, d0, nd0, tail, prev_tail, next_head, coef, gz, nx
    )
    sums = everywhere(sums)
    second = second[:1] + from_cores(second[1:])
    spec, etas = combine_spectra(edge, eta, sums, first, second)
    residual = y_forward(to_chips(spec), data)

    volume = -(etas[0, 0, 0] * d0 + etas[1, 0, 0] * d1)
    volume = volume.reshape(gz, gy, rows, ka).transpose(0, 2, 3, 1).reshape(gz, rows, nx)
    parts = [
        to_core(lax.dynamic_index_in_dim(volume, lax.rem(core + r, gz), 0, False), r)
        for r in range(gz)
    ]
    volume = jnp.zeros((gz, rows, nx), F32)
    for r, part in enumerate(parts):
        volume = lax.dynamic_update_index_in_dim(volume, part, lax.rem(core + gz - r, gz), 0)
    return (volume.reshape(1, gz * rows, nx), residual[None])


NX = 4096
NY = 2048
XB = 64
YB = 64
ITERS = 2
XA = 64
YA = 32
PRECISE = lax.Precision.HIGHEST


def with_halo(block, sides, width):
    for axis, dim in sides:
        count = lax.axis_size(axis)
        forward = [(i, i + 1) for i in range(count - 1)]
        backward = [(target, source) for source, target in forward]
        low = lax.ppermute(
            lax.slice_in_dim(block, block.shape[dim] - width, None, axis=dim), axis, forward
        )
        high = lax.ppermute(lax.slice_in_dim(block, 0, width, axis=dim), axis, backward)
        block = jnp.concatenate([low, block, high], axis=dim)
    return block


def from_behind(block, axis, distance):
    devices = range(lax.axis_size(axis))
    route = [(i - distance, i) for i in devices if i - distance in devices]
    return lax.ppermute(block, axis, route)


def unit_table(length):
    counter = jnp.arange(length, dtype=jnp.int32)
    phase_int = counter[:, None] * counter[None, :] % length
    angles = 2.0 * jnp.pi / length * phase_int.astype(jnp.float32)
    factor = length ** (-0.5)
    return (jnp.cos(angles) * factor, jnp.sin(angles) * factor)


def twiddle_table(row_len, col_len, period):
    phase_int = (
        jnp.arange(row_len, dtype=jnp.int32)[:, None]
        * jnp.arange(col_len, dtype=jnp.int32)[None, :]
        % period
    )
    angles = 2.0 * jnp.pi / period * phase_int.astype(jnp.float32)
    return (jnp.cos(angles), jnp.sin(angles))


def split_parts(packed):
    half_width = packed.shape[-1] // 2
    return (packed[..., :half_width], packed[..., half_width:])


def join_parts(real_part, imag_part):
    return jnp.concatenate([real_part, imag_part], axis=-1)


def complex_contract(packed, cos_table, sin_table, subscripts, conj_sign):
    cos_out = jnp.einsum(subscripts, packed, cos_table, precision=PRECISE)
    sin_out = jnp.einsum(subscripts, packed, sin_table, precision=PRECISE)
    cos_re, cos_im = split_parts(cos_out)
    sin_re, sin_im = split_parts(sin_out)
    return join_parts(cos_re - conj_sign * sin_im, cos_im + conj_sign * sin_re)


def rotate(packed, cos_table, sin_table, conj_sign):
    real_part, imag_part = split_parts(packed)
    return join_parts(
        real_part * cos_table - conj_sign * imag_part * sin_table,
        imag_part * cos_table + conj_sign * real_part * sin_table,
    )


def forward_x(volume):
    slices, row_count = (volume.shape[0], volume.shape[1])
    cos_a, sin_a = unit_table(XA)
    cos_b, sin_b = unit_table(XB)
    first_table = jnp.concatenate([cos_a, -sin_a], axis=1)
    grid_view = volume.reshape(slices, row_count, XA, XB)
    mixing = jnp.einsum("zyab,am->zybm", grid_view, first_table, precision=PRECISE)
    tw_cos, tw_sin = twiddle_table(XB, XA, NX)
    mixing = rotate(mixing, tw_cos, tw_sin, -1.0)
    return complex_contract(mixing, cos_b, sin_b, "zybm,bl->zlym", -1.0)


def inverse_x(packed):
    slices, row_count = (packed.shape[0], packed.shape[2])
    cos_a, sin_a = unit_table(XA)
    cos_b, sin_b = unit_table(XB)
    mixing = complex_contract(packed, cos_b, sin_b, "zlym,lb->zybm", 1.0)
    tw_cos, tw_sin = twiddle_table(XB, XA, NX)
    mixing = rotate(mixing, tw_cos, tw_sin, 1.0)
    last_table = jnp.concatenate([cos_a, -sin_a], axis=0)
    grid_view = jnp.einsum("zybm,ma->zyab", mixing, last_table, precision=PRECISE)
    return grid_view.reshape(slices, row_count, NX)


def forward_y(packed):
    slices, blocks, width = (packed.shape[0], packed.shape[1], packed.shape[3])
    cos_a, sin_a = unit_table(YA)
    cos_b, sin_b = unit_table(YB)
    grid_view = packed.reshape(slices, blocks, YA, YB, width)
    mixing = complex_contract(grid_view, cos_a, sin_a, "zjcdm,ck->zjkdm", -1.0)
    tw_cos, tw_sin = twiddle_table(YA, YB, NY)
    mixing = rotate(mixing, tw_cos[:, :, None], tw_sin[:, :, None], -1.0)
    result = complex_contract(mixing, cos_b, sin_b, "zjkdm,dl->zjlkm", -1.0)
    return result.reshape(slices, blocks, NY, width)


def inverse_y(packed):
    slices, blocks, width = (packed.shape[0], packed.shape[1], packed.shape[3])
    cos_a, sin_a = unit_table(YA)
    cos_b, sin_b = unit_table(YB)
    grid_view = packed.reshape(slices, blocks, YB, YA, width)
    mixing = complex_contract(grid_view, cos_b, sin_b, "zjlkm,ld->zjkdm", 1.0)
    tw_cos, tw_sin = twiddle_table(YA, YB, NY)
    mixing = rotate(mixing, tw_cos[:, :, None], tw_sin[:, :, None], 1.0)
    result = complex_contract(mixing, cos_a, sin_a, "zjkdm,kc->zjcdm", 1.0)
    return result.reshape(slices, blocks, NY, width)


def tilt_coefficients(band_offset, interp_weight, first_block, blocks):
    offsets = lax.dynamic_slice_in_dim(band_offset.reshape(XB, XA), first_block, blocks, 0)
    weights = lax.dynamic_slice_in_dim(interp_weight.reshape(2, XB, XA), first_block, blocks, 1)
    lower_tap = (jnp.concatenate([offsets, offsets], axis=1) < 0)[:, None, :]
    first_weight = jnp.concatenate([weights[0], weights[0]], axis=1)[:, None, :]
    second_weight = jnp.concatenate([weights[1], weights[1]], axis=1)[:, None, :]
    return (lower_tap, first_weight, second_weight)


def tilt(field_in, coefficients, adjoint):
    lower_tap, first_weight, second_weight = coefficients
    padded = with_halo(field_in, (("gz", 0),), 1)
    below_rim = padded[:-2]
    middle = padded[1:-1]
    above_rim = padded[2:]
    if adjoint:
        return jnp.where(
            lower_tap,
            first_weight * above_rim + second_weight * middle,
            first_weight * middle + second_weight * below_rim,
        )
    return jnp.where(
        lower_tap,
        first_weight * below_rim + second_weight * middle,
        first_weight * middle + second_weight * above_rim,
    )


def to_pencil(slab_part):
    return lax.all_to_all(slab_part, "gy", split_axis=1, concat_axis=2, tiled=True)


def to_slab(pencil_part):
    return lax.all_to_all(pencil_part, "gy", split_axis=2, concat_axis=1, tiled=True)


def back_project(packed, pencil_coef):
    return inverse_x(to_slab(inverse_y(tilt(packed, pencil_coef, True))))


def edge_masks(slices, row_count):
    z_global = lax.axis_index("gz") * slices + jnp.arange(slices, dtype=jnp.int32)
    y_global = lax.axis_index("gy") * row_count + jnp.arange(row_count, dtype=jnp.int32)
    keep_z = (z_global < slices * lax.axis_size("gz") - 1).astype(jnp.float32)[:, None, None]
    keep_y = (y_global < row_count * lax.axis_size("gy") - 1).astype(jnp.float32)[None, :, None]
    return (keep_z, keep_y)


def forward_diff(field_in, keep_z, keep_y):
    slices, row_count = (field_in.shape[0], field_in.shape[1])
    next_z = from_behind(field_in, "gz", -1)
    next_y = from_behind(field_in[:, :1], "gy", -1)
    along_z = (jnp.concatenate([field_in[1:], next_z], axis=0) - field_in) * keep_z
    along_y = (jnp.concatenate([field_in[:, 1:], next_y], axis=1) - field_in) * keep_y
    zero_col = jnp.zeros((slices, row_count, 1), jnp.float32)
    along_x = jnp.concatenate([field_in[:, :, 1:] - field_in[:, :, :-1], zero_col], axis=2)
    return jnp.stack([along_z, along_y, along_x])


def transpose_diff(components, keep_z, keep_y):
    slices, row_count = (components.shape[1], components.shape[2])
    zero_col = jnp.zeros((slices, row_count, 1), jnp.float32)
    comp_z = components[0] * keep_z
    comp_y = components[1] * keep_y
    comp_x = jnp.concatenate([components[2][:, :, :-1], zero_col], axis=2)
    prev_z = from_behind(comp_z, "gz", 1)
    prev_y = from_behind(comp_y[:, -1:], "gy", 1)
    result = jnp.concatenate([prev_z, comp_z[:-1]], axis=0) - comp_z
    result = result + jnp.concatenate([prev_y, comp_y[:, :-1]], axis=1) - comp_y
    result = result + jnp.concatenate([zero_col, comp_x[:, :, :-1]], axis=2) - comp_x
    return result


def plain_shards(data, band_offset, interp_weight):
    slices = data.shape[0]
    blocks = data.shape[1]
    width = data.shape[3]
    row_count = NY // lax.axis_size("gy")
    slab_coef = tilt_coefficients(band_offset, interp_weight, 0, XB)
    pencil_coef = tilt_coefficients(
        band_offset, interp_weight, lax.axis_index("gy") * blocks, blocks
    )
    keep_z, keep_y = edge_masks(slices, row_count)
    measured = data.astype(jnp.float32)
    volume = jnp.zeros((slices, row_count, NX), jnp.float32)
    grad_volume = jnp.zeros((3, slices, row_count, NX), jnp.float32)
    split_var = grad_volume
    dual_var = grad_volume
    data_back = back_project(measured, pencil_coef)
    normal_part = jnp.zeros_like(volume)
    tilted = jnp.zeros((slices, XB, row_count, width), jnp.float32)
    for iteration in range(ITERS):
        data_grad = normal_part - data_back
        if iteration > 0:
            tv_gap = grad_volume - split_var + dual_var / PENALTY
            descent = data_grad + PENALTY * transpose_diff(tv_gap, keep_z, keep_y)
        else:
            descent = data_grad
        slope_field = forward_diff(descent, keep_z, keep_y)
        projected = tilt(forward_x(descent), slab_coef, False)
        line_totals = lax.psum(
            (
                jnp.sum(descent * descent),
                jnp.sum(projected * projected),
                jnp.sum(slope_field * slope_field),
            ),
            ("gz", "gy"),
        )
        step_length = line_totals[0] / (line_totals[1] + PENALTY * line_totals[2])
        volume = volume - step_length * descent
        grad_volume = grad_volume - step_length * slope_field
        tilted = tilted - step_length * projected
        if iteration + 1 < ITERS:
            normal_part = normal_part - step_length * inverse_x(tilt(projected, slab_coef, True))
        if iteration + 1 < ITERS:
            shifted = grad_volume + dual_var / PENALTY
            split_var = shifted - jnp.clip(shifted, -TV_WEIGHT / PENALTY, TV_WEIGHT / PENALTY)
            dual_var = PENALTY * (grad_volume - split_var)
    residual = forward_y(to_pencil(tilted)) - measured
    return (volume, residual)


def tiles_fit(mesh, ny, blocks):
    rows = ny // (mesh.shape["gz"] * mesh.shape["gy"])
    return rows % 16 == 0 and mesh.shape["gy"] % YR == 0 and blocks // mesh.shape["gy"] % 2 == 0


def solution(mesh):
    in_specs = (P("gz", "gy", None, None), P(), P())
    out_specs = (P("gz", "gy", None), P("gz", "gy", None, None))

    def run(data, band_offset, interp_weight):
        body = shards if tiles_fit(mesh, data.shape[2], data.shape[1]) else plain_shards
        call = jax.shard_map(
            body, mesh=mesh, in_specs=in_specs, out_specs=out_specs, check_vma=False
        )
        return call(data, band_offset, interp_weight)

    return run
```

```python
import functools

import jax
import jax.numpy as jnp
import numpy as np
from jax import lax
from jax.experimental import pallas as pl
from jax.experimental.pallas import tpu as pltpu
from jax.sharding import PartitionSpec as P

PENALTY = 0.5
TV_WEIGHT = 0.25
CLIP = TV_WEIGHT / PENALTY
HALF = 64
YR = 8
LANES = 128
F32 = jnp.float32
BF16 = jnp.bfloat16
MIB = 1024 * 1024
Y_GRANT = 56 * MIB
X_GRANT = 20 * MIB


def dft_parts(length, scale):
    index = np.arange(length)
    angles = 2.0 * np.pi / length * (index[:, None] * index[None, :] % length)
    return np.cos(angles) * scale, np.sin(angles) * scale


def two_parts(table):
    table = jnp.asarray(table.astype(np.float32))
    high = table.astype(BF16)
    low = (table - high.astype(F32)).astype(BF16)
    return high, low


def host_parts(table):
    table = table.astype(np.float32)
    high = table.astype(BF16)
    low = (table - high.astype(np.float32)).astype(BF16)
    return high, low


def y_matrix(ny, forward, sign):
    n = ny // YR
    cos, sin = dft_parts(n, sign * ny**-0.5)
    if forward:
        table = np.block([[cos, sin], [-sin, cos]])
    else:
        table = np.block([[cos, -sin], [sin, cos]])
    return jnp.asarray(np.concatenate(host_parts(table), axis=0))


def y_twiddle(ny):
    n = ny // YR
    angles = 2.0 * np.pi / ny * (np.arange(1, YR)[:, None] * np.arange(n)[None, :])
    table = np.stack([np.cos(angles), np.sin(angles)]).astype(np.float32)
    return jnp.asarray(np.ascontiguousarray(np.broadcast_to(table[..., None], (2, YR - 1, n, LANES))))


def x_inverse_matrix(nx, ka):
    cos, sin = dft_parts(ka, nx**-0.5)
    return np.concatenate(host_parts(np.concatenate([cos, -sin], axis=0)), axis=1)


def x_forward_matrix(nx, ka):
    cos, sin = dft_parts(ka, nx**-0.5)
    return jnp.asarray(np.concatenate(host_parts(np.concatenate([cos, -sin], axis=1)), axis=1))


def x_twiddle(nx, ka):
    kb = nx // ka
    angles = 2.0 * np.pi / nx * (np.arange(kb)[:, None] * np.arange(ka)[None, :])
    table = np.stack([np.cos(angles), np.sin(angles)]).astype(np.float32)
    return jnp.asarray(np.ascontiguousarray(np.broadcast_to(table[:, :, None], (2, kb, 8, ka))))


def short_fft(planes, sign):
    n = len(planes)
    if n == 1:
        return planes
    even = short_fft(planes[0::2], sign)
    odd = short_fft(planes[1::2], sign)
    half = n // 2
    out = [None] * n
    for k in range(half):
        er, ei = even[k]
        tr, ti = odd[k]
        if 4 * k == n:
            if sign > 0:
                out[k] = (er - ti, ei + tr)
                out[k + half] = (er + ti, ei - tr)
            else:
                out[k] = (er + ti, ei - tr)
                out[k + half] = (er - ti, ei + tr)
            continue
        if k > 0:
            c = float(np.cos(2.0 * np.pi * k / n))
            s = float(sign * np.sin(2.0 * np.pi * k / n))
            if 8 * k == n:
                tr, ti = (tr - ti, ti + tr) if sign > 0 else (tr + ti, ti - tr)
                tr, ti = tr * c, ti * c
            elif 8 * k == 3 * n:
                m = float(np.sin(2.0 * np.pi * k / n))
                tr, ti = (-(tr + ti), tr - ti) if sign > 0 else (ti - tr, -(tr + ti))
                tr, ti = tr * m, ti * m
            else:
                tr, ti = tr * c - ti * s, ti * c + tr * s
        out[k] = (er + tr, ei + ti)
        out[k + half] = (er - tr, ei - ti)
    return out


def split2(x):
    high = x.astype(BF16)
    return high, (x - high.astype(F32)).astype(BF16)


def dot(a, b):
    return jnp.dot(a, b, preferred_element_type=F32)


def fold(x):
    rows, lanes = x.shape
    x = jnp.sum(x.reshape(rows // 8, 8, lanes), axis=0)
    total = x[:, :LANES]
    for i in range(1, lanes // LANES):
        total = total + x[:, i * LANES : (i + 1) * LANES]
    return total


def full_sum(x):
    return jnp.sum(jnp.sum(x, axis=0, keepdims=True), axis=1, keepdims=True)


def step_of(sums_refs):
    total = sum(jnp.sum(sums_ref[...], axis=0) for sums_ref in sums_refs)
    parts = jnp.sum(total, axis=1, keepdims=True)
    return parts[0:1] / (parts[1:2] + PENALTY * parts[2:3])


def put_sums(out_ref, values):
    rows = [jnp.sum(v, axis=0, keepdims=True) for v in values]
    index = lax.broadcasted_iota(jnp.int32, (8, LANES), 0)
    block = jnp.zeros((8, LANES), F32)
    for i, row in enumerate(rows):
        block = jnp.where(index == i, jnp.broadcast_to(row, (8, LANES)), block)
    for i in range(out_ref.shape[0]):
        out_ref[i] = block


def mix_adjoint(coef, planes):
    own, below, above = coef
    out = []
    for z in range(len(planes)):
        value = own * planes[z]
        if z + 1 < len(planes):
            value = value + below * planes[z + 1]
        if z > 0:
            value = value + above * planes[z - 1]
        out.append(value)
    return out


def mix(coef, planes):
    own, below, above = coef
    out = []
    for z in range(len(planes)):
        value = own * planes[z]
        if z > 0:
            value = value + below * planes[z - 1]
        if z + 1 < len(planes):
            value = value + above * planes[z + 1]
        out.append(value)
    return out


def y_inverse_kernel(
    data_hbm, table_hbm, tw_hbm, out_hbm,
    data_ref, table_ref, tw_ref, out_ref, re_s, im_s, mix_s, sems, out_sems,
):
    blocks, ny, _ = data_ref.shape
    n = ny // YR
    gz, _, _, rows, _ = out_ref.shape
    lane = lax.broadcasted_iota(jnp.int32, (n, LANES), 1)
    pairs = blocks // 2

    def fetch(chunk):
        part = pl.ds(2 * chunk, 2)
        return pltpu.make_async_copy(data_hbm.at[part], data_ref.at[part], sems.at[2 + chunk])

    def give(chunk, core):
        at = (core, slice(None), slice(None), slice(None), pl.ds(chunk * LANES, LANES))
        return pltpu.make_async_copy(out_ref.at[at], out_hbm.at[at], out_sems.at[chunk * gz + core])

    fetch_table = pltpu.make_async_copy(table_hbm, table_ref, sems.at[0])
    fetch_tw = pltpu.make_async_copy(tw_hbm, tw_ref, sems.at[1])
    fetch(0).start()
    fetch_table.start()
    fetch_tw.start()
    for chunk in range(1, pairs):
        fetch(chunk).start()

    for chunk in range(pairs):
        lanes = slice(chunk * LANES, (chunk + 1) * LANES)
        fetch(chunk).wait()

        def unpack(i, carry):
            part = pl.ds(pl.multiple_of(i * n, n), n)
            first = data_ref[2 * chunk, part, :].astype(F32)
            second = data_ref[2 * chunk + 1, part, :].astype(F32)
            re_s[part, :] = jnp.where(lane < HALF, first, pltpu.roll(second, HALF, 1))
            im_s[part, :] = jnp.where(lane < HALF, pltpu.roll(first, HALF, 1), second)
            return carry

        lax.fori_loop(0, YR, unpack, 0)
        if chunk == 0:
            fetch_table.wait()

        for k in range(0, YR, 2):
            pieces = [
                jnp.concatenate([s[pl.ds(k + d, n, stride=YR), :] for d in range(2)], axis=1)
                for s in (re_s, im_s)
            ]
            both = dot(table_ref[...], jnp.concatenate(pieces, axis=0).astype(BF16))
            both = both[: 2 * n] + both[2 * n :]
            for d in range(2):
                mix_s[k + d] = both[:, d * LANES : (d + 1) * LANES]

        if chunk == 0:
            fetch_tw.wait()

        tiles = rows // 8
        for core in range(gz):

            def combine(i, carry):
                y2 = ((i // tiles) * gz + core) * rows + lax.rem(i, tiles) * 8
                part = pl.ds(pl.multiple_of(y2, 8), 8)
                planes = []
                for k in range(YR):
                    re = mix_s[k, part, :]
                    im = mix_s[k, pl.ds(pl.multiple_of(n + y2, 8), 8), :]
                    if k > 0:
                        c = tw_ref[0, k - 1, part, :]
                        s = tw_ref[1, k - 1, part, :]
                        re, im = re * c - im * s, im * c + re * s
                    planes.append((re, im))
                at = pl.ds(pl.multiple_of(lax.rem(i, tiles) * 8, 8), 8)
                for k, (re, im) in enumerate(short_fft(planes, 1)):
                    to = k * (n // (gz * rows)) + i // tiles
                    out_ref[core, to, 0, at, lanes] = re
                    out_ref[core, to, 1, at, lanes] = im
                return carry

            lax.fori_loop(0, n // gz // 8, combine, 0, unroll=2)
            give(chunk, core).start()

    for chunk in range(pairs):
        for core in range(gz):
            give(chunk, core).wait()


def y_inverse(data, rows, gz, gy):
    blocks, ny, width = data.shape
    n = ny // YR
    ka = blocks * HALF
    hbm = pl.BlockSpec(memory_space=pltpu.HBM)
    return pl.pallas_call(
        y_inverse_kernel,
        in_specs=[hbm] * 3,
        out_specs=hbm,
        out_shape=jax.ShapeDtypeStruct((gz, gy, 2, rows, ka), F32),
        scratch_shapes=[
            pltpu.VMEM((blocks, ny, width), BF16),
            pltpu.VMEM((4 * n, 2 * n), BF16),
            pltpu.VMEM((2, YR - 1, n, LANES), F32),
            pltpu.VMEM((gz, gy, 2, rows, ka), F32),
            pltpu.VMEM((ny, LANES), F32),
            pltpu.VMEM((ny, LANES), F32),
            pltpu.VMEM((YR, 2 * n, LANES), F32),
            pltpu.SemaphoreType.DMA((2 + blocks // 2,)),
            pltpu.SemaphoreType.DMA((blocks // 2 * gz,)),
        ],
        compiler_params=pltpu.CompilerParams(vmem_limit_bytes=Y_GRANT),
        name="y_inverse",
    )(data, y_matrix(ny, False, -1.0), y_twiddle(ny))


def y_forward_kernel(
    spec_hbm, data_hbm, table_hbm, tw_hbm, out_hbm,
    spec_ref, data_ref, table_ref, tw_ref, out_ref, re_s, im_s, mix_s, sems, spec_sems, out_sems,
):
    blocks, ny, _ = data_ref.shape
    n = ny // YR
    gz, gy, _, rows, _ = spec_ref.shape
    pairs = blocks // 2
    half = n // 2

    def fetch(chunk):
        lanes = pl.ds(chunk * LANES, LANES)
        return pltpu.make_async_copy(
            spec_hbm.at[:, :, :, :, lanes], spec_ref.at[:, :, :, :, lanes], spec_sems.at[chunk]
        )

    def give(chunk, part):
        at = (pl.ds(2 * chunk, 2), slice(None), pl.ds(part * half, half))
        return pltpu.make_async_copy(out_ref.at[at], out_hbm.at[at], out_sems.at[2 * chunk + part])

    fetch_table = pltpu.make_async_copy(table_hbm, table_ref, sems.at[0])
    fetch_tw = pltpu.make_async_copy(tw_hbm, tw_ref, sems.at[1])
    fetch_data = pltpu.make_async_copy(data_hbm, data_ref, sems.at[2])
    fetch(0).start()
    fetch_table.start()
    fetch_tw.start()
    fetch_data.start()
    for chunk in range(1, pairs):
        fetch(chunk).start()

    lane = lax.broadcasted_iota(jnp.int32, (16, LANES), 1)
    for chunk in range(pairs):
        lanes = slice(chunk * LANES, (chunk + 1) * LANES)
        fetch(chunk).wait()

        def unpack(i, carry):
            for core in range(gz):
                part = pl.ds(pl.multiple_of((i * gz + core) * rows, rows), rows)
                re_s[part, :] = spec_ref[core, i, 0, :, lanes]
                im_s[part, :] = spec_ref[core, i, 1, :, lanes]
            return carry

        lax.fori_loop(0, gy, unpack, 0)
        if chunk == 0:
            fetch_table.wait()

        for k in range(0, YR, 2):
            pieces = [
                jnp.concatenate([s[pl.ds(k + d, n, stride=YR), :] for d in range(2)], axis=1)
                for s in (re_s, im_s)
            ]
            high, low = split2(jnp.concatenate(pieces, axis=0))
            both = dot(table_ref[...], high)
            both = both[: 2 * n] + both[2 * n :] + dot(table_ref[: 2 * n], low)
            for d in range(2):
                mix_s[k + d] = both[:, d * LANES : (d + 1) * LANES]
        if chunk == 0:
            fetch_tw.wait()
            fetch_data.wait()

        def combine(i, carry):
            start = pl.multiple_of(i * 16, 16)
            part = pl.ds(start, 16)
            planes = []
            for k in range(YR):
                re = mix_s[k, part, :]
                im = mix_s[k, pl.ds(pl.multiple_of(n + i * 16, 16), 16), :]
                if k > 0:
                    c = tw_ref[0, k - 1, part, :]
                    s = tw_ref[1, k - 1, part, :]
                    re, im = re * c + im * s, im * c - re * s
                planes.append((re, im))
            for k, (re, im) in enumerate(short_fft(planes, -1)):
                at = pl.ds(pl.multiple_of(k * n + start, 16), 16)
                first = jnp.where(lane < HALF, re, pltpu.roll(im, HALF, 1))
                second = jnp.where(lane < HALF, pltpu.roll(re, HALF, 1), im)
                out_ref[2 * chunk, k, part, :] = first - data_ref[2 * chunk, at, :].astype(F32)
                out_ref[2 * chunk + 1, k, part, :] = (
                    second - data_ref[2 * chunk + 1, at, :].astype(F32)
                )
            return carry

        for part in range(2):
            lax.fori_loop(part * half // 16, (part + 1) * half // 16, combine, 0)
            give(chunk, part).start()

    for chunk in range(pairs):
        for part in range(2):
            give(chunk, part).wait()


def y_forward(spec, data):
    blocks, ny, width = data.shape
    n = ny // YR
    hbm = pl.BlockSpec(memory_space=pltpu.HBM)
    out = pl.pallas_call(
        y_forward_kernel,
        in_specs=[hbm] * 4,
        out_specs=hbm,
        out_shape=jax.ShapeDtypeStruct((blocks, YR, n, width), F32),
        scratch_shapes=[
            pltpu.VMEM(spec.shape, F32),
            pltpu.VMEM((blocks, ny, width), BF16),
            pltpu.VMEM((4 * n, 2 * n), BF16),
            pltpu.VMEM((2, YR - 1, n, LANES), F32),
            pltpu.VMEM((blocks, YR, n, width), F32),
            pltpu.VMEM((ny, LANES), F32),
            pltpu.VMEM((ny, LANES), F32),
            pltpu.VMEM((YR, 2 * n, LANES), F32),
            pltpu.SemaphoreType.DMA((3,)),
            pltpu.SemaphoreType.DMA((blocks // 2,)),
            pltpu.SemaphoreType.DMA((blocks,)),
        ],
        compiler_params=pltpu.CompilerParams(vmem_limit_bytes=Y_GRANT),
        name="y_forward",
    )(spec, data, y_matrix(ny, True, 1.0), y_twiddle(ny))
    return out.reshape(blocks, ny, width)


def plane_chunk(planes, rows):
    chunk = max(1, 1024 // rows)
    while planes % chunk:
        chunk -= 1
    return chunk


def turn_rows(kb, planes_of, tw_ref, lanes, sign):
    out = []
    for b in range(kb):
        re, im = planes_of(b)
        if b > 0:
            c = tw_ref[0, b, :, lanes]
            s = tw_ref[1, b, :, lanes]
            if sign > 0:
                re, im = re * c - im * s, im * c + re * s
            else:
                re, im = re * c + im * s, im * c - re * s
        out.append((re, im))
    return out


def inverse_columns(gz, kb, spectra, coef_ref, tw_ref, lanes, part, re_s, im_s):
    mixed = [[None] * kb for _ in range(gz)]
    for k in range(kb):
        coef = [coef_ref[j, k, :, lanes] for j in range(3)]
        re = mix_adjoint(coef, [spectra[z][k][0] for z in range(gz)])
        im = mix_adjoint(coef, [spectra[z][k][1] for z in range(gz)])
        for z in range(gz):
            mixed[z][k] = (re[z], im[z])
    for z in range(gz):
        short = short_fft(mixed[z], 1)
        for b, (re, im) in enumerate(turn_rows(kb, lambda b: short[b], tw_ref, lanes, 1)):
            re_s[z * kb + b, part, lanes] = re
            im_s[z * kb + b, part, lanes] = im


def forward_columns(gz, kb, coef_ref, tw_ref, lanes, part, re_s, im_s):
    spectra = []
    for z in range(gz):
        rows_of = lambda b: (re_s[z * kb + b, part, lanes], im_s[z * kb + b, part, lanes])
        spectra.append(short_fft(turn_rows(kb, rows_of, tw_ref, lanes, -1), -1))
    out = [[None] * kb for _ in range(gz)]
    for k in range(kb):
        coef = [coef_ref[j, k, :, lanes] for j in range(3)]
        re = mix(coef, [spectra[z][k][0] for z in range(gz)])
        im = mix(coef, [spectra[z][k][1] for z in range(gz)])
        for z in range(gz):
            out[z][k] = (re[z], im[z])
    return out


def inverse_product(re, im, table_ref):
    ka = re.shape[1]
    high, low = split2(jnp.concatenate([re, im], axis=1))
    value = dot(high, table_ref[...])
    return value[:, :ka] + value[:, ka:] + dot(low, table_ref[:, :ka])


def forward_product(field, table_ref):
    ka = field.shape[1]
    high, low = split2(field)
    value = dot(high, table_ref[...])
    value = value[:, : 2 * ka] + value[:, 2 * ka :] + dot(low, table_ref[:, : 2 * ka])
    return value[:, :ka], value[:, ka:]


def next_plane(field_ref, p, kb):
    rows, ka = field_ref.shape[1:]
    if (p + 1) % kb:
        return field_ref[p + 1]
    lane = lax.broadcasted_iota(jnp.int32, (rows, ka), 1)
    return jnp.where(lane == ka - 1, field_ref[p], pltpu.roll(field_ref[p + 1 - kb], ka - 1, 1))


def prev_plane(field_ref, p, kb):
    rows, ka = field_ref.shape[1:]
    if p % kb:
        return field_ref[p - 1]
    lane = lax.broadcasted_iota(jnp.int32, (rows, ka), 1)
    return jnp.where(lane == 0, field_ref[p], pltpu.roll(field_ref[p + kb - 1], 1, 1))


def first_kernel(
    gz, edge_ref, field_ref, coef_ref, tw_ref, table_ref, sums_ref, spec_ref, *refs
):
    piece_refs, (re_s, im_s) = refs[:-2], refs[-2:]
    planes, rows, ka = field_ref.shape
    kb = planes // gz
    projected = forward_into(gz, field_ref, coef_ref, tw_ref, table_ref, spec_ref, re_s, im_s)
    cut(gz, edge_ref, spec_ref, piece_refs)
    row = lax.broadcasted_iota(jnp.int32, (rows, ka), 0)
    square = jnp.zeros((8, LANES), F32)
    slope = jnp.zeros((8, LANES), F32)
    for p in range(planes):
        here = field_ref[p]
        square = square + fold(here * here)
        along_x = next_plane(field_ref, p, kb) - here
        along_y = jnp.where(row == rows - 1, 0.0, pltpu.roll(here, rows - 1, 0) - here)
        terms = along_x * along_x + along_y * along_y
        if p + kb < planes:
            along_z = field_ref[p + kb] - here
            terms = terms + along_z * along_z
        slope = slope + fold(terms)
    sums_ref[0] = square
    sums_ref[1] = projected
    sums_ref[2] = slope


def middle_kernel(
    edge_ref, spec_hbm, coef_ref, tw_ref, inverse_ref, forward_ref,
    d0_ref, nd0_ref, head_ref, tail_ref, sums_ref, spec_ref, re_s, im_s, sems,
):
    gz, kb, _, rows, ka = spec_ref.shape
    planes = gz * kb
    lane_parts = [slice(start, start + LANES) for start in range(0, ka, LANES)]
    cuts = sems.shape[0]
    cut = rows // cuts

    def fetch(i):
        part = pl.ds(i * cut, cut)
        return pltpu.make_async_copy(
            spec_hbm.at[:, :, :, part], spec_ref.at[:, :, :, part], sems.at[i]
        )

    for i in range(cuts):
        fetch(i).start()
    for i in range(cuts):
        fetch(i).wait()

        def first_columns(j, carry):
            part = pl.ds(pl.multiple_of(i * cut + j * 8, 8), 8)
            for lanes in lane_parts:
                spectra = [
                    [(spec_ref[z, k, 0, part, lanes], spec_ref[z, k, 1, part, lanes]) for k in range(kb)]
                    for z in range(gz)
                ]
                inverse_columns(gz, kb, spectra, coef_ref, tw_ref, lanes, part, re_s, im_s)
            return carry

        lax.fori_loop(0, cut // 8, first_columns, 0)

    step = plane_chunk(planes, rows)
    shape2, shape3 = (step * rows, ka), (step, rows, ka)

    def there_and_back(i, carry):
        part = pl.ds(i * step, step)
        field = inverse_product(re_s[part].reshape(shape2), im_s[part].reshape(shape2), inverse_ref)
        d0_ref[part] = field.reshape(shape3)
        re, im = forward_product(field, forward_ref)
        re_s[part] = re.reshape(shape3)
        im_s[part] = im.reshape(shape3)
        return carry

    lax.fori_loop(0, planes // step, there_and_back, 0)

    def second_columns(j, total):
        part = pl.ds(pl.multiple_of(j * 8, 8), 8)
        for lanes in lane_parts:
            spectra = forward_columns(gz, kb, coef_ref, tw_ref, lanes, part, re_s, im_s)
            for z in range(gz):
                for k in range(kb):
                    for p in range(2):
                        value = spectra[z][k][p]
                        spec_ref[z, k, p, part, lanes] = value
                        total = total + value * value
            inverse_columns(gz, kb, spectra, coef_ref, tw_ref, lanes, part, re_s, im_s)
        return total

    projected = lax.fori_loop(0, rows // 8, second_columns, jnp.zeros((8, LANES), F32))
    def back(i, carry):
        part = pl.ds(i * step, step)
        field = inverse_product(re_s[part].reshape(shape2), im_s[part].reshape(shape2), inverse_ref)
        nd0_ref[part] = field.reshape(shape3)
        return carry

    lax.fori_loop(0, planes // step, back, 0)

    for p in range(planes):
        head_ref[0, p : p + 1, :] = d0_ref[p, :1, :]
        head_ref[1, p : p + 1, :] = d0_ref[p, 1:2, :]
        head_ref[2, p : p + 1, :] = nd0_ref[p, :1, :]
        tail_ref[p : p + 1, :] = d0_ref[p, rows - 1 : rows, :]

    row = lax.broadcasted_iota(jnp.int32, (rows, ka), 0)
    square = jnp.zeros((8, LANES), F32)
    slope = jnp.zeros((8, LANES), F32)
    for p in range(planes):
        here = d0_ref[p]
        square = square + fold(here * here)
        along_x = next_plane(d0_ref, p, kb) - here
        along_y = jnp.where(row == rows - 1, 0.0, pltpu.roll(here, rows - 1, 0) - here)
        terms = along_x * along_x + along_y * along_y
        if p + kb < planes:
            along_z = d0_ref[p + kb] - here
            terms = terms + along_z * along_z
        slope = slope + fold(terms)
    sums_ref[0] = square
    sums_ref[1] = projected
    sums_ref[2] = slope


def middle(edge, spec, coef, nx):
    gz, kb, _, rows, ka = spec.shape
    planes = gz * kb
    vmem = pl.BlockSpec(memory_space=pltpu.VMEM)
    field = jax.ShapeDtypeStruct((planes, rows, ka), F32)
    return pl.pallas_call(
        middle_kernel,
        in_specs=[pl.BlockSpec(memory_space=pltpu.SMEM), pl.BlockSpec(memory_space=pltpu.HBM)]
        + [vmem] * 4,
        out_specs=[vmem] * 6,
        out_shape=[
            field,
            field,
            jax.ShapeDtypeStruct((3, planes, ka), F32),
            jax.ShapeDtypeStruct((planes, ka), F32),
            jax.ShapeDtypeStruct((3, 8, LANES), F32),
            jax.ShapeDtypeStruct(spec.shape, F32),
        ],
        scratch_shapes=[
            pltpu.VMEM((planes, rows, ka), F32),
            pltpu.VMEM((planes, rows, ka), F32),
            pltpu.SemaphoreType.DMA((2 if rows % 16 == 0 else 1,)),
        ],
        compiler_params=pltpu.CompilerParams(vmem_limit_bytes=X_GRANT),
        name="middle",
    )(
        edge, spec, coef, x_twiddle(nx, ka), jnp.asarray(x_inverse_matrix(nx, ka)),
        x_forward_matrix(nx, ka),
    )


def border_kernel(edge_ref, sums_ref, tail_ref, next_ref, prev_ref, out_ref):
    del prev_ref
    step = (next_ref[0] - tail_ref[...]) * jnp.where(edge_ref[1] > 0, 0.0, 1.0)
    put_sums(out_ref, [sums_ref[0], sums_ref[1], sums_ref[2] + fold(step * step)])


def border_sums(edge, sums, tail, next_head, prev_tail, copies):
    vmem = pl.BlockSpec(memory_space=pltpu.VMEM)
    return pl.pallas_call(
        border_kernel,
        in_specs=[pl.BlockSpec(memory_space=pltpu.SMEM)] + [vmem] * 4,
        out_specs=vmem,
        out_shape=jax.ShapeDtypeStruct((copies, 8, LANES), F32),
        compiler_params=pltpu.CompilerParams(vmem_limit_bytes=2 * MIB),
        name="border_sums",
    )(edge, sums, tail, next_head, prev_tail)


def second_kernel(
    gz, edge_ref, d0_ref, nd0_ref, tail_ref, prev_ref, next_ref,
    coef_ref, tw_ref, table_ref, *refs,
):
    sums_refs, refs = refs[:gz], refs[gz:]
    d1_ref, eta_ref, out_ref, spec_ref, re_s, im_s, row_s = refs
    planes, rows, ka = d0_ref.shape
    kb = planes // gz
    eta_here = step_of(sums_refs)
    eta_ref[...] = jnp.broadcast_to(eta_here, (8, LANES))
    eta = jnp.max(eta_here)
    first = edge_ref[0] > 0
    last = edge_ref[1] > 0

    def shrink(difference):
        return jnp.clip(-eta * difference, -CLIP, CLIP)

    lane2 = lax.broadcasted_iota(jnp.int32, (kb, ka), 1)
    row2 = lax.broadcasted_iota(jnp.int32, (kb, ka), 0)
    for z in range(gz):
        part = slice(z * kb, (z + 1) * kb)
        here = next_ref[0, part, :]
        value = here - eta * next_ref[2, part, :]
        up = pltpu.roll(here, kb - 1, 0)
        up = jnp.where(
            row2 == kb - 1, jnp.where(lane2 == ka - 1, here, pltpu.roll(up, ka - 1, 1)), up
        )
        down = pltpu.roll(here, 1, 0)
        down = jnp.where(row2 == 0, jnp.where(lane2 == 0, here, pltpu.roll(down, 1, 1)), down)
        value = value + shrink(here - down) - shrink(up - here)
        value = value + shrink(here - tail_ref[part, :]) - shrink(next_ref[1, part, :] - here)
        if z > 0:
            value = value + shrink(here - next_ref[0, (z - 1) * kb : z * kb, :])
        if z + 1 < gz:
            value = value - shrink(next_ref[0, (z + 1) * kb : (z + 2) * kb, :] - here)
        row_s[part, :] = value

    row = lax.broadcasted_iota(jnp.int32, (rows, ka), 0)
    square = jnp.zeros((8, LANES), F32)
    for p in range(planes):
        here = d0_ref[p]
        value = here - eta * nd0_ref[p]
        value = value + shrink(here - prev_plane(d0_ref, p, kb))
        value = value - shrink(next_plane(d0_ref, p, kb) - here)
        below = jnp.where(last, here[rows - 1 :, :], next_ref[0, p : p + 1, :])
        above = jnp.where(first, here[:1, :], prev_ref[p : p + 1, :])
        upper = shrink(jnp.where(row == rows - 1, below, pltpu.roll(here, rows - 1, 0)) - here)
        lower = jnp.where(row == 0, shrink(here[:1, :] - above), pltpu.roll(upper, 1, 0))
        value = value + lower - upper
        if p >= kb:
            value = value + shrink(here - d0_ref[p - kb])
        if p + kb < planes:
            value = value - shrink(d0_ref[p + kb] - here)
        d1_ref[p] = value
        square = square + fold(value * value)

    slope = jnp.zeros((8, LANES), F32)
    for p in range(planes):
        here = d1_ref[p]
        along_x = next_plane(d1_ref, p, kb) - here
        below = jnp.where(last, here[rows - 1 :, :], row_s[p : p + 1, :])
        along_y = jnp.where(row == rows - 1, below, pltpu.roll(here, rows - 1, 0)) - here
        terms = along_x * along_x + along_y * along_y
        if p + kb < planes:
            along_z = d1_ref[p + kb] - here
            terms = terms + along_z * along_z
        slope = slope + fold(terms)

    step = plane_chunk(planes, rows)

    def multiply(i, carry):
        part = pl.ds(i * step, step)
        re, im = forward_product(d1_ref[part].reshape(step * rows, ka), table_ref)
        re_s[part] = re.reshape(step, rows, ka)
        im_s[part] = im.reshape(step, rows, ka)
        return carry

    lax.fori_loop(0, planes // step, multiply, 0)

    def columns(j, total):
        part = pl.ds(pl.multiple_of(j * 8, 8), 8)
        for start in range(0, ka, LANES):
            lanes = slice(start, start + LANES)
            spectra = forward_columns(gz, kb, coef_ref, tw_ref, lanes, part, re_s, im_s)
            for z in range(gz):
                for k in range(kb):
                    for p in range(2):
                        value = spectra[z][k][p]
                        spec_ref[z, k, p, part, lanes] = value
                        total = total + value * value
        return total

    projected = lax.fori_loop(0, rows // 8, columns, jnp.zeros((8, LANES), F32))
    put_sums(out_ref, [square, projected, slope])


def second_descent(edge, sums, d0, nd0, tail, prev_tail, next_head, coef, gz, nx):
    planes, rows, ka = d0.shape
    vmem = pl.BlockSpec(memory_space=pltpu.VMEM)
    return pl.pallas_call(
        functools.partial(second_kernel, gz),
        in_specs=[pl.BlockSpec(memory_space=pltpu.SMEM)] + [vmem] * (8 + gz),
        out_specs=[vmem] * 4,
        out_shape=[
            jax.ShapeDtypeStruct((planes, rows, ka), F32),
            jax.ShapeDtypeStruct((8, LANES), F32),
            jax.ShapeDtypeStruct(sums[0].shape, F32),
            jax.ShapeDtypeStruct((gz, planes // gz, 2, rows, ka), F32),
        ],
        scratch_shapes=[
            pltpu.VMEM((planes, rows, ka), F32),
            pltpu.VMEM((planes, rows, ka), F32),
            pltpu.VMEM((planes, ka), F32),
        ],
        compiler_params=pltpu.CompilerParams(vmem_limit_bytes=X_GRANT),
        name="second_descent",
    )(
        edge, d0, nd0, tail, prev_tail, next_head, coef,
        x_twiddle(nx, ka), x_forward_matrix(nx, ka), *sums,
    )


def combine_kernel(gz, eta_ref, *refs):
    sums_refs, (first_ref, second_ref, out_ref, steps_ref) = refs[:gz], refs[gz:]
    eta0 = jnp.max(eta_ref[...])
    eta1 = jnp.max(step_of(sums_refs))
    steps_ref[0] = eta_ref[...]
    steps_ref[1] = jnp.full((8, LANES), eta1, F32)
    count = out_ref.shape[0]
    start = pl.program_id(0) * count
    for i in range(count):
        out_ref[i] = -(eta0 * first_ref[start + i] + eta1 * second_ref[start + i])


def combine_spectra(eta, sums, first, second):
    gz = len(sums)
    planes, *rest = first.shape
    count = 4 if planes % 4 == 0 else 1
    vmem = pl.BlockSpec(memory_space=pltpu.VMEM)
    return pl.pallas_call(
        functools.partial(combine_kernel, gz),
        grid=(planes // count,),
        in_specs=[vmem] * (3 + gz),
        out_specs=[
            pl.BlockSpec((count, *rest), lambda i: (i, 0, 0, 0)),
            pl.BlockSpec((2, 8, LANES), lambda i: (0, 0, 0)),
        ],
        out_shape=[
            jax.ShapeDtypeStruct(first.shape, F32),
            jax.ShapeDtypeStruct((2, 8, LANES), F32),
        ],
        compiler_params=pltpu.CompilerParams(vmem_limit_bytes=6 * MIB),
        name="combine_spectra",
    )(eta, *sums, first, second)


def to_core(piece, r):
    gz = lax.axis_size("gz")
    return lax.ppermute(piece, "gz", [(i, (i + r) % gz) for i in range(gz)]) if r else piece


def to_chips(parts):
    return lax.all_to_all(parts, "gy", 0, 0, tiled=True)


def to_devices(parts):
    gz, gy, *rest = parts.shape
    parts = lax.all_to_all(parts.reshape(gz * gy, *rest), ("gz", "gy"), 0, 0, tiled=True)
    return parts.reshape(gz, gy, *rest)


def everywhere(sums):
    sums = to_chips(sums)
    return [to_core(sums, r) for r in range(lax.axis_size("gz"))]


def shards(data, band_offset, interp_weight):
    gz = lax.axis_size("gz")
    gy = lax.axis_size("gy")
    devices = gz * gy
    data = data[0]
    blocks, ny, width = data.shape
    rows = ny // devices
    ka = blocks * HALF
    nx = ka * gy

    core = lax.axis_index("gz")
    flat = lax.axis_index("gy") * gz + core
    edge = jnp.stack([flat == 0, flat == devices - 1]).astype(jnp.int32)
    order = [(i % gz) * gy + i // gz for i in range(devices)]
    up = [(order[i + 1], order[i]) for i in range(devices - 1)]
    down = [(order[i], order[i + 1]) for i in range(devices - 1)]

    lower = band_offset < 0
    weight = interp_weight
    coef = jnp.stack(
        [
            jnp.where(lower, weight[1], weight[0]),
            jnp.where(lower, weight[0], 0.0),
            jnp.where(lower, 0.0, weight[1]),
        ]
    ).reshape(3, gy, 1, ka)
    coef = jnp.broadcast_to(coef, (3, gy, 8, ka))

    spec = to_devices(y_inverse(data, rows, gz, gy))
    d0, nd0, head, tail, sums, first = middle(edge, spec, coef, nx)
    next_head = lax.ppermute(head, ("gz", "gy"), up)
    prev_tail = lax.ppermute(tail, ("gz", "gy"), down)
    sums = everywhere(border_sums(edge, sums, tail, next_head, prev_tail, gy))
    d1, eta, sums, second = second_descent(
        edge, sums, d0, nd0, tail, prev_tail, next_head, coef, gz, nx
    )
    sums = everywhere(sums)
    flat_shape = (devices, 2, rows, ka)
    spec, etas = combine_spectra(eta, sums, first.reshape(flat_shape), second.reshape(flat_shape))
    residual = y_forward(to_devices(spec.reshape(gz, gy, 2, rows, ka)), data)

    volume = -(etas[0, 0, 0] * d0 + etas[1, 0, 0] * d1)
    volume = volume.reshape(gz, gy, rows, ka).transpose(0, 2, 3, 1).reshape(gz, rows, nx)
    parts = [
        to_core(lax.dynamic_index_in_dim(volume, lax.rem(core + r, gz), 0, False), r)
        for r in range(gz)
    ]
    volume = jnp.zeros((gz, rows, nx), F32)
    for r, part in enumerate(parts):
        volume = lax.dynamic_update_index_in_dim(volume, part, lax.rem(core + gz - r, gz), 0)
    return (volume.reshape(1, gz * rows, nx), residual[None])


NX = 4096
NY = 2048
XB = 64
YB = 64
ITERS = 2
XA = 64
YA = 32
PRECISE = lax.Precision.HIGHEST


def with_halo(block, sides, width):
    for axis, dim in sides:
        count = lax.axis_size(axis)
        forward = [(i, i + 1) for i in range(count - 1)]
        backward = [(target, source) for source, target in forward]
        low = lax.ppermute(
            lax.slice_in_dim(block, block.shape[dim] - width, None, axis=dim), axis, forward
        )
        high = lax.ppermute(lax.slice_in_dim(block, 0, width, axis=dim), axis, backward)
        block = jnp.concatenate([low, block, high], axis=dim)
    return block


def from_behind(block, axis, distance):
    devices = range(lax.axis_size(axis))
    route = [(i - distance, i) for i in devices if i - distance in devices]
    return lax.ppermute(block, axis, route)


def unit_table(length):
    counter = jnp.arange(length, dtype=jnp.int32)
    phase_int = counter[:, None] * counter[None, :] % length
    angles = 2.0 * jnp.pi / length * phase_int.astype(jnp.float32)
    factor = length ** (-0.5)
    return (jnp.cos(angles) * factor, jnp.sin(angles) * factor)


def twiddle_table(row_len, col_len, period):
    phase_int = (
        jnp.arange(row_len, dtype=jnp.int32)[:, None]
        * jnp.arange(col_len, dtype=jnp.int32)[None, :]
        % period
    )
    angles = 2.0 * jnp.pi / period * phase_int.astype(jnp.float32)
    return (jnp.cos(angles), jnp.sin(angles))


def split_parts(packed):
    half_width = packed.shape[-1] // 2
    return (packed[..., :half_width], packed[..., half_width:])


def join_parts(real_part, imag_part):
    return jnp.concatenate([real_part, imag_part], axis=-1)


def complex_contract(packed, cos_table, sin_table, subscripts, conj_sign):
    cos_out = jnp.einsum(subscripts, packed, cos_table, precision=PRECISE)
    sin_out = jnp.einsum(subscripts, packed, sin_table, precision=PRECISE)
    cos_re, cos_im = split_parts(cos_out)
    sin_re, sin_im = split_parts(sin_out)
    return join_parts(cos_re - conj_sign * sin_im, cos_im + conj_sign * sin_re)


def rotate(packed, cos_table, sin_table, conj_sign):
    real_part, imag_part = split_parts(packed)
    return join_parts(
        real_part * cos_table - conj_sign * imag_part * sin_table,
        imag_part * cos_table + conj_sign * real_part * sin_table,
    )


def forward_x(volume):
    slices, row_count = (volume.shape[0], volume.shape[1])
    cos_a, sin_a = unit_table(XA)
    cos_b, sin_b = unit_table(XB)
    first_table = jnp.concatenate([cos_a, -sin_a], axis=1)
    grid_view = volume.reshape(slices, row_count, XA, XB)
    mixing = jnp.einsum("zyab,am->zybm", grid_view, first_table, precision=PRECISE)
    tw_cos, tw_sin = twiddle_table(XB, XA, NX)
    mixing = rotate(mixing, tw_cos, tw_sin, -1.0)
    return complex_contract(mixing, cos_b, sin_b, "zybm,bl->zlym", -1.0)


def inverse_x(packed):
    slices, row_count = (packed.shape[0], packed.shape[2])
    cos_a, sin_a = unit_table(XA)
    cos_b, sin_b = unit_table(XB)
    mixing = complex_contract(packed, cos_b, sin_b, "zlym,lb->zybm", 1.0)
    tw_cos, tw_sin = twiddle_table(XB, XA, NX)
    mixing = rotate(mixing, tw_cos, tw_sin, 1.0)
    last_table = jnp.concatenate([cos_a, -sin_a], axis=0)
    grid_view = jnp.einsum("zybm,ma->zyab", mixing, last_table, precision=PRECISE)
    return grid_view.reshape(slices, row_count, NX)


def forward_y(packed):
    slices, blocks, width = (packed.shape[0], packed.shape[1], packed.shape[3])
    cos_a, sin_a = unit_table(YA)
    cos_b, sin_b = unit_table(YB)
    grid_view = packed.reshape(slices, blocks, YA, YB, width)
    mixing = complex_contract(grid_view, cos_a, sin_a, "zjcdm,ck->zjkdm", -1.0)
    tw_cos, tw_sin = twiddle_table(YA, YB, NY)
    mixing = rotate(mixing, tw_cos[:, :, None], tw_sin[:, :, None], -1.0)
    result = complex_contract(mixing, cos_b, sin_b, "zjkdm,dl->zjlkm", -1.0)
    return result.reshape(slices, blocks, NY, width)


def inverse_y(packed):
    slices, blocks, width = (packed.shape[0], packed.shape[1], packed.shape[3])
    cos_a, sin_a = unit_table(YA)
    cos_b, sin_b = unit_table(YB)
    grid_view = packed.reshape(slices, blocks, YB, YA, width)
    mixing = complex_contract(grid_view, cos_b, sin_b, "zjlkm,ld->zjkdm", 1.0)
    tw_cos, tw_sin = twiddle_table(YA, YB, NY)
    mixing = rotate(mixing, tw_cos[:, :, None], tw_sin[:, :, None], 1.0)
    result = complex_contract(mixing, cos_a, sin_a, "zjkdm,kc->zjcdm", 1.0)
    return result.reshape(slices, blocks, NY, width)


def tilt_coefficients(band_offset, interp_weight, first_block, blocks):
    offsets = lax.dynamic_slice_in_dim(band_offset.reshape(XB, XA), first_block, blocks, 0)
    weights = lax.dynamic_slice_in_dim(interp_weight.reshape(2, XB, XA), first_block, blocks, 1)
    lower_tap = (jnp.concatenate([offsets, offsets], axis=1) < 0)[:, None, :]
    first_weight = jnp.concatenate([weights[0], weights[0]], axis=1)[:, None, :]
    second_weight = jnp.concatenate([weights[1], weights[1]], axis=1)[:, None, :]
    return (lower_tap, first_weight, second_weight)


def tilt(field_in, coefficients, adjoint):
    lower_tap, first_weight, second_weight = coefficients
    padded = with_halo(field_in, (("gz", 0),), 1)
    below_rim = padded[:-2]
    middle = padded[1:-1]
    above_rim = padded[2:]
    if adjoint:
        return jnp.where(
            lower_tap,
            first_weight * above_rim + second_weight * middle,
            first_weight * middle + second_weight * below_rim,
        )
    return jnp.where(
        lower_tap,
        first_weight * below_rim + second_weight * middle,
        first_weight * middle + second_weight * above_rim,
    )


def to_pencil(slab_part):
    return lax.all_to_all(slab_part, "gy", split_axis=1, concat_axis=2, tiled=True)


def to_slab(pencil_part):
    return lax.all_to_all(pencil_part, "gy", split_axis=2, concat_axis=1, tiled=True)


def back_project(packed, pencil_coef):
    return inverse_x(to_slab(inverse_y(tilt(packed, pencil_coef, True))))


def edge_masks(slices, row_count):
    z_global = lax.axis_index("gz") * slices + jnp.arange(slices, dtype=jnp.int32)
    y_global = lax.axis_index("gy") * row_count + jnp.arange(row_count, dtype=jnp.int32)
    keep_z = (z_global < slices * lax.axis_size("gz") - 1).astype(jnp.float32)[:, None, None]
    keep_y = (y_global < row_count * lax.axis_size("gy") - 1).astype(jnp.float32)[None, :, None]
    return (keep_z, keep_y)


def forward_diff(field_in, keep_z, keep_y):
    slices, row_count = (field_in.shape[0], field_in.shape[1])
    next_z = from_behind(field_in, "gz", -1)
    next_y = from_behind(field_in[:, :1], "gy", -1)
    along_z = (jnp.concatenate([field_in[1:], next_z], axis=0) - field_in) * keep_z
    along_y = (jnp.concatenate([field_in[:, 1:], next_y], axis=1) - field_in) * keep_y
    zero_col = jnp.zeros((slices, row_count, 1), jnp.float32)
    along_x = jnp.concatenate([field_in[:, :, 1:] - field_in[:, :, :-1], zero_col], axis=2)
    return jnp.stack([along_z, along_y, along_x])


def transpose_diff(components, keep_z, keep_y):
    slices, row_count = (components.shape[1], components.shape[2])
    zero_col = jnp.zeros((slices, row_count, 1), jnp.float32)
    comp_z = components[0] * keep_z
    comp_y = components[1] * keep_y
    comp_x = jnp.concatenate([components[2][:, :, :-1], zero_col], axis=2)
    prev_z = from_behind(comp_z, "gz", 1)
    prev_y = from_behind(comp_y[:, -1:], "gy", 1)
    result = jnp.concatenate([prev_z, comp_z[:-1]], axis=0) - comp_z
    result = result + jnp.concatenate([prev_y, comp_y[:, :-1]], axis=1) - comp_y
    result = result + jnp.concatenate([zero_col, comp_x[:, :, :-1]], axis=2) - comp_x
    return result


def plain_shards(data, band_offset, interp_weight):
    slices = data.shape[0]
    blocks = data.shape[1]
    width = data.shape[3]
    row_count = NY // lax.axis_size("gy")
    slab_coef = tilt_coefficients(band_offset, interp_weight, 0, XB)
    pencil_coef = tilt_coefficients(
        band_offset, interp_weight, lax.axis_index("gy") * blocks, blocks
    )
    keep_z, keep_y = edge_masks(slices, row_count)
    measured = data.astype(jnp.float32)
    volume = jnp.zeros((slices, row_count, NX), jnp.float32)
    grad_volume = jnp.zeros((3, slices, row_count, NX), jnp.float32)
    split_var = grad_volume
    dual_var = grad_volume
    data_back = back_project(measured, pencil_coef)
    normal_part = jnp.zeros_like(volume)
    tilted = jnp.zeros((slices, XB, row_count, width), jnp.float32)
    for iteration in range(ITERS):
        data_grad = normal_part - data_back
        if iteration > 0:
            tv_gap = grad_volume - split_var + dual_var / PENALTY
            descent = data_grad + PENALTY * transpose_diff(tv_gap, keep_z, keep_y)
        else:
            descent = data_grad
        slope_field = forward_diff(descent, keep_z, keep_y)
        projected = tilt(forward_x(descent), slab_coef, False)
        line_totals = lax.psum(
            (
                jnp.sum(descent * descent),
                jnp.sum(projected * projected),
                jnp.sum(slope_field * slope_field),
            ),
            ("gz", "gy"),
        )
        step_length = line_totals[0] / (line_totals[1] + PENALTY * line_totals[2])
        volume = volume - step_length * descent
        grad_volume = grad_volume - step_length * slope_field
        tilted = tilted - step_length * projected
        if iteration + 1 < ITERS:
            normal_part = normal_part - step_length * inverse_x(tilt(projected, slab_coef, True))
        if iteration + 1 < ITERS:
            shifted = grad_volume + dual_var / PENALTY
            split_var = shifted - jnp.clip(shifted, -TV_WEIGHT / PENALTY, TV_WEIGHT / PENALTY)
            dual_var = PENALTY * (grad_volume - split_var)
    residual = forward_y(to_pencil(tilted)) - measured
    return (volume, residual)


def tiles_fit(mesh, ny, blocks):
    rows = ny // (mesh.shape["gz"] * mesh.shape["gy"])
    return rows % 16 == 0 and mesh.shape["gy"] % YR == 0 and blocks // mesh.shape["gy"] % 2 == 0


def solution(mesh):
    in_specs = (P("gz", "gy", None, None), P(), P())
    out_specs = (P("gz", "gy", None), P("gz", "gy", None, None))

    def run(data, band_offset, interp_weight):
        body = shards if tiles_fit(mesh, data.shape[2], data.shape[1]) else plain_shards
        call = jax.shard_map(
            body, mesh=mesh, in_specs=in_specs, out_specs=out_specs, check_vma=False
        )
        return call(data, band_offset, interp_weight)

    return run
```

```python
import functools

import jax
import jax.numpy as jnp
import numpy as np
from jax import lax
from jax.experimental import pallas as pl
from jax.experimental.pallas import tpu as pltpu
from jax.sharding import PartitionSpec as P

PENALTY = 0.5
TV_WEIGHT = 0.25
CLIP = TV_WEIGHT / PENALTY
HALF = 64
YR = 8
LANES = 128
F32 = jnp.float32
BF16 = jnp.bfloat16
MIB = 1024 * 1024
Y_GRANT = 56 * MIB
X_GRANT = 20 * MIB
COMBINE_GRANT = 53 * MIB


def dft_parts(length, scale):
    index = np.arange(length)
    angles = 2.0 * np.pi / length * (index[:, None] * index[None, :] % length)
    return np.cos(angles) * scale, np.sin(angles) * scale


def two_parts(table):
    table = jnp.asarray(table.astype(np.float32))
    high = table.astype(BF16)
    low = (table - high.astype(F32)).astype(BF16)
    return high, low


def host_parts(table):
    table = table.astype(np.float32)
    high = table.astype(BF16)
    low = (table - high.astype(np.float32)).astype(BF16)
    return high, low


def y_matrix(ny, forward, sign):
    n = ny // YR
    cos, sin = dft_parts(n, sign * ny**-0.5)
    if forward:
        table = np.block([[cos, sin], [-sin, cos]])
    else:
        table = np.block([[cos, -sin], [sin, cos]])
    return jnp.asarray(np.concatenate(host_parts(table), axis=0))


def y_twiddle(ny):
    n = ny // YR
    angles = 2.0 * np.pi / ny * (np.arange(1, YR)[:, None] * np.arange(n)[None, :])
    table = np.stack([np.cos(angles), np.sin(angles)]).astype(np.float32)
    return jnp.asarray(np.ascontiguousarray(np.broadcast_to(table[..., None], (2, YR - 1, n, LANES))))


def x_inverse_matrix(nx, ka):
    cos, sin = dft_parts(ka, nx**-0.5)
    return np.concatenate(host_parts(np.concatenate([cos, -sin], axis=0)), axis=1)


def x_forward_matrix(nx, ka):
    cos, sin = dft_parts(ka, nx**-0.5)
    return jnp.asarray(np.concatenate(host_parts(np.concatenate([cos, -sin], axis=1)), axis=1))


def x_twiddle(nx, ka):
    kb = nx // ka
    angles = 2.0 * np.pi / nx * (np.arange(kb)[:, None] * np.arange(ka)[None, :])
    table = np.stack([np.cos(angles), np.sin(angles)]).astype(np.float32)
    return jnp.asarray(np.ascontiguousarray(np.broadcast_to(table[:, :, None], (2, kb, 8, ka))))


def short_fft(planes, sign):
    n = len(planes)
    if n == 1:
        return planes
    even = short_fft(planes[0::2], sign)
    odd = short_fft(planes[1::2], sign)
    half = n // 2
    out = [None] * n
    for k in range(half):
        er, ei = even[k]
        tr, ti = odd[k]
        if 4 * k == n:
            if sign > 0:
                out[k] = (er - ti, ei + tr)
                out[k + half] = (er + ti, ei - tr)
            else:
                out[k] = (er + ti, ei - tr)
                out[k + half] = (er - ti, ei + tr)
            continue
        if k > 0:
            c = float(np.cos(2.0 * np.pi * k / n))
            s = float(sign * np.sin(2.0 * np.pi * k / n))
            if 8 * k == n:
                tr, ti = (tr - ti, ti + tr) if sign > 0 else (tr + ti, ti - tr)
                tr, ti = tr * c, ti * c
            elif 8 * k == 3 * n:
                m = float(np.sin(2.0 * np.pi * k / n))
                tr, ti = (-(tr + ti), tr - ti) if sign > 0 else (ti - tr, -(tr + ti))
                tr, ti = tr * m, ti * m
            else:
                tr, ti = tr * c - ti * s, ti * c + tr * s
        out[k] = (er + tr, ei + ti)
        out[k + half] = (er - tr, ei - ti)
    return out


def split2(x):
    high = x.astype(BF16)
    return high, (x - high.astype(F32)).astype(BF16)


def dot(a, b):
    return jnp.dot(a, b, preferred_element_type=F32)


def fold(x):
    rows, lanes = x.shape
    x = jnp.sum(x.reshape(rows // 8, 8, lanes), axis=0)
    total = x[:, :LANES]
    for i in range(1, lanes // LANES):
        total = total + x[:, i * LANES : (i + 1) * LANES]
    return total


def full_sum(x):
    return jnp.sum(jnp.sum(x, axis=0, keepdims=True), axis=1, keepdims=True)


def step_of(sums_refs):
    total = sum(jnp.sum(sums_ref[...], axis=0) for sums_ref in sums_refs)
    parts = jnp.sum(total, axis=1, keepdims=True)
    return parts[0:1] / (parts[1:2] + PENALTY * parts[2:3])


def sums_block(values):
    rows = [jnp.sum(v, axis=0, keepdims=True) for v in values]
    index = lax.broadcasted_iota(jnp.int32, (8, LANES), 0)
    block = jnp.zeros((8, LANES), F32)
    for i, row in enumerate(rows):
        block = jnp.where(index == i, jnp.broadcast_to(row, (8, LANES)), block)
    return block


def put_copies(out_ref, block):
    for i in range(out_ref.shape[0]):
        out_ref[i] = block


def mix_adjoint(coef, planes):
    own, below, above = coef
    out = []
    for z in range(len(planes)):
        value = own * planes[z]
        if z + 1 < len(planes):
            value = value + below * planes[z + 1]
        if z > 0:
            value = value + above * planes[z - 1]
        out.append(value)
    return out


def mix(coef, planes):
    own, below, above = coef
    out = []
    for z in range(len(planes)):
        value = own * planes[z]
        if z > 0:
            value = value + below * planes[z - 1]
        if z + 1 < len(planes):
            value = value + above * planes[z + 1]
        out.append(value)
    return out


def y_inverse_kernel(
    data_hbm, table_hbm, tw_hbm, out_hbm,
    data_ref, table_ref, tw_ref, out_ref, re_s, im_s, mix_s, sems, out_sems,
):
    blocks, ny, _ = data_ref.shape
    n = ny // YR
    gz, _, _, rows, _ = out_ref.shape
    lane = lax.broadcasted_iota(jnp.int32, (n, LANES), 1)
    pairs = blocks // 2

    def fetch(chunk):
        part = pl.ds(2 * chunk, 2)
        return pltpu.make_async_copy(data_hbm.at[part], data_ref.at[part], sems.at[2 + chunk])

    def give(chunk, core):
        at = (core, slice(None), slice(None), slice(None), pl.ds(chunk * LANES, LANES))
        return pltpu.make_async_copy(out_ref.at[at], out_hbm.at[at], out_sems.at[chunk * gz + core])

    fetch_table = pltpu.make_async_copy(table_hbm, table_ref, sems.at[0])
    fetch_tw = pltpu.make_async_copy(tw_hbm, tw_ref, sems.at[1])
    fetch(0).start()
    fetch_table.start()
    fetch_tw.start()
    for chunk in range(1, pairs):
        fetch(chunk).start()

    for chunk in range(pairs):
        lanes = slice(chunk * LANES, (chunk + 1) * LANES)
        fetch(chunk).wait()

        def unpack(i, carry):
            part = pl.ds(pl.multiple_of(i * n, n), n)
            first = data_ref[2 * chunk, part, :].astype(F32)
            second = data_ref[2 * chunk + 1, part, :].astype(F32)
            re_s[part, :] = jnp.where(lane < HALF, first, pltpu.roll(second, HALF, 1))
            im_s[part, :] = jnp.where(lane < HALF, pltpu.roll(first, HALF, 1), second)
            return carry

        lax.fori_loop(0, YR, unpack, 0)
        if chunk == 0:
            fetch_table.wait()

        for k in range(0, YR, 2):
            pieces = [
                jnp.concatenate([s[pl.ds(k + d, n, stride=YR), :] for d in range(2)], axis=1)
                for s in (re_s, im_s)
            ]
            both = dot(table_ref[...], jnp.concatenate(pieces, axis=0).astype(BF16))
            both = both[: 2 * n] + both[2 * n :]
            for d in range(2):
                mix_s[k + d] = both[:, d * LANES : (d + 1) * LANES]

        if chunk == 0:
            fetch_tw.wait()

        tiles = rows // 8
        for core in range(gz):

            def combine(i, carry):
                y2 = ((i // tiles) * gz + core) * rows + lax.rem(i, tiles) * 8
                part = pl.ds(pl.multiple_of(y2, 8), 8)
                planes = []
                for k in range(YR):
                    re = mix_s[k, part, :]
                    im = mix_s[k, pl.ds(pl.multiple_of(n + y2, 8), 8), :]
                    if k > 0:
                        c = tw_ref[0, k - 1, part, :]
                        s = tw_ref[1, k - 1, part, :]
                        re, im = re * c - im * s, im * c + re * s
                    planes.append((re, im))
                at = pl.ds(pl.multiple_of(lax.rem(i, tiles) * 8, 8), 8)
                for k, (re, im) in enumerate(short_fft(planes, 1)):
                    to = k * (n // (gz * rows)) + i // tiles
                    out_ref[core, to, 0, at, lanes] = re
                    out_ref[core, to, 1, at, lanes] = im
                return carry

            lax.fori_loop(0, n // gz // 8, combine, 0, unroll=2)
            give(chunk, core).start()

    for chunk in range(pairs):
        for core in range(gz):
            give(chunk, core).wait()


def y_inverse(data, rows, gz, gy):
    blocks, ny, width = data.shape
    n = ny // YR
    ka = blocks * HALF
    hbm = pl.BlockSpec(memory_space=pltpu.HBM)
    return pl.pallas_call(
        y_inverse_kernel,
        in_specs=[hbm] * 3,
        out_specs=hbm,
        out_shape=jax.ShapeDtypeStruct((gz, gy, 2, rows, ka), F32),
        scratch_shapes=[
            pltpu.VMEM((blocks, ny, width), BF16),
            pltpu.VMEM((4 * n, 2 * n), BF16),
            pltpu.VMEM((2, YR - 1, n, LANES), F32),
            pltpu.VMEM((gz, gy, 2, rows, ka), F32),
            pltpu.VMEM((ny, LANES), F32),
            pltpu.VMEM((ny, LANES), F32),
            pltpu.VMEM((YR, 2 * n, LANES), F32),
            pltpu.SemaphoreType.DMA((2 + blocks // 2,)),
            pltpu.SemaphoreType.DMA((blocks // 2 * gz,)),
        ],
        compiler_params=pltpu.CompilerParams(vmem_limit_bytes=Y_GRANT),
        name="y_inverse",
    )(data, y_matrix(ny, False, -1.0), y_twiddle(ny))


def y_forward_kernel(
    spec_hbm, data_hbm, table_hbm, tw_hbm, out_hbm,
    spec_ref, data_ref, table_ref, tw_ref, out_ref, mix_s, sems, spec_sems, out_sems,
):
    blocks, ny, _ = data_ref.shape
    n = ny // YR
    _, gz, gy, _, rows, _ = spec_ref.shape
    pairs = blocks // 2
    half = n // 2

    def fetch(chunk):
        lanes = pl.ds(chunk * LANES, LANES)
        return pltpu.make_async_copy(
            spec_hbm.at[:, :, :, :, lanes], spec_ref.at[chunk], spec_sems.at[chunk]
        )

    def give(chunk, part):
        at = (pl.ds(2 * chunk, 2), slice(None), pl.ds(part * half, half))
        return pltpu.make_async_copy(out_ref.at[at], out_hbm.at[at], out_sems.at[2 * chunk + part])

    fetch_table = pltpu.make_async_copy(table_hbm, table_ref, sems.at[0])
    fetch_tw = pltpu.make_async_copy(tw_hbm, tw_ref, sems.at[1])
    fetch_data = pltpu.make_async_copy(data_hbm, data_ref, sems.at[2])
    fetch(0).start()
    fetch_table.start()
    fetch_tw.start()
    fetch_data.start()
    for chunk in range(1, pairs):
        fetch(chunk).start()

    def rows_of(chunk, p, k):
        part = pl.ds(k, rows // YR, stride=YR)
        return jnp.concatenate(
            [spec_ref[chunk, core, i, p, part, :] for i in range(gy) for core in range(gz)], axis=0
        )

    lane = lax.broadcasted_iota(jnp.int32, (16, LANES), 1)
    for chunk in range(pairs):
        lanes = slice(chunk * LANES, (chunk + 1) * LANES)
        fetch(chunk).wait()

        if chunk == 0:
            fetch_table.wait()

        for k in range(0, YR, 2):
            pieces = [
                jnp.concatenate([rows_of(chunk, p, k + d) for d in range(2)], axis=1)
                for p in range(2)
            ]
            high, low = split2(jnp.concatenate(pieces, axis=0))
            both = dot(table_ref[...], high)
            both = both[: 2 * n] + both[2 * n :] + dot(table_ref[: 2 * n], low)
            for d in range(2):
                mix_s[k + d] = both[:, d * LANES : (d + 1) * LANES]
        if chunk == 0:
            fetch_tw.wait()
            fetch_data.wait()

        def combine(i, carry):
            start = pl.multiple_of(i * 16, 16)
            part = pl.ds(start, 16)
            planes = []
            for k in range(YR):
                re = mix_s[k, part, :]
                im = mix_s[k, pl.ds(pl.multiple_of(n + i * 16, 16), 16), :]
                if k > 0:
                    c = tw_ref[0, k - 1, part, :]
                    s = tw_ref[1, k - 1, part, :]
                    re, im = re * c + im * s, im * c - re * s
                planes.append((re, im))
            for k, (re, im) in enumerate(short_fft(planes, -1)):
                at = pl.ds(pl.multiple_of(k * n + start, 16), 16)
                first = jnp.where(lane < HALF, re, pltpu.roll(im, HALF, 1))
                second = jnp.where(lane < HALF, pltpu.roll(re, HALF, 1), im)
                out_ref[2 * chunk, k, part, :] = first - data_ref[2 * chunk, at, :].astype(F32)
                out_ref[2 * chunk + 1, k, part, :] = (
                    second - data_ref[2 * chunk + 1, at, :].astype(F32)
                )
            return carry

        for part in range(2):
            lax.fori_loop(part * half // 16, (part + 1) * half // 16, combine, 0)
            give(chunk, part).start()

    for chunk in range(pairs):
        for part in range(2):
            give(chunk, part).wait()


def y_forward(spec, data):
    blocks, ny, width = data.shape
    n = ny // YR
    hbm = pl.BlockSpec(memory_space=pltpu.HBM)
    out = pl.pallas_call(
        y_forward_kernel,
        in_specs=[hbm] * 4,
        out_specs=hbm,
        out_shape=jax.ShapeDtypeStruct((blocks, YR, n, width), F32),
        scratch_shapes=[
            pltpu.VMEM((blocks // 2, *spec.shape[:-1], LANES), F32),
            pltpu.VMEM((blocks, ny, width), BF16),
            pltpu.VMEM((4 * n, 2 * n), BF16),
            pltpu.VMEM((2, YR - 1, n, LANES), F32),
            pltpu.VMEM((blocks, YR, n, width), F32),
            pltpu.VMEM((YR, 2 * n, LANES), F32),
            pltpu.SemaphoreType.DMA((3,)),
            pltpu.SemaphoreType.DMA((blocks // 2,)),
            pltpu.SemaphoreType.DMA((blocks,)),
        ],
        compiler_params=pltpu.CompilerParams(vmem_limit_bytes=Y_GRANT),
        name="y_forward",
    )(spec, data, y_matrix(ny, True, 1.0), y_twiddle(ny))
    return out.reshape(blocks, ny, width)


def plane_chunk(planes, rows):
    chunk = max(1, 1024 // rows)
    while planes % chunk:
        chunk -= 1
    return chunk


def turn_rows(kb, planes_of, tw_ref, lanes, sign):
    out = []
    for b in range(kb):
        re, im = planes_of(b)
        if b > 0:
            c = tw_ref[0, b, :, lanes]
            s = tw_ref[1, b, :, lanes]
            if sign > 0:
                re, im = re * c - im * s, im * c + re * s
            else:
                re, im = re * c + im * s, im * c - re * s
        out.append((re, im))
    return out


def inverse_columns(gz, kb, spectra, coef_ref, tw_ref, lanes, part, re_s, im_s):
    mixed = [[None] * kb for _ in range(gz)]
    for k in range(kb):
        coef = [coef_ref[j, k, :, lanes] for j in range(3)]
        re = mix_adjoint(coef, [spectra[z][k][0] for z in range(gz)])
        im = mix_adjoint(coef, [spectra[z][k][1] for z in range(gz)])
        for z in range(gz):
            mixed[z][k] = (re[z], im[z])
    for z in range(gz):
        short = short_fft(mixed[z], 1)
        for b, (re, im) in enumerate(turn_rows(kb, lambda b: short[b], tw_ref, lanes, 1)):
            re_s[z * kb + b, part, lanes] = re
            im_s[z * kb + b, part, lanes] = im


def forward_columns(gz, kb, coef_ref, tw_ref, lanes, part, re_s, im_s):
    spectra = []
    for z in range(gz):
        rows_of = lambda b: (re_s[z * kb + b, part, lanes], im_s[z * kb + b, part, lanes])
        spectra.append(short_fft(turn_rows(kb, rows_of, tw_ref, lanes, -1), -1))
    out = [[None] * kb for _ in range(gz)]
    for k in range(kb):
        coef = [coef_ref[j, k, :, lanes] for j in range(3)]
        re = mix(coef, [spectra[z][k][0] for z in range(gz)])
        im = mix(coef, [spectra[z][k][1] for z in range(gz)])
        for z in range(gz):
            out[z][k] = (re[z], im[z])
    return out


def inverse_product(re, im, table_ref):
    ka = re.shape[1]
    high, low = split2(jnp.concatenate([re, im], axis=1))
    value = dot(high, table_ref[...])
    return value[:, :ka] + value[:, ka:] + dot(low, table_ref[:, :ka])


def forward_product(field, table_ref):
    ka = field.shape[1]
    high, low = split2(field)
    value = dot(high, table_ref[...])
    value = value[:, : 2 * ka] + value[:, 2 * ka :] + dot(low, table_ref[:, : 2 * ka])
    return value[:, :ka], value[:, ka:]


def next_plane(field_ref, p, kb):
    rows, ka = field_ref.shape[1:]
    if (p + 1) % kb:
        return field_ref[p + 1]
    lane = lax.broadcasted_iota(jnp.int32, (rows, ka), 1)
    return jnp.where(lane == ka - 1, field_ref[p], pltpu.roll(field_ref[p + 1 - kb], ka - 1, 1))


def prev_plane(field_ref, p, kb):
    rows, ka = field_ref.shape[1:]
    if p % kb:
        return field_ref[p - 1]
    lane = lax.broadcasted_iota(jnp.int32, (rows, ka), 1)
    return jnp.where(lane == 0, field_ref[p], pltpu.roll(field_ref[p + kb - 1], 1, 1))


def first_kernel(
    gz, edge_ref, field_ref, coef_ref, tw_ref, table_ref, sums_ref, spec_ref, *refs
):
    piece_refs, (re_s, im_s) = refs[:-2], refs[-2:]
    planes, rows, ka = field_ref.shape
    kb = planes // gz
    projected = forward_into(gz, field_ref, coef_ref, tw_ref, table_ref, spec_ref, re_s, im_s)
    cut(gz, edge_ref, spec_ref, piece_refs)
    row = lax.broadcasted_iota(jnp.int32, (rows, ka), 0)
    square = jnp.zeros((8, LANES), F32)
    slope = jnp.zeros((8, LANES), F32)
    for p in range(planes):
        here = field_ref[p]
        square = square + fold(here * here)
        along_x = next_plane(field_ref, p, kb) - here
        along_y = jnp.where(row == rows - 1, 0.0, pltpu.roll(here, rows - 1, 0) - here)
        terms = along_x * along_x + along_y * along_y
        if p + kb < planes:
            along_z = field_ref[p + kb] - here
            terms = terms + along_z * along_z
        slope = slope + fold(terms)
    sums_ref[0] = square
    sums_ref[1] = projected
    sums_ref[2] = slope


def middle_kernel(
    spec_hbm, coef_ref, tw_ref, inverse_ref, forward_ref,
    d0_ref, nd0_ref, head_ref, tail_ref, spec_ref, re_s, im_s, sems,
):
    gz, kb, _, rows, ka = spec_ref.shape
    planes = gz * kb
    lane_parts = [slice(start, start + LANES) for start in range(0, ka, LANES)]
    cuts = sems.shape[0]
    cut = rows // cuts

    def fetch(i):
        part = pl.ds(i * cut, cut)
        return pltpu.make_async_copy(
            spec_hbm.at[:, :, :, part], spec_ref.at[:, :, :, part], sems.at[i]
        )

    def columns_back(j, carry):
        part = pl.ds(pl.multiple_of(j * 8, 8), 8)
        for lanes in lane_parts:
            spectra = [
                [(spec_ref[z, k, 0, part, lanes], spec_ref[z, k, 1, part, lanes]) for k in range(kb)]
                for z in range(gz)
            ]
            inverse_columns(gz, kb, spectra, coef_ref, tw_ref, lanes, part, re_s, im_s)
        return carry

    for i in range(cuts):
        fetch(i).start()
    for i in range(cuts):
        fetch(i).wait()
        lax.fori_loop(i * cut // 8, (i + 1) * cut // 8, columns_back, 0)

    step = plane_chunk(planes, rows)
    shape2, shape3 = (step * rows, ka), (step, rows, ka)

    def there_and_back(i, carry):
        part = pl.ds(i * step, step)
        field = inverse_product(re_s[part].reshape(shape2), im_s[part].reshape(shape2), inverse_ref)
        d0_ref[part] = field.reshape(shape3)
        re, im = forward_product(field, forward_ref)
        re_s[part] = re.reshape(shape3)
        im_s[part] = im.reshape(shape3)
        return carry

    lax.fori_loop(0, planes // step, there_and_back, 0)

    def second_columns(j, total):
        part = pl.ds(pl.multiple_of(j * 8, 8), 8)
        for lanes in lane_parts:
            spectra = forward_columns(gz, kb, coef_ref, tw_ref, lanes, part, re_s, im_s)
            for z in range(gz):
                for k in range(kb):
                    for p in range(2):
                        value = spectra[z][k][p]
                        spec_ref[z, k, p, part, lanes] = value
                        total = total + value * value
        return total

    projected = lax.fori_loop(0, rows // 8, second_columns, jnp.zeros((8, LANES), F32))
    lax.fori_loop(0, rows // 8, columns_back, 0)
    def back(i, carry):
        part = pl.ds(i * step, step)
        field = inverse_product(re_s[part].reshape(shape2), im_s[part].reshape(shape2), inverse_ref)
        nd0_ref[part] = field.reshape(shape3)
        return carry

    lax.fori_loop(0, planes // step, back, 0)

    for p in range(planes):
        head_ref[p : p + 1, :] = d0_ref[p, :1, :]
        head_ref[planes + p : planes + p + 1, :] = d0_ref[p, 1:2, :]
        head_ref[2 * planes + p : 2 * planes + p + 1, :] = nd0_ref[p, :1, :]
        tail_ref[p : p + 1, :] = d0_ref[p, rows - 1 : rows, :]

    row = lax.broadcasted_iota(jnp.int32, (rows, ka), 0)
    square = jnp.zeros((8, LANES), F32)
    slope = jnp.zeros((8, LANES), F32)
    for p in range(planes):
        here = d0_ref[p]
        square = square + fold(here * here)
        along_x = next_plane(d0_ref, p, kb) - here
        along_y = jnp.where(row == rows - 1, 0.0, pltpu.roll(here, rows - 1, 0) - here)
        terms = along_x * along_x + along_y * along_y
        if p + kb < planes:
            along_z = d0_ref[p + kb] - here
            terms = terms + along_z * along_z
        slope = slope + fold(terms)
    block = sums_block([square, projected, slope])
    for ref in (head_ref, tail_ref):
        at = ref.shape[0] - 8
        ref[at:, :] = jnp.zeros((8, ka), F32)
        ref[at:, :LANES] = block


def middle(spec, coef, nx):
    gz, kb, _, rows, ka = spec.shape
    planes = gz * kb
    vmem = pl.BlockSpec(memory_space=pltpu.VMEM)
    field = jax.ShapeDtypeStruct((planes, rows, ka), F32)
    return pl.pallas_call(
        middle_kernel,
        in_specs=[pl.BlockSpec(memory_space=pltpu.HBM)] + [vmem] * 4,
        out_specs=[vmem] * 5,
        out_shape=[
            field,
            field,
            jax.ShapeDtypeStruct((3 * planes + 8, ka), F32),
            jax.ShapeDtypeStruct((planes + 8, ka), F32),
            jax.ShapeDtypeStruct(spec.shape, F32),
        ],
        scratch_shapes=[
            pltpu.VMEM((planes, rows, ka), F32),
            pltpu.VMEM((planes, rows, ka), F32),
            pltpu.SemaphoreType.DMA((4 if rows % 32 == 0 else 1,)),
        ],
        compiler_params=pltpu.CompilerParams(vmem_limit_bytes=X_GRANT),
        name="middle",
    )(
        spec, coef, x_twiddle(nx, ka), jnp.asarray(x_inverse_matrix(nx, ka)),
        x_forward_matrix(nx, ka),
    )


def border_kernel(edge_ref, head_ref, tail_ref, next_ref, prev_ref, out_ref):
    planes = tail_ref.shape[0] - 8

    def sums_of(ref):
        return ref[ref.shape[0] - 8 :, :LANES]

    def border(after, before):
        step = after[:planes, :] - before[:planes, :]
        return fold(step * step)

    second = edge_ref[2] > 0
    below = border(head_ref, prev_ref) * jnp.where(edge_ref[0] > 0, 0.0, 1.0)
    above = border(next_ref, tail_ref) * jnp.where(edge_ref[1] > 0, 0.0, 1.0)
    other = jnp.where(second, sums_of(prev_ref), sums_of(next_ref))
    none = jnp.zeros((8, LANES), F32)
    put_copies(out_ref, sums_of(tail_ref) + other + sums_block([none, none, below + above]))


def border_sums(edge, head, tail, next_head, prev_tail, copies):
    vmem = pl.BlockSpec(memory_space=pltpu.VMEM)
    return pl.pallas_call(
        border_kernel,
        in_specs=[pl.BlockSpec(memory_space=pltpu.SMEM)] + [vmem] * 4,
        out_specs=vmem,
        out_shape=jax.ShapeDtypeStruct((copies, 8, LANES), F32),
        compiler_params=pltpu.CompilerParams(vmem_limit_bytes=2 * MIB),
        name="border_sums",
    )(edge, head, tail, next_head, prev_tail)


def second_kernel(
    gz, edge_ref, d0_ref, nd0_ref, tail_ref, prev_ref, next_ref,
    coef_ref, tw_ref, table_ref, *refs,
):
    sums_refs, refs = refs[:1], refs[1:]
    d1_ref, eta_ref, out_ref, spec_ref, re_s, im_s, row_s = refs
    planes, rows, ka = d0_ref.shape
    kb = planes // gz
    eta_here = step_of(sums_refs)
    eta_ref[...] = jnp.broadcast_to(eta_here, (8, LANES))
    eta = jnp.max(eta_here)
    first = edge_ref[0] > 0
    last = edge_ref[1] > 0

    def shrink(difference):
        return jnp.clip(-eta * difference, -CLIP, CLIP)

    lane2 = lax.broadcasted_iota(jnp.int32, (kb, ka), 1)
    row2 = lax.broadcasted_iota(jnp.int32, (kb, ka), 0)
    for z in range(gz):
        part = slice(z * kb, (z + 1) * kb)
        here = next_ref[part, :]
        value = here - eta * next_ref[2 * planes + z * kb : 2 * planes + (z + 1) * kb, :]
        up = pltpu.roll(here, kb - 1, 0)
        up = jnp.where(
            row2 == kb - 1, jnp.where(lane2 == ka - 1, here, pltpu.roll(up, ka - 1, 1)), up
        )
        down = pltpu.roll(here, 1, 0)
        down = jnp.where(row2 == 0, jnp.where(lane2 == 0, here, pltpu.roll(down, 1, 1)), down)
        value = value + shrink(here - down) - shrink(up - here)
        value = value + shrink(here - tail_ref[part, :]) - shrink(next_ref[planes + z * kb : planes + (z + 1) * kb, :] - here)
        if z > 0:
            value = value + shrink(here - next_ref[(z - 1) * kb : z * kb, :])
        if z + 1 < gz:
            value = value - shrink(next_ref[(z + 1) * kb : (z + 2) * kb, :] - here)
        row_s[part, :] = value

    row = lax.broadcasted_iota(jnp.int32, (rows, ka), 0)
    square = jnp.zeros((8, LANES), F32)
    for p in range(planes):
        here = d0_ref[p]
        value = here - eta * nd0_ref[p]
        value = value + shrink(here - prev_plane(d0_ref, p, kb))
        value = value - shrink(next_plane(d0_ref, p, kb) - here)
        below = jnp.where(last, here[rows - 1 :, :], next_ref[p : p + 1, :])
        above = jnp.where(first, here[:1, :], prev_ref[p : p + 1, :])
        upper = shrink(jnp.where(row == rows - 1, below, pltpu.roll(here, rows - 1, 0)) - here)
        lower = jnp.where(row == 0, shrink(here[:1, :] - above), pltpu.roll(upper, 1, 0))
        value = value + lower - upper
        if p >= kb:
            value = value + shrink(here - d0_ref[p - kb])
        if p + kb < planes:
            value = value - shrink(d0_ref[p + kb] - here)
        d1_ref[p] = value
        square = square + fold(value * value)

    slope = jnp.zeros((8, LANES), F32)
    for p in range(planes):
        here = d1_ref[p]
        along_x = next_plane(d1_ref, p, kb) - here
        below = jnp.where(last, here[rows - 1 :, :], row_s[p : p + 1, :])
        along_y = jnp.where(row == rows - 1, below, pltpu.roll(here, rows - 1, 0)) - here
        terms = along_x * along_x + along_y * along_y
        if p + kb < planes:
            along_z = d1_ref[p + kb] - here
            terms = terms + along_z * along_z
        slope = slope + fold(terms)

    step = plane_chunk(planes, rows)

    def multiply(i, carry):
        part = pl.ds(i * step, step)
        re, im = forward_product(d1_ref[part].reshape(step * rows, ka), table_ref)
        re_s[part] = re.reshape(step, rows, ka)
        im_s[part] = im.reshape(step, rows, ka)
        return carry

    lax.fori_loop(0, planes // step, multiply, 0)

    def columns(j, total):
        part = pl.ds(pl.multiple_of(j * 8, 8), 8)
        for start in range(0, ka, LANES):
            lanes = slice(start, start + LANES)
            spectra = forward_columns(gz, kb, coef_ref, tw_ref, lanes, part, re_s, im_s)
            for z in range(gz):
                for k in range(kb):
                    for p in range(2):
                        value = spectra[z][k][p]
                        spec_ref[z, k, p, part, lanes] = value
                        total = total + value * value
        return total

    projected = lax.fori_loop(0, rows // 8, columns, jnp.zeros((8, LANES), F32))
    put_copies(out_ref, sums_block([square, projected, slope]))


def second_descent(edge, sums, d0, nd0, tail, prev_tail, next_head, coef, gz, nx):
    planes, rows, ka = d0.shape
    vmem = pl.BlockSpec(memory_space=pltpu.VMEM)
    return pl.pallas_call(
        functools.partial(second_kernel, gz),
        in_specs=[pl.BlockSpec(memory_space=pltpu.SMEM)] + [vmem] * 9,
        out_specs=[vmem] * 4,
        out_shape=[
            jax.ShapeDtypeStruct((planes, rows, ka), F32),
            jax.ShapeDtypeStruct((8, LANES), F32),
            jax.ShapeDtypeStruct(sums.shape, F32),
            jax.ShapeDtypeStruct((gz, planes // gz, 2, rows, ka), F32),
        ],
        scratch_shapes=[
            pltpu.VMEM((planes, rows, ka), F32),
            pltpu.VMEM((planes, rows, ka), F32),
            pltpu.VMEM((planes, ka), F32),
        ],
        compiler_params=pltpu.CompilerParams(vmem_limit_bytes=X_GRANT),
        name="second_descent",
    )(
        edge, d0, nd0, tail, prev_tail, next_head, coef,
        x_twiddle(nx, ka), x_forward_matrix(nx, ka), sums,
    )


def combine_kernel(gz, eta_ref, *refs):
    sums_refs, (first_ref, second_ref, out_ref, steps_ref) = refs[:gz], refs[gz:]
    eta0 = jnp.max(eta_ref[...])
    eta1 = jnp.max(step_of(sums_refs))
    steps_ref[0] = eta_ref[...]
    steps_ref[1] = jnp.full((8, LANES), eta1, F32)
    count = out_ref.shape[0]
    start = pl.program_id(0) * count
    for i in range(count):
        out_ref[i] = -(eta0 * first_ref[start + i] + eta1 * second_ref[start + i])


def combine_spectra(eta, sums, first, second):
    gz = len(sums)
    planes, *rest = first.shape
    count = 4 if planes % 4 == 0 else 1
    vmem = pl.BlockSpec(memory_space=pltpu.VMEM)
    return pl.pallas_call(
        functools.partial(combine_kernel, gz),
        grid=(planes // count,),
        in_specs=[vmem] * (3 + gz),
        out_specs=[
            pl.BlockSpec((count, *rest), lambda i: (i, 0, 0, 0)),
            pl.BlockSpec((2, 8, LANES), lambda i: (0, 0, 0)),
        ],
        out_shape=[
            jax.ShapeDtypeStruct(first.shape, F32),
            jax.ShapeDtypeStruct((2, 8, LANES), F32),
        ],
        compiler_params=pltpu.CompilerParams(vmem_limit_bytes=COMBINE_GRANT),
        name="combine_spectra",
    )(eta, *sums, first, second)


def to_core(piece, r):
    gz = lax.axis_size("gz")
    return lax.ppermute(piece, "gz", [(i, (i + r) % gz) for i in range(gz)]) if r else piece


def to_chips(parts):
    return lax.all_to_all(parts, "gy", 0, 0, tiled=True)


def to_devices(parts):
    gz, gy, *rest = parts.shape
    parts = lax.all_to_all(parts.reshape(gz * gy, *rest), ("gz", "gy"), 0, 0, tiled=True)
    return parts.reshape(gz, gy, *rest)


def everywhere(sums):
    sums = to_chips(sums)
    return [to_core(sums, r) for r in range(lax.axis_size("gz"))]


def shards(data, band_offset, interp_weight):
    gz = lax.axis_size("gz")
    gy = lax.axis_size("gy")
    devices = gz * gy
    data = data[0]
    blocks, ny, width = data.shape
    rows = ny // devices
    ka = blocks * HALF
    nx = ka * gy

    core = lax.axis_index("gz")
    flat = lax.axis_index("gy") * gz + core
    edge = jnp.stack([flat == 0, flat == devices - 1, core]).astype(jnp.int32)
    order = [(i % gz) * gy + i // gz for i in range(devices)]
    up = [(order[i + 1], order[i]) for i in range(devices - 1)]
    down = [(order[i], order[i + 1]) for i in range(devices - 1)]

    lower = band_offset < 0
    weight = interp_weight
    coef = jnp.stack(
        [
            jnp.where(lower, weight[1], weight[0]),
            jnp.where(lower, weight[0], 0.0),
            jnp.where(lower, 0.0, weight[1]),
        ]
    ).reshape(3, gy, 1, ka)
    coef = jnp.broadcast_to(coef, (3, gy, 8, ka))

    spec = to_devices(y_inverse(data, rows, gz, gy))
    d0, nd0, head, tail, first = middle(spec, coef, nx)
    next_head = lax.ppermute(head, ("gz", "gy"), up)
    prev_tail = lax.ppermute(tail, ("gz", "gy"), down)
    sums = to_chips(border_sums(edge, head, tail, next_head, prev_tail, gy))
    d1, eta, sums, second = second_descent(
        edge, sums, d0, nd0, tail, prev_tail, next_head, coef, gz, nx
    )
    sums = everywhere(sums)
    flat_shape = (devices, 2, rows, ka)
    spec, etas = combine_spectra(eta, sums, first.reshape(flat_shape), second.reshape(flat_shape))
    residual = y_forward(to_devices(spec.reshape(gz, gy, 2, rows, ka)), data)

    volume = -(etas[0, 0, 0] * d0 + etas[1, 0, 0] * d1)
    volume = volume.reshape(gz, gy, rows, ka).transpose(0, 2, 3, 1).reshape(gz, rows, nx)
    parts = [
        to_core(lax.dynamic_index_in_dim(volume, lax.rem(core + r, gz), 0, False), r)
        for r in range(gz)
    ]
    volume = jnp.zeros((gz, rows, nx), F32)
    for r, part in enumerate(parts):
        volume = lax.dynamic_update_index_in_dim(volume, part, lax.rem(core + gz - r, gz), 0)
    return (volume.reshape(1, gz * rows, nx), residual[None])


NX = 4096
NY = 2048
XB = 64
YB = 64
ITERS = 2
XA = 64
YA = 32
PRECISE = lax.Precision.HIGHEST


def with_halo(block, sides, width):
    for axis, dim in sides:
        count = lax.axis_size(axis)
        forward = [(i, i + 1) for i in range(count - 1)]
        backward = [(target, source) for source, target in forward]
        low = lax.ppermute(
            lax.slice_in_dim(block, block.shape[dim] - width, None, axis=dim), axis, forward
        )
        high = lax.ppermute(lax.slice_in_dim(block, 0, width, axis=dim), axis, backward)
        block = jnp.concatenate([low, block, high], axis=dim)
    return block


def from_behind(block, axis, distance):
    devices = range(lax.axis_size(axis))
    route = [(i - distance, i) for i in devices if i - distance in devices]
    return lax.ppermute(block, axis, route)


def unit_table(length):
    counter = jnp.arange(length, dtype=jnp.int32)
    phase_int = counter[:, None] * counter[None, :] % length
    angles = 2.0 * jnp.pi / length * phase_int.astype(jnp.float32)
    factor = length ** (-0.5)
    return (jnp.cos(angles) * factor, jnp.sin(angles) * factor)


def twiddle_table(row_len, col_len, period):
    phase_int = (
        jnp.arange(row_len, dtype=jnp.int32)[:, None]
        * jnp.arange(col_len, dtype=jnp.int32)[None, :]
        % period
    )
    angles = 2.0 * jnp.pi / period * phase_int.astype(jnp.float32)
    return (jnp.cos(angles), jnp.sin(angles))


def split_parts(packed):
    half_width = packed.shape[-1] // 2
    return (packed[..., :half_width], packed[..., half_width:])


def join_parts(real_part, imag_part):
    return jnp.concatenate([real_part, imag_part], axis=-1)


def complex_contract(packed, cos_table, sin_table, subscripts, conj_sign):
    cos_out = jnp.einsum(subscripts, packed, cos_table, precision=PRECISE)
    sin_out = jnp.einsum(subscripts, packed, sin_table, precision=PRECISE)
    cos_re, cos_im = split_parts(cos_out)
    sin_re, sin_im = split_parts(sin_out)
    return join_parts(cos_re - conj_sign * sin_im, cos_im + conj_sign * sin_re)


def rotate(packed, cos_table, sin_table, conj_sign):
    real_part, imag_part = split_parts(packed)
    return join_parts(
        real_part * cos_table - conj_sign * imag_part * sin_table,
        imag_part * cos_table + conj_sign * real_part * sin_table,
    )


def forward_x(volume):
    slices, row_count = (volume.shape[0], volume.shape[1])
    cos_a, sin_a = unit_table(XA)
    cos_b, sin_b = unit_table(XB)
    first_table = jnp.concatenate([cos_a, -sin_a], axis=1)
    grid_view = volume.reshape(slices, row_count, XA, XB)
    mixing = jnp.einsum("zyab,am->zybm", grid_view, first_table, precision=PRECISE)
    tw_cos, tw_sin = twiddle_table(XB, XA, NX)
    mixing = rotate(mixing, tw_cos, tw_sin, -1.0)
    return complex_contract(mixing, cos_b, sin_b, "zybm,bl->zlym", -1.0)


def inverse_x(packed):
    slices, row_count = (packed.shape[0], packed.shape[2])
    cos_a, sin_a = unit_table(XA)
    cos_b, sin_b = unit_table(XB)
    mixing = complex_contract(packed, cos_b, sin_b, "zlym,lb->zybm", 1.0)
    tw_cos, tw_sin = twiddle_table(XB, XA, NX)
    mixing = rotate(mixing, tw_cos, tw_sin, 1.0)
    last_table = jnp.concatenate([cos_a, -sin_a], axis=0)
    grid_view = jnp.einsum("zybm,ma->zyab", mixing, last_table, precision=PRECISE)
    return grid_view.reshape(slices, row_count, NX)


def forward_y(packed):
    slices, blocks, width = (packed.shape[0], packed.shape[1], packed.shape[3])
    cos_a, sin_a = unit_table(YA)
    cos_b, sin_b = unit_table(YB)
    grid_view = packed.reshape(slices, blocks, YA, YB, width)
    mixing = complex_contract(grid_view, cos_a, sin_a, "zjcdm,ck->zjkdm", -1.0)
    tw_cos, tw_sin = twiddle_table(YA, YB, NY)
    mixing = rotate(mixing, tw_cos[:, :, None], tw_sin[:, :, None], -1.0)
    result = complex_contract(mixing, cos_b, sin_b, "zjkdm,dl->zjlkm", -1.0)
    return result.reshape(slices, blocks, NY, width)


def inverse_y(packed):
    slices, blocks, width = (packed.shape[0], packed.shape[1], packed.shape[3])
    cos_a, sin_a = unit_table(YA)
    cos_b, sin_b = unit_table(YB)
    grid_view = packed.reshape(slices, blocks, YB, YA, width)
    mixing = complex_contract(grid_view, cos_b, sin_b, "zjlkm,ld->zjkdm", 1.0)
    tw_cos, tw_sin = twiddle_table(YA, YB, NY)
    mixing = rotate(mixing, tw_cos[:, :, None], tw_sin[:, :, None], 1.0)
    result = complex_contract(mixing, cos_a, sin_a, "zjkdm,kc->zjcdm", 1.0)
    return result.reshape(slices, blocks, NY, width)


def tilt_coefficients(band_offset, interp_weight, first_block, blocks):
    offsets = lax.dynamic_slice_in_dim(band_offset.reshape(XB, XA), first_block, blocks, 0)
    weights = lax.dynamic_slice_in_dim(interp_weight.reshape(2, XB, XA), first_block, blocks, 1)
    lower_tap = (jnp.concatenate([offsets, offsets], axis=1) < 0)[:, None, :]
    first_weight = jnp.concatenate([weights[0], weights[0]], axis=1)[:, None, :]
    second_weight = jnp.concatenate([weights[1], weights[1]], axis=1)[:, None, :]
    return (lower_tap, first_weight, second_weight)


def tilt(field_in, coefficients, adjoint):
    lower_tap, first_weight, second_weight = coefficients
    padded = with_halo(field_in, (("gz", 0),), 1)
    below_rim = padded[:-2]
    middle = padded[1:-1]
    above_rim = padded[2:]
    if adjoint:
        return jnp.where(
            lower_tap,
            first_weight * above_rim + second_weight * middle,
            first_weight * middle + second_weight * below_rim,
        )
    return jnp.where(
        lower_tap,
        first_weight * below_rim + second_weight * middle,
        first_weight * middle + second_weight * above_rim,
    )


def to_pencil(slab_part):
    return lax.all_to_all(slab_part, "gy", split_axis=1, concat_axis=2, tiled=True)


def to_slab(pencil_part):
    return lax.all_to_all(pencil_part, "gy", split_axis=2, concat_axis=1, tiled=True)


def back_project(packed, pencil_coef):
    return inverse_x(to_slab(inverse_y(tilt(packed, pencil_coef, True))))


def edge_masks(slices, row_count):
    z_global = lax.axis_index("gz") * slices + jnp.arange(slices, dtype=jnp.int32)
    y_global = lax.axis_index("gy") * row_count + jnp.arange(row_count, dtype=jnp.int32)
    keep_z = (z_global < slices * lax.axis_size("gz") - 1).astype(jnp.float32)[:, None, None]
    keep_y = (y_global < row_count * lax.axis_size("gy") - 1).astype(jnp.float32)[None, :, None]
    return (keep_z, keep_y)


def forward_diff(field_in, keep_z, keep_y):
    slices, row_count = (field_in.shape[0], field_in.shape[1])
    next_z = from_behind(field_in, "gz", -1)
    next_y = from_behind(field_in[:, :1], "gy", -1)
    along_z = (jnp.concatenate([field_in[1:], next_z], axis=0) - field_in) * keep_z
    along_y = (jnp.concatenate([field_in[:, 1:], next_y], axis=1) - field_in) * keep_y
    zero_col = jnp.zeros((slices, row_count, 1), jnp.float32)
    along_x = jnp.concatenate([field_in[:, :, 1:] - field_in[:, :, :-1], zero_col], axis=2)
    return jnp.stack([along_z, along_y, along_x])


def transpose_diff(components, keep_z, keep_y):
    slices, row_count = (components.shape[1], components.shape[2])
    zero_col = jnp.zeros((slices, row_count, 1), jnp.float32)
    comp_z = components[0] * keep_z
    comp_y = components[1] * keep_y
    comp_x = jnp.concatenate([components[2][:, :, :-1], zero_col], axis=2)
    prev_z = from_behind(comp_z, "gz", 1)
    prev_y = from_behind(comp_y[:, -1:], "gy", 1)
    result = jnp.concatenate([prev_z, comp_z[:-1]], axis=0) - comp_z
    result = result + jnp.concatenate([prev_y, comp_y[:, :-1]], axis=1) - comp_y
    result = result + jnp.concatenate([zero_col, comp_x[:, :, :-1]], axis=2) - comp_x
    return result


def plain_shards(data, band_offset, interp_weight):
    slices = data.shape[0]
    blocks = data.shape[1]
    width = data.shape[3]
    row_count = NY // lax.axis_size("gy")
    slab_coef = tilt_coefficients(band_offset, interp_weight, 0, XB)
    pencil_coef = tilt_coefficients(
        band_offset, interp_weight, lax.axis_index("gy") * blocks, blocks
    )
    keep_z, keep_y = edge_masks(slices, row_count)
    measured = data.astype(jnp.float32)
    volume = jnp.zeros((slices, row_count, NX), jnp.float32)
    grad_volume = jnp.zeros((3, slices, row_count, NX), jnp.float32)
    split_var = grad_volume
    dual_var = grad_volume
    data_back = back_project(measured, pencil_coef)
    normal_part = jnp.zeros_like(volume)
    tilted = jnp.zeros((slices, XB, row_count, width), jnp.float32)
    for iteration in range(ITERS):
        data_grad = normal_part - data_back
        if iteration > 0:
            tv_gap = grad_volume - split_var + dual_var / PENALTY
            descent = data_grad + PENALTY * transpose_diff(tv_gap, keep_z, keep_y)
        else:
            descent = data_grad
        slope_field = forward_diff(descent, keep_z, keep_y)
        projected = tilt(forward_x(descent), slab_coef, False)
        line_totals = lax.psum(
            (
                jnp.sum(descent * descent),
                jnp.sum(projected * projected),
                jnp.sum(slope_field * slope_field),
            ),
            ("gz", "gy"),
        )
        step_length = line_totals[0] / (line_totals[1] + PENALTY * line_totals[2])
        volume = volume - step_length * descent
        grad_volume = grad_volume - step_length * slope_field
        tilted = tilted - step_length * projected
        if iteration + 1 < ITERS:
            normal_part = normal_part - step_length * inverse_x(tilt(projected, slab_coef, True))
        if iteration + 1 < ITERS:
            shifted = grad_volume + dual_var / PENALTY
            split_var = shifted - jnp.clip(shifted, -TV_WEIGHT / PENALTY, TV_WEIGHT / PENALTY)
            dual_var = PENALTY * (grad_volume - split_var)
    residual = forward_y(to_pencil(tilted)) - measured
    return (volume, residual)


def tiles_fit(mesh, ny, blocks):
    rows = ny // (mesh.shape["gz"] * mesh.shape["gy"])
    return mesh.shape["gz"] == 2 and rows % 16 == 0 and mesh.shape["gy"] % YR == 0 and blocks // mesh.shape["gy"] % 2 == 0


def solution(mesh):
    in_specs = (P("gz", "gy", None, None), P(), P())
    out_specs = (P("gz", "gy", None), P("gz", "gy", None, None))

    def run(data, band_offset, interp_weight):
        body = shards if tiles_fit(mesh, data.shape[2], data.shape[1]) else plain_shards
        call = jax.shard_map(
            body, mesh=mesh, in_specs=in_specs, out_specs=out_specs, check_vma=False
        )
        return call(data, band_offset, interp_weight)

    return run
```

```python
import functools

import jax
import jax.numpy as jnp
import numpy as np
from jax import lax
from jax.experimental import pallas as pl
from jax.experimental.pallas import tpu as pltpu
from jax.sharding import PartitionSpec as P

PENALTY = 0.5
TV_WEIGHT = 0.25
CLIP = TV_WEIGHT / PENALTY
HALF = 64
YR = 8
LANES = 128
F32 = jnp.float32
BF16 = jnp.bfloat16
MIB = 1024 * 1024
Y_GRANT = 56 * MIB
X_GRANT = 20 * MIB


def dft_parts(length, scale):
    index = np.arange(length)
    angles = 2.0 * np.pi / length * (index[:, None] * index[None, :] % length)
    return np.cos(angles) * scale, np.sin(angles) * scale


def two_parts(table):
    table = jnp.asarray(table.astype(np.float32))
    high = table.astype(BF16)
    low = (table - high.astype(F32)).astype(BF16)
    return high, low


def host_parts(table):
    table = table.astype(np.float32)
    high = table.astype(BF16)
    low = (table - high.astype(np.float32)).astype(BF16)
    return high, low


def y_matrix(ny, forward, sign):
    n = ny // YR
    cos, sin = dft_parts(n, sign * ny**-0.5)
    if forward:
        table = np.block([[cos, sin], [-sin, cos]])
    else:
        table = np.block([[cos, -sin], [sin, cos]])
    return jnp.asarray(np.concatenate(host_parts(table), axis=0))


def y_twiddle(ny):
    n = ny // YR
    angles = 2.0 * np.pi / ny * (np.arange(1, YR)[:, None] * np.arange(n)[None, :])
    table = np.stack([np.cos(angles), np.sin(angles)]).astype(np.float32)
    return jnp.asarray(np.ascontiguousarray(np.broadcast_to(table[..., None], (2, YR - 1, n, LANES))))


def x_inverse_matrix(nx, ka):
    cos, sin = dft_parts(ka, nx**-0.5)
    return np.concatenate(host_parts(np.concatenate([cos, -sin], axis=0)), axis=1)


def x_forward_matrix(nx, ka):
    cos, sin = dft_parts(ka, nx**-0.5)
    return jnp.asarray(np.concatenate(host_parts(np.concatenate([cos, -sin], axis=1)), axis=1))


def x_twiddle(nx, ka):
    kb = nx // ka
    angles = 2.0 * np.pi / nx * (np.arange(kb)[:, None] * np.arange(ka)[None, :])
    table = np.stack([np.cos(angles), np.sin(angles)]).astype(np.float32)
    return jnp.asarray(np.ascontiguousarray(np.broadcast_to(table[:, :, None], (2, kb, 8, ka))))


def short_fft(planes, sign):
    n = len(planes)
    if n == 1:
        return planes
    even = short_fft(planes[0::2], sign)
    odd = short_fft(planes[1::2], sign)
    half = n // 2
    out = [None] * n
    for k in range(half):
        er, ei = even[k]
        tr, ti = odd[k]
        if 4 * k == n:
            if sign > 0:
                out[k] = (er - ti, ei + tr)
                out[k + half] = (er + ti, ei - tr)
            else:
                out[k] = (er + ti, ei - tr)
                out[k + half] = (er - ti, ei + tr)
            continue
        if k > 0:
            c = float(np.cos(2.0 * np.pi * k / n))
            s = float(sign * np.sin(2.0 * np.pi * k / n))
            if 8 * k == n:
                tr, ti = (tr - ti, ti + tr) if sign > 0 else (tr + ti, ti - tr)
                tr, ti = tr * c, ti * c
            elif 8 * k == 3 * n:
                m = float(np.sin(2.0 * np.pi * k / n))
                tr, ti = (-(tr + ti), tr - ti) if sign > 0 else (ti - tr, -(tr + ti))
                tr, ti = tr * m, ti * m
            else:
                tr, ti = tr * c - ti * s, ti * c + tr * s
        out[k] = (er + tr, ei + ti)
        out[k + half] = (er - tr, ei - ti)
    return out


def split2(x):
    high = x.astype(BF16)
    return high, (x - high.astype(F32)).astype(BF16)


def dot(a, b):
    return jnp.dot(a, b, preferred_element_type=F32)


def fold(x):
    rows, lanes = x.shape
    x = jnp.sum(x.reshape(rows // 8, 8, lanes), axis=0)
    total = x[:, :LANES]
    for i in range(1, lanes // LANES):
        total = total + x[:, i * LANES : (i + 1) * LANES]
    return total


def full_sum(x):
    return jnp.sum(jnp.sum(x, axis=0, keepdims=True), axis=1, keepdims=True)


def step_of(sums_refs):
    total = sum(jnp.sum(sums_ref[...], axis=0) for sums_ref in sums_refs)
    parts = jnp.sum(total, axis=1, keepdims=True)
    return parts[0:1] / (parts[1:2] + PENALTY * parts[2:3])


def sums_block(values):
    rows = [jnp.sum(v, axis=0, keepdims=True) for v in values]
    index = lax.broadcasted_iota(jnp.int32, (8, LANES), 0)
    block = jnp.zeros((8, LANES), F32)
    for i, row in enumerate(rows):
        block = jnp.where(index == i, jnp.broadcast_to(row, (8, LANES)), block)
    return block


def put_copies(out_ref, block):
    for i in range(out_ref.shape[0]):
        out_ref[i] = block


def mix_adjoint(coef, planes):
    own, below, above = coef
    out = []
    for z in range(len(planes)):
        value = own * planes[z]
        if z + 1 < len(planes):
            value = value + below * planes[z + 1]
        if z > 0:
            value = value + above * planes[z - 1]
        out.append(value)
    return out


def mix(coef, planes):
    own, below, above = coef
    out = []
    for z in range(len(planes)):
        value = own * planes[z]
        if z > 0:
            value = value + below * planes[z - 1]
        if z + 1 < len(planes):
            value = value + above * planes[z + 1]
        out.append(value)
    return out


def y_inverse_kernel(
    data_hbm, table_hbm, tw_hbm, out_hbm,
    data_ref, table_ref, tw_ref, out_ref, re_s, im_s, mix_s, sems, out_sems,
):
    blocks, ny, _ = data_ref.shape
    n = ny // YR
    gz, _, _, rows, _ = out_ref.shape
    lane = lax.broadcasted_iota(jnp.int32, (n, LANES), 1)
    pairs = blocks // 2

    def fetch(chunk):
        part = pl.ds(2 * chunk, 2)
        return pltpu.make_async_copy(data_hbm.at[part], data_ref.at[part], sems.at[2 + chunk])

    def give(chunk, core):
        at = (core, slice(None), slice(None), slice(None), pl.ds(chunk * LANES, LANES))
        return pltpu.make_async_copy(out_ref.at[at], out_hbm.at[at], out_sems.at[chunk * gz + core])

    fetch_table = pltpu.make_async_copy(table_hbm, table_ref, sems.at[0])
    fetch_tw = pltpu.make_async_copy(tw_hbm, tw_ref, sems.at[1])
    fetch(0).start()
    fetch_table.start()
    fetch_tw.start()
    for chunk in range(1, pairs):
        fetch(chunk).start()

    for chunk in range(pairs):
        lanes = slice(chunk * LANES, (chunk + 1) * LANES)
        fetch(chunk).wait()

        def unpack(i, carry):
            part = pl.ds(pl.multiple_of(i * n, n), n)
            first = data_ref[2 * chunk, part, :].astype(F32)
            second = data_ref[2 * chunk + 1, part, :].astype(F32)
            re_s[part, :] = jnp.where(lane < HALF, first, pltpu.roll(second, HALF, 1))
            im_s[part, :] = jnp.where(lane < HALF, pltpu.roll(first, HALF, 1), second)
            return carry

        lax.fori_loop(0, YR, unpack, 0)
        if chunk == 0:
            fetch_table.wait()

        for k in range(0, YR, 2):
            pieces = [
                jnp.concatenate([s[pl.ds(k + d, n, stride=YR), :] for d in range(2)], axis=1)
                for s in (re_s, im_s)
            ]
            both = dot(table_ref[...], jnp.concatenate(pieces, axis=0).astype(BF16))
            both = both[: 2 * n] + both[2 * n :]
            for d in range(2):
                mix_s[k + d] = both[:, d * LANES : (d + 1) * LANES]

        if chunk == 0:
            fetch_tw.wait()

        tiles = rows // 8
        for core in range(gz):

            def combine(i, carry):
                y2 = ((i // tiles) * gz + core) * rows + lax.rem(i, tiles) * 8
                part = pl.ds(pl.multiple_of(y2, 8), 8)
                planes = []
                for k in range(YR):
                    re = mix_s[k, part, :]
                    im = mix_s[k, pl.ds(pl.multiple_of(n + y2, 8), 8), :]
                    if k > 0:
                        c = tw_ref[0, k - 1, part, :]
                        s = tw_ref[1, k - 1, part, :]
                        re, im = re * c - im * s, im * c + re * s
                    planes.append((re, im))
                at = pl.ds(pl.multiple_of(lax.rem(i, tiles) * 8, 8), 8)
                for k, (re, im) in enumerate(short_fft(planes, 1)):
                    to = k * (n // (gz * rows)) + i // tiles
                    out_ref[core, to, 0, at, lanes] = re
                    out_ref[core, to, 1, at, lanes] = im
                return carry

            lax.fori_loop(0, n // gz // 8, combine, 0, unroll=2)
            give(chunk, core).start()

    for chunk in range(pairs):
        for core in range(gz):
            give(chunk, core).wait()


def y_inverse(data, rows, gz, gy):
    blocks, ny, width = data.shape
    n = ny // YR
    ka = blocks * HALF
    hbm = pl.BlockSpec(memory_space=pltpu.HBM)
    return pl.pallas_call(
        y_inverse_kernel,
        in_specs=[hbm] * 3,
        out_specs=hbm,
        out_shape=jax.ShapeDtypeStruct((gz, gy, 2, rows, ka), F32),
        scratch_shapes=[
            pltpu.VMEM((blocks, ny, width), BF16),
            pltpu.VMEM((4 * n, 2 * n), BF16),
            pltpu.VMEM((2, YR - 1, n, LANES), F32),
            pltpu.VMEM((gz, gy, 2, rows, ka), F32),
            pltpu.VMEM((ny, LANES), F32),
            pltpu.VMEM((ny, LANES), F32),
            pltpu.VMEM((YR, 2 * n, LANES), F32),
            pltpu.SemaphoreType.DMA((2 + blocks // 2,)),
            pltpu.SemaphoreType.DMA((blocks // 2 * gz,)),
        ],
        compiler_params=pltpu.CompilerParams(vmem_limit_bytes=Y_GRANT),
        name="y_inverse",
    )(data, y_matrix(ny, False, -1.0), y_twiddle(ny))


def y_forward_kernel(
    spec_hbm, data_hbm, table_hbm, tw_hbm, out_hbm,
    spec_ref, data_ref, table_ref, tw_ref, out_ref, mix_s, sems, spec_sems, out_sems,
):
    blocks, ny, _ = data_ref.shape
    n = ny // YR
    _, gz, gy, _, rows, _ = spec_ref.shape
    pairs = blocks // 2
    half = n // 2

    def fetch(chunk):
        lanes = pl.ds(chunk * LANES, LANES)
        return pltpu.make_async_copy(
            spec_hbm.at[:, :, :, :, lanes], spec_ref.at[chunk], spec_sems.at[chunk]
        )

    def give(chunk, part):
        at = (pl.ds(2 * chunk, 2), slice(None), pl.ds(part * half, half))
        return pltpu.make_async_copy(out_ref.at[at], out_hbm.at[at], out_sems.at[2 * chunk + part])

    fetch_table = pltpu.make_async_copy(table_hbm, table_ref, sems.at[0])
    fetch_tw = pltpu.make_async_copy(tw_hbm, tw_ref, sems.at[1])
    fetch_data = pltpu.make_async_copy(data_hbm, data_ref, sems.at[2])
    fetch(0).start()
    fetch_table.start()
    fetch_tw.start()
    fetch_data.start()
    for chunk in range(1, pairs):
        fetch(chunk).start()

    def rows_of(chunk, p, k):
        part = pl.ds(k, rows // YR, stride=YR)
        return jnp.concatenate(
            [spec_ref[chunk, core, i, p, part, :] for i in range(gy) for core in range(gz)], axis=0
        )

    lane = lax.broadcasted_iota(jnp.int32, (16, LANES), 1)
    for chunk in range(pairs):
        lanes = slice(chunk * LANES, (chunk + 1) * LANES)
        fetch(chunk).wait()

        if chunk == 0:
            fetch_table.wait()

        for k in range(0, YR, 2):
            pieces = [
                jnp.concatenate([rows_of(chunk, p, k + d) for d in range(2)], axis=1)
                for p in range(2)
            ]
            high, low = split2(jnp.concatenate(pieces, axis=0))
            both = dot(table_ref[...], high)
            both = both[: 2 * n] + both[2 * n :] + dot(table_ref[: 2 * n], low)
            for d in range(2):
                mix_s[k + d] = both[:, d * LANES : (d + 1) * LANES]
        if chunk == 0:
            fetch_tw.wait()
            fetch_data.wait()

        def combine(i, carry):
            start = pl.multiple_of(i * 16, 16)
            part = pl.ds(start, 16)
            planes = []
            for k in range(YR):
                re = mix_s[k, part, :]
                im = mix_s[k, pl.ds(pl.multiple_of(n + i * 16, 16), 16), :]
                if k > 0:
                    c = tw_ref[0, k - 1, part, :]
                    s = tw_ref[1, k - 1, part, :]
                    re, im = re * c + im * s, im * c - re * s
                planes.append((re, im))
            for k, (re, im) in enumerate(short_fft(planes, -1)):
                at = pl.ds(pl.multiple_of(k * n + start, 16), 16)
                first = jnp.where(lane < HALF, re, pltpu.roll(im, HALF, 1))
                second = jnp.where(lane < HALF, pltpu.roll(re, HALF, 1), im)
                out_ref[2 * chunk, k, part, :] = first - data_ref[2 * chunk, at, :].astype(F32)
                out_ref[2 * chunk + 1, k, part, :] = (
                    second - data_ref[2 * chunk + 1, at, :].astype(F32)
                )
            return carry

        for part in range(2):
            lax.fori_loop(part * half // 16, (part + 1) * half // 16, combine, 0)
            give(chunk, part).start()

    for chunk in range(pairs):
        for part in range(2):
            give(chunk, part).wait()


def y_forward(spec, data):
    blocks, ny, width = data.shape
    n = ny // YR
    hbm = pl.BlockSpec(memory_space=pltpu.HBM)
    out = pl.pallas_call(
        y_forward_kernel,
        in_specs=[hbm] * 4,
        out_specs=hbm,
        out_shape=jax.ShapeDtypeStruct((blocks, YR, n, width), F32),
        scratch_shapes=[
            pltpu.VMEM((blocks // 2, *spec.shape[:-1], LANES), F32),
            pltpu.VMEM((blocks, ny, width), BF16),
            pltpu.VMEM((4 * n, 2 * n), BF16),
            pltpu.VMEM((2, YR - 1, n, LANES), F32),
            pltpu.VMEM((blocks, YR, n, width), F32),
            pltpu.VMEM((YR, 2 * n, LANES), F32),
            pltpu.SemaphoreType.DMA((3,)),
            pltpu.SemaphoreType.DMA((blocks // 2,)),
            pltpu.SemaphoreType.DMA((blocks,)),
        ],
        compiler_params=pltpu.CompilerParams(vmem_limit_bytes=Y_GRANT),
        name="y_forward",
    )(spec, data, y_matrix(ny, True, 1.0), y_twiddle(ny))
    return out.reshape(blocks, ny, width)


def plane_chunk(planes, rows):
    chunk = max(1, 1024 // rows)
    while planes % chunk:
        chunk -= 1
    return chunk


def turn_rows(kb, planes_of, tw_ref, lanes, sign):
    out = []
    for b in range(kb):
        re, im = planes_of(b)
        if b > 0:
            c = tw_ref[0, b, :, lanes]
            s = tw_ref[1, b, :, lanes]
            if sign > 0:
                re, im = re * c - im * s, im * c + re * s
            else:
                re, im = re * c + im * s, im * c - re * s
        out.append((re, im))
    return out


def inverse_columns(gz, kb, spectra, coef_ref, tw_ref, lanes, part, re_s, im_s):
    mixed = [[None] * kb for _ in range(gz)]
    for k in range(kb):
        coef = [coef_ref[j, k, :, lanes] for j in range(3)]
        re = mix_adjoint(coef, [spectra[z][k][0] for z in range(gz)])
        im = mix_adjoint(coef, [spectra[z][k][1] for z in range(gz)])
        for z in range(gz):
            mixed[z][k] = (re[z], im[z])
    for z in range(gz):
        short = short_fft(mixed[z], 1)
        for b, (re, im) in enumerate(turn_rows(kb, lambda b: short[b], tw_ref, lanes, 1)):
            re_s[z * kb + b, part, lanes] = re
            im_s[z * kb + b, part, lanes] = im


def forward_columns(gz, kb, coef_ref, tw_ref, lanes, part, re_s, im_s):
    spectra = []
    for z in range(gz):
        rows_of = lambda b: (re_s[z * kb + b, part, lanes], im_s[z * kb + b, part, lanes])
        spectra.append(short_fft(turn_rows(kb, rows_of, tw_ref, lanes, -1), -1))
    out = [[None] * kb for _ in range(gz)]
    for k in range(kb):
        coef = [coef_ref[j, k, :, lanes] for j in range(3)]
        re = mix(coef, [spectra[z][k][0] for z in range(gz)])
        im = mix(coef, [spectra[z][k][1] for z in range(gz)])
        for z in range(gz):
            out[z][k] = (re[z], im[z])
    return out


def inverse_product(re, im, table_ref):
    ka = re.shape[1]
    high, low = split2(jnp.concatenate([re, im], axis=1))
    value = dot(high, table_ref[...])
    return value[:, :ka] + value[:, ka:] + dot(low, table_ref[:, :ka])


def forward_product(field, table_ref):
    ka = field.shape[1]
    high, low = split2(field)
    value = dot(high, table_ref[...])
    value = value[:, : 2 * ka] + value[:, 2 * ka :] + dot(low, table_ref[:, : 2 * ka])
    return value[:, :ka], value[:, ka:]


def next_plane(field_ref, p, kb):
    rows, ka = field_ref.shape[1:]
    if (p + 1) % kb:
        return field_ref[p + 1]
    lane = lax.broadcasted_iota(jnp.int32, (rows, ka), 1)
    return jnp.where(lane == ka - 1, field_ref[p], pltpu.roll(field_ref[p + 1 - kb], ka - 1, 1))


def prev_plane(field_ref, p, kb):
    rows, ka = field_ref.shape[1:]
    if p % kb:
        return field_ref[p - 1]
    lane = lax.broadcasted_iota(jnp.int32, (rows, ka), 1)
    return jnp.where(lane == 0, field_ref[p], pltpu.roll(field_ref[p + kb - 1], 1, 1))


def first_kernel(
    gz, edge_ref, field_ref, coef_ref, tw_ref, table_ref, sums_ref, spec_ref, *refs
):
    piece_refs, (re_s, im_s) = refs[:-2], refs[-2:]
    planes, rows, ka = field_ref.shape
    kb = planes // gz
    projected = forward_into(gz, field_ref, coef_ref, tw_ref, table_ref, spec_ref, re_s, im_s)
    cut(gz, edge_ref, spec_ref, piece_refs)
    row = lax.broadcasted_iota(jnp.int32, (rows, ka), 0)
    square = jnp.zeros((8, LANES), F32)
    slope = jnp.zeros((8, LANES), F32)
    for p in range(planes):
        here = field_ref[p]
        square = square + fold(here * here)
        along_x = next_plane(field_ref, p, kb) - here
        along_y = jnp.where(row == rows - 1, 0.0, pltpu.roll(here, rows - 1, 0) - here)
        terms = along_x * along_x + along_y * along_y
        if p + kb < planes:
            along_z = field_ref[p + kb] - here
            terms = terms + along_z * along_z
        slope = slope + fold(terms)
    sums_ref[0] = square
    sums_ref[1] = projected
    sums_ref[2] = slope


def middle_kernel(
    spec_hbm, coef_ref, tw_ref, inverse_ref, forward_ref,
    d0_ref, head_ref, tail_ref, spec_ref, re_s, im_s, sems,
):
    gz, kb, _, rows, ka = spec_ref.shape
    planes = gz * kb
    lane_parts = [slice(start, start + LANES) for start in range(0, ka, LANES)]
    cuts = sems.shape[0]
    cut = rows // cuts

    def fetch(i):
        part = pl.ds(i * cut, cut)
        return pltpu.make_async_copy(
            spec_hbm.at[:, :, :, part], spec_ref.at[:, :, :, part], sems.at[i]
        )

    def columns_back(j, carry):
        part = pl.ds(pl.multiple_of(j * 8, 8), 8)
        for lanes in lane_parts:
            spectra = [
                [(spec_ref[z, k, 0, part, lanes], spec_ref[z, k, 1, part, lanes]) for k in range(kb)]
                for z in range(gz)
            ]
            inverse_columns(gz, kb, spectra, coef_ref, tw_ref, lanes, part, re_s, im_s)
        return carry

    for i in range(cuts):
        fetch(i).start()
    for i in range(cuts):
        fetch(i).wait()
        lax.fori_loop(i * cut // 8, (i + 1) * cut // 8, columns_back, 0)

    step = plane_chunk(planes, rows)
    shape2, shape3 = (step * rows, ka), (step, rows, ka)

    def there_and_back(i, carry):
        part = pl.ds(i * step, step)
        field = inverse_product(re_s[part].reshape(shape2), im_s[part].reshape(shape2), inverse_ref)
        d0_ref[part] = field.reshape(shape3)
        re, im = forward_product(field, forward_ref)
        re_s[part] = re.reshape(shape3)
        im_s[part] = im.reshape(shape3)
        return carry

    lax.fori_loop(0, planes // step, there_and_back, 0)

    def second_columns(j, total):
        part = pl.ds(pl.multiple_of(j * 8, 8), 8)
        for lanes in lane_parts:
            spectra = forward_columns(gz, kb, coef_ref, tw_ref, lanes, part, re_s, im_s)
            for z in range(gz):
                for k in range(kb):
                    for p in range(2):
                        value = spectra[z][k][p]
                        spec_ref[z, k, p, part, lanes] = value
                        total = total + value * value
        return total

    projected = lax.fori_loop(0, rows // 8, second_columns, jnp.zeros((8, LANES), F32))
    for p in range(planes):
        head_ref[p : p + 1, :] = d0_ref[p, :1, :]
        head_ref[planes + p : planes + p + 1, :] = d0_ref[p, 1:2, :]
        for part in range(2):
            at = 2 * planes + 2 * p + part
            head_ref[at : at + 1, :] = spec_ref[p // kb, p % kb, part, :1, :]
        tail_ref[p : p + 1, :] = d0_ref[p, rows - 1 : rows, :]

    row = lax.broadcasted_iota(jnp.int32, (rows, ka), 0)
    square = jnp.zeros((8, LANES), F32)
    slope = jnp.zeros((8, LANES), F32)
    for p in range(planes):
        here = d0_ref[p]
        square = square + fold(here * here)
        along_x = next_plane(d0_ref, p, kb) - here
        along_y = jnp.where(row == rows - 1, 0.0, pltpu.roll(here, rows - 1, 0) - here)
        terms = along_x * along_x + along_y * along_y
        if p + kb < planes:
            along_z = d0_ref[p + kb] - here
            terms = terms + along_z * along_z
        slope = slope + fold(terms)
    block = sums_block([square, projected, slope])
    for ref in (head_ref, tail_ref):
        at = ref.shape[0] - 8
        ref[at:, :] = jnp.zeros((8, ka), F32)
        ref[at:, :LANES] = block


def middle(spec, coef, nx):
    gz, kb, _, rows, ka = spec.shape
    planes = gz * kb
    vmem = pl.BlockSpec(memory_space=pltpu.VMEM)
    field = jax.ShapeDtypeStruct((planes, rows, ka), F32)
    return pl.pallas_call(
        middle_kernel,
        in_specs=[pl.BlockSpec(memory_space=pltpu.HBM)] + [vmem] * 4,
        out_specs=[vmem] * 4,
        out_shape=[
            field,
            jax.ShapeDtypeStruct((4 * planes + 8, ka), F32),
            jax.ShapeDtypeStruct((planes + 8, ka), F32),
            jax.ShapeDtypeStruct(spec.shape, F32),
        ],
        scratch_shapes=[
            pltpu.VMEM((planes, rows, ka), F32),
            pltpu.VMEM((planes, rows, ka), F32),
            pltpu.SemaphoreType.DMA((4 if rows % 32 == 0 else 1,)),
        ],
        compiler_params=pltpu.CompilerParams(vmem_limit_bytes=X_GRANT),
        name="middle",
    )(
        spec, coef, x_twiddle(nx, ka), jnp.asarray(x_inverse_matrix(nx, ka)),
        x_forward_matrix(nx, ka),
    )


def normal_kernel(spec_ref, next_ref, coef_ref, tw_ref, table_ref, out_ref, row_ref, re_s, im_s):
    gz, kb, _, rows, ka = spec_ref.shape
    planes = gz * kb
    lane_parts = [slice(start, start + LANES) for start in range(0, ka, LANES)]

    def columns(j, carry):
        part = pl.ds(pl.multiple_of(j * 8, 8), 8)
        for lanes in lane_parts:
            spectra = [
                [(spec_ref[z, k, 0, part, lanes], spec_ref[z, k, 1, part, lanes]) for k in range(kb)]
                for z in range(gz)
            ]
            inverse_columns(gz, kb, spectra, coef_ref, tw_ref, lanes, part, re_s, im_s)
        return carry

    lax.fori_loop(0, rows // 8, columns, 0)

    for lanes in lane_parts:

        def row_of(z, k, part):
            at = 2 * planes + 2 * (z * kb + k) + part
            return jnp.broadcast_to(next_ref[at : at + 1, lanes], (8, LANES))

        spectra = [[(row_of(z, k, 0), row_of(z, k, 1)) for k in range(kb)] for z in range(gz)]
        inverse_columns(gz, kb, spectra, coef_ref, tw_ref, lanes, slice(rows, rows + 8), re_s, im_s)

    step = plane_chunk(planes, rows)
    high_rows = rows + 8
    for start in range(0, planes, step):
        part = slice(start, start + step)
        shape = (step * high_rows, ka)
        field = inverse_product(re_s[part].reshape(shape), im_s[part].reshape(shape), table_ref)
        field = field.reshape(step, high_rows, ka)
        out_ref[part] = field[:, :rows]
        for p in range(step):
            row_ref[start + p : start + p + 1, :] = field[p, rows : rows + 1, :]


def normal_product(spec, next_head, coef, nx):
    gz, kb, _, rows, ka = spec.shape
    planes = gz * kb
    vmem = pl.BlockSpec(memory_space=pltpu.VMEM)
    return pl.pallas_call(
        normal_kernel,
        in_specs=[vmem] * 5,
        out_specs=[vmem] * 2,
        out_shape=[
            jax.ShapeDtypeStruct((planes, rows, ka), F32),
            jax.ShapeDtypeStruct((planes, ka), F32),
        ],
        scratch_shapes=[pltpu.VMEM((planes, rows + 8, ka), F32)] * 2,
        compiler_params=pltpu.CompilerParams(vmem_limit_bytes=X_GRANT),
        cost_estimate=pl.CostEstimate(
            flops=12 * planes * rows * ka * ka, bytes_accessed=12 * planes * rows * ka, transcendentals=0
        ),
        name="normal_product",
    )(spec, next_head, coef, x_twiddle(nx, ka), jnp.asarray(x_inverse_matrix(nx, ka)))


def border_kernel(edge_ref, head_ref, tail_ref, next_ref, prev_ref, out_ref):
    planes = tail_ref.shape[0] - 8

    def sums_of(ref):
        return ref[ref.shape[0] - 8 :, :LANES]

    def border(after, before):
        step = after[:planes, :] - before[:planes, :]
        return fold(step * step)

    second = edge_ref[2] > 0
    below = border(head_ref, prev_ref) * jnp.where(edge_ref[0] > 0, 0.0, 1.0)
    above = border(next_ref, tail_ref) * jnp.where(edge_ref[1] > 0, 0.0, 1.0)
    other = jnp.where(second, sums_of(prev_ref), sums_of(next_ref))
    none = jnp.zeros((8, LANES), F32)
    put_copies(out_ref, sums_of(tail_ref) + other + sums_block([none, none, below + above]))


def border_sums(edge, head, tail, next_head, prev_tail, copies):
    vmem = pl.BlockSpec(memory_space=pltpu.VMEM)
    return pl.pallas_call(
        border_kernel,
        in_specs=[pl.BlockSpec(memory_space=pltpu.SMEM)] + [vmem] * 4,
        out_specs=vmem,
        out_shape=jax.ShapeDtypeStruct((copies, 8, LANES), F32),
        compiler_params=pltpu.CompilerParams(vmem_limit_bytes=2 * MIB),
        name="border_sums",
    )(edge, head, tail, next_head, prev_tail)


def second_kernel(
    gz, edge_ref, d0_ref, nd0_ref, nrow_ref, tail_ref, prev_ref, next_ref,
    coef_ref, tw_ref, table_ref, *refs,
):
    sums_refs, refs = refs[:1], refs[1:]
    d1_ref, eta_ref, out_ref, spec_ref, re_s, im_s, row_s = refs
    planes, rows, ka = d0_ref.shape
    kb = planes // gz
    eta_here = step_of(sums_refs)
    eta_ref[...] = jnp.broadcast_to(eta_here, (8, LANES))
    eta = jnp.max(eta_here)
    first = edge_ref[0] > 0
    last = edge_ref[1] > 0

    def shrink(difference):
        return jnp.clip(-eta * difference, -CLIP, CLIP)

    lane2 = lax.broadcasted_iota(jnp.int32, (kb, ka), 1)
    row2 = lax.broadcasted_iota(jnp.int32, (kb, ka), 0)
    for z in range(gz):
        part = slice(z * kb, (z + 1) * kb)
        here = next_ref[part, :]
        value = here - eta * nrow_ref[part, :]
        up = pltpu.roll(here, kb - 1, 0)
        up = jnp.where(
            row2 == kb - 1, jnp.where(lane2 == ka - 1, here, pltpu.roll(up, ka - 1, 1)), up
        )
        down = pltpu.roll(here, 1, 0)
        down = jnp.where(row2 == 0, jnp.where(lane2 == 0, here, pltpu.roll(down, 1, 1)), down)
        value = value + shrink(here - down) - shrink(up - here)
        value = value + shrink(here - tail_ref[part, :]) - shrink(next_ref[planes + z * kb : planes + (z + 1) * kb, :] - here)
        if z > 0:
            value = value + shrink(here - next_ref[(z - 1) * kb : z * kb, :])
        if z + 1 < gz:
            value = value - shrink(next_ref[(z + 1) * kb : (z + 2) * kb, :] - here)
        row_s[part, :] = value

    row = lax.broadcasted_iota(jnp.int32, (rows, ka), 0)
    square = jnp.zeros((8, LANES), F32)
    for p in range(planes):
        here = d0_ref[p]
        value = here - eta * nd0_ref[p]
        value = value + shrink(here - prev_plane(d0_ref, p, kb))
        value = value - shrink(next_plane(d0_ref, p, kb) - here)
        below = jnp.where(last, here[rows - 1 :, :], next_ref[p : p + 1, :])
        above = jnp.where(first, here[:1, :], prev_ref[p : p + 1, :])
        upper = shrink(jnp.where(row == rows - 1, below, pltpu.roll(here, rows - 1, 0)) - here)
        lower = jnp.where(row == 0, shrink(here[:1, :] - above), pltpu.roll(upper, 1, 0))
        value = value + lower - upper
        if p >= kb:
            value = value + shrink(here - d0_ref[p - kb])
        if p + kb < planes:
            value = value - shrink(d0_ref[p + kb] - here)
        d1_ref[p] = value
        square = square + fold(value * value)

    slope = jnp.zeros((8, LANES), F32)
    for p in range(planes):
        here = d1_ref[p]
        along_x = next_plane(d1_ref, p, kb) - here
        below = jnp.where(last, here[rows - 1 :, :], row_s[p : p + 1, :])
        along_y = jnp.where(row == rows - 1, below, pltpu.roll(here, rows - 1, 0)) - here
        terms = along_x * along_x + along_y * along_y
        if p + kb < planes:
            along_z = d1_ref[p + kb] - here
            terms = terms + along_z * along_z
        slope = slope + fold(terms)

    step = plane_chunk(planes, rows)

    def multiply(i, carry):
        part = pl.ds(i * step, step)
        re, im = forward_product(d1_ref[part].reshape(step * rows, ka), table_ref)
        re_s[part] = re.reshape(step, rows, ka)
        im_s[part] = im.reshape(step, rows, ka)
        return carry

    lax.fori_loop(0, planes // step, multiply, 0)

    def columns(j, total):
        part = pl.ds(pl.multiple_of(j * 8, 8), 8)
        for start in range(0, ka, LANES):
            lanes = slice(start, start + LANES)
            spectra = forward_columns(gz, kb, coef_ref, tw_ref, lanes, part, re_s, im_s)
            for z in range(gz):
                for k in range(kb):
                    for p in range(2):
                        value = spectra[z][k][p]
                        spec_ref[z, k, p, part, lanes] = value
                        total = total + value * value
        return total

    projected = lax.fori_loop(0, rows // 8, columns, jnp.zeros((8, LANES), F32))
    put_copies(out_ref, sums_block([square, projected, slope]))


def second_descent(edge, sums, d0, nd0, nrow, tail, prev_tail, next_head, coef, gz, nx):
    planes, rows, ka = d0.shape
    vmem = pl.BlockSpec(memory_space=pltpu.VMEM)
    return pl.pallas_call(
        functools.partial(second_kernel, gz),
        in_specs=[pl.BlockSpec(memory_space=pltpu.SMEM)] + [vmem] * 10,
        out_specs=[vmem] * 4,
        out_shape=[
            jax.ShapeDtypeStruct((planes, rows, ka), F32),
            jax.ShapeDtypeStruct((8, LANES), F32),
            jax.ShapeDtypeStruct(sums.shape, F32),
            jax.ShapeDtypeStruct((gz, planes // gz, 2, rows, ka), F32),
        ],
        scratch_shapes=[
            pltpu.VMEM((planes, rows, ka), F32),
            pltpu.VMEM((planes, rows, ka), F32),
            pltpu.VMEM((planes, ka), F32),
        ],
        compiler_params=pltpu.CompilerParams(vmem_limit_bytes=X_GRANT),
        name="second_descent",
    )(
        edge, d0, nd0, nrow, tail, prev_tail, next_head, coef,
        x_twiddle(nx, ka), x_forward_matrix(nx, ka), sums,
    )


def combine_kernel(gz, eta_ref, *refs):
    sums_refs, (first_ref, second_ref, out_ref, steps_ref) = refs[:gz], refs[gz:]
    eta0 = jnp.max(eta_ref[...])
    eta1 = jnp.max(step_of(sums_refs))
    steps_ref[0] = eta_ref[...]
    steps_ref[1] = jnp.full((8, LANES), eta1, F32)
    count = out_ref.shape[0]
    start = pl.program_id(0) * count
    for i in range(count):
        out_ref[i] = -(eta0 * first_ref[start + i] + eta1 * second_ref[start + i])


def combine_spectra(eta, sums, first, second):
    gz = len(sums)
    planes, *rest = first.shape
    count = 4 if planes % 4 == 0 else 1
    vmem = pl.BlockSpec(memory_space=pltpu.VMEM)
    return pl.pallas_call(
        functools.partial(combine_kernel, gz),
        grid=(planes // count,),
        in_specs=[vmem] * (3 + gz),
        out_specs=[
            pl.BlockSpec((count, *rest), lambda i: (i, 0, 0, 0)),
            pl.BlockSpec((2, 8, LANES), lambda i: (0, 0, 0)),
        ],
        out_shape=[
            jax.ShapeDtypeStruct(first.shape, F32),
            jax.ShapeDtypeStruct((2, 8, LANES), F32),
        ],
        compiler_params=pltpu.CompilerParams(vmem_limit_bytes=6 * MIB),
        name="combine_spectra",
    )(eta, *sums, first, second)


def to_core(piece, r):
    gz = lax.axis_size("gz")
    return lax.ppermute(piece, "gz", [(i, (i + r) % gz) for i in range(gz)]) if r else piece


def to_chips(parts):
    return lax.all_to_all(parts, "gy", 0, 0, tiled=True)


def to_devices(parts):
    gz, gy, *rest = parts.shape
    parts = lax.all_to_all(parts.reshape(gz * gy, *rest), ("gz", "gy"), 0, 0, tiled=True)
    return parts.reshape(gz, gy, *rest)


def everywhere(sums):
    sums = to_chips(sums)
    return [to_core(sums, r) for r in range(lax.axis_size("gz"))]


def shards(data, band_offset, interp_weight):
    gz = lax.axis_size("gz")
    gy = lax.axis_size("gy")
    devices = gz * gy
    data = data[0]
    blocks, ny, width = data.shape
    rows = ny // devices
    ka = blocks * HALF
    nx = ka * gy

    core = lax.axis_index("gz")
    flat = lax.axis_index("gy") * gz + core
    edge = jnp.stack([flat == 0, flat == devices - 1, core]).astype(jnp.int32)
    order = [(i % gz) * gy + i // gz for i in range(devices)]
    up = [(order[i + 1], order[i]) for i in range(devices - 1)]
    down = [(order[i], order[i + 1]) for i in range(devices - 1)]

    lower = band_offset < 0
    weight = interp_weight
    coef = jnp.stack(
        [
            jnp.where(lower, weight[1], weight[0]),
            jnp.where(lower, weight[0], 0.0),
            jnp.where(lower, 0.0, weight[1]),
        ]
    ).reshape(3, gy, 1, ka)
    coef = jnp.broadcast_to(coef, (3, gy, 8, ka))

    spec = to_devices(y_inverse(data, rows, gz, gy))
    d0, head, tail, first = middle(spec, coef, nx)
    next_head = lax.ppermute(head, ("gz", "gy"), up)
    prev_tail = lax.ppermute(tail, ("gz", "gy"), down)
    sums = to_chips(border_sums(edge, head, tail, next_head, prev_tail, gy))
    nd0, nrow = normal_product(first, next_head, coef, nx)
    d1, eta, sums, second = second_descent(
        edge, sums, d0, nd0, nrow, tail, prev_tail, next_head, coef, gz, nx
    )
    sums = everywhere(sums)
    flat_shape = (devices, 2, rows, ka)
    spec, etas = combine_spectra(eta, sums, first.reshape(flat_shape), second.reshape(flat_shape))
    residual = y_forward(to_devices(spec.reshape(gz, gy, 2, rows, ka)), data)

    volume = -(etas[0, 0, 0] * d0 + etas[1, 0, 0] * d1)
    volume = volume.reshape(gz, gy, rows, ka).transpose(0, 2, 3, 1).reshape(gz, rows, nx)
    parts = [
        to_core(lax.dynamic_index_in_dim(volume, lax.rem(core + r, gz), 0, False), r)
        for r in range(gz)
    ]
    volume = jnp.zeros((gz, rows, nx), F32)
    for r, part in enumerate(parts):
        volume = lax.dynamic_update_index_in_dim(volume, part, lax.rem(core + gz - r, gz), 0)
    return (volume.reshape(1, gz * rows, nx), residual[None])


NX = 4096
NY = 2048
XB = 64
YB = 64
ITERS = 2
XA = 64
YA = 32
PRECISE = lax.Precision.HIGHEST


def with_halo(block, sides, width):
    for axis, dim in sides:
        count = lax.axis_size(axis)
        forward = [(i, i + 1) for i in range(count - 1)]
        backward = [(target, source) for source, target in forward]
        low = lax.ppermute(
            lax.slice_in_dim(block, block.shape[dim] - width, None, axis=dim), axis, forward
        )
        high = lax.ppermute(lax.slice_in_dim(block, 0, width, axis=dim), axis, backward)
        block = jnp.concatenate([low, block, high], axis=dim)
    return block


def from_behind(block, axis, distance):
    devices = range(lax.axis_size(axis))
    route = [(i - distance, i) for i in devices if i - distance in devices]
    return lax.ppermute(block, axis, route)


def unit_table(length):
    counter = jnp.arange(length, dtype=jnp.int32)
    phase_int = counter[:, None] * counter[None, :] % length
    angles = 2.0 * jnp.pi / length * phase_int.astype(jnp.float32)
    factor = length ** (-0.5)
    return (jnp.cos(angles) * factor, jnp.sin(angles) * factor)


def twiddle_table(row_len, col_len, period):
    phase_int = (
        jnp.arange(row_len, dtype=jnp.int32)[:, None]
        * jnp.arange(col_len, dtype=jnp.int32)[None, :]
        % period
    )
    angles = 2.0 * jnp.pi / period * phase_int.astype(jnp.float32)
    return (jnp.cos(angles), jnp.sin(angles))


def split_parts(packed):
    half_width = packed.shape[-1] // 2
    return (packed[..., :half_width], packed[..., half_width:])


def join_parts(real_part, imag_part):
    return jnp.concatenate([real_part, imag_part], axis=-1)


def complex_contract(packed, cos_table, sin_table, subscripts, conj_sign):
    cos_out = jnp.einsum(subscripts, packed, cos_table, precision=PRECISE)
    sin_out = jnp.einsum(subscripts, packed, sin_table, precision=PRECISE)
    cos_re, cos_im = split_parts(cos_out)
    sin_re, sin_im = split_parts(sin_out)
    return join_parts(cos_re - conj_sign * sin_im, cos_im + conj_sign * sin_re)


def rotate(packed, cos_table, sin_table, conj_sign):
    real_part, imag_part = split_parts(packed)
    return join_parts(
        real_part * cos_table - conj_sign * imag_part * sin_table,
        imag_part * cos_table + conj_sign * real_part * sin_table,
    )


def forward_x(volume):
    slices, row_count = (volume.shape[0], volume.shape[1])
    cos_a, sin_a = unit_table(XA)
    cos_b, sin_b = unit_table(XB)
    first_table = jnp.concatenate([cos_a, -sin_a], axis=1)
    grid_view = volume.reshape(slices, row_count, XA, XB)
    mixing = jnp.einsum("zyab,am->zybm", grid_view, first_table, precision=PRECISE)
    tw_cos, tw_sin = twiddle_table(XB, XA, NX)
    mixing = rotate(mixing, tw_cos, tw_sin, -1.0)
    return complex_contract(mixing, cos_b, sin_b, "zybm,bl->zlym", -1.0)


def inverse_x(packed):
    slices, row_count = (packed.shape[0], packed.shape[2])
    cos_a, sin_a = unit_table(XA)
    cos_b, sin_b = unit_table(XB)
    mixing = complex_contract(packed, cos_b, sin_b, "zlym,lb->zybm", 1.0)
    tw_cos, tw_sin = twiddle_table(XB, XA, NX)
    mixing = rotate(mixing, tw_cos, tw_sin, 1.0)
    last_table = jnp.concatenate([cos_a, -sin_a], axis=0)
    grid_view = jnp.einsum("zybm,ma->zyab", mixing, last_table, precision=PRECISE)
    return grid_view.reshape(slices, row_count, NX)


def forward_y(packed):
    slices, blocks, width = (packed.shape[0], packed.shape[1], packed.shape[3])
    cos_a, sin_a = unit_table(YA)
    cos_b, sin_b = unit_table(YB)
    grid_view = packed.reshape(slices, blocks, YA, YB, width)
    mixing = complex_contract(grid_view, cos_a, sin_a, "zjcdm,ck->zjkdm", -1.0)
    tw_cos, tw_sin = twiddle_table(YA, YB, NY)
    mixing = rotate(mixing, tw_cos[:, :, None], tw_sin[:, :, None], -1.0)
    result = complex_contract(mixing, cos_b, sin_b, "zjkdm,dl->zjlkm", -1.0)
    return result.reshape(slices, blocks, NY, width)


def inverse_y(packed):
    slices, blocks, width = (packed.shape[0], packed.shape[1], packed.shape[3])
    cos_a, sin_a = unit_table(YA)
    cos_b, sin_b = unit_table(YB)
    grid_view = packed.reshape(slices, blocks, YB, YA, width)
    mixing = complex_contract(grid_view, cos_b, sin_b, "zjlkm,ld->zjkdm", 1.0)
    tw_cos, tw_sin = twiddle_table(YA, YB, NY)
    mixing = rotate(mixing, tw_cos[:, :, None], tw_sin[:, :, None], 1.0)
    result = complex_contract(mixing, cos_a, sin_a, "zjkdm,kc->zjcdm", 1.0)
    return result.reshape(slices, blocks, NY, width)


def tilt_coefficients(band_offset, interp_weight, first_block, blocks):
    offsets = lax.dynamic_slice_in_dim(band_offset.reshape(XB, XA), first_block, blocks, 0)
    weights = lax.dynamic_slice_in_dim(interp_weight.reshape(2, XB, XA), first_block, blocks, 1)
    lower_tap = (jnp.concatenate([offsets, offsets], axis=1) < 0)[:, None, :]
    first_weight = jnp.concatenate([weights[0], weights[0]], axis=1)[:, None, :]
    second_weight = jnp.concatenate([weights[1], weights[1]], axis=1)[:, None, :]
    return (lower_tap, first_weight, second_weight)


def tilt(field_in, coefficients, adjoint):
    lower_tap, first_weight, second_weight = coefficients
    padded = with_halo(field_in, (("gz", 0),), 1)
    below_rim = padded[:-2]
    middle = padded[1:-1]
    above_rim = padded[2:]
    if adjoint:
        return jnp.where(
            lower_tap,
            first_weight * above_rim + second_weight * middle,
            first_weight * middle + second_weight * below_rim,
        )
    return jnp.where(
        lower_tap,
        first_weight * below_rim + second_weight * middle,
        first_weight * middle + second_weight * above_rim,
    )


def to_pencil(slab_part):
    return lax.all_to_all(slab_part, "gy", split_axis=1, concat_axis=2, tiled=True)


def to_slab(pencil_part):
    return lax.all_to_all(pencil_part, "gy", split_axis=2, concat_axis=1, tiled=True)


def back_project(packed, pencil_coef):
    return inverse_x(to_slab(inverse_y(tilt(packed, pencil_coef, True))))


def edge_masks(slices, row_count):
    z_global = lax.axis_index("gz") * slices + jnp.arange(slices, dtype=jnp.int32)
    y_global = lax.axis_index("gy") * row_count + jnp.arange(row_count, dtype=jnp.int32)
    keep_z = (z_global < slices * lax.axis_size("gz") - 1).astype(jnp.float32)[:, None, None]
    keep_y = (y_global < row_count * lax.axis_size("gy") - 1).astype(jnp.float32)[None, :, None]
    return (keep_z, keep_y)


def forward_diff(field_in, keep_z, keep_y):
    slices, row_count = (field_in.shape[0], field_in.shape[1])
    next_z = from_behind(field_in, "gz", -1)
    next_y = from_behind(field_in[:, :1], "gy", -1)
    along_z = (jnp.concatenate([field_in[1:], next_z], axis=0) - field_in) * keep_z
    along_y = (jnp.concatenate([field_in[:, 1:], next_y], axis=1) - field_in) * keep_y
    zero_col = jnp.zeros((slices, row_count, 1), jnp.float32)
    along_x = jnp.concatenate([field_in[:, :, 1:] - field_in[:, :, :-1], zero_col], axis=2)
    return jnp.stack([along_z, along_y, along_x])


def transpose_diff(components, keep_z, keep_y):
    slices, row_count = (components.shape[1], components.shape[2])
    zero_col = jnp.zeros((slices, row_count, 1), jnp.float32)
    comp_z = components[0] * keep_z
    comp_y = components[1] * keep_y
    comp_x = jnp.concatenate([components[2][:, :, :-1], zero_col], axis=2)
    prev_z = from_behind(comp_z, "gz", 1)
    prev_y = from_behind(comp_y[:, -1:], "gy", 1)
    result = jnp.concatenate([prev_z, comp_z[:-1]], axis=0) - comp_z
    result = result + jnp.concatenate([prev_y, comp_y[:, :-1]], axis=1) - comp_y
    result = result + jnp.concatenate([zero_col, comp_x[:, :, :-1]], axis=2) - comp_x
    return result


def plain_shards(data, band_offset, interp_weight):
    slices = data.shape[0]
    blocks = data.shape[1]
    width = data.shape[3]
    row_count = NY // lax.axis_size("gy")
    slab_coef = tilt_coefficients(band_offset, interp_weight, 0, XB)
    pencil_coef = tilt_coefficients(
        band_offset, interp_weight, lax.axis_index("gy") * blocks, blocks
    )
    keep_z, keep_y = edge_masks(slices, row_count)
    measured = data.astype(jnp.float32)
    volume = jnp.zeros((slices, row_count, NX), jnp.float32)
    grad_volume = jnp.zeros((3, slices, row_count, NX), jnp.float32)
    split_var = grad_volume
    dual_var = grad_volume
    data_back = back_project(measured, pencil_coef)
    normal_part = jnp.zeros_like(volume)
    tilted = jnp.zeros((slices, XB, row_count, width), jnp.float32)
    for iteration in range(ITERS):
        data_grad = normal_part - data_back
        if iteration > 0:
            tv_gap = grad_volume - split_var + dual_var / PENALTY
            descent = data_grad + PENALTY * transpose_diff(tv_gap, keep_z, keep_y)
        else:
            descent = data_grad
        slope_field = forward_diff(descent, keep_z, keep_y)
        projected = tilt(forward_x(descent), slab_coef, False)
        line_totals = lax.psum(
            (
                jnp.sum(descent * descent),
                jnp.sum(projected * projected),
                jnp.sum(slope_field * slope_field),
            ),
            ("gz", "gy"),
        )
        step_length = line_totals[0] / (line_totals[1] + PENALTY * line_totals[2])
        volume = volume - step_length * descent
        grad_volume = grad_volume - step_length * slope_field
        tilted = tilted - step_length * projected
        if iteration + 1 < ITERS:
            normal_part = normal_part - step_length * inverse_x(tilt(projected, slab_coef, True))
        if iteration + 1 < ITERS:
            shifted = grad_volume + dual_var / PENALTY
            split_var = shifted - jnp.clip(shifted, -TV_WEIGHT / PENALTY, TV_WEIGHT / PENALTY)
            dual_var = PENALTY * (grad_volume - split_var)
    residual = forward_y(to_pencil(tilted)) - measured
    return (volume, residual)


def tiles_fit(mesh, ny, blocks):
    rows = ny // (mesh.shape["gz"] * mesh.shape["gy"])
    return mesh.shape["gz"] == 2 and rows % 16 == 0 and mesh.shape["gy"] % YR == 0 and blocks // mesh.shape["gy"] % 2 == 0


def solution(mesh):
    in_specs = (P("gz", "gy", None, None), P(), P())
    out_specs = (P("gz", "gy", None), P("gz", "gy", None, None))

    def run(data, band_offset, interp_weight):
        body = shards if tiles_fit(mesh, data.shape[2], data.shape[1]) else plain_shards
        call = jax.shard_map(
            body, mesh=mesh, in_specs=in_specs, out_specs=out_specs, check_vma=False
        )
        return call(data, band_offset, interp_weight)

    return run
```

```python
import functools

import jax
import jax.numpy as jnp
import numpy as np
from jax import lax
from jax.experimental import pallas as pl
from jax.experimental.pallas import tpu as pltpu
from jax.sharding import PartitionSpec as P

PENALTY = 0.5
TV_WEIGHT = 0.25
CLIP = TV_WEIGHT / PENALTY
HALF = 64
YR = 8
LANES = 128
F32 = jnp.float32
BF16 = jnp.bfloat16
MIB = 1024 * 1024
Y_GRANT = 56 * MIB
X_GRANT = 20 * MIB


def dft_parts(length, scale):
    index = np.arange(length)
    angles = 2.0 * np.pi / length * (index[:, None] * index[None, :] % length)
    return np.cos(angles) * scale, np.sin(angles) * scale


def host_parts(table):
    table = table.astype(np.float32)
    high = table.astype(BF16)
    low = (table - high.astype(np.float32)).astype(BF16)
    return high, low


def y_matrix(ny, forward, sign):
    n = ny // YR
    cos, sin = dft_parts(n, sign * ny**-0.5)
    if forward:
        table = np.block([[cos, sin], [-sin, cos]])
    else:
        table = np.block([[cos, -sin], [sin, cos]])
    high, low = host_parts(table)
    return jnp.asarray(np.concatenate([high, high, low] if forward else [high, low], axis=1))


def y_twiddle(ny):
    n = ny // YR
    angles = 2.0 * np.pi / ny * (np.arange(1, YR)[:, None] * np.arange(n)[None, :])
    table = np.stack([np.cos(angles), np.sin(angles)]).astype(np.float32)
    return jnp.asarray(np.ascontiguousarray(np.broadcast_to(table[..., None], (2, YR - 1, n, LANES))))


def x_inverse_matrix(nx, ka):
    cos, sin = dft_parts(ka, nx**-0.5)
    high, low = host_parts(np.concatenate([cos, -sin], axis=0))
    return jnp.asarray(np.concatenate([high, high, low], axis=0))


def x_forward_matrix(nx, ka):
    cos, sin = dft_parts(ka, nx**-0.5)
    high, low = host_parts(np.concatenate([cos, -sin], axis=1))
    return jnp.asarray(np.concatenate([high, high, low], axis=0))


def x_twiddle(nx, ka):
    kb = nx // ka
    angles = 2.0 * np.pi / nx * (np.arange(kb)[:, None] * np.arange(ka)[None, :])
    table = np.stack([np.cos(angles), np.sin(angles)]).astype(np.float32)
    return jnp.asarray(np.ascontiguousarray(np.broadcast_to(table[:, :, None], (2, kb, 8, ka))))


def short_fft(planes, sign):
    n = len(planes)
    if n == 1:
        return planes
    even = short_fft(planes[0::2], sign)
    odd = short_fft(planes[1::2], sign)
    half = n // 2
    out = [None] * n
    for k in range(half):
        er, ei = even[k]
        tr, ti = odd[k]
        if 4 * k == n:
            if sign > 0:
                out[k] = (er - ti, ei + tr)
                out[k + half] = (er + ti, ei - tr)
            else:
                out[k] = (er + ti, ei - tr)
                out[k + half] = (er - ti, ei + tr)
            continue
        if k > 0:
            c = float(np.cos(2.0 * np.pi * k / n))
            s = float(sign * np.sin(2.0 * np.pi * k / n))
            if 8 * k == n:
                tr, ti = (tr - ti, ti + tr) if sign > 0 else (tr + ti, ti - tr)
                tr, ti = tr * c, ti * c
            elif 8 * k == 3 * n:
                m = float(np.sin(2.0 * np.pi * k / n))
                tr, ti = (-(tr + ti), tr - ti) if sign > 0 else (ti - tr, -(tr + ti))
                tr, ti = tr * m, ti * m
            else:
                tr, ti = tr * c - ti * s, ti * c + tr * s
        out[k] = (er + tr, ei + ti)
        out[k + half] = (er - tr, ei - ti)
    return out


def split2(x):
    high = x.astype(BF16)
    return high, (x - high.astype(F32)).astype(BF16)


def dot(a, b):
    return jnp.dot(a, b, preferred_element_type=F32)


def fold(x):
    rows, lanes = x.shape
    x = jnp.sum(x.reshape(rows // 8, 8, lanes), axis=0)
    total = x[:, :LANES]
    for i in range(1, lanes // LANES):
        total = total + x[:, i * LANES : (i + 1) * LANES]
    return total


def full_sum(x):
    return jnp.sum(jnp.sum(x, axis=0, keepdims=True), axis=1, keepdims=True)


def step_of(sums_refs):
    total = sum(jnp.sum(sums_ref[...], axis=0) for sums_ref in sums_refs)
    parts = jnp.sum(total, axis=1, keepdims=True)
    return parts[0:1] / (parts[1:2] + PENALTY * parts[2:3])


def sums_block(values):
    rows = [jnp.sum(v, axis=0, keepdims=True) for v in values]
    index = lax.broadcasted_iota(jnp.int32, (8, LANES), 0)
    block = jnp.zeros((8, LANES), F32)
    for i, row in enumerate(rows):
        block = jnp.where(index == i, jnp.broadcast_to(row, (8, LANES)), block)
    return block


def put_copies(out_ref, block):
    for i in range(out_ref.shape[0]):
        out_ref[i] = block


def mix_adjoint(coef, planes):
    own, below, above = coef
    out = []
    for z in range(len(planes)):
        value = own * planes[z]
        if z + 1 < len(planes):
            value = value + below * planes[z + 1]
        if z > 0:
            value = value + above * planes[z - 1]
        out.append(value)
    return out


def mix(coef, planes):
    own, below, above = coef
    out = []
    for z in range(len(planes)):
        value = own * planes[z]
        if z > 0:
            value = value + below * planes[z - 1]
        if z + 1 < len(planes):
            value = value + above * planes[z + 1]
        out.append(value)
    return out


def y_inverse_kernel(
    data_hbm, table_hbm, tw_hbm, out_hbm,
    data_ref, table_ref, tw_ref, out_ref, re_s, im_s, mix_s, sems, out_sems,
):
    blocks, ny, _ = data_ref.shape
    n = ny // YR
    gz, _, _, rows, _ = out_ref.shape
    lane = lax.broadcasted_iota(jnp.int32, (n, LANES), 1)
    pairs = blocks // 2

    def fetch(chunk):
        part = pl.ds(2 * chunk, 2)
        return pltpu.make_async_copy(data_hbm.at[part], data_ref.at[part], sems.at[2 + chunk])

    def give(chunk, core):
        at = (core, slice(None), slice(None), slice(None), pl.ds(chunk * LANES, LANES))
        return pltpu.make_async_copy(out_ref.at[at], out_hbm.at[at], out_sems.at[chunk * gz + core])

    fetch_table = pltpu.make_async_copy(table_hbm, table_ref, sems.at[0])
    fetch_tw = pltpu.make_async_copy(tw_hbm, tw_ref, sems.at[1])
    fetch(0).start()
    fetch_table.start()
    fetch_tw.start()
    for chunk in range(1, pairs):
        fetch(chunk).start()

    for chunk in range(pairs):
        lanes = slice(chunk * LANES, (chunk + 1) * LANES)
        fetch(chunk).wait()

        def unpack(i, carry):
            part = pl.ds(pl.multiple_of(i * n, n), n)
            first = data_ref[2 * chunk, part, :].astype(F32)
            second = data_ref[2 * chunk + 1, part, :].astype(F32)
            re_s[part, :] = jnp.where(lane < HALF, first, pltpu.roll(second, HALF, 1))
            im_s[part, :] = jnp.where(lane < HALF, pltpu.roll(first, HALF, 1), second)
            return carry

        lax.fori_loop(0, YR, unpack, 0)
        if chunk == 0:
            fetch_table.wait()

        for k in range(0, YR, 2):
            pieces = [
                jnp.concatenate([s[pl.ds(k + d, n, stride=YR), :] for d in range(2)], axis=1)
                for s in (re_s, im_s)
            ]
            piece = jnp.concatenate(pieces, axis=0).astype(BF16)
            both = dot(table_ref[...], jnp.concatenate([piece, piece], axis=0))
            for d in range(2):
                mix_s[k + d] = both[:, d * LANES : (d + 1) * LANES]

        if chunk == 0:
            fetch_tw.wait()

        tiles = rows // 8
        for core in range(gz):

            def combine(i, carry):
                y2 = ((i // tiles) * gz + core) * rows + lax.rem(i, tiles) * 8
                part = pl.ds(pl.multiple_of(y2, 8), 8)
                planes = []
                for k in range(YR):
                    re = mix_s[k, part, :]
                    im = mix_s[k, pl.ds(pl.multiple_of(n + y2, 8), 8), :]
                    if k > 0:
                        c = tw_ref[0, k - 1, part, :]
                        s = tw_ref[1, k - 1, part, :]
                        re, im = re * c - im * s, im * c + re * s
                    planes.append((re, im))
                at = pl.ds(pl.multiple_of(lax.rem(i, tiles) * 8, 8), 8)
                for k, (re, im) in enumerate(short_fft(planes, 1)):
                    to = k * (n // (gz * rows)) + i // tiles
                    out_ref[core, to, 0, at, lanes] = re
                    out_ref[core, to, 1, at, lanes] = im
                return carry

            lax.fori_loop(0, n // gz // 8, combine, 0, unroll=2)
            give(chunk, core).start()

    for chunk in range(pairs):
        for core in range(gz):
            give(chunk, core).wait()


def y_inverse(data, rows, gz, gy):
    blocks, ny, width = data.shape
    n = ny // YR
    ka = blocks * HALF
    hbm = pl.BlockSpec(memory_space=pltpu.HBM)
    return pl.pallas_call(
        y_inverse_kernel,
        in_specs=[hbm] * 3,
        out_specs=hbm,
        out_shape=jax.ShapeDtypeStruct((gz, gy, 2, rows, ka), F32),
        scratch_shapes=[
            pltpu.VMEM((blocks, ny, width), BF16),
            pltpu.VMEM((2 * n, 4 * n), BF16),
            pltpu.VMEM((2, YR - 1, n, LANES), F32),
            pltpu.VMEM((gz, gy, 2, rows, ka), F32),
            pltpu.VMEM((ny, LANES), F32),
            pltpu.VMEM((ny, LANES), F32),
            pltpu.VMEM((YR, 2 * n, LANES), F32),
            pltpu.SemaphoreType.DMA((2 + blocks // 2,)),
            pltpu.SemaphoreType.DMA((blocks // 2 * gz,)),
        ],
        compiler_params=pltpu.CompilerParams(vmem_limit_bytes=Y_GRANT),
        name="y_inverse",
    )(data, y_matrix(ny, False, -1.0), y_twiddle(ny))


def y_forward_kernel(
    spec_hbm, data_hbm, table_hbm, tw_hbm, out_hbm,
    spec_ref, data_ref, table_ref, tw_ref, out_ref, mix_s, sems, spec_sems, out_sems,
):
    blocks, ny, _ = data_ref.shape
    n = ny // YR
    _, gz, gy, _, rows, _ = spec_ref.shape
    pairs = blocks // 2
    half = n // 2

    def fetch(chunk):
        lanes = pl.ds(chunk * LANES, LANES)
        return pltpu.make_async_copy(
            spec_hbm.at[:, :, :, :, lanes], spec_ref.at[chunk], spec_sems.at[chunk]
        )

    def give(chunk, part):
        at = (pl.ds(2 * chunk, 2), slice(None), pl.ds(part * half, half))
        return pltpu.make_async_copy(out_ref.at[at], out_hbm.at[at], out_sems.at[2 * chunk + part])

    fetch_table = pltpu.make_async_copy(table_hbm, table_ref, sems.at[0])
    fetch_tw = pltpu.make_async_copy(tw_hbm, tw_ref, sems.at[1])
    fetch_data = pltpu.make_async_copy(data_hbm, data_ref, sems.at[2])
    fetch(0).start()
    fetch_table.start()
    fetch_tw.start()
    fetch_data.start()
    for chunk in range(1, pairs):
        fetch(chunk).start()

    def rows_of(chunk, p, k):
        part = pl.ds(k, rows // YR, stride=YR)
        return jnp.concatenate(
            [spec_ref[chunk, core, i, p, part, :] for i in range(gy) for core in range(gz)], axis=0
        )

    lane = lax.broadcasted_iota(jnp.int32, (16, LANES), 1)
    for chunk in range(pairs):
        lanes = slice(chunk * LANES, (chunk + 1) * LANES)
        fetch(chunk).wait()

        if chunk == 0:
            fetch_table.wait()

        for k in range(0, YR, 2):
            pieces = [
                jnp.concatenate([rows_of(chunk, p, k + d) for d in range(2)], axis=1)
                for p in range(2)
            ]
            high, low = split2(jnp.concatenate(pieces, axis=0))
            both = dot(table_ref[...], jnp.concatenate([high, low, high], axis=0))
            for d in range(2):
                mix_s[k + d] = both[:, d * LANES : (d + 1) * LANES]
        if chunk == 0:
            fetch_tw.wait()
            fetch_data.wait()

        def combine(i, carry):
            start = pl.multiple_of(i * 16, 16)
            part = pl.ds(start, 16)
            planes = []
            for k in range(YR):
                re = mix_s[k, part, :]
                im = mix_s[k, pl.ds(pl.multiple_of(n + i * 16, 16), 16), :]
                if k > 0:
                    c = tw_ref[0, k - 1, part, :]
                    s = tw_ref[1, k - 1, part, :]
                    re, im = re * c + im * s, im * c - re * s
                planes.append((re, im))
            for k, (re, im) in enumerate(short_fft(planes, -1)):
                at = pl.ds(pl.multiple_of(k * n + start, 16), 16)
                first = jnp.where(lane < HALF, re, pltpu.roll(im, HALF, 1))
                second = jnp.where(lane < HALF, pltpu.roll(re, HALF, 1), im)
                out_ref[2 * chunk, k, part, :] = first - data_ref[2 * chunk, at, :].astype(F32)
                out_ref[2 * chunk + 1, k, part, :] = (
                    second - data_ref[2 * chunk + 1, at, :].astype(F32)
                )
            return carry

        for part in range(2):
            lax.fori_loop(part * half // 16, (part + 1) * half // 16, combine, 0)
            give(chunk, part).start()

    for chunk in range(pairs):
        for part in range(2):
            give(chunk, part).wait()


def y_forward(spec, data):
    blocks, ny, width = data.shape
    n = ny // YR
    hbm = pl.BlockSpec(memory_space=pltpu.HBM)
    out = pl.pallas_call(
        y_forward_kernel,
        in_specs=[hbm] * 4,
        out_specs=hbm,
        out_shape=jax.ShapeDtypeStruct((blocks, YR, n, width), F32),
        scratch_shapes=[
            pltpu.VMEM((blocks // 2, *spec.shape[:-1], LANES), F32),
            pltpu.VMEM((blocks, ny, width), BF16),
            pltpu.VMEM((2 * n, 6 * n), BF16),
            pltpu.VMEM((2, YR - 1, n, LANES), F32),
            pltpu.VMEM((blocks, YR, n, width), F32),
            pltpu.VMEM((YR, 2 * n, LANES), F32),
            pltpu.SemaphoreType.DMA((3,)),
            pltpu.SemaphoreType.DMA((blocks // 2,)),
            pltpu.SemaphoreType.DMA((blocks,)),
        ],
        compiler_params=pltpu.CompilerParams(vmem_limit_bytes=Y_GRANT),
        name="y_forward",
    )(spec, data, y_matrix(ny, True, 1.0), y_twiddle(ny))
    return out.reshape(blocks, ny, width)


def plane_chunk(planes, rows):
    chunk = max(1, 1024 // rows)
    while planes % chunk:
        chunk -= 1
    return chunk


def turn_rows(kb, planes_of, tw_ref, lanes, sign):
    out = []
    for b in range(kb):
        re, im = planes_of(b)
        if b > 0:
            c = tw_ref[0, b, :, lanes]
            s = tw_ref[1, b, :, lanes]
            if sign > 0:
                re, im = re * c - im * s, im * c + re * s
            else:
                re, im = re * c + im * s, im * c - re * s
        out.append((re, im))
    return out


def inverse_columns(gz, kb, spectra, coef_ref, tw_ref, lanes, part, re_s, im_s):
    mixed = [[None] * kb for _ in range(gz)]
    for k in range(kb):
        coef = [coef_ref[j, k, :, lanes] for j in range(3)]
        re = mix_adjoint(coef, [spectra[z][k][0] for z in range(gz)])
        im = mix_adjoint(coef, [spectra[z][k][1] for z in range(gz)])
        for z in range(gz):
            mixed[z][k] = (re[z], im[z])
    for z in range(gz):
        short = short_fft(mixed[z], 1)
        for b, (re, im) in enumerate(turn_rows(kb, lambda b: short[b], tw_ref, lanes, 1)):
            re_s[z * kb + b, part, lanes] = re
            im_s[z * kb + b, part, lanes] = im


def forward_columns(gz, kb, coef_ref, tw_ref, lanes, part, re_s, im_s):
    spectra = []
    for z in range(gz):
        rows_of = lambda b: (re_s[z * kb + b, part, lanes], im_s[z * kb + b, part, lanes])
        spectra.append(short_fft(turn_rows(kb, rows_of, tw_ref, lanes, -1), -1))
    out = [[None] * kb for _ in range(gz)]
    for k in range(kb):
        coef = [coef_ref[j, k, :, lanes] for j in range(3)]
        re = mix(coef, [spectra[z][k][0] for z in range(gz)])
        im = mix(coef, [spectra[z][k][1] for z in range(gz)])
        for z in range(gz):
            out[z][k] = (re[z], im[z])
    return out


def inverse_product(re, im, table_ref):
    high, low = split2(jnp.concatenate([re, im], axis=1))
    return dot(jnp.concatenate([high, low, high], axis=1), table_ref[...])


def forward_product(field, table_ref):
    ka = field.shape[1]
    high, low = split2(field)
    value = dot(jnp.concatenate([high, low, high], axis=1), table_ref[...])
    return value[:, :ka], value[:, ka:]


def next_plane(field_ref, p, kb):
    rows, ka = field_ref.shape[1:]
    if (p + 1) % kb:
        return field_ref[p + 1]
    lane = lax.broadcasted_iota(jnp.int32, (rows, ka), 1)
    return jnp.where(lane == ka - 1, field_ref[p], pltpu.roll(field_ref[p + 1 - kb], ka - 1, 1))


def prev_plane(field_ref, p, kb):
    rows, ka = field_ref.shape[1:]
    if p % kb:
        return field_ref[p - 1]
    lane = lax.broadcasted_iota(jnp.int32, (rows, ka), 1)
    return jnp.where(lane == 0, field_ref[p], pltpu.roll(field_ref[p + kb - 1], 1, 1))


def first_kernel(
    gz, edge_ref, field_ref, coef_ref, tw_ref, table_ref, sums_ref, spec_ref, *refs
):
    piece_refs, (re_s, im_s) = refs[:-2], refs[-2:]
    planes, rows, ka = field_ref.shape
    kb = planes // gz
    projected = forward_into(gz, field_ref, coef_ref, tw_ref, table_ref, spec_ref, re_s, im_s)
    cut(gz, edge_ref, spec_ref, piece_refs)
    row = lax.broadcasted_iota(jnp.int32, (rows, ka), 0)
    square = jnp.zeros((8, LANES), F32)
    slope = jnp.zeros((8, LANES), F32)
    for p in range(planes):
        here = field_ref[p]
        square = square + fold(here * here)
        along_x = next_plane(field_ref, p, kb) - here
        along_y = jnp.where(row == rows - 1, 0.0, pltpu.roll(here, rows - 1, 0) - here)
        terms = along_x * along_x + along_y * along_y
        if p + kb < planes:
            along_z = field_ref[p + kb] - here
            terms = terms + along_z * along_z
        slope = slope + fold(terms)
    sums_ref[0] = square
    sums_ref[1] = projected
    sums_ref[2] = slope


def middle_kernel(
    spec_hbm, coef_ref, tw_ref, inverse_ref, forward_ref,
    d0_ref, nd0_ref, head_ref, tail_ref, spec_ref, re_s, im_s, sems,
):
    gz, kb, _, rows, ka = spec_ref.shape
    planes = gz * kb
    lane_parts = [slice(start, start + LANES) for start in range(0, ka, LANES)]
    cuts = sems.shape[0]
    cut = rows // cuts

    def fetch(i):
        part = pl.ds(i * cut, cut)
        return pltpu.make_async_copy(
            spec_hbm.at[:, :, :, part], spec_ref.at[:, :, :, part], sems.at[i]
        )

    def columns_back(j, carry):
        part = pl.ds(pl.multiple_of(j * 8, 8), 8)
        for lanes in lane_parts:
            spectra = [
                [(spec_ref[z, k, 0, part, lanes], spec_ref[z, k, 1, part, lanes]) for k in range(kb)]
                for z in range(gz)
            ]
            inverse_columns(gz, kb, spectra, coef_ref, tw_ref, lanes, part, re_s, im_s)
        return carry

    for i in range(cuts):
        fetch(i).start()
    for i in range(cuts):
        fetch(i).wait()
        lax.fori_loop(i * cut // 8, (i + 1) * cut // 8, columns_back, 0)

    step = plane_chunk(planes, rows)
    shape2, shape3 = (step * rows, ka), (step, rows, ka)

    def there_and_back(i, carry):
        part = pl.ds(i * step, step)
        field = inverse_product(re_s[part].reshape(shape2), im_s[part].reshape(shape2), inverse_ref)
        d0_ref[part] = field.reshape(shape3)
        re, im = forward_product(field, forward_ref)
        re_s[part] = re.reshape(shape3)
        im_s[part] = im.reshape(shape3)
        return carry

    lax.fori_loop(0, planes // step, there_and_back, 0)

    def second_columns(j, total):
        part = pl.ds(pl.multiple_of(j * 8, 8), 8)
        for lanes in lane_parts:
            spectra = forward_columns(gz, kb, coef_ref, tw_ref, lanes, part, re_s, im_s)
            for z in range(gz):
                for k in range(kb):
                    for p in range(2):
                        value = spectra[z][k][p]
                        spec_ref[z, k, p, part, lanes] = value
                        total = total + value * value
        return total

    projected = lax.fori_loop(0, rows // 8, second_columns, jnp.zeros((8, LANES), F32))
    lax.fori_loop(0, rows // 8, columns_back, 0)
    def back(i, carry):
        part = pl.ds(i * step, step)
        field = inverse_product(re_s[part].reshape(shape2), im_s[part].reshape(shape2), inverse_ref)
        nd0_ref[part] = field.reshape(shape3)
        return carry

    lax.fori_loop(0, planes // step, back, 0)

    for p in range(planes):
        head_ref[p : p + 1, :] = d0_ref[p, :1, :]
        head_ref[planes + p : planes + p + 1, :] = d0_ref[p, 1:2, :]
        head_ref[2 * planes + p : 2 * planes + p + 1, :] = nd0_ref[p, :1, :]
        tail_ref[p : p + 1, :] = d0_ref[p, rows - 1 : rows, :]

    row = lax.broadcasted_iota(jnp.int32, (rows, ka), 0)
    square = jnp.zeros((8, LANES), F32)
    slope = jnp.zeros((8, LANES), F32)
    for p in range(planes):
        here = d0_ref[p]
        square = square + fold(here * here)
        along_x = next_plane(d0_ref, p, kb) - here
        along_y = jnp.where(row == rows - 1, 0.0, pltpu.roll(here, rows - 1, 0) - here)
        terms = along_x * along_x + along_y * along_y
        if p + kb < planes:
            along_z = d0_ref[p + kb] - here
            terms = terms + along_z * along_z
        slope = slope + fold(terms)
    block = sums_block([square, projected, slope])
    for ref in (head_ref, tail_ref):
        at = ref.shape[0] - 8
        ref[at:, :] = jnp.zeros((8, ka), F32)
        ref[at:, :LANES] = block


def middle(spec, coef, nx):
    gz, kb, _, rows, ka = spec.shape
    planes = gz * kb
    vmem = pl.BlockSpec(memory_space=pltpu.VMEM)
    field = jax.ShapeDtypeStruct((planes, rows, ka), F32)
    return pl.pallas_call(
        middle_kernel,
        in_specs=[pl.BlockSpec(memory_space=pltpu.HBM)] + [vmem] * 4,
        out_specs=[vmem] * 5,
        out_shape=[
            field,
            field,
            jax.ShapeDtypeStruct((3 * planes + 8, ka), F32),
            jax.ShapeDtypeStruct((planes + 8, ka), F32),
            jax.ShapeDtypeStruct(spec.shape, F32),
        ],
        scratch_shapes=[
            pltpu.VMEM((planes, rows, ka), F32),
            pltpu.VMEM((planes, rows, ka), F32),
            pltpu.SemaphoreType.DMA((4 if rows % 32 == 0 else 1,)),
        ],
        compiler_params=pltpu.CompilerParams(vmem_limit_bytes=X_GRANT),
        name="middle",
    )(
        spec, coef, x_twiddle(nx, ka), x_inverse_matrix(nx, ka),
        x_forward_matrix(nx, ka),
    )


def border_kernel(edge_ref, head_ref, tail_ref, next_ref, prev_ref, out_ref):
    planes = tail_ref.shape[0] - 8

    def sums_of(ref):
        return ref[ref.shape[0] - 8 :, :LANES]

    def border(after, before):
        step = after[:planes, :] - before[:planes, :]
        return fold(step * step)

    second = edge_ref[2] > 0
    below = border(head_ref, prev_ref) * jnp.where(edge_ref[0] > 0, 0.0, 1.0)
    above = border(next_ref, tail_ref) * jnp.where(edge_ref[1] > 0, 0.0, 1.0)
    other = jnp.where(second, sums_of(prev_ref), sums_of(next_ref))
    none = jnp.zeros((8, LANES), F32)
    put_copies(out_ref, sums_of(tail_ref) + other + sums_block([none, none, below + above]))


def border_sums(edge, head, tail, next_head, prev_tail, copies):
    vmem = pl.BlockSpec(memory_space=pltpu.VMEM)
    return pl.pallas_call(
        border_kernel,
        in_specs=[pl.BlockSpec(memory_space=pltpu.SMEM)] + [vmem] * 4,
        out_specs=vmem,
        out_shape=jax.ShapeDtypeStruct((copies, 8, LANES), F32),
        compiler_params=pltpu.CompilerParams(vmem_limit_bytes=2 * MIB),
        name="border_sums",
    )(edge, head, tail, next_head, prev_tail)


def second_kernel(
    gz, edge_ref, d0_ref, nd0_ref, tail_ref, prev_ref, next_ref,
    coef_ref, tw_ref, table_ref, *refs,
):
    sums_refs, refs = refs[:1], refs[1:]
    d1_ref, eta_ref, out_ref, spec_ref, re_s, im_s, row_s = refs
    planes, rows, ka = d0_ref.shape
    kb = planes // gz
    eta_here = step_of(sums_refs)
    eta_ref[...] = jnp.broadcast_to(eta_here, (8, LANES))
    eta = jnp.max(eta_here)
    first = edge_ref[0] > 0
    last = edge_ref[1] > 0

    def shrink(difference):
        return jnp.clip(-eta * difference, -CLIP, CLIP)

    lane2 = lax.broadcasted_iota(jnp.int32, (kb, ka), 1)
    row2 = lax.broadcasted_iota(jnp.int32, (kb, ka), 0)
    for z in range(gz):
        part = slice(z * kb, (z + 1) * kb)
        here = next_ref[part, :]
        value = here - eta * next_ref[2 * planes + z * kb : 2 * planes + (z + 1) * kb, :]
        up = pltpu.roll(here, kb - 1, 0)
        up = jnp.where(
            row2 == kb - 1, jnp.where(lane2 == ka - 1, here, pltpu.roll(up, ka - 1, 1)), up
        )
        down = pltpu.roll(here, 1, 0)
        down = jnp.where(row2 == 0, jnp.where(lane2 == 0, here, pltpu.roll(down, 1, 1)), down)
        value = value + shrink(here - down) - shrink(up - here)
        value = value + shrink(here - tail_ref[part, :]) - shrink(next_ref[planes + z * kb : planes + (z + 1) * kb, :] - here)
        if z > 0:
            value = value + shrink(here - next_ref[(z - 1) * kb : z * kb, :])
        if z + 1 < gz:
            value = value - shrink(next_ref[(z + 1) * kb : (z + 2) * kb, :] - here)
        row_s[part, :] = value

    row = lax.broadcasted_iota(jnp.int32, (rows, ka), 0)
    square = jnp.zeros((8, LANES), F32)
    for p in range(planes):
        here = d0_ref[p]
        value = here - eta * nd0_ref[p]
        value = value + shrink(here - prev_plane(d0_ref, p, kb))
        value = value - shrink(next_plane(d0_ref, p, kb) - here)
        below = jnp.where(last, here[rows - 1 :, :], next_ref[p : p + 1, :])
        above = jnp.where(first, here[:1, :], prev_ref[p : p + 1, :])
        upper = shrink(jnp.where(row == rows - 1, below, pltpu.roll(here, rows - 1, 0)) - here)
        lower = jnp.where(row == 0, shrink(here[:1, :] - above), pltpu.roll(upper, 1, 0))
        value = value + lower - upper
        if p >= kb:
            value = value + shrink(here - d0_ref[p - kb])
        if p + kb < planes:
            value = value - shrink(d0_ref[p + kb] - here)
        d1_ref[p] = value
        square = square + fold(value * value)

    slope = jnp.zeros((8, LANES), F32)
    for p in range(planes):
        here = d1_ref[p]
        along_x = next_plane(d1_ref, p, kb) - here
        below = jnp.where(last, here[rows - 1 :, :], row_s[p : p + 1, :])
        along_y = jnp.where(row == rows - 1, below, pltpu.roll(here, rows - 1, 0)) - here
        terms = along_x * along_x + along_y * along_y
        if p + kb < planes:
            along_z = d1_ref[p + kb] - here
            terms = terms + along_z * along_z
        slope = slope + fold(terms)

    step = plane_chunk(planes, rows)

    def multiply(i, carry):
        part = pl.ds(i * step, step)
        re, im = forward_product(d1_ref[part].reshape(step * rows, ka), table_ref)
        re_s[part] = re.reshape(step, rows, ka)
        im_s[part] = im.reshape(step, rows, ka)
        return carry

    lax.fori_loop(0, planes // step, multiply, 0)

    def columns(j, total):
        part = pl.ds(pl.multiple_of(j * 8, 8), 8)
        for start in range(0, ka, LANES):
            lanes = slice(start, start + LANES)
            spectra = forward_columns(gz, kb, coef_ref, tw_ref, lanes, part, re_s, im_s)
            for z in range(gz):
                for k in range(kb):
                    for p in range(2):
                        value = spectra[z][k][p]
                        spec_ref[z, k, p, part, lanes] = value
                        total = total + value * value
        return total

    projected = lax.fori_loop(0, rows // 8, columns, jnp.zeros((8, LANES), F32))
    put_copies(out_ref, sums_block([square, projected, slope]))


def second_descent(edge, sums, d0, nd0, tail, prev_tail, next_head, coef, gz, nx):
    planes, rows, ka = d0.shape
    vmem = pl.BlockSpec(memory_space=pltpu.VMEM)
    return pl.pallas_call(
        functools.partial(second_kernel, gz),
        in_specs=[pl.BlockSpec(memory_space=pltpu.SMEM)] + [vmem] * 9,
        out_specs=[vmem] * 4,
        out_shape=[
            jax.ShapeDtypeStruct((planes, rows, ka), F32),
            jax.ShapeDtypeStruct((8, LANES), F32),
            jax.ShapeDtypeStruct(sums.shape, F32),
            jax.ShapeDtypeStruct((gz, planes // gz, 2, rows, ka), F32),
        ],
        scratch_shapes=[
            pltpu.VMEM((planes, rows, ka), F32),
            pltpu.VMEM((planes, rows, ka), F32),
            pltpu.VMEM((planes, ka), F32),
        ],
        compiler_params=pltpu.CompilerParams(vmem_limit_bytes=X_GRANT),
        name="second_descent",
    )(
        edge, d0, nd0, tail, prev_tail, next_head, coef,
        x_twiddle(nx, ka), x_forward_matrix(nx, ka), sums,
    )


def combine_kernel(gz, eta_ref, *refs):
    sums_refs, (first_ref, second_ref, out_ref, steps_ref) = refs[:gz], refs[gz:]
    eta0 = jnp.max(eta_ref[...])
    eta1 = jnp.max(step_of(sums_refs))
    steps_ref[0] = eta_ref[...]
    steps_ref[1] = jnp.full((8, LANES), eta1, F32)
    count = out_ref.shape[0]
    start = pl.program_id(0) * count
    for i in range(count):
        out_ref[i] = -(eta0 * first_ref[start + i] + eta1 * second_ref[start + i])


def combine_spectra(eta, sums, first, second):
    gz = len(sums)
    planes, *rest = first.shape
    count = 4 if planes % 4 == 0 else 1
    vmem = pl.BlockSpec(memory_space=pltpu.VMEM)
    return pl.pallas_call(
        functools.partial(combine_kernel, gz),
        grid=(planes // count,),
        in_specs=[vmem] * (3 + gz),
        out_specs=[
            pl.BlockSpec((count, *rest), lambda i: (i, 0, 0, 0)),
            pl.BlockSpec((2, 8, LANES), lambda i: (0, 0, 0)),
        ],
        out_shape=[
            jax.ShapeDtypeStruct(first.shape, F32),
            jax.ShapeDtypeStruct((2, 8, LANES), F32),
        ],
        compiler_params=pltpu.CompilerParams(vmem_limit_bytes=6 * MIB),
        name="combine_spectra",
    )(eta, *sums, first, second)


def to_core(piece, r):
    gz = lax.axis_size("gz")
    return lax.ppermute(piece, "gz", [(i, (i + r) % gz) for i in range(gz)]) if r else piece


def to_chips(parts):
    return lax.all_to_all(parts, "gy", 0, 0, tiled=True)


def to_devices(parts):
    gz, gy, *rest = parts.shape
    parts = lax.all_to_all(parts.reshape(gz * gy, *rest), ("gz", "gy"), 0, 0, tiled=True)
    return parts.reshape(gz, gy, *rest)


def everywhere(sums):
    sums = to_chips(sums)
    return [to_core(sums, r) for r in range(lax.axis_size("gz"))]


def shards(data, band_offset, interp_weight):
    gz = lax.axis_size("gz")
    gy = lax.axis_size("gy")
    devices = gz * gy
    data = data[0]
    blocks, ny, width = data.shape
    rows = ny // devices
    ka = blocks * HALF
    nx = ka * gy

    core = lax.axis_index("gz")
    flat = lax.axis_index("gy") * gz + core
    edge = jnp.stack([flat == 0, flat == devices - 1, core]).astype(jnp.int32)
    order = [(i % gz) * gy + i // gz for i in range(devices)]
    up = [(order[i + 1], order[i]) for i in range(devices - 1)]
    down = [(order[i], order[i + 1]) for i in range(devices - 1)]

    lower = band_offset < 0
    weight = interp_weight
    coef = jnp.stack(
        [
            jnp.where(lower, weight[1], weight[0]),
            jnp.where(lower, weight[0], 0.0),
            jnp.where(lower, 0.0, weight[1]),
        ]
    ).reshape(3, gy, 1, ka)
    coef = jnp.broadcast_to(coef, (3, gy, 8, ka))

    spec = to_devices(y_inverse(data, rows, gz, gy))
    d0, nd0, head, tail, first = middle(spec, coef, nx)
    next_head = lax.ppermute(head, ("gz", "gy"), up)
    prev_tail = lax.ppermute(tail, ("gz", "gy"), down)
    sums = to_chips(border_sums(edge, head, tail, next_head, prev_tail, gy))
    d1, eta, sums, second = second_descent(
        edge, sums, d0, nd0, tail, prev_tail, next_head, coef, gz, nx
    )
    sums = everywhere(sums)
    flat_shape = (devices, 2, rows, ka)
    spec, etas = combine_spectra(eta, sums, first.reshape(flat_shape), second.reshape(flat_shape))
    residual = y_forward(to_devices(spec.reshape(gz, gy, 2, rows, ka)), data)

    volume = -(etas[0, 0, 0] * d0 + etas[1, 0, 0] * d1)
    volume = volume.reshape(gz, gy, rows, ka).transpose(0, 2, 3, 1).reshape(gz, rows, nx)
    parts = [
        to_core(lax.dynamic_index_in_dim(volume, lax.rem(core + r, gz), 0, False), r)
        for r in range(gz)
    ]
    volume = jnp.zeros((gz, rows, nx), F32)
    for r, part in enumerate(parts):
        volume = lax.dynamic_update_index_in_dim(volume, part, lax.rem(core + gz - r, gz), 0)
    return (volume.reshape(1, gz * rows, nx), residual[None])


NX = 4096
NY = 2048
XB = 64
YB = 64
ITERS = 2
XA = 64
YA = 32
PRECISE = lax.Precision.HIGHEST


def with_halo(block, sides, width):
    for axis, dim in sides:
        count = lax.axis_size(axis)
        forward = [(i, i + 1) for i in range(count - 1)]
        backward = [(target, source) for source, target in forward]
        low = lax.ppermute(
            lax.slice_in_dim(block, block.shape[dim] - width, None, axis=dim), axis, forward
        )
        high = lax.ppermute(lax.slice_in_dim(block, 0, width, axis=dim), axis, backward)
        block = jnp.concatenate([low, block, high], axis=dim)
    return block


def from_behind(block, axis, distance):
    devices = range(lax.axis_size(axis))
    route = [(i - distance, i) for i in devices if i - distance in devices]
    return lax.ppermute(block, axis, route)


def unit_table(length):
    counter = jnp.arange(length, dtype=jnp.int32)
    phase_int = counter[:, None] * counter[None, :] % length
    angles = 2.0 * jnp.pi / length * phase_int.astype(jnp.float32)
    factor = length ** (-0.5)
    return (jnp.cos(angles) * factor, jnp.sin(angles) * factor)


def twiddle_table(row_len, col_len, period):
    phase_int = (
        jnp.arange(row_len, dtype=jnp.int32)[:, None]
        * jnp.arange(col_len, dtype=jnp.int32)[None, :]
        % period
    )
    angles = 2.0 * jnp.pi / period * phase_int.astype(jnp.float32)
    return (jnp.cos(angles), jnp.sin(angles))


def split_parts(packed):
    half_width = packed.shape[-1] // 2
    return (packed[..., :half_width], packed[..., half_width:])


def join_parts(real_part, imag_part):
    return jnp.concatenate([real_part, imag_part], axis=-1)


def complex_contract(packed, cos_table, sin_table, subscripts, conj_sign):
    cos_out = jnp.einsum(subscripts, packed, cos_table, precision=PRECISE)
    sin_out = jnp.einsum(subscripts, packed, sin_table, precision=PRECISE)
    cos_re, cos_im = split_parts(cos_out)
    sin_re, sin_im = split_parts(sin_out)
    return join_parts(cos_re - conj_sign * sin_im, cos_im + conj_sign * sin_re)


def rotate(packed, cos_table, sin_table, conj_sign):
    real_part, imag_part = split_parts(packed)
    return join_parts(
        real_part * cos_table - conj_sign * imag_part * sin_table,
        imag_part * cos_table + conj_sign * real_part * sin_table,
    )


def forward_x(volume):
    slices, row_count = (volume.shape[0], volume.shape[1])
    cos_a, sin_a = unit_table(XA)
    cos_b, sin_b = unit_table(XB)
    first_table = jnp.concatenate([cos_a, -sin_a], axis=1)
    grid_view = volume.reshape(slices, row_count, XA, XB)
    mixing = jnp.einsum("zyab,am->zybm", grid_view, first_table, precision=PRECISE)
    tw_cos, tw_sin = twiddle_table(XB, XA, NX)
    mixing = rotate(mixing, tw_cos, tw_sin, -1.0)
    return complex_contract(mixing, cos_b, sin_b, "zybm,bl->zlym", -1.0)


def inverse_x(packed):
    slices, row_count = (packed.shape[0], packed.shape[2])
    cos_a, sin_a = unit_table(XA)
    cos_b, sin_b = unit_table(XB)
    mixing = complex_contract(packed, cos_b, sin_b, "zlym,lb->zybm", 1.0)
    tw_cos, tw_sin = twiddle_table(XB, XA, NX)
    mixing = rotate(mixing, tw_cos, tw_sin, 1.0)
    last_table = jnp.concatenate([cos_a, -sin_a], axis=0)
    grid_view = jnp.einsum("zybm,ma->zyab", mixing, last_table, precision=PRECISE)
    return grid_view.reshape(slices, row_count, NX)


def forward_y(packed):
    slices, blocks, width = (packed.shape[0], packed.shape[1], packed.shape[3])
    cos_a, sin_a = unit_table(YA)
    cos_b, sin_b = unit_table(YB)
    grid_view = packed.reshape(slices, blocks, YA, YB, width)
    mixing = complex_contract(grid_view, cos_a, sin_a, "zjcdm,ck->zjkdm", -1.0)
    tw_cos, tw_sin = twiddle_table(YA, YB, NY)
    mixing = rotate(mixing, tw_cos[:, :, None], tw_sin[:, :, None], -1.0)
    result = complex_contract(mixing, cos_b, sin_b, "zjkdm,dl->zjlkm", -1.0)
    return result.reshape(slices, blocks, NY, width)


def inverse_y(packed):
    slices, blocks, width = (packed.shape[0], packed.shape[1], packed.shape[3])
    cos_a, sin_a = unit_table(YA)
    cos_b, sin_b = unit_table(YB)
    grid_view = packed.reshape(slices, blocks, YB, YA, width)
    mixing = complex_contract(grid_view, cos_b, sin_b, "zjlkm,ld->zjkdm", 1.0)
    tw_cos, tw_sin = twiddle_table(YA, YB, NY)
    mixing = rotate(mixing, tw_cos[:, :, None], tw_sin[:, :, None], 1.0)
    result = complex_contract(mixing, cos_a, sin_a, "zjkdm,kc->zjcdm", 1.0)
    return result.reshape(slices, blocks, NY, width)


def tilt_coefficients(band_offset, interp_weight, first_block, blocks):
    offsets = lax.dynamic_slice_in_dim(band_offset.reshape(XB, XA), first_block, blocks, 0)
    weights = lax.dynamic_slice_in_dim(interp_weight.reshape(2, XB, XA), first_block, blocks, 1)
    lower_tap = (jnp.concatenate([offsets, offsets], axis=1) < 0)[:, None, :]
    first_weight = jnp.concatenate([weights[0], weights[0]], axis=1)[:, None, :]
    second_weight = jnp.concatenate([weights[1], weights[1]], axis=1)[:, None, :]
    return (lower_tap, first_weight, second_weight)


def tilt(field_in, coefficients, adjoint):
    lower_tap, first_weight, second_weight = coefficients
    padded = with_halo(field_in, (("gz", 0),), 1)
    below_rim = padded[:-2]
    middle = padded[1:-1]
    above_rim = padded[2:]
    if adjoint:
        return jnp.where(
            lower_tap,
            first_weight * above_rim + second_weight * middle,
            first_weight * middle + second_weight * below_rim,
        )
    return jnp.where(
        lower_tap,
        first_weight * below_rim + second_weight * middle,
        first_weight * middle + second_weight * above_rim,
    )


def to_pencil(slab_part):
    return lax.all_to_all(slab_part, "gy", split_axis=1, concat_axis=2, tiled=True)


def to_slab(pencil_part):
    return lax.all_to_all(pencil_part, "gy", split_axis=2, concat_axis=1, tiled=True)


def back_project(packed, pencil_coef):
    return inverse_x(to_slab(inverse_y(tilt(packed, pencil_coef, True))))


def edge_masks(slices, row_count):
    z_global = lax.axis_index("gz") * slices + jnp.arange(slices, dtype=jnp.int32)
    y_global = lax.axis_index("gy") * row_count + jnp.arange(row_count, dtype=jnp.int32)
    keep_z = (z_global < slices * lax.axis_size("gz") - 1).astype(jnp.float32)[:, None, None]
    keep_y = (y_global < row_count * lax.axis_size("gy") - 1).astype(jnp.float32)[None, :, None]
    return (keep_z, keep_y)


def forward_diff(field_in, keep_z, keep_y):
    slices, row_count = (field_in.shape[0], field_in.shape[1])
    next_z = from_behind(field_in, "gz", -1)
    next_y = from_behind(field_in[:, :1], "gy", -1)
    along_z = (jnp.concatenate([field_in[1:], next_z], axis=0) - field_in) * keep_z
    along_y = (jnp.concatenate([field_in[:, 1:], next_y], axis=1) - field_in) * keep_y
    zero_col = jnp.zeros((slices, row_count, 1), jnp.float32)
    along_x = jnp.concatenate([field_in[:, :, 1:] - field_in[:, :, :-1], zero_col], axis=2)
    return jnp.stack([along_z, along_y, along_x])


def transpose_diff(components, keep_z, keep_y):
    slices, row_count = (components.shape[1], components.shape[2])
    zero_col = jnp.zeros((slices, row_count, 1), jnp.float32)
    comp_z = components[0] * keep_z
    comp_y = components[1] * keep_y
    comp_x = jnp.concatenate([components[2][:, :, :-1], zero_col], axis=2)
    prev_z = from_behind(comp_z, "gz", 1)
    prev_y = from_behind(comp_y[:, -1:], "gy", 1)
    result = jnp.concatenate([prev_z, comp_z[:-1]], axis=0) - comp_z
    result = result + jnp.concatenate([prev_y, comp_y[:, :-1]], axis=1) - comp_y
    result = result + jnp.concatenate([zero_col, comp_x[:, :, :-1]], axis=2) - comp_x
    return result


def plain_shards(data, band_offset, interp_weight):
    slices = data.shape[0]
    blocks = data.shape[1]
    width = data.shape[3]
    row_count = NY // lax.axis_size("gy")
    slab_coef = tilt_coefficients(band_offset, interp_weight, 0, XB)
    pencil_coef = tilt_coefficients(
        band_offset, interp_weight, lax.axis_index("gy") * blocks, blocks
    )
    keep_z, keep_y = edge_masks(slices, row_count)
    measured = data.astype(jnp.float32)
    volume = jnp.zeros((slices, row_count, NX), jnp.float32)
    grad_volume = jnp.zeros((3, slices, row_count, NX), jnp.float32)
    split_var = grad_volume
    dual_var = grad_volume
    data_back = back_project(measured, pencil_coef)
    normal_part = jnp.zeros_like(volume)
    tilted = jnp.zeros((slices, XB, row_count, width), jnp.float32)
    for iteration in range(ITERS):
        data_grad = normal_part - data_back
        if iteration > 0:
            tv_gap = grad_volume - split_var + dual_var / PENALTY
            descent = data_grad + PENALTY * transpose_diff(tv_gap, keep_z, keep_y)
        else:
            descent = data_grad
        slope_field = forward_diff(descent, keep_z, keep_y)
        projected = tilt(forward_x(descent), slab_coef, False)
        line_totals = lax.psum(
            (
                jnp.sum(descent * descent),
                jnp.sum(projected * projected),
                jnp.sum(slope_field * slope_field),
            ),
            ("gz", "gy"),
        )
        step_length = line_totals[0] / (line_totals[1] + PENALTY * line_totals[2])
        volume = volume - step_length * descent
        grad_volume = grad_volume - step_length * slope_field
        tilted = tilted - step_length * projected
        if iteration + 1 < ITERS:
            normal_part = normal_part - step_length * inverse_x(tilt(projected, slab_coef, True))
        if iteration + 1 < ITERS:
            shifted = grad_volume + dual_var / PENALTY
            split_var = shifted - jnp.clip(shifted, -TV_WEIGHT / PENALTY, TV_WEIGHT / PENALTY)
            dual_var = PENALTY * (grad_volume - split_var)
    residual = forward_y(to_pencil(tilted)) - measured
    return (volume, residual)


def tiles_fit(mesh, ny, blocks):
    rows = ny // (mesh.shape["gz"] * mesh.shape["gy"])
    return mesh.shape["gz"] == 2 and rows % 16 == 0 and mesh.shape["gy"] % YR == 0 and blocks // mesh.shape["gy"] % 2 == 0


def solution(mesh):
    in_specs = (P("gz", "gy", None, None), P(), P())
    out_specs = (P("gz", "gy", None), P("gz", "gy", None, None))

    def run(data, band_offset, interp_weight):
        body = shards if tiles_fit(mesh, data.shape[2], data.shape[1]) else plain_shards
        call = jax.shard_map(
            body, mesh=mesh, in_specs=in_specs, out_specs=out_specs, check_vma=False
        )
        return call(data, band_offset, interp_weight)

    return run
```

```python
import functools

import jax
import jax.numpy as jnp
import numpy as np
from jax import lax
from jax.experimental import pallas as pl
from jax.experimental.pallas import tpu as pltpu
from jax.sharding import PartitionSpec as P

PENALTY = 0.5
TV_WEIGHT = 0.25
CLIP = TV_WEIGHT / PENALTY
HALF = 64
YR = 8
LANES = 128
F32 = jnp.float32
BF16 = jnp.bfloat16
MIB = 1024 * 1024
Y_GRANT = 56 * MIB
X_GRANT = 20 * MIB


def dft_parts(length, scale):
    index = np.arange(length)
    angles = 2.0 * np.pi / length * (index[:, None] * index[None, :] % length)
    return np.cos(angles) * scale, np.sin(angles) * scale


def host_parts(table):
    table = table.astype(np.float32)
    high = table.astype(BF16)
    low = (table - high.astype(np.float32)).astype(BF16)
    return high, low


def y_matrix(ny, forward, sign):
    n = ny // YR
    cos, sin = dft_parts(n, sign * ny**-0.5)
    if forward:
        table = np.block([[cos, sin], [-sin, cos]])
    else:
        table = np.block([[cos, -sin], [sin, cos]])
    return jnp.asarray(np.concatenate(host_parts(table), axis=0))


def y_twiddle(ny):
    n = ny // YR
    angles = 2.0 * np.pi / ny * (np.arange(1, YR)[:, None] * np.arange(n)[None, :])
    table = np.stack([np.cos(angles), np.sin(angles)]).astype(np.float32)
    return jnp.asarray(np.ascontiguousarray(np.broadcast_to(table[..., None], (2, YR - 1, n, LANES))))


def x_inverse_matrix(nx, ka):
    cos, sin = dft_parts(ka, nx**-0.5)
    return np.concatenate(host_parts(np.concatenate([cos, -sin], axis=0)), axis=1)


def x_forward_matrix(nx, ka):
    cos, sin = dft_parts(ka, nx**-0.5)
    return jnp.asarray(np.concatenate(host_parts(np.concatenate([cos, -sin], axis=1)), axis=1))


def x_twiddle(nx, ka):
    kb = nx // ka
    angles = 2.0 * np.pi / nx * (np.arange(kb)[:, None] * np.arange(ka)[None, :])
    table = np.stack([np.cos(angles), np.sin(angles)]).astype(np.float32)
    return jnp.asarray(np.ascontiguousarray(np.broadcast_to(table[:, :, None], (2, kb, 8, ka))))


def short_fft(planes, sign):
    n = len(planes)
    if n == 1:
        return planes
    even = short_fft(planes[0::2], sign)
    odd = short_fft(planes[1::2], sign)
    half = n // 2
    out = [None] * n
    for k in range(half):
        er, ei = even[k]
        tr, ti = odd[k]
        if 4 * k == n:
            if sign > 0:
                out[k] = (er - ti, ei + tr)
                out[k + half] = (er + ti, ei - tr)
            else:
                out[k] = (er + ti, ei - tr)
                out[k + half] = (er - ti, ei + tr)
            continue
        if k > 0:
            c = float(np.cos(2.0 * np.pi * k / n))
            s = float(sign * np.sin(2.0 * np.pi * k / n))
            if 8 * k == n:
                tr, ti = (tr - ti, ti + tr) if sign > 0 else (tr + ti, ti - tr)
                tr, ti = tr * c, ti * c
            elif 8 * k == 3 * n:
                m = float(np.sin(2.0 * np.pi * k / n))
                tr, ti = (-(tr + ti), tr - ti) if sign > 0 else (ti - tr, -(tr + ti))
                tr, ti = tr * m, ti * m
            else:
                tr, ti = tr * c - ti * s, ti * c + tr * s
        out[k] = (er + tr, ei + ti)
        out[k + half] = (er - tr, ei - ti)
    return out


def split2(x):
    high = x.astype(BF16)
    return high, (x - high.astype(F32)).astype(BF16)


def dot(a, b):
    return jnp.dot(a, b, preferred_element_type=F32)


def fold(x):
    rows, lanes = x.shape
    x = jnp.sum(x.reshape(rows // 8, 8, lanes), axis=0)
    total = x[:, :LANES]
    for i in range(1, lanes // LANES):
        total = total + x[:, i * LANES : (i + 1) * LANES]
    return total


def full_sum(x):
    return jnp.sum(jnp.sum(x, axis=0, keepdims=True), axis=1, keepdims=True)


def step_of(sums_refs):
    total = sum(jnp.sum(sums_ref[...], axis=0) for sums_ref in sums_refs)
    parts = jnp.sum(total, axis=1, keepdims=True)
    return parts[0:1] / (parts[1:2] + PENALTY * parts[2:3])


def sums_block(values):
    rows = [jnp.sum(v, axis=0, keepdims=True) for v in values]
    index = lax.broadcasted_iota(jnp.int32, (8, LANES), 0)
    block = jnp.zeros((8, LANES), F32)
    for i, row in enumerate(rows):
        block = jnp.where(index == i, jnp.broadcast_to(row, (8, LANES)), block)
    return block


def put_copies(out_ref, block):
    for i in range(out_ref.shape[0]):
        out_ref[i] = block


def mix_adjoint(coef, planes):
    own, below, above = coef
    out = []
    for z in range(len(planes)):
        value = own * planes[z]
        if z + 1 < len(planes):
            value = value + below * planes[z + 1]
        if z > 0:
            value = value + above * planes[z - 1]
        out.append(value)
    return out


def mix(coef, planes):
    own, below, above = coef
    out = []
    for z in range(len(planes)):
        value = own * planes[z]
        if z > 0:
            value = value + below * planes[z - 1]
        if z + 1 < len(planes):
            value = value + above * planes[z + 1]
        out.append(value)
    return out


def y_inverse_kernel(
    data_hbm, table_hbm, tw_hbm, out_hbm,
    data_ref, table_ref, tw_ref, out_ref, re_s, im_s, mix_s, sems, out_sems,
):
    blocks, ny, _ = data_ref.shape
    n = ny // YR
    gz, _, _, rows, _ = out_ref.shape
    lane = lax.broadcasted_iota(jnp.int32, (n, LANES), 1)
    pairs = blocks // 2

    def fetch(chunk):
        part = pl.ds(2 * chunk, 2)
        return pltpu.make_async_copy(data_hbm.at[part], data_ref.at[part], sems.at[2 + chunk])

    def give(chunk, core):
        at = (core, slice(None), slice(None), slice(None), pl.ds(chunk * LANES, LANES))
        return pltpu.make_async_copy(out_ref.at[at], out_hbm.at[at], out_sems.at[chunk * gz + core])

    fetch_table = pltpu.make_async_copy(table_hbm, table_ref, sems.at[0])
    fetch_tw = pltpu.make_async_copy(tw_hbm, tw_ref, sems.at[1])
    fetch(0).start()

    for chunk in range(pairs):
        lanes = slice(chunk * LANES, (chunk + 1) * LANES)
        fetch(chunk).wait()
        if chunk == 0:
            fetch_table.start()

        def unpack(i, carry):
            part = pl.ds(pl.multiple_of(i * n, n), n)
            first = data_ref[2 * chunk, part, :].astype(F32)
            second = data_ref[2 * chunk + 1, part, :].astype(F32)
            re_s[part, :] = jnp.where(lane < HALF, first, pltpu.roll(second, HALF, 1))
            im_s[part, :] = jnp.where(lane < HALF, pltpu.roll(first, HALF, 1), second)
            return carry

        lax.fori_loop(0, YR, unpack, 0)
        if chunk == 0:
            fetch_table.wait()
            fetch_tw.start()
        if chunk + 1 < pairs:
            fetch(chunk + 1).start()

        for k in range(0, YR, 2):
            pieces = [
                jnp.concatenate([s[pl.ds(k + d, n, stride=YR), :] for d in range(2)], axis=1)
                for s in (re_s, im_s)
            ]
            both = dot(table_ref[...], jnp.concatenate(pieces, axis=0).astype(BF16))
            both = both[: 2 * n] + both[2 * n :]
            for d in range(2):
                mix_s[k + d] = both[:, d * LANES : (d + 1) * LANES]

        if chunk == 0:
            fetch_tw.wait()

        tiles = rows // 8
        for core in range(gz):

            def combine(i, carry):
                y2 = ((i // tiles) * gz + core) * rows + lax.rem(i, tiles) * 8
                part = pl.ds(pl.multiple_of(y2, 8), 8)
                planes = []
                for k in range(YR):
                    re = mix_s[k, part, :]
                    im = mix_s[k, pl.ds(pl.multiple_of(n + y2, 8), 8), :]
                    if k > 0:
                        c = tw_ref[0, k - 1, part, :]
                        s = tw_ref[1, k - 1, part, :]
                        re, im = re * c - im * s, im * c + re * s
                    planes.append((re, im))
                at = pl.ds(pl.multiple_of(lax.rem(i, tiles) * 8, 8), 8)
                for k, (re, im) in enumerate(short_fft(planes, 1)):
                    to = k * (n // (gz * rows)) + i // tiles
                    out_ref[core, to, 0, at, lanes] = re
                    out_ref[core, to, 1, at, lanes] = im
                return carry

            lax.fori_loop(0, n // gz // 8, combine, 0, unroll=2)
            give(chunk, core).start()

    for chunk in range(pairs):
        for core in range(gz):
            give(chunk, core).wait()


def y_inverse(data, rows, gz, gy):
    blocks, ny, width = data.shape
    n = ny // YR
    ka = blocks * HALF
    hbm = pl.BlockSpec(memory_space=pltpu.HBM)
    return pl.pallas_call(
        y_inverse_kernel,
        in_specs=[hbm] * 3,
        out_specs=hbm,
        out_shape=jax.ShapeDtypeStruct((gz, gy, 2, rows, ka), F32),
        scratch_shapes=[
            pltpu.VMEM((blocks, ny, width), BF16),
            pltpu.VMEM((4 * n, 2 * n), BF16),
            pltpu.VMEM((2, YR - 1, n, LANES), F32),
            pltpu.VMEM((gz, gy, 2, rows, ka), F32),
            pltpu.VMEM((ny, LANES), F32),
            pltpu.VMEM((ny, LANES), F32),
            pltpu.VMEM((YR, 2 * n, LANES), F32),
            pltpu.SemaphoreType.DMA((2 + blocks // 2,)),
            pltpu.SemaphoreType.DMA((blocks // 2 * gz,)),
        ],
        compiler_params=pltpu.CompilerParams(vmem_limit_bytes=Y_GRANT),
        name="y_inverse",
    )(data, y_matrix(ny, False, -1.0), y_twiddle(ny))


def y_forward_kernel(
    spec_hbm, data_hbm, table_hbm, tw_hbm, out_hbm,
    spec_ref, data_ref, table_ref, tw_ref, out_ref, mix_s, sems, spec_sems, out_sems,
):
    blocks, ny, _ = data_ref.shape
    n = ny // YR
    _, gz, gy, _, rows, _ = spec_ref.shape
    pairs = blocks // 2
    half = n // 2

    def fetch(chunk):
        lanes = pl.ds(chunk * LANES, LANES)
        return pltpu.make_async_copy(
            spec_hbm.at[:, :, :, :, lanes], spec_ref.at[chunk], spec_sems.at[chunk]
        )

    def give(chunk, part):
        at = (pl.ds(2 * chunk, 2), slice(None), pl.ds(part * half, half))
        return pltpu.make_async_copy(out_ref.at[at], out_hbm.at[at], out_sems.at[2 * chunk + part])

    fetch_table = pltpu.make_async_copy(table_hbm, table_ref, sems.at[0])
    fetch_tw = pltpu.make_async_copy(tw_hbm, tw_ref, sems.at[1])
    fetch_data = pltpu.make_async_copy(data_hbm, data_ref, sems.at[2])
    fetch(0).start()
    fetch_table.start()

    def rows_of(chunk, p, k):
        part = pl.ds(k, rows // YR, stride=YR)
        return jnp.concatenate(
            [spec_ref[chunk, core, i, p, part, :] for i in range(gy) for core in range(gz)], axis=0
        )

    lane = lax.broadcasted_iota(jnp.int32, (16, LANES), 1)
    for chunk in range(pairs):
        lanes = slice(chunk * LANES, (chunk + 1) * LANES)
        fetch(chunk).wait()

        if chunk == 0:
            fetch_table.wait()
            fetch_tw.start()
            fetch_data.start()

        for k in range(0, YR, 2):
            pieces = [
                jnp.concatenate([rows_of(chunk, p, k + d) for d in range(2)], axis=1)
                for p in range(2)
            ]
            high, low = split2(jnp.concatenate(pieces, axis=0))
            both = dot(table_ref[...], high)
            both = both[: 2 * n] + both[2 * n :] + dot(table_ref[: 2 * n], low)
            for d in range(2):
                mix_s[k + d] = both[:, d * LANES : (d + 1) * LANES]
        if chunk == 0:
            fetch_tw.wait()
            fetch_data.wait()
        if chunk + 1 < pairs:
            fetch(chunk + 1).start()

        def combine(i, carry):
            start = pl.multiple_of(i * 16, 16)
            part = pl.ds(start, 16)
            planes = []
            for k in range(YR):
                re = mix_s[k, part, :]
                im = mix_s[k, pl.ds(pl.multiple_of(n + i * 16, 16), 16), :]
                if k > 0:
                    c = tw_ref[0, k - 1, part, :]
                    s = tw_ref[1, k - 1, part, :]
                    re, im = re * c + im * s, im * c - re * s
                planes.append((re, im))
            for k, (re, im) in enumerate(short_fft(planes, -1)):
                at = pl.ds(pl.multiple_of(k * n + start, 16), 16)
                first = jnp.where(lane < HALF, re, pltpu.roll(im, HALF, 1))
                second = jnp.where(lane < HALF, pltpu.roll(re, HALF, 1), im)
                out_ref[2 * chunk, k, part, :] = first - data_ref[2 * chunk, at, :].astype(F32)
                out_ref[2 * chunk + 1, k, part, :] = (
                    second - data_ref[2 * chunk + 1, at, :].astype(F32)
                )
            return carry

        for part in range(2):
            lax.fori_loop(part * half // 16, (part + 1) * half // 16, combine, 0)
            give(chunk, part).start()

    for chunk in range(pairs):
        for part in range(2):
            give(chunk, part).wait()


def y_forward(spec, data):
    blocks, ny, width = data.shape
    n = ny // YR
    hbm = pl.BlockSpec(memory_space=pltpu.HBM)
    out = pl.pallas_call(
        y_forward_kernel,
        in_specs=[hbm] * 4,
        out_specs=hbm,
        out_shape=jax.ShapeDtypeStruct((blocks, YR, n, width), F32),
        scratch_shapes=[
            pltpu.VMEM((blocks // 2, *spec.shape[:-1], LANES), F32),
            pltpu.VMEM((blocks, ny, width), BF16),
            pltpu.VMEM((4 * n, 2 * n), BF16),
            pltpu.VMEM((2, YR - 1, n, LANES), F32),
            pltpu.VMEM((blocks, YR, n, width), F32),
            pltpu.VMEM((YR, 2 * n, LANES), F32),
            pltpu.SemaphoreType.DMA((3,)),
            pltpu.SemaphoreType.DMA((blocks // 2,)),
            pltpu.SemaphoreType.DMA((blocks,)),
        ],
        compiler_params=pltpu.CompilerParams(vmem_limit_bytes=Y_GRANT),
        name="y_forward",
    )(spec, data, y_matrix(ny, True, 1.0), y_twiddle(ny))
    return out.reshape(blocks, ny, width)


def plane_chunk(planes, rows):
    chunk = max(1, 1024 // rows)
    while planes % chunk:
        chunk -= 1
    return chunk


def turn_rows(kb, planes_of, tw_ref, lanes, sign):
    out = []
    for b in range(kb):
        re, im = planes_of(b)
        if b > 0:
            c = tw_ref[0, b, :, lanes]
            s = tw_ref[1, b, :, lanes]
            if sign > 0:
                re, im = re * c - im * s, im * c + re * s
            else:
                re, im = re * c + im * s, im * c - re * s
        out.append((re, im))
    return out


def inverse_columns(gz, kb, spectra, coef_ref, tw_ref, lanes, part, re_s, im_s):
    mixed = [[None] * kb for _ in range(gz)]
    for k in range(kb):
        coef = [coef_ref[j, k, :, lanes] for j in range(3)]
        re = mix_adjoint(coef, [spectra[z][k][0] for z in range(gz)])
        im = mix_adjoint(coef, [spectra[z][k][1] for z in range(gz)])
        for z in range(gz):
            mixed[z][k] = (re[z], im[z])
    for z in range(gz):
        short = short_fft(mixed[z], 1)
        for b, (re, im) in enumerate(turn_rows(kb, lambda b: short[b], tw_ref, lanes, 1)):
            re_s[z * kb + b, part, lanes] = re
            im_s[z * kb + b, part, lanes] = im


def forward_columns(gz, kb, coef_ref, tw_ref, lanes, part, re_s, im_s):
    spectra = []
    for z in range(gz):
        rows_of = lambda b: (re_s[z * kb + b, part, lanes], im_s[z * kb + b, part, lanes])
        spectra.append(short_fft(turn_rows(kb, rows_of, tw_ref, lanes, -1), -1))
    out = [[None] * kb for _ in range(gz)]
    for k in range(kb):
        coef = [coef_ref[j, k, :, lanes] for j in range(3)]
        re = mix(coef, [spectra[z][k][0] for z in range(gz)])
        im = mix(coef, [spectra[z][k][1] for z in range(gz)])
        for z in range(gz):
            out[z][k] = (re[z], im[z])
    return out


def inverse_product(re, im, table_ref):
    ka = re.shape[1]
    high, low = split2(jnp.concatenate([re, im], axis=1))
    value = dot(high, table_ref[...])
    return value[:, :ka] + value[:, ka:] + dot(low, table_ref[:, :ka])


def forward_product(field, table_ref):
    ka = field.shape[1]
    high, low = split2(field)
    value = dot(high, table_ref[...])
    value = value[:, : 2 * ka] + value[:, 2 * ka :] + dot(low, table_ref[:, : 2 * ka])
    return value[:, :ka], value[:, ka:]


def next_plane(field_ref, p, kb):
    rows, ka = field_ref.shape[1:]
    if (p + 1) % kb:
        return field_ref[p + 1]
    lane = lax.broadcasted_iota(jnp.int32, (rows, ka), 1)
    return jnp.where(lane == ka - 1, field_ref[p], pltpu.roll(field_ref[p + 1 - kb], ka - 1, 1))


def prev_plane(field_ref, p, kb):
    rows, ka = field_ref.shape[1:]
    if p % kb:
        return field_ref[p - 1]
    lane = lax.broadcasted_iota(jnp.int32, (rows, ka), 1)
    return jnp.where(lane == 0, field_ref[p], pltpu.roll(field_ref[p + kb - 1], 1, 1))


def first_kernel(
    gz, edge_ref, field_ref, coef_ref, tw_ref, table_ref, sums_ref, spec_ref, *refs
):
    piece_refs, (re_s, im_s) = refs[:-2], refs[-2:]
    planes, rows, ka = field_ref.shape
    kb = planes // gz
    projected = forward_into(gz, field_ref, coef_ref, tw_ref, table_ref, spec_ref, re_s, im_s)
    cut(gz, edge_ref, spec_ref, piece_refs)
    row = lax.broadcasted_iota(jnp.int32, (rows, ka), 0)
    square = jnp.zeros((8, LANES), F32)
    slope = jnp.zeros((8, LANES), F32)
    for p in range(planes):
        here = field_ref[p]
        square = square + fold(here * here)
        along_x = next_plane(field_ref, p, kb) - here
        along_y = jnp.where(row == rows - 1, 0.0, pltpu.roll(here, rows - 1, 0) - here)
        terms = along_x * along_x + along_y * along_y
        if p + kb < planes:
            along_z = field_ref[p + kb] - here
            terms = terms + along_z * along_z
        slope = slope + fold(terms)
    sums_ref[0] = square
    sums_ref[1] = projected
    sums_ref[2] = slope


def middle_kernel(
    spec_hbm, coef_ref, tw_ref, inverse_ref, forward_ref,
    d0_ref, head_ref, tail_ref, spec_ref, re_s, im_s, sems,
):
    gz, kb, _, rows, ka = spec_ref.shape
    planes = gz * kb
    lane_parts = [slice(start, start + LANES) for start in range(0, ka, LANES)]
    cuts = sems.shape[0]
    cut = rows // cuts

    def fetch(i):
        part = pl.ds(i * cut, cut)
        return pltpu.make_async_copy(
            spec_hbm.at[:, :, :, part], spec_ref.at[:, :, :, part], sems.at[i]
        )

    def columns_back(j, carry):
        part = pl.ds(pl.multiple_of(j * 8, 8), 8)
        for lanes in lane_parts:
            spectra = [
                [(spec_ref[z, k, 0, part, lanes], spec_ref[z, k, 1, part, lanes]) for k in range(kb)]
                for z in range(gz)
            ]
            inverse_columns(gz, kb, spectra, coef_ref, tw_ref, lanes, part, re_s, im_s)
        return carry

    fetch(0).start()
    for i in range(cuts):
        fetch(i).wait()
        if i + 1 < cuts:
            fetch(i + 1).start()
        lax.fori_loop(i * cut // 8, (i + 1) * cut // 8, columns_back, 0)

    step = plane_chunk(planes, rows)
    shape2, shape3 = (step * rows, ka), (step, rows, ka)

    def there_and_back(i, carry):
        part = pl.ds(i * step, step)
        field = inverse_product(re_s[part].reshape(shape2), im_s[part].reshape(shape2), inverse_ref)
        d0_ref[part] = field.reshape(shape3)
        re, im = forward_product(field, forward_ref)
        re_s[part] = re.reshape(shape3)
        im_s[part] = im.reshape(shape3)
        return carry

    lax.fori_loop(0, planes // step, there_and_back, 0)

    def second_columns(j, total):
        part = pl.ds(pl.multiple_of(j * 8, 8), 8)
        for lanes in lane_parts:
            spectra = forward_columns(gz, kb, coef_ref, tw_ref, lanes, part, re_s, im_s)
            for z in range(gz):
                for k in range(kb):
                    for p in range(2):
                        value = spectra[z][k][p]
                        spec_ref[z, k, p, part, lanes] = value
                        total = total + value * value
        return total

    projected = lax.fori_loop(0, rows // 8, second_columns, jnp.zeros((8, LANES), F32))
    for p in range(planes):
        head_ref[p : p + 1, :] = d0_ref[p, :1, :]
        head_ref[planes + p : planes + p + 1, :] = d0_ref[p, 1:2, :]
        for part in range(2):
            at = 2 * planes + 2 * p + part
            head_ref[at : at + 1, :] = spec_ref[p // kb, p % kb, part, :1, :]
        tail_ref[p : p + 1, :] = d0_ref[p, rows - 1 : rows, :]

    row = lax.broadcasted_iota(jnp.int32, (rows, ka), 0)
    square = jnp.zeros((8, LANES), F32)
    slope = jnp.zeros((8, LANES), F32)
    for p in range(planes):
        here = d0_ref[p]
        square = square + fold(here * here)
        along_x = next_plane(d0_ref, p, kb) - here
        along_y = jnp.where(row == rows - 1, 0.0, pltpu.roll(here, rows - 1, 0) - here)
        terms = along_x * along_x + along_y * along_y
        if p + kb < planes:
            along_z = d0_ref[p + kb] - here
            terms = terms + along_z * along_z
        slope = slope + fold(terms)
    block = sums_block([square, projected, slope])
    for ref in (head_ref, tail_ref):
        at = ref.shape[0] - 8
        ref[at:, :] = jnp.zeros((8, ka), F32)
        ref[at:, :LANES] = block


def middle(spec, coef, nx):
    gz, kb, _, rows, ka = spec.shape
    planes = gz * kb
    vmem = pl.BlockSpec(memory_space=pltpu.VMEM)
    field = jax.ShapeDtypeStruct((planes, rows, ka), F32)
    return pl.pallas_call(
        middle_kernel,
        in_specs=[pl.BlockSpec(memory_space=pltpu.HBM)] + [vmem] * 4,
        out_specs=[vmem] * 4,
        out_shape=[
            field,
            jax.ShapeDtypeStruct((4 * planes + 8, ka), F32),
            jax.ShapeDtypeStruct((planes + 8, ka), F32),
            jax.ShapeDtypeStruct(spec.shape, F32),
        ],
        scratch_shapes=[
            pltpu.VMEM((planes, rows, ka), F32),
            pltpu.VMEM((planes, rows, ka), F32),
            pltpu.SemaphoreType.DMA((4 if rows % 32 == 0 else 1,)),
        ],
        compiler_params=pltpu.CompilerParams(vmem_limit_bytes=X_GRANT),
        name="middle",
    )(
        spec, coef, x_twiddle(nx, ka), jnp.asarray(x_inverse_matrix(nx, ka)),
        x_forward_matrix(nx, ka),
    )


def normal_kernel(spec_ref, coef_ref, tw_ref, table_ref, out_ref, re_s, im_s):
    gz, kb, _, rows, ka = spec_ref.shape
    planes = gz * kb
    lane_parts = [slice(start, start + LANES) for start in range(0, ka, LANES)]

    def columns(j, carry):
        part = pl.ds(pl.multiple_of(j * 8, 8), 8)
        for lanes in lane_parts:
            spectra = [
                [(spec_ref[z, k, 0, part, lanes], spec_ref[z, k, 1, part, lanes]) for k in range(kb)]
                for z in range(gz)
            ]
            inverse_columns(gz, kb, spectra, coef_ref, tw_ref, lanes, part, re_s, im_s)
        return carry

    lax.fori_loop(0, rows // 8, columns, 0)

    step = plane_chunk(planes, rows)
    shape = (step * rows, ka)
    for start in range(0, planes, step):
        part = slice(start, start + step)
        field = inverse_product(re_s[part].reshape(shape), im_s[part].reshape(shape), table_ref)
        out_ref[part] = field.reshape(step, rows, ka)


def normal_product(spec, coef, nx):
    gz, kb, _, rows, ka = spec.shape
    planes = gz * kb
    vmem = pl.BlockSpec(memory_space=pltpu.VMEM)
    return pl.pallas_call(
        normal_kernel,
        in_specs=[vmem] * 4,
        out_specs=vmem,
        out_shape=jax.ShapeDtypeStruct((planes, rows, ka), F32),
        scratch_shapes=[pltpu.VMEM((planes, rows, ka), F32)] * 2,
        compiler_params=pltpu.CompilerParams(vmem_limit_bytes=X_GRANT),
        cost_estimate=pl.CostEstimate(
            flops=12 * planes * rows * ka * ka, bytes_accessed=12 * planes * rows * ka, transcendentals=0
        ),
        name="normal_product",
    )(spec, coef, x_twiddle(nx, ka), jnp.asarray(x_inverse_matrix(nx, ka)))


def next_normal_row(gz, next_ref, coef_ref, tw_ref, table_ref, row_s, re_s, im_s):
    planes, ka = row_s.shape
    kb = planes // gz
    for start in range(0, ka, LANES):
        lanes = slice(start, start + LANES)

        def row_of(z, k, part):
            at = 2 * planes + 2 * (z * kb + k) + part
            return jnp.broadcast_to(next_ref[at : at + 1, lanes], (8, LANES))

        spectra = [[(row_of(z, k, 0), row_of(z, k, 1)) for k in range(kb)] for z in range(gz)]
        inverse_columns(gz, kb, spectra, coef_ref, tw_ref, lanes, slice(0, 8), re_s, im_s)
    shape = (planes * 8, ka)
    field = inverse_product(re_s[...].reshape(shape), im_s[...].reshape(shape), table_ref)
    for p in range(planes):
        row_s[p : p + 1, :] = field[8 * p : 8 * p + 1, :]


def border_kernel(edge_ref, head_ref, tail_ref, next_ref, prev_ref, after_ref, out_ref):
    del after_ref
    planes = tail_ref.shape[0] - 8

    def sums_of(ref):
        return ref[ref.shape[0] - 8 :, :LANES]

    def border(after, before):
        step = after[:planes, :] - before[:planes, :]
        return fold(step * step)

    second = edge_ref[2] > 0
    below = border(head_ref, prev_ref) * jnp.where(edge_ref[0] > 0, 0.0, 1.0)
    above = border(next_ref, tail_ref) * jnp.where(edge_ref[1] > 0, 0.0, 1.0)
    other = jnp.where(second, sums_of(prev_ref), sums_of(next_ref))
    none = jnp.zeros((8, LANES), F32)
    put_copies(out_ref, sums_of(tail_ref) + other + sums_block([none, none, below + above]))


def border_sums(edge, head, tail, next_head, prev_tail, after, copies):
    vmem = pl.BlockSpec(memory_space=pltpu.VMEM)
    return pl.pallas_call(
        border_kernel,
        in_specs=[pl.BlockSpec(memory_space=pltpu.SMEM)]
        + [vmem] * 4
        + [pl.BlockSpec(memory_space=pl.ANY)],
        out_specs=vmem,
        out_shape=jax.ShapeDtypeStruct((copies, 8, LANES), F32),
        compiler_params=pltpu.CompilerParams(vmem_limit_bytes=2 * MIB),
        name="border_sums",
    )(edge, head, tail, next_head, prev_tail, after)


def second_kernel(
    gz, edge_ref, d0_ref, nd0_ref, tail_ref, prev_ref, next_ref,
    coef_ref, tw_ref, table_ref, inverse_ref, *refs,
):
    sums_refs, refs = refs[:1], refs[1:]
    d1_ref, eta_ref, out_ref, spec_ref, re_s, im_s, row_s, nrow_s, re8_s, im8_s = refs
    next_normal_row(gz, next_ref, coef_ref, tw_ref, inverse_ref, nrow_s, re8_s, im8_s)
    planes, rows, ka = d0_ref.shape
    kb = planes // gz
    eta_here = step_of(sums_refs)
    eta_ref[...] = jnp.broadcast_to(eta_here, (8, LANES))
    eta = jnp.max(eta_here)
    first = edge_ref[0] > 0
    last = edge_ref[1] > 0

    def shrink(difference):
        return jnp.clip(-eta * difference, -CLIP, CLIP)

    lane2 = lax.broadcasted_iota(jnp.int32, (kb, ka), 1)
    row2 = lax.broadcasted_iota(jnp.int32, (kb, ka), 0)
    for z in range(gz):
        part = slice(z * kb, (z + 1) * kb)
        here = next_ref[part, :]
        value = here - eta * nrow_s[part, :]
        up = pltpu.roll(here, kb - 1, 0)
        up = jnp.where(
            row2 == kb - 1, jnp.where(lane2 == ka - 1, here, pltpu.roll(up, ka - 1, 1)), up
        )
        down = pltpu.roll(here, 1, 0)
        down = jnp.where(row2 == 0, jnp.where(lane2 == 0, here, pltpu.roll(down, 1, 1)), down)
        value = value + shrink(here - down) - shrink(up - here)
        value = value + shrink(here - tail_ref[part, :]) - shrink(next_ref[planes + z * kb : planes + (z + 1) * kb, :] - here)
        if z > 0:
            value = value + shrink(here - next_ref[(z - 1) * kb : z * kb, :])
        if z + 1 < gz:
            value = value - shrink(next_ref[(z + 1) * kb : (z + 2) * kb, :] - here)
        row_s[part, :] = value

    row = lax.broadcasted_iota(jnp.int32, (rows, ka), 0)
    square = jnp.zeros((8, LANES), F32)
    for p in range(planes):
        here = d0_ref[p]
        value = here - eta * nd0_ref[p]
        value = value + shrink(here - prev_plane(d0_ref, p, kb))
        value = value - shrink(next_plane(d0_ref, p, kb) - here)
        below = jnp.where(last, here[rows - 1 :, :], next_ref[p : p + 1, :])
        above = jnp.where(first, here[:1, :], prev_ref[p : p + 1, :])
        upper = shrink(jnp.where(row == rows - 1, below, pltpu.roll(here, rows - 1, 0)) - here)
        lower = jnp.where(row == 0, shrink(here[:1, :] - above), pltpu.roll(upper, 1, 0))
        value = value + lower - upper
        if p >= kb:
            value = value + shrink(here - d0_ref[p - kb])
        if p + kb < planes:
            value = value - shrink(d0_ref[p + kb] - here)
        d1_ref[p] = value
        square = square + fold(value * value)

    slope = jnp.zeros((8, LANES), F32)
    for p in range(planes):
        here = d1_ref[p]
        along_x = next_plane(d1_ref, p, kb) - here
        below = jnp.where(last, here[rows - 1 :, :], row_s[p : p + 1, :])
        along_y = jnp.where(row == rows - 1, below, pltpu.roll(here, rows - 1, 0)) - here
        terms = along_x * along_x + along_y * along_y
        if p + kb < planes:
            along_z = d1_ref[p + kb] - here
            terms = terms + along_z * along_z
        slope = slope + fold(terms)

    step = plane_chunk(planes, rows)

    def multiply(i, carry):
        part = pl.ds(i * step, step)
        re, im = forward_product(d1_ref[part].reshape(step * rows, ka), table_ref)
        re_s[part] = re.reshape(step, rows, ka)
        im_s[part] = im.reshape(step, rows, ka)
        return carry

    lax.fori_loop(0, planes // step, multiply, 0)

    def columns(j, total):
        part = pl.ds(pl.multiple_of(j * 8, 8), 8)
        for start in range(0, ka, LANES):
            lanes = slice(start, start + LANES)
            spectra = forward_columns(gz, kb, coef_ref, tw_ref, lanes, part, re_s, im_s)
            for z in range(gz):
                for k in range(kb):
                    for p in range(2):
                        value = spectra[z][k][p]
                        spec_ref[z, k, p, part, lanes] = value
                        total = total + value * value
        return total

    projected = lax.fori_loop(0, rows // 8, columns, jnp.zeros((8, LANES), F32))
    put_copies(out_ref, sums_block([square, projected, slope]))


def second_descent(edge, sums, d0, nd0, tail, prev_tail, next_head, coef, gz, nx):
    planes, rows, ka = d0.shape
    vmem = pl.BlockSpec(memory_space=pltpu.VMEM)
    return pl.pallas_call(
        functools.partial(second_kernel, gz),
        in_specs=[pl.BlockSpec(memory_space=pltpu.SMEM)] + [vmem] * 10,
        out_specs=[vmem] * 4,
        out_shape=[
            jax.ShapeDtypeStruct((planes, rows, ka), F32),
            jax.ShapeDtypeStruct((8, LANES), F32),
            jax.ShapeDtypeStruct(sums.shape, F32),
            jax.ShapeDtypeStruct((gz, planes // gz, 2, rows, ka), F32),
        ],
        scratch_shapes=[
            pltpu.VMEM((planes, rows, ka), F32),
            pltpu.VMEM((planes, rows, ka), F32),
            pltpu.VMEM((planes, ka), F32),
            pltpu.VMEM((planes, ka), F32),
            pltpu.VMEM((planes, 8, ka), F32),
            pltpu.VMEM((planes, 8, ka), F32),
        ],
        compiler_params=pltpu.CompilerParams(vmem_limit_bytes=X_GRANT),
        name="second_descent",
    )(
        edge, d0, nd0, tail, prev_tail, next_head, coef,
        x_twiddle(nx, ka), x_forward_matrix(nx, ka), jnp.asarray(x_inverse_matrix(nx, ka)), sums,
    )


def combine_kernel(gz, eta_ref, *refs):
    sums_refs, (first_ref, second_ref, out_ref, steps_ref) = refs[:gz], refs[gz:]
    eta0 = jnp.max(eta_ref[...])
    eta1 = jnp.max(step_of(sums_refs))
    steps_ref[0] = eta_ref[...]
    steps_ref[1] = jnp.full((8, LANES), eta1, F32)
    count = out_ref.shape[0]
    start = pl.program_id(0) * count
    for i in range(count):
        out_ref[i] = -(eta0 * first_ref[start + i] + eta1 * second_ref[start + i])


def combine_spectra(eta, sums, first, second):
    gz = len(sums)
    planes, *rest = first.shape
    count = 4 if planes % 4 == 0 else 1
    vmem = pl.BlockSpec(memory_space=pltpu.VMEM)
    return pl.pallas_call(
        functools.partial(combine_kernel, gz),
        grid=(planes // count,),
        in_specs=[vmem] * (3 + gz),
        out_specs=[
            pl.BlockSpec((count, *rest), lambda i: (i, 0, 0, 0)),
            pl.BlockSpec((2, 8, LANES), lambda i: (0, 0, 0)),
        ],
        out_shape=[
            jax.ShapeDtypeStruct(first.shape, F32),
            jax.ShapeDtypeStruct((2, 8, LANES), F32),
        ],
        compiler_params=pltpu.CompilerParams(vmem_limit_bytes=6 * MIB),
        name="combine_spectra",
    )(eta, *sums, first, second)


def to_core(piece, r):
    gz = lax.axis_size("gz")
    return lax.ppermute(piece, "gz", [(i, (i + r) % gz) for i in range(gz)]) if r else piece


def to_chips(parts):
    return lax.all_to_all(parts, "gy", 0, 0, tiled=True)


def to_devices(parts):
    gz, gy, *rest = parts.shape
    parts = lax.all_to_all(parts.reshape(gz * gy, *rest), ("gz", "gy"), 0, 0, tiled=True)
    return parts.reshape(gz, gy, *rest)


def everywhere(sums):
    sums = to_chips(sums)
    return [to_core(sums, r) for r in range(lax.axis_size("gz"))]


def shards(data, band_offset, interp_weight):
    gz = lax.axis_size("gz")
    gy = lax.axis_size("gy")
    devices = gz * gy
    data = data[0]
    blocks, ny, width = data.shape
    rows = ny // devices
    ka = blocks * HALF
    nx = ka * gy

    core = lax.axis_index("gz")
    flat = lax.axis_index("gy") * gz + core
    edge = jnp.stack([flat == 0, flat == devices - 1, core]).astype(jnp.int32)
    order = [(i % gz) * gy + i // gz for i in range(devices)]
    up = [(order[i + 1], order[i]) for i in range(devices - 1)]
    down = [(order[i], order[i + 1]) for i in range(devices - 1)]

    lower = band_offset < 0
    weight = interp_weight
    coef = jnp.stack(
        [
            jnp.where(lower, weight[1], weight[0]),
            jnp.where(lower, weight[0], 0.0),
            jnp.where(lower, 0.0, weight[1]),
        ]
    ).reshape(3, gy, 1, ka)
    coef = jnp.broadcast_to(coef, (3, gy, 8, ka))

    spec = to_devices(y_inverse(data, rows, gz, gy))
    d0, head, tail, first = middle(spec, coef, nx)
    next_head = lax.ppermute(head, ("gz", "gy"), up)
    prev_tail = lax.ppermute(tail, ("gz", "gy"), down)
    nd0 = normal_product(first, coef, nx)
    sums = to_chips(border_sums(edge, head, tail, next_head, prev_tail, nd0, gy))
    d1, eta, sums, second = second_descent(
        edge, sums, d0, nd0, tail, prev_tail, next_head, coef, gz, nx
    )
    sums = everywhere(sums)
    flat_shape = (devices, 2, rows, ka)
    spec, etas = combine_spectra(eta, sums, first.reshape(flat_shape), second.reshape(flat_shape))
    residual = y_forward(to_devices(spec.reshape(gz, gy, 2, rows, ka)), data)

    volume = -(etas[0, 0, 0] * d0 + etas[1, 0, 0] * d1)
    volume = volume.reshape(gz, gy, rows, ka).transpose(0, 2, 3, 1).reshape(gz, rows, nx)
    parts = [
        to_core(lax.dynamic_index_in_dim(volume, lax.rem(core + r, gz), 0, False), r)
        for r in range(gz)
    ]
    volume = jnp.zeros((gz, rows, nx), F32)
    for r, part in enumerate(parts):
        volume = lax.dynamic_update_index_in_dim(volume, part, lax.rem(core + gz - r, gz), 0)
    return (volume.reshape(1, gz * rows, nx), residual[None])


NX = 4096
NY = 2048
XB = 64
YB = 64
ITERS = 2
XA = 64
YA = 32
PRECISE = lax.Precision.HIGHEST


def with_halo(block, sides, width):
    for axis, dim in sides:
        count = lax.axis_size(axis)
        forward = [(i, i + 1) for i in range(count - 1)]
        backward = [(target, source) for source, target in forward]
        low = lax.ppermute(
            lax.slice_in_dim(block, block.shape[dim] - width, None, axis=dim), axis, forward
        )
        high = lax.ppermute(lax.slice_in_dim(block, 0, width, axis=dim), axis, backward)
        block = jnp.concatenate([low, block, high], axis=dim)
    return block


def from_behind(block, axis, distance):
    devices = range(lax.axis_size(axis))
    route = [(i - distance, i) for i in devices if i - distance in devices]
    return lax.ppermute(block, axis, route)


def unit_table(length):
    counter = jnp.arange(length, dtype=jnp.int32)
    phase_int = counter[:, None] * counter[None, :] % length
    angles = 2.0 * jnp.pi / length * phase_int.astype(jnp.float32)
    factor = length ** (-0.5)
    return (jnp.cos(angles) * factor, jnp.sin(angles) * factor)


def twiddle_table(row_len, col_len, period):
    phase_int = (
        jnp.arange(row_len, dtype=jnp.int32)[:, None]
        * jnp.arange(col_len, dtype=jnp.int32)[None, :]
        % period
    )
    angles = 2.0 * jnp.pi / period * phase_int.astype(jnp.float32)
    return (jnp.cos(angles), jnp.sin(angles))


def split_parts(packed):
    half_width = packed.shape[-1] // 2
    return (packed[..., :half_width], packed[..., half_width:])


def join_parts(real_part, imag_part):
    return jnp.concatenate([real_part, imag_part], axis=-1)


def complex_contract(packed, cos_table, sin_table, subscripts, conj_sign):
    cos_out = jnp.einsum(subscripts, packed, cos_table, precision=PRECISE)
    sin_out = jnp.einsum(subscripts, packed, sin_table, precision=PRECISE)
    cos_re, cos_im = split_parts(cos_out)
    sin_re, sin_im = split_parts(sin_out)
    return join_parts(cos_re - conj_sign * sin_im, cos_im + conj_sign * sin_re)


def rotate(packed, cos_table, sin_table, conj_sign):
    real_part, imag_part = split_parts(packed)
    return join_parts(
        real_part * cos_table - conj_sign * imag_part * sin_table,
        imag_part * cos_table + conj_sign * real_part * sin_table,
    )


def forward_x(volume):
    slices, row_count = (volume.shape[0], volume.shape[1])
    cos_a, sin_a = unit_table(XA)
    cos_b, sin_b = unit_table(XB)
    first_table = jnp.concatenate([cos_a, -sin_a], axis=1)
    grid_view = volume.reshape(slices, row_count, XA, XB)
    mixing = jnp.einsum("zyab,am->zybm", grid_view, first_table, precision=PRECISE)
    tw_cos, tw_sin = twiddle_table(XB, XA, NX)
    mixing = rotate(mixing, tw_cos, tw_sin, -1.0)
    return complex_contract(mixing, cos_b, sin_b, "zybm,bl->zlym", -1.0)


def inverse_x(packed):
    slices, row_count = (packed.shape[0], packed.shape[2])
    cos_a, sin_a = unit_table(XA)
    cos_b, sin_b = unit_table(XB)
    mixing = complex_contract(packed, cos_b, sin_b, "zlym,lb->zybm", 1.0)
    tw_cos, tw_sin = twiddle_table(XB, XA, NX)
    mixing = rotate(mixing, tw_cos, tw_sin, 1.0)
    last_table = jnp.concatenate([cos_a, -sin_a], axis=0)
    grid_view = jnp.einsum("zybm,ma->zyab", mixing, last_table, precision=PRECISE)
    return grid_view.reshape(slices, row_count, NX)


def forward_y(packed):
    slices, blocks, width = (packed.shape[0], packed.shape[1], packed.shape[3])
    cos_a, sin_a = unit_table(YA)
    cos_b, sin_b = unit_table(YB)
    grid_view = packed.reshape(slices, blocks, YA, YB, width)
    mixing = complex_contract(grid_view, cos_a, sin_a, "zjcdm,ck->zjkdm", -1.0)
    tw_cos, tw_sin = twiddle_table(YA, YB, NY)
    mixing = rotate(mixing, tw_cos[:, :, None], tw_sin[:, :, None], -1.0)
    result = complex_contract(mixing, cos_b, sin_b, "zjkdm,dl->zjlkm", -1.0)
    return result.reshape(slices, blocks, NY, width)


def inverse_y(packed):
    slices, blocks, width = (packed.shape[0], packed.shape[1], packed.shape[3])
    cos_a, sin_a = unit_table(YA)
    cos_b, sin_b = unit_table(YB)
    grid_view = packed.reshape(slices, blocks, YB, YA, width)
    mixing = complex_contract(grid_view, cos_b, sin_b, "zjlkm,ld->zjkdm", 1.0)
    tw_cos, tw_sin = twiddle_table(YA, YB, NY)
    mixing = rotate(mixing, tw_cos[:, :, None], tw_sin[:, :, None], 1.0)
    result = complex_contract(mixing, cos_a, sin_a, "zjkdm,kc->zjcdm", 1.0)
    return result.reshape(slices, blocks, NY, width)


def tilt_coefficients(band_offset, interp_weight, first_block, blocks):
    offsets = lax.dynamic_slice_in_dim(band_offset.reshape(XB, XA), first_block, blocks, 0)
    weights = lax.dynamic_slice_in_dim(interp_weight.reshape(2, XB, XA), first_block, blocks, 1)
    lower_tap = (jnp.concatenate([offsets, offsets], axis=1) < 0)[:, None, :]
    first_weight = jnp.concatenate([weights[0], weights[0]], axis=1)[:, None, :]
    second_weight = jnp.concatenate([weights[1], weights[1]], axis=1)[:, None, :]
    return (lower_tap, first_weight, second_weight)


def tilt(field_in, coefficients, adjoint):
    lower_tap, first_weight, second_weight = coefficients
    padded = with_halo(field_in, (("gz", 0),), 1)
    below_rim = padded[:-2]
    middle = padded[1:-1]
    above_rim = padded[2:]
    if adjoint:
        return jnp.where(
            lower_tap,
            first_weight * above_rim + second_weight * middle,
            first_weight * middle + second_weight * below_rim,
        )
    return jnp.where(
        lower_tap,
        first_weight * below_rim + second_weight * middle,
        first_weight * middle + second_weight * above_rim,
    )


def to_pencil(slab_part):
    return lax.all_to_all(slab_part, "gy", split_axis=1, concat_axis=2, tiled=True)


def to_slab(pencil_part):
    return lax.all_to_all(pencil_part, "gy", split_axis=2, concat_axis=1, tiled=True)


def back_project(packed, pencil_coef):
    return inverse_x(to_slab(inverse_y(tilt(packed, pencil_coef, True))))


def edge_masks(slices, row_count):
    z_global = lax.axis_index("gz") * slices + jnp.arange(slices, dtype=jnp.int32)
    y_global = lax.axis_index("gy") * row_count + jnp.arange(row_count, dtype=jnp.int32)
    keep_z = (z_global < slices * lax.axis_size("gz") - 1).astype(jnp.float32)[:, None, None]
    keep_y = (y_global < row_count * lax.axis_size("gy") - 1).astype(jnp.float32)[None, :, None]
    return (keep_z, keep_y)


def forward_diff(field_in, keep_z, keep_y):
    slices, row_count = (field_in.shape[0], field_in.shape[1])
    next_z = from_behind(field_in, "gz", -1)
    next_y = from_behind(field_in[:, :1], "gy", -1)
    along_z = (jnp.concatenate([field_in[1:], next_z], axis=0) - field_in) * keep_z
    along_y = (jnp.concatenate([field_in[:, 1:], next_y], axis=1) - field_in) * keep_y
    zero_col = jnp.zeros((slices, row_count, 1), jnp.float32)
    along_x = jnp.concatenate([field_in[:, :, 1:] - field_in[:, :, :-1], zero_col], axis=2)
    return jnp.stack([along_z, along_y, along_x])


def transpose_diff(components, keep_z, keep_y):
    slices, row_count = (components.shape[1], components.shape[2])
    zero_col = jnp.zeros((slices, row_count, 1), jnp.float32)
    comp_z = components[0] * keep_z
    comp_y = components[1] * keep_y
    comp_x = jnp.concatenate([components[2][:, :, :-1], zero_col], axis=2)
    prev_z = from_behind(comp_z, "gz", 1)
    prev_y = from_behind(comp_y[:, -1:], "gy", 1)
    result = jnp.concatenate([prev_z, comp_z[:-1]], axis=0) - comp_z
    result = result + jnp.concatenate([prev_y, comp_y[:, :-1]], axis=1) - comp_y
    result = result + jnp.concatenate([zero_col, comp_x[:, :, :-1]], axis=2) - comp_x
    return result


def plain_shards(data, band_offset, interp_weight):
    slices = data.shape[0]
    blocks = data.shape[1]
    width = data.shape[3]
    row_count = NY // lax.axis_size("gy")
    slab_coef = tilt_coefficients(band_offset, interp_weight, 0, XB)
    pencil_coef = tilt_coefficients(
        band_offset, interp_weight, lax.axis_index("gy") * blocks, blocks
    )
    keep_z, keep_y = edge_masks(slices, row_count)
    measured = data.astype(jnp.float32)
    volume = jnp.zeros((slices, row_count, NX), jnp.float32)
    grad_volume = jnp.zeros((3, slices, row_count, NX), jnp.float32)
    split_var = grad_volume
    dual_var = grad_volume
    data_back = back_project(measured, pencil_coef)
    normal_part = jnp.zeros_like(volume)
    tilted = jnp.zeros((slices, XB, row_count, width), jnp.float32)
    for iteration in range(ITERS):
        data_grad = normal_part - data_back
        if iteration > 0:
            tv_gap = grad_volume - split_var + dual_var / PENALTY
            descent = data_grad + PENALTY * transpose_diff(tv_gap, keep_z, keep_y)
        else:
            descent = data_grad
        slope_field = forward_diff(descent, keep_z, keep_y)
        projected = tilt(forward_x(descent), slab_coef, False)
        line_totals = lax.psum(
            (
                jnp.sum(descent * descent),
                jnp.sum(projected * projected),
                jnp.sum(slope_field * slope_field),
            ),
            ("gz", "gy"),
        )
        step_length = line_totals[0] / (line_totals[1] + PENALTY * line_totals[2])
        volume = volume - step_length * descent
        grad_volume = grad_volume - step_length * slope_field
        tilted = tilted - step_length * projected
        if iteration + 1 < ITERS:
            normal_part = normal_part - step_length * inverse_x(tilt(projected, slab_coef, True))
        if iteration + 1 < ITERS:
            shifted = grad_volume + dual_var / PENALTY
            split_var = shifted - jnp.clip(shifted, -TV_WEIGHT / PENALTY, TV_WEIGHT / PENALTY)
            dual_var = PENALTY * (grad_volume - split_var)
    residual = forward_y(to_pencil(tilted)) - measured
    return (volume, residual)


def tiles_fit(mesh, ny, blocks):
    rows = ny // (mesh.shape["gz"] * mesh.shape["gy"])
    return mesh.shape["gz"] == 2 and rows % 16 == 0 and mesh.shape["gy"] % YR == 0 and blocks // mesh.shape["gy"] % 2 == 0


def solution(mesh):
    in_specs = (P("gz", "gy", None, None), P(), P())
    out_specs = (P("gz", "gy", None), P("gz", "gy", None, None))

    def run(data, band_offset, interp_weight):
        body = shards if tiles_fit(mesh, data.shape[2], data.shape[1]) else plain_shards
        call = jax.shard_map(
            body, mesh=mesh, in_specs=in_specs, out_specs=out_specs, check_vma=False
        )
        return call(data, band_offset, interp_weight)

    return run
```

```python
import functools

import jax
import jax.numpy as jnp
import numpy as np
from jax import lax
from jax.experimental import pallas as pl
from jax.experimental.pallas import tpu as pltpu
from jax.sharding import PartitionSpec as P

PENALTY = 0.5
TV_WEIGHT = 0.25
CLIP = TV_WEIGHT / PENALTY
HALF = 64
YR = 8
LANES = 128
F32 = jnp.float32
BF16 = jnp.bfloat16
MIB = 1024 * 1024
Y_GRANT = 56 * MIB
X_GRANT = 20 * MIB


def dft_parts(length, scale):
    index = np.arange(length)
    angles = 2.0 * np.pi / length * (index[:, None] * index[None, :] % length)
    return np.cos(angles) * scale, np.sin(angles) * scale


def host_parts(table):
    table = table.astype(np.float32)
    high = table.astype(BF16)
    low = (table - high.astype(np.float32)).astype(BF16)
    return high, low


def y_matrix(ny, forward, sign):
    n = ny // YR
    cos, sin = dft_parts(n, sign * ny**-0.5)
    if forward:
        table = np.block([[cos, sin], [-sin, cos]])
    else:
        table = np.block([[cos, -sin], [sin, cos]])
    return jnp.asarray(np.concatenate(host_parts(table), axis=0))


def y_twiddle(ny):
    n = ny // YR
    angles = 2.0 * np.pi / ny * (np.arange(1, YR)[:, None] * np.arange(n)[None, :])
    table = np.stack([np.cos(angles), np.sin(angles)]).astype(np.float32)
    return jnp.asarray(np.ascontiguousarray(np.broadcast_to(table[..., None], (2, YR - 1, n, LANES))))


def x_inverse_matrix(nx, ka):
    cos, sin = dft_parts(ka, nx**-0.5)
    return np.concatenate(host_parts(np.concatenate([cos, -sin], axis=0)), axis=1)


def x_forward_matrix(nx, ka):
    cos, sin = dft_parts(ka, nx**-0.5)
    return jnp.asarray(np.concatenate(host_parts(np.concatenate([cos, -sin], axis=1)), axis=1))


def x_twiddle(nx, ka):
    kb = nx // ka
    angles = 2.0 * np.pi / nx * (np.arange(kb)[:, None] * np.arange(ka)[None, :])
    table = np.stack([np.cos(angles), np.sin(angles)]).astype(np.float32)
    return jnp.asarray(np.ascontiguousarray(np.broadcast_to(table[:, :, None], (2, kb, 8, ka))))


def short_fft(planes, sign):
    n = len(planes)
    if n == 1:
        return planes
    even = short_fft(planes[0::2], sign)
    odd = short_fft(planes[1::2], sign)
    half = n // 2
    out = [None] * n
    for k in range(half):
        er, ei = even[k]
        tr, ti = odd[k]
        if 4 * k == n:
            if sign > 0:
                out[k] = (er - ti, ei + tr)
                out[k + half] = (er + ti, ei - tr)
            else:
                out[k] = (er + ti, ei - tr)
                out[k + half] = (er - ti, ei + tr)
            continue
        if k > 0:
            c = float(np.cos(2.0 * np.pi * k / n))
            s = float(sign * np.sin(2.0 * np.pi * k / n))
            if 8 * k == n:
                tr, ti = (tr - ti, ti + tr) if sign > 0 else (tr + ti, ti - tr)
                tr, ti = tr * c, ti * c
            elif 8 * k == 3 * n:
                m = float(np.sin(2.0 * np.pi * k / n))
                tr, ti = (-(tr + ti), tr - ti) if sign > 0 else (ti - tr, -(tr + ti))
                tr, ti = tr * m, ti * m
            else:
                tr, ti = tr * c - ti * s, ti * c + tr * s
        out[k] = (er + tr, ei + ti)
        out[k + half] = (er - tr, ei - ti)
    return out


def split2(x):
    high = x.astype(BF16)
    return high, (x - high.astype(F32)).astype(BF16)


def dot(a, b):
    return jnp.dot(a, b, preferred_element_type=F32)


def fold(x):
    rows, lanes = x.shape
    x = jnp.sum(x.reshape(rows // 8, 8, lanes), axis=0)
    total = x[:, :LANES]
    for i in range(1, lanes // LANES):
        total = total + x[:, i * LANES : (i + 1) * LANES]
    return total


def full_sum(x):
    return jnp.sum(jnp.sum(x, axis=0, keepdims=True), axis=1, keepdims=True)


def step_of(sums_refs):
    total = sum(jnp.sum(sums_ref[...], axis=0) for sums_ref in sums_refs)
    parts = jnp.sum(total, axis=1, keepdims=True)
    return parts[0:1] / (parts[1:2] + PENALTY * parts[2:3])


def sums_block(values):
    rows = [jnp.sum(v, axis=0, keepdims=True) for v in values]
    index = lax.broadcasted_iota(jnp.int32, (8, LANES), 0)
    block = jnp.zeros((8, LANES), F32)
    for i, row in enumerate(rows):
        block = jnp.where(index == i, jnp.broadcast_to(row, (8, LANES)), block)
    return block


def put_copies(out_ref, block):
    for i in range(out_ref.shape[0]):
        out_ref[i] = block


def mix_adjoint(coef, planes):
    own, below, above = coef
    out = []
    for z in range(len(planes)):
        value = own * planes[z]
        if z + 1 < len(planes):
            value = value + below * planes[z + 1]
        if z > 0:
            value = value + above * planes[z - 1]
        out.append(value)
    return out


def mix(coef, planes):
    own, below, above = coef
    out = []
    for z in range(len(planes)):
        value = own * planes[z]
        if z > 0:
            value = value + below * planes[z - 1]
        if z + 1 < len(planes):
            value = value + above * planes[z + 1]
        out.append(value)
    return out


def y_inverse_kernel(
    data_hbm, table_hbm, tw_hbm, out_hbm,
    data_ref, table_ref, tw_ref, out_ref, re_s, im_s, mix_s, sems, out_sems,
):
    blocks, ny, _ = data_ref.shape
    n = ny // YR
    gz, _, _, _, rows, _ = out_ref.shape
    lane = lax.broadcasted_iota(jnp.int32, (n, LANES), 1)
    pairs = blocks // 2

    def fetch(chunk):
        part = pl.ds(2 * chunk, 2)
        return pltpu.make_async_copy(data_hbm.at[part], data_ref.at[part], sems.at[2 + chunk])

    def give(chunk, core):
        at = (core, slice(None), chunk)
        return pltpu.make_async_copy(out_ref.at[at], out_hbm.at[at], out_sems.at[chunk * gz + core])

    fetch_table = pltpu.make_async_copy(table_hbm, table_ref, sems.at[0])
    fetch_tw = pltpu.make_async_copy(tw_hbm, tw_ref, sems.at[1])
    fetch(0).start()
    fetch_table.start()
    fetch_tw.start()
    for chunk in range(1, pairs):
        fetch(chunk).start()

    for chunk in range(pairs):
        fetch(chunk).wait()

        def unpack(i, carry):
            part = pl.ds(pl.multiple_of(i * n, n), n)
            first = data_ref[2 * chunk, part, :].astype(F32)
            second = data_ref[2 * chunk + 1, part, :].astype(F32)
            re_s[part, :] = jnp.where(lane < HALF, first, pltpu.roll(second, HALF, 1))
            im_s[part, :] = jnp.where(lane < HALF, pltpu.roll(first, HALF, 1), second)
            return carry

        lax.fori_loop(0, YR, unpack, 0)
        if chunk == 0:
            fetch_table.wait()

        for k in range(0, YR, 2):
            pieces = [
                jnp.concatenate([s[pl.ds(k + d, n, stride=YR), :] for d in range(2)], axis=1)
                for s in (re_s, im_s)
            ]
            both = dot(table_ref[...], jnp.concatenate(pieces, axis=0).astype(BF16))
            both = both[: 2 * n] + both[2 * n :]
            for d in range(2):
                mix_s[k + d] = both[:, d * LANES : (d + 1) * LANES]

        if chunk == 0:
            fetch_tw.wait()

        tiles = rows // 8
        for core in range(gz):

            def combine(i, carry):
                y2 = ((i // tiles) * gz + core) * rows + lax.rem(i, tiles) * 8
                part = pl.ds(pl.multiple_of(y2, 8), 8)
                planes = []
                for k in range(YR):
                    re = mix_s[k, part, :]
                    im = mix_s[k, pl.ds(pl.multiple_of(n + y2, 8), 8), :]
                    if k > 0:
                        c = tw_ref[0, k - 1, part, :]
                        s = tw_ref[1, k - 1, part, :]
                        re, im = re * c - im * s, im * c + re * s
                    planes.append((re, im))
                at = pl.ds(pl.multiple_of(lax.rem(i, tiles) * 8, 8), 8)
                for k, (re, im) in enumerate(short_fft(planes, 1)):
                    to = k * (n // (gz * rows)) + i // tiles
                    out_ref[core, to, chunk, 0, at, :] = re
                    out_ref[core, to, chunk, 1, at, :] = im
                return carry

            lax.fori_loop(0, n // gz // 8, combine, 0, unroll=2)
            give(chunk, core).start()

    for chunk in range(pairs):
        for core in range(gz):
            give(chunk, core).wait()


def y_inverse(data, rows, gz, gy):
    blocks, ny, width = data.shape
    n = ny // YR
    shape = (gz, gy, blocks // 2, 2, rows, LANES)
    hbm = pl.BlockSpec(memory_space=pltpu.HBM)
    return pl.pallas_call(
        y_inverse_kernel,
        in_specs=[hbm] * 3,
        out_specs=hbm,
        out_shape=jax.ShapeDtypeStruct(shape, F32),
        scratch_shapes=[
            pltpu.VMEM((blocks, ny, width), BF16),
            pltpu.VMEM((4 * n, 2 * n), BF16),
            pltpu.VMEM((2, YR - 1, n, LANES), F32),
            pltpu.VMEM(shape, F32),
            pltpu.VMEM((ny, LANES), F32),
            pltpu.VMEM((ny, LANES), F32),
            pltpu.VMEM((YR, 2 * n, LANES), F32),
            pltpu.SemaphoreType.DMA((2 + blocks // 2,)),
            pltpu.SemaphoreType.DMA((blocks // 2 * gz,)),
        ],
        compiler_params=pltpu.CompilerParams(vmem_limit_bytes=Y_GRANT),
        name="y_inverse",
    )(data, y_matrix(ny, False, -1.0), y_twiddle(ny))


def y_forward_kernel(
    spec_hbm, data_hbm, table_hbm, tw_hbm, out_hbm,
    spec_ref, data_ref, table_ref, tw_ref, out_ref, mix_s, sems, spec_sems, out_sems,
):
    blocks, ny, _ = data_ref.shape
    n = ny // YR
    _, gz, gy, _, rows, _ = spec_ref.shape
    pairs = blocks // 2
    half = n // 2

    def fetch(chunk):
        return pltpu.make_async_copy(
            spec_hbm.at[:, :, chunk], spec_ref.at[chunk], spec_sems.at[chunk]
        )

    def give(chunk, part):
        at = (pl.ds(2 * chunk, 2), slice(None), pl.ds(part * half, half))
        return pltpu.make_async_copy(out_ref.at[at], out_hbm.at[at], out_sems.at[2 * chunk + part])

    fetch_table = pltpu.make_async_copy(table_hbm, table_ref, sems.at[0])
    fetch_tw = pltpu.make_async_copy(tw_hbm, tw_ref, sems.at[1])
    fetch_data = pltpu.make_async_copy(data_hbm, data_ref, sems.at[2])
    fetch(0).start()
    fetch_table.start()
    fetch_tw.start()
    fetch_data.start()
    for chunk in range(1, pairs):
        fetch(chunk).start()

    def rows_of(chunk, p, k):
        part = pl.ds(k, rows // YR, stride=YR)
        return jnp.concatenate(
            [spec_ref[chunk, core, i, p, part, :] for i in range(gy) for core in range(gz)], axis=0
        )

    lane = lax.broadcasted_iota(jnp.int32, (16, LANES), 1)
    for chunk in range(pairs):
        fetch(chunk).wait()

        if chunk == 0:
            fetch_table.wait()

        for k in range(0, YR, 2):
            pieces = [
                jnp.concatenate([rows_of(chunk, p, k + d) for d in range(2)], axis=1)
                for p in range(2)
            ]
            high, low = split2(jnp.concatenate(pieces, axis=0))
            both = dot(table_ref[...], high)
            both = both[: 2 * n] + both[2 * n :] + dot(table_ref[: 2 * n], low)
            for d in range(2):
                mix_s[k + d] = both[:, d * LANES : (d + 1) * LANES]
        if chunk == 0:
            fetch_tw.wait()
            fetch_data.wait()

        def combine(i, carry):
            start = pl.multiple_of(i * 16, 16)
            part = pl.ds(start, 16)
            planes = []
            for k in range(YR):
                re = mix_s[k, part, :]
                im = mix_s[k, pl.ds(pl.multiple_of(n + i * 16, 16), 16), :]
                if k > 0:
                    c = tw_ref[0, k - 1, part, :]
                    s = tw_ref[1, k - 1, part, :]
                    re, im = re * c + im * s, im * c - re * s
                planes.append((re, im))
            for k, (re, im) in enumerate(short_fft(planes, -1)):
                at = pl.ds(pl.multiple_of(k * n + start, 16), 16)
                first = jnp.where(lane < HALF, re, pltpu.roll(im, HALF, 1))
                second = jnp.where(lane < HALF, pltpu.roll(re, HALF, 1), im)
                out_ref[2 * chunk, k, part, :] = first - data_ref[2 * chunk, at, :].astype(F32)
                out_ref[2 * chunk + 1, k, part, :] = (
                    second - data_ref[2 * chunk + 1, at, :].astype(F32)
                )
            return carry

        for part in range(2):
            lax.fori_loop(part * half // 16, (part + 1) * half // 16, combine, 0)
            give(chunk, part).start()

    for chunk in range(pairs):
        for part in range(2):
            give(chunk, part).wait()


def y_forward(spec, data):
    blocks, ny, width = data.shape
    n = ny // YR
    hbm = pl.BlockSpec(memory_space=pltpu.HBM)
    out = pl.pallas_call(
        y_forward_kernel,
        in_specs=[hbm] * 4,
        out_specs=hbm,
        out_shape=jax.ShapeDtypeStruct((blocks, YR, n, width), F32),
        scratch_shapes=[
            pltpu.VMEM((blocks // 2, *spec.shape[:2], *spec.shape[3:]), F32),
            pltpu.VMEM((blocks, ny, width), BF16),
            pltpu.VMEM((4 * n, 2 * n), BF16),
            pltpu.VMEM((2, YR - 1, n, LANES), F32),
            pltpu.VMEM((blocks, YR, n, width), F32),
            pltpu.VMEM((YR, 2 * n, LANES), F32),
            pltpu.SemaphoreType.DMA((3,)),
            pltpu.SemaphoreType.DMA((blocks // 2,)),
            pltpu.SemaphoreType.DMA((blocks,)),
        ],
        compiler_params=pltpu.CompilerParams(vmem_limit_bytes=Y_GRANT),
        name="y_forward",
    )(spec, data, y_matrix(ny, True, 1.0), y_twiddle(ny))
    return out.reshape(blocks, ny, width)


def plane_chunk(planes, rows):
    chunk = max(1, 1024 // rows)
    while planes % chunk:
        chunk -= 1
    return chunk


def turn_rows(kb, planes_of, tw_ref, lanes, sign):
    out = []
    for b in range(kb):
        re, im = planes_of(b)
        if b > 0:
            c = tw_ref[0, b, :, lanes]
            s = tw_ref[1, b, :, lanes]
            if sign > 0:
                re, im = re * c - im * s, im * c + re * s
            else:
                re, im = re * c + im * s, im * c - re * s
        out.append((re, im))
    return out


def inverse_columns(gz, kb, spectra, coef_ref, tw_ref, lanes, part, re_s, im_s):
    mixed = [[None] * kb for _ in range(gz)]
    for k in range(kb):
        coef = [coef_ref[j, k, :, lanes] for j in range(3)]
        re = mix_adjoint(coef, [spectra[z][k][0] for z in range(gz)])
        im = mix_adjoint(coef, [spectra[z][k][1] for z in range(gz)])
        for z in range(gz):
            mixed[z][k] = (re[z], im[z])
    for z in range(gz):
        short = short_fft(mixed[z], 1)
        for b, (re, im) in enumerate(turn_rows(kb, lambda b: short[b], tw_ref, lanes, 1)):
            re_s[z * kb + b, part, lanes] = re
            im_s[z * kb + b, part, lanes] = im


def forward_columns(gz, kb, coef_ref, tw_ref, lanes, part, re_s, im_s):
    spectra = []
    for z in range(gz):
        rows_of = lambda b: (re_s[z * kb + b, part, lanes], im_s[z * kb + b, part, lanes])
        spectra.append(short_fft(turn_rows(kb, rows_of, tw_ref, lanes, -1), -1))
    out = [[None] * kb for _ in range(gz)]
    for k in range(kb):
        coef = [coef_ref[j, k, :, lanes] for j in range(3)]
        re = mix(coef, [spectra[z][k][0] for z in range(gz)])
        im = mix(coef, [spectra[z][k][1] for z in range(gz)])
        for z in range(gz):
            out[z][k] = (re[z], im[z])
    return out


def inverse_product(re, im, table_ref):
    ka = re.shape[1]
    high, low = split2(jnp.concatenate([re, im], axis=1))
    value = dot(high, table_ref[...])
    return value[:, :ka] + value[:, ka:] + dot(low, table_ref[:, :ka])


def forward_product(field, table_ref):
    ka = field.shape[1]
    high, low = split2(field)
    value = dot(high, table_ref[...])
    value = value[:, : 2 * ka] + value[:, 2 * ka :] + dot(low, table_ref[:, : 2 * ka])
    return value[:, :ka], value[:, ka:]


def next_plane(field_ref, p, kb):
    rows, ka = field_ref.shape[1:]
    if (p + 1) % kb:
        return field_ref[p + 1]
    lane = lax.broadcasted_iota(jnp.int32, (rows, ka), 1)
    return jnp.where(lane == ka - 1, field_ref[p], pltpu.roll(field_ref[p + 1 - kb], ka - 1, 1))


def prev_plane(field_ref, p, kb):
    rows, ka = field_ref.shape[1:]
    if p % kb:
        return field_ref[p - 1]
    lane = lax.broadcasted_iota(jnp.int32, (rows, ka), 1)
    return jnp.where(lane == 0, field_ref[p], pltpu.roll(field_ref[p + kb - 1], 1, 1))


def first_kernel(
    gz, edge_ref, field_ref, coef_ref, tw_ref, table_ref, sums_ref, spec_ref, *refs
):
    piece_refs, (re_s, im_s) = refs[:-2], refs[-2:]
    planes, rows, ka = field_ref.shape
    kb = planes // gz
    projected = forward_into(gz, field_ref, coef_ref, tw_ref, table_ref, spec_ref, re_s, im_s)
    cut(gz, edge_ref, spec_ref, piece_refs)
    row = lax.broadcasted_iota(jnp.int32, (rows, ka), 0)
    square = jnp.zeros((8, LANES), F32)
    slope = jnp.zeros((8, LANES), F32)
    for p in range(planes):
        here = field_ref[p]
        square = square + fold(here * here)
        along_x = next_plane(field_ref, p, kb) - here
        along_y = jnp.where(row == rows - 1, 0.0, pltpu.roll(here, rows - 1, 0) - here)
        terms = along_x * along_x + along_y * along_y
        if p + kb < planes:
            along_z = field_ref[p + kb] - here
            terms = terms + along_z * along_z
        slope = slope + fold(terms)
    sums_ref[0] = square
    sums_ref[1] = projected
    sums_ref[2] = slope


def columns_back(spec_ref, chunk, coef_ref, tw_ref, re_s, im_s, j, carry):
    gz, kb = spec_ref.shape[:2]
    lanes = slice(chunk * LANES, (chunk + 1) * LANES)
    part = pl.ds(pl.multiple_of(j * 8, 8), 8)
    spectra = [
        [(spec_ref[z, k, chunk, 0, part, :], spec_ref[z, k, chunk, 1, part, :]) for k in range(kb)]
        for z in range(gz)
    ]
    inverse_columns(gz, kb, spectra, coef_ref, tw_ref, lanes, part, re_s, im_s)
    return carry


def middle_kernel(
    spec_hbm, coef_ref, tw_ref, inverse_ref, forward_ref,
    d0_ref, head_ref, tail_ref, spec_ref, re_s, im_s, sems,
):
    gz, kb, chunks, _, rows, _ = spec_ref.shape
    ka = chunks * LANES
    planes = gz * kb

    def fetch(chunk):
        return pltpu.make_async_copy(
            spec_hbm.at[:, :, chunk], spec_ref.at[:, :, chunk], sems.at[chunk]
        )

    for chunk in range(chunks):
        fetch(chunk).start()
    for chunk in range(chunks):
        fetch(chunk).wait()
        lax.fori_loop(
            0, rows // 8,
            functools.partial(columns_back, spec_ref, chunk, coef_ref, tw_ref, re_s, im_s), 0,
        )

    step = plane_chunk(planes, rows)
    shape2, shape3 = (step * rows, ka), (step, rows, ka)

    def there_and_back(i, carry):
        part = pl.ds(i * step, step)
        field = inverse_product(re_s[part].reshape(shape2), im_s[part].reshape(shape2), inverse_ref)
        d0_ref[part] = field.reshape(shape3)
        re, im = forward_product(field, forward_ref)
        re_s[part] = re.reshape(shape3)
        im_s[part] = im.reshape(shape3)
        return carry

    lax.fori_loop(0, planes // step, there_and_back, 0)

    def second_columns(j, total):
        part = pl.ds(pl.multiple_of(j * 8, 8), 8)
        for chunk in range(chunks):
            lanes = slice(chunk * LANES, (chunk + 1) * LANES)
            spectra = forward_columns(gz, kb, coef_ref, tw_ref, lanes, part, re_s, im_s)
            for z in range(gz):
                for k in range(kb):
                    for p in range(2):
                        value = spectra[z][k][p]
                        spec_ref[z, k, chunk, p, part, :] = value
                        total = total + value * value
        return total

    projected = lax.fori_loop(0, rows // 8, second_columns, jnp.zeros((8, LANES), F32))
    for p in range(planes):
        head_ref[p : p + 1, :] = d0_ref[p, :1, :]
        head_ref[planes + p : planes + p + 1, :] = d0_ref[p, 1:2, :]
        for part in range(2):
            at = 2 * planes + 2 * p + part
            for chunk in range(chunks):
                lanes = slice(chunk * LANES, (chunk + 1) * LANES)
                head_ref[at : at + 1, lanes] = spec_ref[p // kb, p % kb, chunk, part, :1, :]
        tail_ref[p : p + 1, :] = d0_ref[p, rows - 1 : rows, :]

    row = lax.broadcasted_iota(jnp.int32, (rows, ka), 0)
    square = jnp.zeros((8, LANES), F32)
    slope = jnp.zeros((8, LANES), F32)
    for p in range(planes):
        here = d0_ref[p]
        square = square + fold(here * here)
        along_x = next_plane(d0_ref, p, kb) - here
        along_y = jnp.where(row == rows - 1, 0.0, pltpu.roll(here, rows - 1, 0) - here)
        terms = along_x * along_x + along_y * along_y
        if p + kb < planes:
            along_z = d0_ref[p + kb] - here
            terms = terms + along_z * along_z
        slope = slope + fold(terms)
    block = sums_block([square, projected, slope])
    for ref in (head_ref, tail_ref):
        at = ref.shape[0] - 8
        ref[at:, :] = jnp.zeros((8, ka), F32)
        ref[at:, :LANES] = block


def middle(spec, coef, nx):
    gz, kb, chunks, _, rows, _ = spec.shape
    ka = chunks * LANES
    planes = gz * kb
    vmem = pl.BlockSpec(memory_space=pltpu.VMEM)
    field = jax.ShapeDtypeStruct((planes, rows, ka), F32)
    return pl.pallas_call(
        middle_kernel,
        in_specs=[pl.BlockSpec(memory_space=pltpu.HBM)] + [vmem] * 4,
        out_specs=[vmem] * 4,
        out_shape=[
            field,
            jax.ShapeDtypeStruct((4 * planes + 8, ka), F32),
            jax.ShapeDtypeStruct((planes + 8, ka), F32),
            jax.ShapeDtypeStruct(spec.shape, F32),
        ],
        scratch_shapes=[
            pltpu.VMEM((planes, rows, ka), F32),
            pltpu.VMEM((planes, rows, ka), F32),
            pltpu.SemaphoreType.DMA((chunks,)),
        ],
        compiler_params=pltpu.CompilerParams(vmem_limit_bytes=X_GRANT),
        name="middle",
    )(
        spec, coef, x_twiddle(nx, ka), jnp.asarray(x_inverse_matrix(nx, ka)),
        x_forward_matrix(nx, ka),
    )


def normal_kernel(spec_ref, coef_ref, tw_ref, table_ref, out_ref, re_s, im_s):
    gz, kb, chunks, _, rows, _ = spec_ref.shape
    planes, ka = gz * kb, chunks * LANES

    for chunk in range(chunks):
        lax.fori_loop(
            0, rows // 8,
            functools.partial(columns_back, spec_ref, chunk, coef_ref, tw_ref, re_s, im_s), 0,
        )

    step = plane_chunk(planes, rows)
    shape = (step * rows, ka)
    for start in range(0, planes, step):
        part = slice(start, start + step)
        field = inverse_product(re_s[part].reshape(shape), im_s[part].reshape(shape), table_ref)
        out_ref[part] = field.reshape(step, rows, ka)


def normal_product(spec, coef, nx):
    gz, kb, chunks, _, rows, _ = spec.shape
    planes, ka = gz * kb, chunks * LANES
    vmem = pl.BlockSpec(memory_space=pltpu.VMEM)
    return pl.pallas_call(
        normal_kernel,
        in_specs=[vmem] * 4,
        out_specs=vmem,
        out_shape=jax.ShapeDtypeStruct((planes, rows, ka), F32),
        scratch_shapes=[pltpu.VMEM((planes, rows, ka), F32)] * 2,
        compiler_params=pltpu.CompilerParams(vmem_limit_bytes=X_GRANT),
        cost_estimate=pl.CostEstimate(
            flops=12 * planes * rows * ka * ka, bytes_accessed=12 * planes * rows * ka, transcendentals=0
        ),
        name="normal_product",
    )(spec, coef, x_twiddle(nx, ka), jnp.asarray(x_inverse_matrix(nx, ka)))


def next_normal_row(gz, next_ref, coef_ref, tw_ref, table_ref, row_s, re_s, im_s):
    planes, ka = row_s.shape
    kb = planes // gz
    for start in range(0, ka, LANES):
        lanes = slice(start, start + LANES)

        def row_of(z, k, part):
            at = 2 * planes + 2 * (z * kb + k) + part
            return jnp.broadcast_to(next_ref[at : at + 1, lanes], (8, LANES))

        spectra = [[(row_of(z, k, 0), row_of(z, k, 1)) for k in range(kb)] for z in range(gz)]
        inverse_columns(gz, kb, spectra, coef_ref, tw_ref, lanes, slice(0, 8), re_s, im_s)
    shape = (planes * 8, ka)
    field = inverse_product(re_s[...].reshape(shape), im_s[...].reshape(shape), table_ref)
    for p in range(planes):
        row_s[p : p + 1, :] = field[8 * p : 8 * p + 1, :]


def border_kernel(edge_ref, head_ref, tail_ref, next_ref, prev_ref, after_ref, out_ref):
    del after_ref
    planes = tail_ref.shape[0] - 8

    def sums_of(ref):
        return ref[ref.shape[0] - 8 :, :LANES]

    def border(after, before):
        step = after[:planes, :] - before[:planes, :]
        return fold(step * step)

    second = edge_ref[2] > 0
    below = border(head_ref, prev_ref) * jnp.where(edge_ref[0] > 0, 0.0, 1.0)
    above = border(next_ref, tail_ref) * jnp.where(edge_ref[1] > 0, 0.0, 1.0)
    other = jnp.where(second, sums_of(prev_ref), sums_of(next_ref))
    none = jnp.zeros((8, LANES), F32)
    put_copies(out_ref, sums_of(tail_ref) + other + sums_block([none, none, below + above]))


def border_sums(edge, head, tail, next_head, prev_tail, after, copies):
    vmem = pl.BlockSpec(memory_space=pltpu.VMEM)
    return pl.pallas_call(
        border_kernel,
        in_specs=[pl.BlockSpec(memory_space=pltpu.SMEM)]
        + [vmem] * 4
        + [pl.BlockSpec(memory_space=pl.ANY)],
        out_specs=vmem,
        out_shape=jax.ShapeDtypeStruct((copies, 8, LANES), F32),
        compiler_params=pltpu.CompilerParams(vmem_limit_bytes=2 * MIB),
        name="border_sums",
    )(edge, head, tail, next_head, prev_tail, after)


def second_kernel(
    gz, edge_ref, d0_ref, nd0_ref, tail_ref, prev_ref, next_ref,
    coef_ref, tw_ref, table_ref, inverse_ref, *refs,
):
    sums_refs, refs = refs[:1], refs[1:]
    d1_ref, eta_ref, out_ref, spec_ref, re_s, im_s, row_s, nrow_s, re8_s, im8_s = refs
    next_normal_row(gz, next_ref, coef_ref, tw_ref, inverse_ref, nrow_s, re8_s, im8_s)
    planes, rows, ka = d0_ref.shape
    kb = planes // gz
    eta_here = step_of(sums_refs)
    eta_ref[...] = jnp.broadcast_to(eta_here, (8, LANES))
    eta = jnp.max(eta_here)
    first = edge_ref[0] > 0
    last = edge_ref[1] > 0

    def shrink(difference):
        return jnp.clip(-eta * difference, -CLIP, CLIP)

    lane2 = lax.broadcasted_iota(jnp.int32, (kb, ka), 1)
    row2 = lax.broadcasted_iota(jnp.int32, (kb, ka), 0)
    for z in range(gz):
        part = slice(z * kb, (z + 1) * kb)
        here = next_ref[part, :]
        value = here - eta * nrow_s[part, :]
        up = pltpu.roll(here, kb - 1, 0)
        up = jnp.where(
            row2 == kb - 1, jnp.where(lane2 == ka - 1, here, pltpu.roll(up, ka - 1, 1)), up
        )
        down = pltpu.roll(here, 1, 0)
        down = jnp.where(row2 == 0, jnp.where(lane2 == 0, here, pltpu.roll(down, 1, 1)), down)
        value = value + shrink(here - down) - shrink(up - here)
        value = value + shrink(here - tail_ref[part, :]) - shrink(next_ref[planes + z * kb : planes + (z + 1) * kb, :] - here)
        if z > 0:
            value = value + shrink(here - next_ref[(z - 1) * kb : z * kb, :])
        if z + 1 < gz:
            value = value - shrink(next_ref[(z + 1) * kb : (z + 2) * kb, :] - here)
        row_s[part, :] = value

    row = lax.broadcasted_iota(jnp.int32, (rows, ka), 0)
    square = jnp.zeros((8, LANES), F32)
    for p in range(planes):
        here = d0_ref[p]
        value = here - eta * nd0_ref[p]
        value = value + shrink(here - prev_plane(d0_ref, p, kb))
        value = value - shrink(next_plane(d0_ref, p, kb) - here)
        below = jnp.where(last, here[rows - 1 :, :], next_ref[p : p + 1, :])
        above = jnp.where(first, here[:1, :], prev_ref[p : p + 1, :])
        upper = shrink(jnp.where(row == rows - 1, below, pltpu.roll(here, rows - 1, 0)) - here)
        lower = jnp.where(row == 0, shrink(here[:1, :] - above), pltpu.roll(upper, 1, 0))
        value = value + lower - upper
        if p >= kb:
            value = value + shrink(here - d0_ref[p - kb])
        if p + kb < planes:
            value = value - shrink(d0_ref[p + kb] - here)
        d1_ref[p] = value
        square = square + fold(value * value)

    slope = jnp.zeros((8, LANES), F32)
    for p in range(planes):
        here = d1_ref[p]
        along_x = next_plane(d1_ref, p, kb) - here
        below = jnp.where(last, here[rows - 1 :, :], row_s[p : p + 1, :])
        along_y = jnp.where(row == rows - 1, below, pltpu.roll(here, rows - 1, 0)) - here
        terms = along_x * along_x + along_y * along_y
        if p + kb < planes:
            along_z = d1_ref[p + kb] - here
            terms = terms + along_z * along_z
        slope = slope + fold(terms)

    step = plane_chunk(planes, rows)

    def multiply(i, carry):
        part = pl.ds(i * step, step)
        re, im = forward_product(d1_ref[part].reshape(step * rows, ka), table_ref)
        re_s[part] = re.reshape(step, rows, ka)
        im_s[part] = im.reshape(step, rows, ka)
        return carry

    lax.fori_loop(0, planes // step, multiply, 0)

    def columns(j, total):
        part = pl.ds(pl.multiple_of(j * 8, 8), 8)
        for chunk in range(ka // LANES):
            lanes = slice(chunk * LANES, (chunk + 1) * LANES)
            spectra = forward_columns(gz, kb, coef_ref, tw_ref, lanes, part, re_s, im_s)
            for z in range(gz):
                for k in range(kb):
                    for p in range(2):
                        value = spectra[z][k][p]
                        spec_ref[z, k, chunk, p, part, :] = value
                        total = total + value * value
        return total

    projected = lax.fori_loop(0, rows // 8, columns, jnp.zeros((8, LANES), F32))
    put_copies(out_ref, sums_block([square, projected, slope]))


def second_descent(edge, sums, d0, nd0, tail, prev_tail, next_head, coef, gz, nx):
    planes, rows, ka = d0.shape
    vmem = pl.BlockSpec(memory_space=pltpu.VMEM)
    return pl.pallas_call(
        functools.partial(second_kernel, gz),
        in_specs=[pl.BlockSpec(memory_space=pltpu.SMEM)] + [vmem] * 10,
        out_specs=[vmem] * 4,
        out_shape=[
            jax.ShapeDtypeStruct((planes, rows, ka), F32),
            jax.ShapeDtypeStruct((8, LANES), F32),
            jax.ShapeDtypeStruct(sums.shape, F32),
            jax.ShapeDtypeStruct((gz, planes // gz, ka // LANES, 2, rows, LANES), F32),
        ],
        scratch_shapes=[
            pltpu.VMEM((planes, rows, ka), F32),
            pltpu.VMEM((planes, rows, ka), F32),
            pltpu.VMEM((planes, ka), F32),
            pltpu.VMEM((planes, ka), F32),
            pltpu.VMEM((planes, 8, ka), F32),
            pltpu.VMEM((planes, 8, ka), F32),
        ],
        compiler_params=pltpu.CompilerParams(vmem_limit_bytes=X_GRANT),
        name="second_descent",
    )(
        edge, d0, nd0, tail, prev_tail, next_head, coef,
        x_twiddle(nx, ka), x_forward_matrix(nx, ka), jnp.asarray(x_inverse_matrix(nx, ka)), sums,
    )


def combine_kernel(gz, eta_ref, *refs):
    sums_refs, (first_ref, second_ref, out_ref, steps_ref) = refs[:gz], refs[gz:]
    eta0 = jnp.max(eta_ref[...])
    eta1 = jnp.max(step_of(sums_refs))
    steps_ref[0] = eta_ref[...]
    steps_ref[1] = jnp.full((8, LANES), eta1, F32)
    count = out_ref.shape[0]
    start = pl.program_id(0) * count
    for i in range(count):
        out_ref[i] = -(eta0 * first_ref[start + i] + eta1 * second_ref[start + i])


def combine_spectra(eta, sums, first, second):
    gz = len(sums)
    planes, *rest = first.shape
    count = 4 if planes % 4 == 0 else 1
    vmem = pl.BlockSpec(memory_space=pltpu.VMEM)
    return pl.pallas_call(
        functools.partial(combine_kernel, gz),
        grid=(planes // count,),
        in_specs=[vmem] * (3 + gz),
        out_specs=[
            pl.BlockSpec((count, *rest), lambda i: (i, 0, 0, 0, 0)),
            pl.BlockSpec((2, 8, LANES), lambda i: (0, 0, 0)),
        ],
        out_shape=[
            jax.ShapeDtypeStruct(first.shape, F32),
            jax.ShapeDtypeStruct((2, 8, LANES), F32),
        ],
        compiler_params=pltpu.CompilerParams(vmem_limit_bytes=6 * MIB),
        name="combine_spectra",
    )(eta, *sums, first, second)


def to_core(piece, r):
    gz = lax.axis_size("gz")
    return lax.ppermute(piece, "gz", [(i, (i + r) % gz) for i in range(gz)]) if r else piece


def to_chips(parts):
    return lax.all_to_all(parts, "gy", 0, 0, tiled=True)


def to_devices(parts):
    gz, gy, *rest = parts.shape
    parts = lax.all_to_all(parts.reshape(gz * gy, *rest), ("gz", "gy"), 0, 0, tiled=True)
    return parts.reshape(gz, gy, *rest)


def everywhere(sums):
    sums = to_chips(sums)
    return [to_core(sums, r) for r in range(lax.axis_size("gz"))]


def shards(data, band_offset, interp_weight):
    gz = lax.axis_size("gz")
    gy = lax.axis_size("gy")
    devices = gz * gy
    data = data[0]
    blocks, ny, width = data.shape
    rows = ny // devices
    ka = blocks * HALF
    nx = ka * gy

    core = lax.axis_index("gz")
    flat = lax.axis_index("gy") * gz + core
    edge = jnp.stack([flat == 0, flat == devices - 1, core]).astype(jnp.int32)
    order = [(i % gz) * gy + i // gz for i in range(devices)]
    up = [(order[i + 1], order[i]) for i in range(devices - 1)]
    down = [(order[i], order[i + 1]) for i in range(devices - 1)]

    lower = band_offset < 0
    weight = interp_weight
    coef = jnp.stack(
        [
            jnp.where(lower, weight[1], weight[0]),
            jnp.where(lower, weight[0], 0.0),
            jnp.where(lower, 0.0, weight[1]),
        ]
    ).reshape(3, gy, 1, ka)
    coef = jnp.broadcast_to(coef, (3, gy, 8, ka))

    spec = to_devices(y_inverse(data, rows, gz, gy))
    d0, head, tail, first = middle(spec, coef, nx)
    next_head = lax.ppermute(head, ("gz", "gy"), up)
    prev_tail = lax.ppermute(tail, ("gz", "gy"), down)
    nd0 = normal_product(first, coef, nx)
    sums = to_chips(border_sums(edge, head, tail, next_head, prev_tail, nd0, gy))
    d1, eta, sums, second = second_descent(
        edge, sums, d0, nd0, tail, prev_tail, next_head, coef, gz, nx
    )
    sums = everywhere(sums)
    flat_shape = (devices, ka // LANES, 2, rows, LANES)
    spec, etas = combine_spectra(eta, sums, first.reshape(flat_shape), second.reshape(flat_shape))
    residual = y_forward(to_devices(spec.reshape(first.shape)), data)

    volume = -(etas[0, 0, 0] * d0 + etas[1, 0, 0] * d1)
    volume = volume.reshape(gz, gy, rows, ka).transpose(0, 2, 3, 1).reshape(gz, rows, nx)
    parts = [
        to_core(lax.dynamic_index_in_dim(volume, lax.rem(core + r, gz), 0, False), r)
        for r in range(gz)
    ]
    volume = jnp.zeros((gz, rows, nx), F32)
    for r, part in enumerate(parts):
        volume = lax.dynamic_update_index_in_dim(volume, part, lax.rem(core + gz - r, gz), 0)
    return (volume.reshape(1, gz * rows, nx), residual[None])


NX = 4096
NY = 2048
XB = 64
YB = 64
ITERS = 2
XA = 64
YA = 32
PRECISE = lax.Precision.HIGHEST


def with_halo(block, sides, width):
    for axis, dim in sides:
        count = lax.axis_size(axis)
        forward = [(i, i + 1) for i in range(count - 1)]
        backward = [(target, source) for source, target in forward]
        low = lax.ppermute(
            lax.slice_in_dim(block, block.shape[dim] - width, None, axis=dim), axis, forward
        )
        high = lax.ppermute(lax.slice_in_dim(block, 0, width, axis=dim), axis, backward)
        block = jnp.concatenate([low, block, high], axis=dim)
    return block


def from_behind(block, axis, distance):
    devices = range(lax.axis_size(axis))
    route = [(i - distance, i) for i in devices if i - distance in devices]
    return lax.ppermute(block, axis, route)


def unit_table(length):
    counter = jnp.arange(length, dtype=jnp.int32)
    phase_int = counter[:, None] * counter[None, :] % length
    angles = 2.0 * jnp.pi / length * phase_int.astype(jnp.float32)
    factor = length ** (-0.5)
    return (jnp.cos(angles) * factor, jnp.sin(angles) * factor)


def twiddle_table(row_len, col_len, period):
    phase_int = (
        jnp.arange(row_len, dtype=jnp.int32)[:, None]
        * jnp.arange(col_len, dtype=jnp.int32)[None, :]
        % period
    )
    angles = 2.0 * jnp.pi / period * phase_int.astype(jnp.float32)
    return (jnp.cos(angles), jnp.sin(angles))


def split_parts(packed):
    half_width = packed.shape[-1] // 2
    return (packed[..., :half_width], packed[..., half_width:])


def join_parts(real_part, imag_part):
    return jnp.concatenate([real_part, imag_part], axis=-1)


def complex_contract(packed, cos_table, sin_table, subscripts, conj_sign):
    cos_out = jnp.einsum(subscripts, packed, cos_table, precision=PRECISE)
    sin_out = jnp.einsum(subscripts, packed, sin_table, precision=PRECISE)
    cos_re, cos_im = split_parts(cos_out)
    sin_re, sin_im = split_parts(sin_out)
    return join_parts(cos_re - conj_sign * sin_im, cos_im + conj_sign * sin_re)


def rotate(packed, cos_table, sin_table, conj_sign):
    real_part, imag_part = split_parts(packed)
    return join_parts(
        real_part * cos_table - conj_sign * imag_part * sin_table,
        imag_part * cos_table + conj_sign * real_part * sin_table,
    )


def forward_x(volume):
    slices, row_count = (volume.shape[0], volume.shape[1])
    cos_a, sin_a = unit_table(XA)
    cos_b, sin_b = unit_table(XB)
    first_table = jnp.concatenate([cos_a, -sin_a], axis=1)
    grid_view = volume.reshape(slices, row_count, XA, XB)
    mixing = jnp.einsum("zyab,am->zybm", grid_view, first_table, precision=PRECISE)
    tw_cos, tw_sin = twiddle_table(XB, XA, NX)
    mixing = rotate(mixing, tw_cos, tw_sin, -1.0)
    return complex_contract(mixing, cos_b, sin_b, "zybm,bl->zlym", -1.0)


def inverse_x(packed):
    slices, row_count = (packed.shape[0], packed.shape[2])
    cos_a, sin_a = unit_table(XA)
    cos_b, sin_b = unit_table(XB)
    mixing = complex_contract(packed, cos_b, sin_b, "zlym,lb->zybm", 1.0)
    tw_cos, tw_sin = twiddle_table(XB, XA, NX)
    mixing = rotate(mixing, tw_cos, tw_sin, 1.0)
    last_table = jnp.concatenate([cos_a, -sin_a], axis=0)
    grid_view = jnp.einsum("zybm,ma->zyab", mixing, last_table, precision=PRECISE)
    return grid_view.reshape(slices, row_count, NX)


def forward_y(packed):
    slices, blocks, width = (packed.shape[0], packed.shape[1], packed.shape[3])
    cos_a, sin_a = unit_table(YA)
    cos_b, sin_b = unit_table(YB)
    grid_view = packed.reshape(slices, blocks, YA, YB, width)
    mixing = complex_contract(grid_view, cos_a, sin_a, "zjcdm,ck->zjkdm", -1.0)
    tw_cos, tw_sin = twiddle_table(YA, YB, NY)
    mixing = rotate(mixing, tw_cos[:, :, None], tw_sin[:, :, None], -1.0)
    result = complex_contract(mixing, cos_b, sin_b, "zjkdm,dl->zjlkm", -1.0)
    return result.reshape(slices, blocks, NY, width)


def inverse_y(packed):
    slices, blocks, width = (packed.shape[0], packed.shape[1], packed.shape[3])
    cos_a, sin_a = unit_table(YA)
    cos_b, sin_b = unit_table(YB)
    grid_view = packed.reshape(slices, blocks, YB, YA, width)
    mixing = complex_contract(grid_view, cos_b, sin_b, "zjlkm,ld->zjkdm", 1.0)
    tw_cos, tw_sin = twiddle_table(YA, YB, NY)
    mixing = rotate(mixing, tw_cos[:, :, None], tw_sin[:, :, None], 1.0)
    result = complex_contract(mixing, cos_a, sin_a, "zjkdm,kc->zjcdm", 1.0)
    return result.reshape(slices, blocks, NY, width)


def tilt_coefficients(band_offset, interp_weight, first_block, blocks):
    offsets = lax.dynamic_slice_in_dim(band_offset.reshape(XB, XA), first_block, blocks, 0)
    weights = lax.dynamic_slice_in_dim(interp_weight.reshape(2, XB, XA), first_block, blocks, 1)
    lower_tap = (jnp.concatenate([offsets, offsets], axis=1) < 0)[:, None, :]
    first_weight = jnp.concatenate([weights[0], weights[0]], axis=1)[:, None, :]
    second_weight = jnp.concatenate([weights[1], weights[1]], axis=1)[:, None, :]
    return (lower_tap, first_weight, second_weight)


def tilt(field_in, coefficients, adjoint):
    lower_tap, first_weight, second_weight = coefficients
    padded = with_halo(field_in, (("gz", 0),), 1)
    below_rim = padded[:-2]
    middle = padded[1:-1]
    above_rim = padded[2:]
    if adjoint:
        return jnp.where(
            lower_tap,
            first_weight * above_rim + second_weight * middle,
            first_weight * middle + second_weight * below_rim,
        )
    return jnp.where(
        lower_tap,
        first_weight * below_rim + second_weight * middle,
        first_weight * middle + second_weight * above_rim,
    )


def to_pencil(slab_part):
    return lax.all_to_all(slab_part, "gy", split_axis=1, concat_axis=2, tiled=True)


def to_slab(pencil_part):
    return lax.all_to_all(pencil_part, "gy", split_axis=2, concat_axis=1, tiled=True)


def back_project(packed, pencil_coef):
    return inverse_x(to_slab(inverse_y(tilt(packed, pencil_coef, True))))


def edge_masks(slices, row_count):
    z_global = lax.axis_index("gz") * slices + jnp.arange(slices, dtype=jnp.int32)
    y_global = lax.axis_index("gy") * row_count + jnp.arange(row_count, dtype=jnp.int32)
    keep_z = (z_global < slices * lax.axis_size("gz") - 1).astype(jnp.float32)[:, None, None]
    keep_y = (y_global < row_count * lax.axis_size("gy") - 1).astype(jnp.float32)[None, :, None]
    return (keep_z, keep_y)


def forward_diff(field_in, keep_z, keep_y):
    slices, row_count = (field_in.shape[0], field_in.shape[1])
    next_z = from_behind(field_in, "gz", -1)
    next_y = from_behind(field_in[:, :1], "gy", -1)
    along_z = (jnp.concatenate([field_in[1:], next_z], axis=0) - field_in) * keep_z
    along_y = (jnp.concatenate([field_in[:, 1:], next_y], axis=1) - field_in) * keep_y
    zero_col = jnp.zeros((slices, row_count, 1), jnp.float32)
    along_x = jnp.concatenate([field_in[:, :, 1:] - field_in[:, :, :-1], zero_col], axis=2)
    return jnp.stack([along_z, along_y, along_x])


def transpose_diff(components, keep_z, keep_y):
    slices, row_count = (components.shape[1], components.shape[2])
    zero_col = jnp.zeros((slices, row_count, 1), jnp.float32)
    comp_z = components[0] * keep_z
    comp_y = components[1] * keep_y
    comp_x = jnp.concatenate([components[2][:, :, :-1], zero_col], axis=2)
    prev_z = from_behind(comp_z, "gz", 1)
    prev_y = from_behind(comp_y[:, -1:], "gy", 1)
    result = jnp.concatenate([prev_z, comp_z[:-1]], axis=0) - comp_z
    result = result + jnp.concatenate([prev_y, comp_y[:, :-1]], axis=1) - comp_y
    result = result + jnp.concatenate([zero_col, comp_x[:, :, :-1]], axis=2) - comp_x
    return result


def plain_shards(data, band_offset, interp_weight):
    slices = data.shape[0]
    blocks = data.shape[1]
    width = data.shape[3]
    row_count = NY // lax.axis_size("gy")
    slab_coef = tilt_coefficients(band_offset, interp_weight, 0, XB)
    pencil_coef = tilt_coefficients(
        band_offset, interp_weight, lax.axis_index("gy") * blocks, blocks
    )
    keep_z, keep_y = edge_masks(slices, row_count)
    measured = data.astype(jnp.float32)
    volume = jnp.zeros((slices, row_count, NX), jnp.float32)
    grad_volume = jnp.zeros((3, slices, row_count, NX), jnp.float32)
    split_var = grad_volume
    dual_var = grad_volume
    data_back = back_project(measured, pencil_coef)
    normal_part = jnp.zeros_like(volume)
    tilted = jnp.zeros((slices, XB, row_count, width), jnp.float32)
    for iteration in range(ITERS):
        data_grad = normal_part - data_back
        if iteration > 0:
            tv_gap = grad_volume - split_var + dual_var / PENALTY
            descent = data_grad + PENALTY * transpose_diff(tv_gap, keep_z, keep_y)
        else:
            descent = data_grad
        slope_field = forward_diff(descent, keep_z, keep_y)
        projected = tilt(forward_x(descent), slab_coef, False)
        line_totals = lax.psum(
            (
                jnp.sum(descent * descent),
                jnp.sum(projected * projected),
                jnp.sum(slope_field * slope_field),
            ),
            ("gz", "gy"),
        )
        step_length = line_totals[0] / (line_totals[1] + PENALTY * line_totals[2])
        volume = volume - step_length * descent
        grad_volume = grad_volume - step_length * slope_field
        tilted = tilted - step_length * projected
        if iteration + 1 < ITERS:
            normal_part = normal_part - step_length * inverse_x(tilt(projected, slab_coef, True))
        if iteration + 1 < ITERS:
            shifted = grad_volume + dual_var / PENALTY
            split_var = shifted - jnp.clip(shifted, -TV_WEIGHT / PENALTY, TV_WEIGHT / PENALTY)
            dual_var = PENALTY * (grad_volume - split_var)
    residual = forward_y(to_pencil(tilted)) - measured
    return (volume, residual)


def tiles_fit(mesh, ny, blocks):
    rows = ny // (mesh.shape["gz"] * mesh.shape["gy"])
    return mesh.shape["gz"] == 2 and rows % 16 == 0 and mesh.shape["gy"] % YR == 0 and blocks // mesh.shape["gy"] % 2 == 0


def solution(mesh):
    in_specs = (P("gz", "gy", None, None), P(), P())
    out_specs = (P("gz", "gy", None), P("gz", "gy", None, None))

    def run(data, band_offset, interp_weight):
        body = shards if tiles_fit(mesh, data.shape[2], data.shape[1]) else plain_shards
        call = jax.shard_map(
            body, mesh=mesh, in_specs=in_specs, out_specs=out_specs, check_vma=False
        )
        return call(data, band_offset, interp_weight)

    return run
```

```python
import functools

import jax
import jax.numpy as jnp
import numpy as np
from jax import lax
from jax.experimental import pallas as pl
from jax.experimental.pallas import tpu as pltpu
from jax.sharding import PartitionSpec as P

PENALTY = 0.5
TV_WEIGHT = 0.25
CLIP = TV_WEIGHT / PENALTY
HALF = 64
YR = 8
LANES = 128
F32 = jnp.float32
BF16 = jnp.bfloat16
MIB = 1024 * 1024
Y_GRANT = 56 * MIB
X_GRANT = 20 * MIB


def dft_parts(length, scale):
    index = np.arange(length)
    angles = 2.0 * np.pi / length * (index[:, None] * index[None, :] % length)
    return np.cos(angles) * scale, np.sin(angles) * scale


def host_parts(table):
    table = table.astype(np.float32)
    high = table.astype(BF16)
    low = (table - high.astype(np.float32)).astype(BF16)
    return high, low


def y_matrix(ny, forward, sign):
    n = ny // YR
    cos, sin = dft_parts(n, sign * ny**-0.5)
    if forward:
        table = np.block([[cos, sin], [-sin, cos]])
    else:
        table = np.block([[cos, -sin], [sin, cos]])
    return jnp.asarray(np.concatenate(host_parts(table), axis=0))


def y_twiddle(ny):
    n = ny // YR
    angles = 2.0 * np.pi / ny * (np.arange(1, YR)[:, None] * np.arange(n)[None, :])
    table = np.stack([np.cos(angles), np.sin(angles)]).astype(np.float32)
    return jnp.asarray(np.ascontiguousarray(np.broadcast_to(table[..., None], (2, YR - 1, n, LANES))))


def x_inverse_matrix(nx, ka):
    cos, sin = dft_parts(ka, nx**-0.5)
    return np.concatenate(host_parts(np.concatenate([cos, -sin], axis=0)), axis=1)


def x_forward_matrix(nx, ka):
    cos, sin = dft_parts(ka, nx**-0.5)
    return jnp.asarray(np.concatenate(host_parts(np.concatenate([cos, -sin], axis=1)), axis=1))


def x_twiddle(nx, ka):
    kb = nx // ka
    angles = 2.0 * np.pi / nx * (np.arange(kb)[:, None] * np.arange(ka)[None, :])
    table = np.stack([np.cos(angles), np.sin(angles)]).astype(np.float32)
    return jnp.asarray(np.ascontiguousarray(np.broadcast_to(table[:, :, None], (2, kb, 8, ka))))


def short_fft(planes, sign):
    n = len(planes)
    if n == 1:
        return planes
    even = short_fft(planes[0::2], sign)
    odd = short_fft(planes[1::2], sign)
    half = n // 2
    out = [None] * n
    for k in range(half):
        er, ei = even[k]
        tr, ti = odd[k]
        if 4 * k == n:
            if sign > 0:
                out[k] = (er - ti, ei + tr)
                out[k + half] = (er + ti, ei - tr)
            else:
                out[k] = (er + ti, ei - tr)
                out[k + half] = (er - ti, ei + tr)
            continue
        if k > 0:
            c = float(np.cos(2.0 * np.pi * k / n))
            s = float(sign * np.sin(2.0 * np.pi * k / n))
            if 8 * k == n:
                tr, ti = (tr - ti, ti + tr) if sign > 0 else (tr + ti, ti - tr)
                tr, ti = tr * c, ti * c
            elif 8 * k == 3 * n:
                m = float(np.sin(2.0 * np.pi * k / n))
                tr, ti = (-(tr + ti), tr - ti) if sign > 0 else (ti - tr, -(tr + ti))
                tr, ti = tr * m, ti * m
            else:
                tr, ti = tr * c - ti * s, ti * c + tr * s
        out[k] = (er + tr, ei + ti)
        out[k + half] = (er - tr, ei - ti)
    return out


def split2(x):
    high = x.astype(BF16)
    return high, (x - high.astype(F32)).astype(BF16)


def dot(a, b):
    return jnp.dot(a, b, preferred_element_type=F32)


def fold(x):
    rows, lanes = x.shape
    x = jnp.sum(x.reshape(rows // 8, 8, lanes), axis=0)
    total = x[:, :LANES]
    for i in range(1, lanes // LANES):
        total = total + x[:, i * LANES : (i + 1) * LANES]
    return total


def full_sum(x):
    return jnp.sum(jnp.sum(x, axis=0, keepdims=True), axis=1, keepdims=True)


def step_of(sums_ref):
    total = jnp.sum(sums_ref[...], axis=0)
    parts = jnp.sum(total, axis=1, keepdims=True)
    return parts[0:1] / (parts[1:2] + PENALTY * parts[2:3])


def sums_block(values):
    rows = [jnp.sum(v, axis=0, keepdims=True) for v in values]
    index = lax.broadcasted_iota(jnp.int32, (8, LANES), 0)
    block = jnp.zeros((8, LANES), F32)
    for i, row in enumerate(rows):
        block = jnp.where(index == i, jnp.broadcast_to(row, (8, LANES)), block)
    return block


def put_copies(out_ref, block):
    for i in range(out_ref.shape[0]):
        out_ref[i] = block


def mix_adjoint(coef, planes):
    own, below, above = coef
    out = []
    for z in range(len(planes)):
        value = own * planes[z]
        if z + 1 < len(planes):
            value = value + below * planes[z + 1]
        if z > 0:
            value = value + above * planes[z - 1]
        out.append(value)
    return out


def mix(coef, planes):
    own, below, above = coef
    out = []
    for z in range(len(planes)):
        value = own * planes[z]
        if z > 0:
            value = value + below * planes[z - 1]
        if z + 1 < len(planes):
            value = value + above * planes[z + 1]
        out.append(value)
    return out


def y_inverse_kernel(
    data_hbm, table_hbm, tw_hbm, out_hbm,
    data_ref, table_ref, tw_ref, out_ref, re_s, im_s, mix_s, sems, out_sems,
):
    blocks, ny, _ = data_ref.shape
    n = ny // YR
    gz, _, _, _, rows, _ = out_ref.shape
    lane = lax.broadcasted_iota(jnp.int32, (n, LANES), 1)
    pairs = blocks // 2

    def fetch(chunk):
        part = pl.ds(2 * chunk, 2)
        return pltpu.make_async_copy(data_hbm.at[part], data_ref.at[part], sems.at[2 + chunk])

    def give(chunk, core):
        at = (core, slice(None), chunk)
        return pltpu.make_async_copy(out_ref.at[at], out_hbm.at[at], out_sems.at[chunk * gz + core])

    fetch_table = pltpu.make_async_copy(table_hbm, table_ref, sems.at[0])
    fetch_tw = pltpu.make_async_copy(tw_hbm, tw_ref, sems.at[1])
    fetch(0).start()
    fetch_table.start()
    fetch_tw.start()
    for chunk in range(1, pairs):
        fetch(chunk).start()

    for chunk in range(pairs):
        fetch(chunk).wait()

        def unpack(i, carry):
            part = pl.ds(pl.multiple_of(i * n, n), n)
            first = data_ref[2 * chunk, part, :].astype(F32)
            second = data_ref[2 * chunk + 1, part, :].astype(F32)
            re_s[part, :] = jnp.where(lane < HALF, first, pltpu.roll(second, HALF, 1))
            im_s[part, :] = jnp.where(lane < HALF, pltpu.roll(first, HALF, 1), second)
            return carry

        lax.fori_loop(0, YR, unpack, 0)
        if chunk == 0:
            fetch_table.wait()

        for k in range(0, YR, 2):
            pieces = [
                jnp.concatenate([s[pl.ds(k + d, n, stride=YR), :] for d in range(2)], axis=1)
                for s in (re_s, im_s)
            ]
            both = dot(table_ref[...], jnp.concatenate(pieces, axis=0).astype(BF16))
            both = both[: 2 * n] + both[2 * n :]
            for d in range(2):
                mix_s[k + d] = both[:, d * LANES : (d + 1) * LANES]

        if chunk == 0:
            fetch_tw.wait()

        tiles = rows // 8
        for core in range(gz):

            def combine(i, carry):
                y2 = ((i // tiles) * gz + core) * rows + lax.rem(i, tiles) * 8
                part = pl.ds(pl.multiple_of(y2, 8), 8)
                planes = []
                for k in range(YR):
                    re = mix_s[k, part, :]
                    im = mix_s[k, pl.ds(pl.multiple_of(n + y2, 8), 8), :]
                    if k > 0:
                        c = tw_ref[0, k - 1, part, :]
                        s = tw_ref[1, k - 1, part, :]
                        re, im = re * c - im * s, im * c + re * s
                    planes.append((re, im))
                at = pl.ds(pl.multiple_of(lax.rem(i, tiles) * 8, 8), 8)
                for k, (re, im) in enumerate(short_fft(planes, 1)):
                    to = k * (n // (gz * rows)) + i // tiles
                    out_ref[core, to, chunk, 0, at, :] = re
                    out_ref[core, to, chunk, 1, at, :] = im
                return carry

            lax.fori_loop(0, n // gz // 8, combine, 0, unroll=2)
            give(chunk, core).start()

    for chunk in range(pairs):
        for core in range(gz):
            give(chunk, core).wait()


def y_inverse(data, rows, gz, gy):
    blocks, ny, width = data.shape
    n = ny // YR
    shape = (gz, gy, blocks // 2, 2, rows, LANES)
    hbm = pl.BlockSpec(memory_space=pltpu.HBM)
    return pl.pallas_call(
        y_inverse_kernel,
        in_specs=[hbm] * 3,
        out_specs=hbm,
        out_shape=jax.ShapeDtypeStruct(shape, F32),
        scratch_shapes=[
            pltpu.VMEM((blocks, ny, width), BF16),
            pltpu.VMEM((4 * n, 2 * n), BF16),
            pltpu.VMEM((2, YR - 1, n, LANES), F32),
            pltpu.VMEM(shape, F32),
            pltpu.VMEM((ny, LANES), F32),
            pltpu.VMEM((ny, LANES), F32),
            pltpu.VMEM((YR, 2 * n, LANES), F32),
            pltpu.SemaphoreType.DMA((2 + blocks // 2,)),
            pltpu.SemaphoreType.DMA((blocks // 2 * gz,)),
        ],
        compiler_params=pltpu.CompilerParams(vmem_limit_bytes=Y_GRANT),
        name="y_inverse",
    )(data, y_matrix(ny, False, -1.0), y_twiddle(ny))


def y_forward_kernel(
    spec_hbm, data_hbm, table_hbm, tw_hbm, out_hbm,
    spec_ref, data_ref, table_ref, tw_ref, out_ref, mix_s, sems, spec_sems, out_sems,
):
    blocks, ny, _ = data_ref.shape
    n = ny // YR
    _, gz, gy, _, rows, _ = spec_ref.shape
    pairs = blocks // 2
    half = n // 2

    def fetch(chunk):
        return pltpu.make_async_copy(
            spec_hbm.at[:, :, chunk], spec_ref.at[chunk], spec_sems.at[chunk]
        )

    def give(chunk, part):
        at = (pl.ds(2 * chunk, 2), slice(None), pl.ds(part * half, half))
        return pltpu.make_async_copy(out_ref.at[at], out_hbm.at[at], out_sems.at[2 * chunk + part])

    fetch_table = pltpu.make_async_copy(table_hbm, table_ref, sems.at[0])
    fetch_tw = pltpu.make_async_copy(tw_hbm, tw_ref, sems.at[1])
    fetch_data = pltpu.make_async_copy(data_hbm, data_ref, sems.at[2])
    fetch(0).start()
    fetch_table.start()
    fetch_tw.start()
    fetch_data.start()
    for chunk in range(1, pairs):
        fetch(chunk).start()

    def rows_of(chunk, p, k):
        part = pl.ds(k, rows // YR, stride=YR)
        return jnp.concatenate(
            [spec_ref[chunk, core, i, p, part, :] for i in range(gy) for core in range(gz)], axis=0
        )

    lane = lax.broadcasted_iota(jnp.int32, (16, LANES), 1)
    for chunk in range(pairs):
        fetch(chunk).wait()

        if chunk == 0:
            fetch_table.wait()

        for k in range(0, YR, 2):
            pieces = [
                jnp.concatenate([rows_of(chunk, p, k + d) for d in range(2)], axis=1)
                for p in range(2)
            ]
            high, low = split2(jnp.concatenate(pieces, axis=0))
            both = dot(table_ref[...], high)
            both = both[: 2 * n] + both[2 * n :] + dot(table_ref[: 2 * n], low)
            for d in range(2):
                mix_s[k + d] = both[:, d * LANES : (d + 1) * LANES]
        if chunk == 0:
            fetch_tw.wait()
            fetch_data.wait()

        def combine(i, carry):
            start = pl.multiple_of(i * 16, 16)
            part = pl.ds(start, 16)
            planes = []
            for k in range(YR):
                re = mix_s[k, part, :]
                im = mix_s[k, pl.ds(pl.multiple_of(n + i * 16, 16), 16), :]
                if k > 0:
                    c = tw_ref[0, k - 1, part, :]
                    s = tw_ref[1, k - 1, part, :]
                    re, im = re * c + im * s, im * c - re * s
                planes.append((re, im))
            for k, (re, im) in enumerate(short_fft(planes, -1)):
                at = pl.ds(pl.multiple_of(k * n + start, 16), 16)
                first = jnp.where(lane < HALF, re, pltpu.roll(im, HALF, 1))
                second = jnp.where(lane < HALF, pltpu.roll(re, HALF, 1), im)
                out_ref[2 * chunk, k, part, :] = first - data_ref[2 * chunk, at, :].astype(F32)
                out_ref[2 * chunk + 1, k, part, :] = (
                    second - data_ref[2 * chunk + 1, at, :].astype(F32)
                )
            return carry

        for part in range(2):
            lax.fori_loop(part * half // 16, (part + 1) * half // 16, combine, 0)
            give(chunk, part).start()

    for chunk in range(pairs):
        for part in range(2):
            give(chunk, part).wait()


def y_forward(spec, data):
    blocks, ny, width = data.shape
    n = ny // YR
    hbm = pl.BlockSpec(memory_space=pltpu.HBM)
    out = pl.pallas_call(
        y_forward_kernel,
        in_specs=[hbm] * 4,
        out_specs=hbm,
        out_shape=jax.ShapeDtypeStruct((blocks, YR, n, width), F32),
        scratch_shapes=[
            pltpu.VMEM((blocks // 2, *spec.shape[:2], *spec.shape[3:]), F32),
            pltpu.VMEM((blocks, ny, width), BF16),
            pltpu.VMEM((4 * n, 2 * n), BF16),
            pltpu.VMEM((2, YR - 1, n, LANES), F32),
            pltpu.VMEM((blocks, YR, n, width), F32),
            pltpu.VMEM((YR, 2 * n, LANES), F32),
            pltpu.SemaphoreType.DMA((3,)),
            pltpu.SemaphoreType.DMA((blocks // 2,)),
            pltpu.SemaphoreType.DMA((blocks,)),
        ],
        compiler_params=pltpu.CompilerParams(vmem_limit_bytes=Y_GRANT),
        name="y_forward",
    )(spec, data, y_matrix(ny, True, 1.0), y_twiddle(ny))
    return out.reshape(blocks, ny, width)


def plane_chunk(planes, rows):
    chunk = max(1, 1024 // rows)
    while planes % chunk:
        chunk -= 1
    return chunk


def turn_rows(kb, planes_of, tw_ref, lanes, sign):
    out = []
    for b in range(kb):
        re, im = planes_of(b)
        if b > 0:
            c = tw_ref[0, b, :, lanes]
            s = tw_ref[1, b, :, lanes]
            if sign > 0:
                re, im = re * c - im * s, im * c + re * s
            else:
                re, im = re * c + im * s, im * c - re * s
        out.append((re, im))
    return out


def inverse_columns(gz, kb, spectra, coef_ref, tw_ref, lanes, part, re_s, im_s):
    mixed = [[None] * kb for _ in range(gz)]
    for k in range(kb):
        coef = [coef_ref[j, k, :, lanes] for j in range(3)]
        re = mix_adjoint(coef, [spectra[z][k][0] for z in range(gz)])
        im = mix_adjoint(coef, [spectra[z][k][1] for z in range(gz)])
        for z in range(gz):
            mixed[z][k] = (re[z], im[z])
    for z in range(gz):
        short = short_fft(mixed[z], 1)
        for b, (re, im) in enumerate(turn_rows(kb, lambda b: short[b], tw_ref, lanes, 1)):
            re_s[z * kb + b, part, lanes] = re
            im_s[z * kb + b, part, lanes] = im


def forward_columns(gz, kb, coef_ref, tw_ref, lanes, part, re_s, im_s):
    spectra = []
    for z in range(gz):
        rows_of = lambda b: (re_s[z * kb + b, part, lanes], im_s[z * kb + b, part, lanes])
        spectra.append(short_fft(turn_rows(kb, rows_of, tw_ref, lanes, -1), -1))
    out = [[None] * kb for _ in range(gz)]
    for k in range(kb):
        coef = [coef_ref[j, k, :, lanes] for j in range(3)]
        re = mix(coef, [spectra[z][k][0] for z in range(gz)])
        im = mix(coef, [spectra[z][k][1] for z in range(gz)])
        for z in range(gz):
            out[z][k] = (re[z], im[z])
    return out


def inverse_product(re, im, table_ref):
    ka = re.shape[1]
    high, low = split2(jnp.concatenate([re, im], axis=1))
    value = dot(high, table_ref[...])
    return value[:, :ka] + value[:, ka:] + dot(low, table_ref[:, :ka])


def forward_product(field, table_ref):
    ka = field.shape[1]
    high, low = split2(field)
    value = dot(high, table_ref[...])
    value = value[:, : 2 * ka] + value[:, 2 * ka :] + dot(low, table_ref[:, : 2 * ka])
    return value[:, :ka], value[:, ka:]


def next_plane(field_ref, p, kb):
    rows, ka = field_ref.shape[1:]
    if (p + 1) % kb:
        return field_ref[p + 1]
    lane = lax.broadcasted_iota(jnp.int32, (rows, ka), 1)
    return jnp.where(lane == ka - 1, field_ref[p], pltpu.roll(field_ref[p + 1 - kb], ka - 1, 1))


def prev_plane(field_ref, p, kb):
    rows, ka = field_ref.shape[1:]
    if p % kb:
        return field_ref[p - 1]
    lane = lax.broadcasted_iota(jnp.int32, (rows, ka), 1)
    return jnp.where(lane == 0, field_ref[p], pltpu.roll(field_ref[p + kb - 1], 1, 1))


def first_kernel(
    gz, edge_ref, field_ref, coef_ref, tw_ref, table_ref, sums_ref, spec_ref, *refs
):
    piece_refs, (re_s, im_s) = refs[:-2], refs[-2:]
    planes, rows, ka = field_ref.shape
    kb = planes // gz
    projected = forward_into(gz, field_ref, coef_ref, tw_ref, table_ref, spec_ref, re_s, im_s)
    cut(gz, edge_ref, spec_ref, piece_refs)
    row = lax.broadcasted_iota(jnp.int32, (rows, ka), 0)
    square = jnp.zeros((8, LANES), F32)
    slope = jnp.zeros((8, LANES), F32)
    for p in range(planes):
        here = field_ref[p]
        square = square + fold(here * here)
        along_x = next_plane(field_ref, p, kb) - here
        along_y = jnp.where(row == rows - 1, 0.0, pltpu.roll(here, rows - 1, 0) - here)
        terms = along_x * along_x + along_y * along_y
        if p + kb < planes:
            along_z = field_ref[p + kb] - here
            terms = terms + along_z * along_z
        slope = slope + fold(terms)
    sums_ref[0] = square
    sums_ref[1] = projected
    sums_ref[2] = slope


def columns_back(spec_ref, chunk, coef_ref, tw_ref, re_s, im_s, j, carry):
    gz, kb = spec_ref.shape[:2]
    lanes = slice(chunk * LANES, (chunk + 1) * LANES)
    part = pl.ds(pl.multiple_of(j * 8, 8), 8)
    spectra = [
        [(spec_ref[z, k, chunk, 0, part, :], spec_ref[z, k, chunk, 1, part, :]) for k in range(kb)]
        for z in range(gz)
    ]
    inverse_columns(gz, kb, spectra, coef_ref, tw_ref, lanes, part, re_s, im_s)
    return carry


def middle_kernel(
    spec_hbm, coef_ref, tw_ref, inverse_ref, forward_ref,
    d0_ref, head_ref, tail_ref, spec_ref, re_s, im_s, sems,
):
    gz, kb, chunks, _, rows, _ = spec_ref.shape
    ka = chunks * LANES
    planes = gz * kb

    def fetch(chunk):
        return pltpu.make_async_copy(
            spec_hbm.at[:, :, chunk], spec_ref.at[:, :, chunk], sems.at[chunk]
        )

    for chunk in range(chunks):
        fetch(chunk).start()
    for chunk in range(chunks):
        fetch(chunk).wait()
        lax.fori_loop(
            0, rows // 8,
            functools.partial(columns_back, spec_ref, chunk, coef_ref, tw_ref, re_s, im_s), 0,
        )

    step = plane_chunk(planes, rows)
    shape2, shape3 = (step * rows, ka), (step, rows, ka)

    def there_and_back(i, carry):
        part = pl.ds(i * step, step)
        field = inverse_product(re_s[part].reshape(shape2), im_s[part].reshape(shape2), inverse_ref)
        d0_ref[part] = field.reshape(shape3)
        re, im = forward_product(field, forward_ref)
        re_s[part] = re.reshape(shape3)
        im_s[part] = im.reshape(shape3)
        return carry

    lax.fori_loop(0, planes // step, there_and_back, 0)

    def second_columns(j, total):
        part = pl.ds(pl.multiple_of(j * 8, 8), 8)
        for chunk in range(chunks):
            lanes = slice(chunk * LANES, (chunk + 1) * LANES)
            spectra = forward_columns(gz, kb, coef_ref, tw_ref, lanes, part, re_s, im_s)
            for z in range(gz):
                for k in range(kb):
                    for p in range(2):
                        value = spectra[z][k][p]
                        spec_ref[z, k, chunk, p, part, :] = value
                        total = total + value * value
        return total

    projected = lax.fori_loop(0, rows // 8, second_columns, jnp.zeros((8, LANES), F32))
    for p in range(planes):
        head_ref[p : p + 1, :] = d0_ref[p, :1, :]
        head_ref[planes + p : planes + p + 1, :] = d0_ref[p, 1:2, :]
        for part in range(2):
            at = 2 * planes + 2 * p + part
            for chunk in range(chunks):
                lanes = slice(chunk * LANES, (chunk + 1) * LANES)
                head_ref[at : at + 1, lanes] = spec_ref[p // kb, p % kb, chunk, part, :1, :]
        tail_ref[p : p + 1, :] = d0_ref[p, rows - 1 : rows, :]

    row = lax.broadcasted_iota(jnp.int32, (rows, ka), 0)
    square = jnp.zeros((8, LANES), F32)
    slope = jnp.zeros((8, LANES), F32)
    for p in range(planes):
        here = d0_ref[p]
        square = square + fold(here * here)
        along_x = next_plane(d0_ref, p, kb) - here
        along_y = jnp.where(row == rows - 1, 0.0, pltpu.roll(here, rows - 1, 0) - here)
        terms = along_x * along_x + along_y * along_y
        if p + kb < planes:
            along_z = d0_ref[p + kb] - here
            terms = terms + along_z * along_z
        slope = slope + fold(terms)
    block = sums_block([square, projected, slope])
    for ref in (head_ref, tail_ref):
        at = ref.shape[0] - 8
        ref[at:, :] = jnp.zeros((8, ka), F32)
        ref[at:, :LANES] = block


def middle(spec, coef, nx):
    gz, kb, chunks, _, rows, _ = spec.shape
    ka = chunks * LANES
    planes = gz * kb
    vmem = pl.BlockSpec(memory_space=pltpu.VMEM)
    field = jax.ShapeDtypeStruct((planes, rows, ka), F32)
    return pl.pallas_call(
        middle_kernel,
        in_specs=[pl.BlockSpec(memory_space=pltpu.HBM)] + [vmem] * 4,
        out_specs=[vmem] * 4,
        out_shape=[
            field,
            jax.ShapeDtypeStruct((4 * planes + 8, ka), F32),
            jax.ShapeDtypeStruct((planes + 8, ka), F32),
            jax.ShapeDtypeStruct(spec.shape, F32),
        ],
        scratch_shapes=[
            pltpu.VMEM((planes, rows, ka), F32),
            pltpu.VMEM((planes, rows, ka), F32),
            pltpu.SemaphoreType.DMA((chunks,)),
        ],
        compiler_params=pltpu.CompilerParams(vmem_limit_bytes=X_GRANT),
        name="middle",
    )(
        spec, coef, x_twiddle(nx, ka), jnp.asarray(x_inverse_matrix(nx, ka)),
        x_forward_matrix(nx, ka),
    )


def normal_kernel(spec_ref, coef_ref, tw_ref, table_ref, out_ref, re_s, im_s):
    gz, kb, chunks, _, rows, _ = spec_ref.shape
    planes, ka = gz * kb, chunks * LANES

    for chunk in range(chunks):
        lax.fori_loop(
            0, rows // 8,
            functools.partial(columns_back, spec_ref, chunk, coef_ref, tw_ref, re_s, im_s), 0,
        )

    step = plane_chunk(planes, rows)
    shape = (step * rows, ka)
    for start in range(0, planes, step):
        part = slice(start, start + step)
        field = inverse_product(re_s[part].reshape(shape), im_s[part].reshape(shape), table_ref)
        out_ref[part] = field.reshape(step, rows, ka)


def normal_product(spec, coef, nx):
    gz, kb, chunks, _, rows, _ = spec.shape
    planes, ka = gz * kb, chunks * LANES
    vmem = pl.BlockSpec(memory_space=pltpu.VMEM)
    return pl.pallas_call(
        normal_kernel,
        in_specs=[vmem] * 4,
        out_specs=vmem,
        out_shape=jax.ShapeDtypeStruct((planes, rows, ka), F32),
        scratch_shapes=[pltpu.VMEM((planes, rows, ka), F32)] * 2,
        compiler_params=pltpu.CompilerParams(vmem_limit_bytes=X_GRANT),
        cost_estimate=pl.CostEstimate(
            flops=12 * planes * rows * ka * ka, bytes_accessed=12 * planes * rows * ka, transcendentals=0
        ),
        name="normal_product",
    )(spec, coef, x_twiddle(nx, ka), jnp.asarray(x_inverse_matrix(nx, ka)))


def next_normal_row(gz, next_ref, coef_ref, tw_ref, table_ref, row_s, re_s, im_s):
    planes, ka = row_s.shape
    kb = planes // gz
    for start in range(0, ka, LANES):
        lanes = slice(start, start + LANES)

        def row_of(z, k, part):
            at = 2 * planes + 2 * (z * kb + k) + part
            return jnp.broadcast_to(next_ref[at : at + 1, lanes], (8, LANES))

        spectra = [[(row_of(z, k, 0), row_of(z, k, 1)) for k in range(kb)] for z in range(gz)]
        inverse_columns(gz, kb, spectra, coef_ref, tw_ref, lanes, slice(0, 8), re_s, im_s)
    shape = (planes * 8, ka)
    field = inverse_product(re_s[...].reshape(shape), im_s[...].reshape(shape), table_ref)
    for p in range(planes):
        row_s[p : p + 1, :] = field[8 * p : 8 * p + 1, :]


def border_kernel(edge_ref, head_ref, tail_ref, next_ref, prev_ref, after_ref, out_ref):
    del after_ref
    planes = tail_ref.shape[0] - 8

    def sums_of(ref):
        return ref[ref.shape[0] - 8 :, :LANES]

    def border(after, before):
        step = after[:planes, :] - before[:planes, :]
        return fold(step * step)

    second = edge_ref[2] > 0
    below = border(head_ref, prev_ref) * jnp.where(edge_ref[0] > 0, 0.0, 1.0)
    above = border(next_ref, tail_ref) * jnp.where(edge_ref[1] > 0, 0.0, 1.0)
    other = jnp.where(second, sums_of(prev_ref), sums_of(next_ref))
    none = jnp.zeros((8, LANES), F32)
    put_copies(out_ref, sums_of(tail_ref) + other + sums_block([none, none, below + above]))


def border_sums(edge, head, tail, next_head, prev_tail, after, copies):
    vmem = pl.BlockSpec(memory_space=pltpu.VMEM)
    return pl.pallas_call(
        border_kernel,
        in_specs=[pl.BlockSpec(memory_space=pltpu.SMEM)]
        + [vmem] * 4
        + [pl.BlockSpec(memory_space=pl.ANY)],
        out_specs=vmem,
        out_shape=jax.ShapeDtypeStruct((copies, 8, LANES), F32),
        compiler_params=pltpu.CompilerParams(vmem_limit_bytes=2 * MIB),
        name="border_sums",
    )(edge, head, tail, next_head, prev_tail, after)


def second_kernel(
    gz, edge_ref, d0_ref, nd0_ref, tail_ref, prev_ref, next_ref,
    coef_ref, tw_ref, table_ref, inverse_ref, *refs,
):
    sums_ref, d1_ref, eta_ref, out_ref, spec_ref, re_s, im_s, row_s, nrow_s, re8_s, im8_s = refs
    next_normal_row(gz, next_ref, coef_ref, tw_ref, inverse_ref, nrow_s, re8_s, im8_s)
    planes, rows, ka = d0_ref.shape
    kb = planes // gz
    eta_here = step_of(sums_ref)
    eta_ref[...] = jnp.broadcast_to(eta_here, (8, LANES))
    eta = jnp.max(eta_here)
    first = edge_ref[0] > 0
    last = edge_ref[1] > 0

    def shrink(difference):
        return jnp.clip(-eta * difference, -CLIP, CLIP)

    lane2 = lax.broadcasted_iota(jnp.int32, (kb, ka), 1)
    row2 = lax.broadcasted_iota(jnp.int32, (kb, ka), 0)
    for z in range(gz):
        part = slice(z * kb, (z + 1) * kb)
        here = next_ref[part, :]
        value = here - eta * nrow_s[part, :]
        up = pltpu.roll(here, kb - 1, 0)
        up = jnp.where(
            row2 == kb - 1, jnp.where(lane2 == ka - 1, here, pltpu.roll(up, ka - 1, 1)), up
        )
        down = pltpu.roll(here, 1, 0)
        down = jnp.where(row2 == 0, jnp.where(lane2 == 0, here, pltpu.roll(down, 1, 1)), down)
        value = value + shrink(here - down) - shrink(up - here)
        value = value + shrink(here - tail_ref[part, :]) - shrink(next_ref[planes + z * kb : planes + (z + 1) * kb, :] - here)
        if z > 0:
            value = value + shrink(here - next_ref[(z - 1) * kb : z * kb, :])
        if z + 1 < gz:
            value = value - shrink(next_ref[(z + 1) * kb : (z + 2) * kb, :] - here)
        row_s[part, :] = value

    row = lax.broadcasted_iota(jnp.int32, (rows, ka), 0)
    square = jnp.zeros((8, LANES), F32)
    for p in range(planes):
        here = d0_ref[p]
        value = here - eta * nd0_ref[p]
        value = value + shrink(here - prev_plane(d0_ref, p, kb))
        value = value - shrink(next_plane(d0_ref, p, kb) - here)
        below = jnp.where(last, here[rows - 1 :, :], next_ref[p : p + 1, :])
        above = jnp.where(first, here[:1, :], prev_ref[p : p + 1, :])
        upper = shrink(jnp.where(row == rows - 1, below, pltpu.roll(here, rows - 1, 0)) - here)
        lower = jnp.where(row == 0, shrink(here[:1, :] - above), pltpu.roll(upper, 1, 0))
        value = value + lower - upper
        if p >= kb:
            value = value + shrink(here - d0_ref[p - kb])
        if p + kb < planes:
            value = value - shrink(d0_ref[p + kb] - here)
        d1_ref[p] = value
        square = square + fold(value * value)

    slope = jnp.zeros((8, LANES), F32)
    for p in range(planes):
        here = d1_ref[p]
        along_x = next_plane(d1_ref, p, kb) - here
        below = jnp.where(last, here[rows - 1 :, :], row_s[p : p + 1, :])
        along_y = jnp.where(row == rows - 1, below, pltpu.roll(here, rows - 1, 0)) - here
        terms = along_x * along_x + along_y * along_y
        if p + kb < planes:
            along_z = d1_ref[p + kb] - here
            terms = terms + along_z * along_z
        slope = slope + fold(terms)

    step = plane_chunk(planes, rows)

    def multiply(i, carry):
        part = pl.ds(i * step, step)
        re, im = forward_product(d1_ref[part].reshape(step * rows, ka), table_ref)
        re_s[part] = re.reshape(step, rows, ka)
        im_s[part] = im.reshape(step, rows, ka)
        return carry

    lax.fori_loop(0, planes // step, multiply, 0)

    def columns(j, total):
        part = pl.ds(pl.multiple_of(j * 8, 8), 8)
        for chunk in range(ka // LANES):
            lanes = slice(chunk * LANES, (chunk + 1) * LANES)
            spectra = forward_columns(gz, kb, coef_ref, tw_ref, lanes, part, re_s, im_s)
            for z in range(gz):
                for k in range(kb):
                    for p in range(2):
                        value = spectra[z][k][p]
                        spec_ref[z, k, chunk, p, part, :] = value
                        total = total + value * value
        return total

    projected = lax.fori_loop(0, rows // 8, columns, jnp.zeros((8, LANES), F32))
    put_copies(out_ref, sums_block([square, projected, slope]))


def second_descent(edge, sums, d0, nd0, tail, prev_tail, next_head, coef, gz, nx, copies):
    planes, rows, ka = d0.shape
    vmem = pl.BlockSpec(memory_space=pltpu.VMEM)
    return pl.pallas_call(
        functools.partial(second_kernel, gz),
        in_specs=[pl.BlockSpec(memory_space=pltpu.SMEM)] + [vmem] * 10,
        out_specs=[vmem] * 4,
        out_shape=[
            jax.ShapeDtypeStruct((planes, rows, ka), F32),
            jax.ShapeDtypeStruct((8, LANES), F32),
            jax.ShapeDtypeStruct((copies, 8, LANES), F32),
            jax.ShapeDtypeStruct((gz, planes // gz, ka // LANES, 2, rows, LANES), F32),
        ],
        scratch_shapes=[
            pltpu.VMEM((planes, rows, ka), F32),
            pltpu.VMEM((planes, rows, ka), F32),
            pltpu.VMEM((planes, ka), F32),
            pltpu.VMEM((planes, ka), F32),
            pltpu.VMEM((planes, 8, ka), F32),
            pltpu.VMEM((planes, 8, ka), F32),
        ],
        compiler_params=pltpu.CompilerParams(vmem_limit_bytes=X_GRANT),
        name="second_descent",
    )(
        edge, d0, nd0, tail, prev_tail, next_head, coef,
        x_twiddle(nx, ka), x_forward_matrix(nx, ka), jnp.asarray(x_inverse_matrix(nx, ka)), sums,
    )


def combine_kernel(eta_ref, sums_ref, first_ref, second_ref, out_ref, steps_ref):
    eta0 = jnp.max(eta_ref[...])
    eta1 = jnp.max(step_of(sums_ref))
    steps_ref[0] = eta_ref[...]
    steps_ref[1] = jnp.full((8, LANES), eta1, F32)
    count = out_ref.shape[0]
    start = pl.program_id(0) * count
    for i in range(count):
        out_ref[i] = -(eta0 * first_ref[start + i] + eta1 * second_ref[start + i])


def combine_spectra(eta, sums, first, second):
    planes, *rest = first.shape
    count = 4 if planes % 4 == 0 else 1
    vmem = pl.BlockSpec(memory_space=pltpu.VMEM)
    return pl.pallas_call(
        combine_kernel,
        grid=(planes // count,),
        in_specs=[vmem] * 4,
        out_specs=[
            pl.BlockSpec((count, *rest), lambda i: (i, 0, 0, 0, 0)),
            pl.BlockSpec((2, 8, LANES), lambda i: (0, 0, 0)),
        ],
        out_shape=[
            jax.ShapeDtypeStruct(first.shape, F32),
            jax.ShapeDtypeStruct((2, 8, LANES), F32),
        ],
        compiler_params=pltpu.CompilerParams(vmem_limit_bytes=6 * MIB),
        name="combine_spectra",
    )(eta, sums, first, second)


def to_core(piece, r):
    gz = lax.axis_size("gz")
    return lax.ppermute(piece, "gz", [(i, (i + r) % gz) for i in range(gz)]) if r else piece


def near_chips(gy):
    near = 1
    while near * near < gy:
        near *= 2
    return near


def resum_kernel(in_ref, out_ref):
    put_copies(out_ref, jnp.sum(in_ref[...], axis=0))


def everywhere(sums, both_cores):
    gz, gy = lax.axis_size("gz"), lax.axis_size("gy")
    near = near_chips(gy)
    far = gy // near
    cores = range(gz) if both_cores else range(1)
    groups = [[g * gy + k * near + j for g in cores for j in range(near)] for k in range(far)]
    axes = ("gz", "gy") if both_cores else "gy"
    sums = lax.all_to_all(sums, axes, 0, 0, tiled=True, axis_index_groups=groups)
    vmem = pl.BlockSpec(memory_space=pltpu.VMEM)
    sums = pl.pallas_call(
        resum_kernel,
        in_specs=[vmem],
        out_specs=vmem,
        out_shape=jax.ShapeDtypeStruct((far, 8, LANES), F32),
        compiler_params=pltpu.CompilerParams(vmem_limit_bytes=2 * MIB),
        name="resum",
    )(sums)
    groups = [[j + k * near for k in range(far)] for j in range(near)]
    return lax.all_to_all(sums, "gy", 0, 0, tiled=True, axis_index_groups=groups)


def to_devices(parts):
    gz, gy, *rest = parts.shape
    parts = lax.all_to_all(parts.reshape(gz * gy, *rest), ("gz", "gy"), 0, 0, tiled=True)
    return parts.reshape(gz, gy, *rest)


def shards(data, band_offset, interp_weight):
    gz = lax.axis_size("gz")
    gy = lax.axis_size("gy")
    devices = gz * gy
    data = data[0]
    blocks, ny, width = data.shape
    rows = ny // devices
    ka = blocks * HALF
    nx = ka * gy

    core = lax.axis_index("gz")
    flat = lax.axis_index("gy") * gz + core
    edge = jnp.stack([flat == 0, flat == devices - 1, core]).astype(jnp.int32)
    order = [(i % gz) * gy + i // gz for i in range(devices)]
    up = [(order[i + 1], order[i]) for i in range(devices - 1)]
    down = [(order[i], order[i + 1]) for i in range(devices - 1)]

    lower = band_offset < 0
    weight = interp_weight
    coef = jnp.stack(
        [
            jnp.where(lower, weight[1], weight[0]),
            jnp.where(lower, weight[0], 0.0),
            jnp.where(lower, 0.0, weight[1]),
        ]
    ).reshape(3, gy, 1, ka)
    coef = jnp.broadcast_to(coef, (3, gy, 8, ka))

    spec = to_devices(y_inverse(data, rows, gz, gy))
    d0, head, tail, first = middle(spec, coef, nx)
    next_head = lax.ppermute(head, ("gz", "gy"), up)
    prev_tail = lax.ppermute(tail, ("gz", "gy"), down)
    nd0 = normal_product(first, coef, nx)
    near = near_chips(gy)
    sums = everywhere(border_sums(edge, head, tail, next_head, prev_tail, nd0, near), False)
    d1, eta, sums, second = second_descent(
        edge, sums, d0, nd0, tail, prev_tail, next_head, coef, gz, nx, gz * near
    )
    sums = everywhere(sums, True)
    flat_shape = (devices, ka // LANES, 2, rows, LANES)
    spec, etas = combine_spectra(eta, sums, first.reshape(flat_shape), second.reshape(flat_shape))
    residual = y_forward(to_devices(spec.reshape(first.shape)), data)

    volume = -(etas[0, 0, 0] * d0 + etas[1, 0, 0] * d1)
    volume = volume.reshape(gz, gy, rows, ka).transpose(0, 2, 3, 1).reshape(gz, rows, nx)
    parts = [
        to_core(lax.dynamic_index_in_dim(volume, lax.rem(core + r, gz), 0, False), r)
        for r in range(gz)
    ]
    volume = jnp.zeros((gz, rows, nx), F32)
    for r, part in enumerate(parts):
        volume = lax.dynamic_update_index_in_dim(volume, part, lax.rem(core + gz - r, gz), 0)
    return (volume.reshape(1, gz * rows, nx), residual[None])


NX = 4096
NY = 2048
XB = 64
YB = 64
ITERS = 2
XA = 64
YA = 32
PRECISE = lax.Precision.HIGHEST


def with_halo(block, sides, width):
    for axis, dim in sides:
        count = lax.axis_size(axis)
        forward = [(i, i + 1) for i in range(count - 1)]
        backward = [(target, source) for source, target in forward]
        low = lax.ppermute(
            lax.slice_in_dim(block, block.shape[dim] - width, None, axis=dim), axis, forward
        )
        high = lax.ppermute(lax.slice_in_dim(block, 0, width, axis=dim), axis, backward)
        block = jnp.concatenate([low, block, high], axis=dim)
    return block


def from_behind(block, axis, distance):
    devices = range(lax.axis_size(axis))
    route = [(i - distance, i) for i in devices if i - distance in devices]
    return lax.ppermute(block, axis, route)


def unit_table(length):
    counter = jnp.arange(length, dtype=jnp.int32)
    phase_int = counter[:, None] * counter[None, :] % length
    angles = 2.0 * jnp.pi / length * phase_int.astype(jnp.float32)
    factor = length ** (-0.5)
    return (jnp.cos(angles) * factor, jnp.sin(angles) * factor)


def twiddle_table(row_len, col_len, period):
    phase_int = (
        jnp.arange(row_len, dtype=jnp.int32)[:, None]
        * jnp.arange(col_len, dtype=jnp.int32)[None, :]
        % period
    )
    angles = 2.0 * jnp.pi / period * phase_int.astype(jnp.float32)
    return (jnp.cos(angles), jnp.sin(angles))


def split_parts(packed):
    half_width = packed.shape[-1] // 2
    return (packed[..., :half_width], packed[..., half_width:])


def join_parts(real_part, imag_part):
    return jnp.concatenate([real_part, imag_part], axis=-1)


def complex_contract(packed, cos_table, sin_table, subscripts, conj_sign):
    cos_out = jnp.einsum(subscripts, packed, cos_table, precision=PRECISE)
    sin_out = jnp.einsum(subscripts, packed, sin_table, precision=PRECISE)
    cos_re, cos_im = split_parts(cos_out)
    sin_re, sin_im = split_parts(sin_out)
    return join_parts(cos_re - conj_sign * sin_im, cos_im + conj_sign * sin_re)


def rotate(packed, cos_table, sin_table, conj_sign):
    real_part, imag_part = split_parts(packed)
    return join_parts(
        real_part * cos_table - conj_sign * imag_part * sin_table,
        imag_part * cos_table + conj_sign * real_part * sin_table,
    )


def forward_x(volume):
    slices, row_count = (volume.shape[0], volume.shape[1])
    cos_a, sin_a = unit_table(XA)
    cos_b, sin_b = unit_table(XB)
    first_table = jnp.concatenate([cos_a, -sin_a], axis=1)
    grid_view = volume.reshape(slices, row_count, XA, XB)
    mixing = jnp.einsum("zyab,am->zybm", grid_view, first_table, precision=PRECISE)
    tw_cos, tw_sin = twiddle_table(XB, XA, NX)
    mixing = rotate(mixing, tw_cos, tw_sin, -1.0)
    return complex_contract(mixing, cos_b, sin_b, "zybm,bl->zlym", -1.0)


def inverse_x(packed):
    slices, row_count = (packed.shape[0], packed.shape[2])
    cos_a, sin_a = unit_table(XA)
    cos_b, sin_b = unit_table(XB)
    mixing = complex_contract(packed, cos_b, sin_b, "zlym,lb->zybm", 1.0)
    tw_cos, tw_sin = twiddle_table(XB, XA, NX)
    mixing = rotate(mixing, tw_cos, tw_sin, 1.0)
    last_table = jnp.concatenate([cos_a, -sin_a], axis=0)
    grid_view = jnp.einsum("zybm,ma->zyab", mixing, last_table, precision=PRECISE)
    return grid_view.reshape(slices, row_count, NX)


def forward_y(packed):
    slices, blocks, width = (packed.shape[0], packed.shape[1], packed.shape[3])
    cos_a, sin_a = unit_table(YA)
    cos_b, sin_b = unit_table(YB)
    grid_view = packed.reshape(slices, blocks, YA, YB, width)
    mixing = complex_contract(grid_view, cos_a, sin_a, "zjcdm,ck->zjkdm", -1.0)
    tw_cos, tw_sin = twiddle_table(YA, YB, NY)
    mixing = rotate(mixing, tw_cos[:, :, None], tw_sin[:, :, None], -1.0)
    result = complex_contract(mixing, cos_b, sin_b, "zjkdm,dl->zjlkm", -1.0)
    return result.reshape(slices, blocks, NY, width)


def inverse_y(packed):
    slices, blocks, width = (packed.shape[0], packed.shape[1], packed.shape[3])
    cos_a, sin_a = unit_table(YA)
    cos_b, sin_b = unit_table(YB)
    grid_view = packed.reshape(slices, blocks, YB, YA, width)
    mixing = complex_contract(grid_view, cos_b, sin_b, "zjlkm,ld->zjkdm", 1.0)
    tw_cos, tw_sin = twiddle_table(YA, YB, NY)
    mixing = rotate(mixing, tw_cos[:, :, None], tw_sin[:, :, None], 1.0)
    result = complex_contract(mixing, cos_a, sin_a, "zjkdm,kc->zjcdm", 1.0)
    return result.reshape(slices, blocks, NY, width)


def tilt_coefficients(band_offset, interp_weight, first_block, blocks):
    offsets = lax.dynamic_slice_in_dim(band_offset.reshape(XB, XA), first_block, blocks, 0)
    weights = lax.dynamic_slice_in_dim(interp_weight.reshape(2, XB, XA), first_block, blocks, 1)
    lower_tap = (jnp.concatenate([offsets, offsets], axis=1) < 0)[:, None, :]
    first_weight = jnp.concatenate([weights[0], weights[0]], axis=1)[:, None, :]
    second_weight = jnp.concatenate([weights[1], weights[1]], axis=1)[:, None, :]
    return (lower_tap, first_weight, second_weight)


def tilt(field_in, coefficients, adjoint):
    lower_tap, first_weight, second_weight = coefficients
    padded = with_halo(field_in, (("gz", 0),), 1)
    below_rim = padded[:-2]
    middle = padded[1:-1]
    above_rim = padded[2:]
    if adjoint:
        return jnp.where(
            lower_tap,
            first_weight * above_rim + second_weight * middle,
            first_weight * middle + second_weight * below_rim,
        )
    return jnp.where(
        lower_tap,
        first_weight * below_rim + second_weight * middle,
        first_weight * middle + second_weight * above_rim,
    )


def to_pencil(slab_part):
    return lax.all_to_all(slab_part, "gy", split_axis=1, concat_axis=2, tiled=True)


def to_slab(pencil_part):
    return lax.all_to_all(pencil_part, "gy", split_axis=2, concat_axis=1, tiled=True)


def back_project(packed, pencil_coef):
    return inverse_x(to_slab(inverse_y(tilt(packed, pencil_coef, True))))


def edge_masks(slices, row_count):
    z_global = lax.axis_index("gz") * slices + jnp.arange(slices, dtype=jnp.int32)
    y_global = lax.axis_index("gy") * row_count + jnp.arange(row_count, dtype=jnp.int32)
    keep_z = (z_global < slices * lax.axis_size("gz") - 1).astype(jnp.float32)[:, None, None]
    keep_y = (y_global < row_count * lax.axis_size("gy") - 1).astype(jnp.float32)[None, :, None]
    return (keep_z, keep_y)


def forward_diff(field_in, keep_z, keep_y):
    slices, row_count = (field_in.shape[0], field_in.shape[1])
    next_z = from_behind(field_in, "gz", -1)
    next_y = from_behind(field_in[:, :1], "gy", -1)
    along_z = (jnp.concatenate([field_in[1:], next_z], axis=0) - field_in) * keep_z
    along_y = (jnp.concatenate([field_in[:, 1:], next_y], axis=1) - field_in) * keep_y
    zero_col = jnp.zeros((slices, row_count, 1), jnp.float32)
    along_x = jnp.concatenate([field_in[:, :, 1:] - field_in[:, :, :-1], zero_col], axis=2)
    return jnp.stack([along_z, along_y, along_x])


def transpose_diff(components, keep_z, keep_y):
    slices, row_count = (components.shape[1], components.shape[2])
    zero_col = jnp.zeros((slices, row_count, 1), jnp.float32)
    comp_z = components[0] * keep_z
    comp_y = components[1] * keep_y
    comp_x = jnp.concatenate([components[2][:, :, :-1], zero_col], axis=2)
    prev_z = from_behind(comp_z, "gz", 1)
    prev_y = from_behind(comp_y[:, -1:], "gy", 1)
    result = jnp.concatenate([prev_z, comp_z[:-1]], axis=0) - comp_z
    result = result + jnp.concatenate([prev_y, comp_y[:, :-1]], axis=1) - comp_y
    result = result + jnp.concatenate([zero_col, comp_x[:, :, :-1]], axis=2) - comp_x
    return result


def plain_shards(data, band_offset, interp_weight):
    slices = data.shape[0]
    blocks = data.shape[1]
    width = data.shape[3]
    row_count = NY // lax.axis_size("gy")
    slab_coef = tilt_coefficients(band_offset, interp_weight, 0, XB)
    pencil_coef = tilt_coefficients(
        band_offset, interp_weight, lax.axis_index("gy") * blocks, blocks
    )
    keep_z, keep_y = edge_masks(slices, row_count)
    measured = data.astype(jnp.float32)
    volume = jnp.zeros((slices, row_count, NX), jnp.float32)
    grad_volume = jnp.zeros((3, slices, row_count, NX), jnp.float32)
    split_var = grad_volume
    dual_var = grad_volume
    data_back = back_project(measured, pencil_coef)
    normal_part = jnp.zeros_like(volume)
    tilted = jnp.zeros((slices, XB, row_count, width), jnp.float32)
    for iteration in range(ITERS):
        data_grad = normal_part - data_back
        if iteration > 0:
            tv_gap = grad_volume - split_var + dual_var / PENALTY
            descent = data_grad + PENALTY * transpose_diff(tv_gap, keep_z, keep_y)
        else:
            descent = data_grad
        slope_field = forward_diff(descent, keep_z, keep_y)
        projected = tilt(forward_x(descent), slab_coef, False)
        line_totals = lax.psum(
            (
                jnp.sum(descent * descent),
                jnp.sum(projected * projected),
                jnp.sum(slope_field * slope_field),
            ),
            ("gz", "gy"),
        )
        step_length = line_totals[0] / (line_totals[1] + PENALTY * line_totals[2])
        volume = volume - step_length * descent
        grad_volume = grad_volume - step_length * slope_field
        tilted = tilted - step_length * projected
        if iteration + 1 < ITERS:
            normal_part = normal_part - step_length * inverse_x(tilt(projected, slab_coef, True))
        if iteration + 1 < ITERS:
            shifted = grad_volume + dual_var / PENALTY
            split_var = shifted - jnp.clip(shifted, -TV_WEIGHT / PENALTY, TV_WEIGHT / PENALTY)
            dual_var = PENALTY * (grad_volume - split_var)
    residual = forward_y(to_pencil(tilted)) - measured
    return (volume, residual)


def tiles_fit(mesh, ny, blocks):
    rows = ny // (mesh.shape["gz"] * mesh.shape["gy"])
    return mesh.shape["gz"] == 2 and rows % 16 == 0 and mesh.shape["gy"] % YR == 0 and blocks // mesh.shape["gy"] % 2 == 0


def solution(mesh):
    in_specs = (P("gz", "gy", None, None), P(), P())
    out_specs = (P("gz", "gy", None), P("gz", "gy", None, None))

    def run(data, band_offset, interp_weight):
        body = shards if tiles_fit(mesh, data.shape[2], data.shape[1]) else plain_shards
        call = jax.shard_map(
            body, mesh=mesh, in_specs=in_specs, out_specs=out_specs, check_vma=False
        )
        return call(data, band_offset, interp_weight)

    return run
```

```python
import functools

import jax
import jax.numpy as jnp
import numpy as np
from jax import lax
from jax.experimental import pallas as pl
from jax.experimental.pallas import tpu as pltpu
from jax.sharding import PartitionSpec as P

PENALTY = 0.5
TV_WEIGHT = 0.25
CLIP = TV_WEIGHT / PENALTY
HALF = 64
YR = 8
LANES = 128
F32 = jnp.float32
BF16 = jnp.bfloat16
MIB = 1024 * 1024
Y_GRANT = 56 * MIB
X_GRANT = 20 * MIB


def dft_parts(length, scale):
    index = np.arange(length)
    angles = 2.0 * np.pi / length * (index[:, None] * index[None, :] % length)
    return np.cos(angles) * scale, np.sin(angles) * scale


def host_parts(table):
    table = table.astype(np.float32)
    high = table.astype(BF16)
    low = (table - high.astype(np.float32)).astype(BF16)
    return high, low


def y_matrix(ny, forward, sign):
    n = ny // YR
    cos, sin = dft_parts(n, sign * ny**-0.5)
    if forward:
        table = np.block([[cos, sin], [-sin, cos]])
    else:
        table = np.block([[cos, -sin], [sin, cos]])
    return jnp.asarray(np.concatenate(host_parts(table), axis=0))


def y_twiddle(ny):
    n = ny // YR
    angles = 2.0 * np.pi / ny * (np.arange(1, YR)[:, None] * np.arange(n)[None, :])
    table = np.stack([np.cos(angles), np.sin(angles)]).astype(np.float32)
    return jnp.asarray(np.ascontiguousarray(np.broadcast_to(table[..., None], (2, YR - 1, n, LANES))))


def x_inverse_matrix(nx, ka):
    cos, sin = dft_parts(ka, nx**-0.5)
    return np.concatenate(host_parts(np.concatenate([cos, -sin], axis=0)), axis=1)


def x_forward_matrix(nx, ka):
    cos, sin = dft_parts(ka, nx**-0.5)
    return jnp.asarray(np.concatenate(host_parts(np.concatenate([cos, -sin], axis=1)), axis=1))


def x_twiddle(nx, ka):
    kb = nx // ka
    angles = 2.0 * np.pi / nx * (np.arange(kb)[:, None] * np.arange(ka)[None, :])
    table = np.stack([np.cos(angles), np.sin(angles)]).astype(np.float32)
    return jnp.asarray(np.ascontiguousarray(np.broadcast_to(table[:, :, None], (2, kb, 8, ka))))


def short_fft(planes, sign):
    n = len(planes)
    if n == 1:
        return planes
    even = short_fft(planes[0::2], sign)
    odd = short_fft(planes[1::2], sign)
    half = n // 2
    out = [None] * n
    for k in range(half):
        er, ei = even[k]
        tr, ti = odd[k]
        if 4 * k == n:
            if sign > 0:
                out[k] = (er - ti, ei + tr)
                out[k + half] = (er + ti, ei - tr)
            else:
                out[k] = (er + ti, ei - tr)
                out[k + half] = (er - ti, ei + tr)
            continue
        if k > 0:
            c = float(np.cos(2.0 * np.pi * k / n))
            s = float(sign * np.sin(2.0 * np.pi * k / n))
            if 8 * k == n:
                tr, ti = (tr - ti, ti + tr) if sign > 0 else (tr + ti, ti - tr)
                tr, ti = tr * c, ti * c
            elif 8 * k == 3 * n:
                m = float(np.sin(2.0 * np.pi * k / n))
                tr, ti = (-(tr + ti), tr - ti) if sign > 0 else (ti - tr, -(tr + ti))
                tr, ti = tr * m, ti * m
            else:
                tr, ti = tr * c - ti * s, ti * c + tr * s
        out[k] = (er + tr, ei + ti)
        out[k + half] = (er - tr, ei - ti)
    return out


def split2(x):
    high = x.astype(BF16)
    return high, (x - high.astype(F32)).astype(BF16)


def dot(a, b):
    return jnp.dot(a, b, preferred_element_type=F32)


def fold(x):
    rows, lanes = x.shape
    x = jnp.sum(x.reshape(rows // 8, 8, lanes), axis=0)
    total = x[:, :LANES]
    for i in range(1, lanes // LANES):
        total = total + x[:, i * LANES : (i + 1) * LANES]
    return total


def full_sum(x):
    return jnp.sum(jnp.sum(x, axis=0, keepdims=True), axis=1, keepdims=True)


def step_of(sums_refs):
    total = sum(jnp.sum(sums_ref[...], axis=0) for sums_ref in sums_refs)
    parts = jnp.sum(total, axis=1, keepdims=True)
    return parts[0:1] / (parts[1:2] + PENALTY * parts[2:3])


def sums_block(values):
    rows = [jnp.sum(v, axis=0, keepdims=True) for v in values]
    index = lax.broadcasted_iota(jnp.int32, (8, LANES), 0)
    block = jnp.zeros((8, LANES), F32)
    for i, row in enumerate(rows):
        block = jnp.where(index == i, jnp.broadcast_to(row, (8, LANES)), block)
    return block


def put_copies(out_ref, block):
    for i in range(out_ref.shape[0]):
        out_ref[i] = block


def mix_adjoint(coef, planes):
    own, below, above = coef
    out = []
    for z in range(len(planes)):
        value = own * planes[z]
        if z + 1 < len(planes):
            value = value + below * planes[z + 1]
        if z > 0:
            value = value + above * planes[z - 1]
        out.append(value)
    return out


def mix(coef, planes):
    own, below, above = coef
    out = []
    for z in range(len(planes)):
        value = own * planes[z]
        if z > 0:
            value = value + below * planes[z - 1]
        if z + 1 < len(planes):
            value = value + above * planes[z + 1]
        out.append(value)
    return out


def y_inverse_kernel(
    data_hbm, table_hbm, tw_hbm, out_hbm,
    data_ref, table_ref, tw_ref, out_ref, re_s, im_s, mix_s, sems, out_sems,
):
    blocks, ny, _ = data_ref.shape
    n = ny // YR
    gz, _, _, _, rows, _ = out_ref.shape
    lane = lax.broadcasted_iota(jnp.int32, (n, LANES), 1)
    pairs = blocks // 2

    def fetch(chunk):
        part = pl.ds(2 * chunk, 2)
        return pltpu.make_async_copy(data_hbm.at[part], data_ref.at[part], sems.at[2 + chunk])

    def give(chunk, core):
        at = (core, slice(None), chunk)
        return pltpu.make_async_copy(out_ref.at[at], out_hbm.at[at], out_sems.at[chunk * gz + core])

    fetch_table = pltpu.make_async_copy(table_hbm, table_ref, sems.at[0])
    fetch_tw = pltpu.make_async_copy(tw_hbm, tw_ref, sems.at[1])
    fetch(0).start()
    fetch_table.start()
    fetch_tw.start()
    for chunk in range(1, pairs):
        fetch(chunk).start()

    for chunk in range(pairs):
        fetch(chunk).wait()

        def unpack(i, carry):
            part = pl.ds(pl.multiple_of(i * n, n), n)
            first = data_ref[2 * chunk, part, :].astype(F32)
            second = data_ref[2 * chunk + 1, part, :].astype(F32)
            re_s[part, :] = jnp.where(lane < HALF, first, pltpu.roll(second, HALF, 1))
            im_s[part, :] = jnp.where(lane < HALF, pltpu.roll(first, HALF, 1), second)
            return carry

        lax.fori_loop(0, YR, unpack, 0)
        if chunk == 0:
            fetch_table.wait()

        for k in range(0, YR, 2):
            pieces = [
                jnp.concatenate([s[pl.ds(k + d, n, stride=YR), :] for d in range(2)], axis=1)
                for s in (re_s, im_s)
            ]
            both = dot(table_ref[...], jnp.concatenate(pieces, axis=0).astype(BF16))
            both = both[: 2 * n] + both[2 * n :]
            for d in range(2):
                mix_s[k + d] = both[:, d * LANES : (d + 1) * LANES]

        if chunk == 0:
            fetch_tw.wait()

        tiles = rows // 8
        for core in range(gz):

            def combine(i, carry):
                y2 = ((i // tiles) * gz + core) * rows + lax.rem(i, tiles) * 8
                part = pl.ds(pl.multiple_of(y2, 8), 8)
                planes = []
                for k in range(YR):
                    re = mix_s[k, part, :]
                    im = mix_s[k, pl.ds(pl.multiple_of(n + y2, 8), 8), :]
                    if k > 0:
                        c = tw_ref[0, k - 1, part, :]
                        s = tw_ref[1, k - 1, part, :]
                        re, im = re * c - im * s, im * c + re * s
                    planes.append((re, im))
                at = pl.ds(pl.multiple_of(lax.rem(i, tiles) * 8, 8), 8)
                for k, (re, im) in enumerate(short_fft(planes, 1)):
                    to = k * (n // (gz * rows)) + i // tiles
                    out_ref[core, to, chunk, 0, at, :] = re
                    out_ref[core, to, chunk, 1, at, :] = im
                return carry

            lax.fori_loop(0, n // gz // 8, combine, 0, unroll=2)
            give(chunk, core).start()

    for chunk in range(pairs):
        for core in range(gz):
            give(chunk, core).wait()


def y_inverse(data, rows, gz, gy):
    blocks, ny, width = data.shape
    n = ny // YR
    shape = (gz, gy, blocks // 2, 2, rows, LANES)
    hbm = pl.BlockSpec(memory_space=pltpu.HBM)
    return pl.pallas_call(
        y_inverse_kernel,
        in_specs=[hbm] * 3,
        out_specs=hbm,
        out_shape=jax.ShapeDtypeStruct(shape, F32),
        scratch_shapes=[
            pltpu.VMEM((blocks, ny, width), BF16),
            pltpu.VMEM((4 * n, 2 * n), BF16),
            pltpu.VMEM((2, YR - 1, n, LANES), F32),
            pltpu.VMEM(shape, F32),
            pltpu.VMEM((ny, LANES), F32),
            pltpu.VMEM((ny, LANES), F32),
            pltpu.VMEM((YR, 2 * n, LANES), F32),
            pltpu.SemaphoreType.DMA((2 + blocks // 2,)),
            pltpu.SemaphoreType.DMA((blocks // 2 * gz,)),
        ],
        compiler_params=pltpu.CompilerParams(vmem_limit_bytes=Y_GRANT),
        name="y_inverse",
    )(data, y_matrix(ny, False, -1.0), y_twiddle(ny))


def y_forward_kernel(
    spec_hbm, data_hbm, table_hbm, tw_hbm, out_hbm,
    spec_ref, data_ref, table_ref, tw_ref, out_ref, mix_s, sems, spec_sems, out_sems,
):
    blocks, ny, _ = data_ref.shape
    n = ny // YR
    _, gz, gy, _, rows, _ = spec_ref.shape
    pairs = blocks // 2
    half = n // 2

    def fetch(chunk):
        return pltpu.make_async_copy(
            spec_hbm.at[:, :, chunk], spec_ref.at[chunk], spec_sems.at[chunk]
        )

    def give(chunk, part):
        at = (pl.ds(2 * chunk, 2), slice(None), pl.ds(part * half, half))
        return pltpu.make_async_copy(out_ref.at[at], out_hbm.at[at], out_sems.at[2 * chunk + part])

    fetch_table = pltpu.make_async_copy(table_hbm, table_ref, sems.at[0])
    fetch_tw = pltpu.make_async_copy(tw_hbm, tw_ref, sems.at[1])
    fetch_data = pltpu.make_async_copy(data_hbm, data_ref, sems.at[2])
    fetch(0).start()
    fetch_table.start()
    fetch_tw.start()
    fetch_data.start()
    for chunk in range(1, pairs):
        fetch(chunk).start()

    def rows_of(chunk, p, k):
        part = pl.ds(k, rows // YR, stride=YR)
        return jnp.concatenate(
            [spec_ref[chunk, core, i, p, part, :] for i in range(gy) for core in range(gz)], axis=0
        )

    lane = lax.broadcasted_iota(jnp.int32, (16, LANES), 1)
    for chunk in range(pairs):
        fetch(chunk).wait()

        if chunk == 0:
            fetch_table.wait()

        for k in range(0, YR, 2):
            pieces = [
                jnp.concatenate([rows_of(chunk, p, k + d) for d in range(2)], axis=1)
                for p in range(2)
            ]
            high, low = split2(jnp.concatenate(pieces, axis=0))
            both = dot(table_ref[...], high)
            both = both[: 2 * n] + both[2 * n :] + dot(table_ref[: 2 * n], low)
            for d in range(2):
                mix_s[k + d] = both[:, d * LANES : (d + 1) * LANES]
        if chunk == 0:
            fetch_tw.wait()
            fetch_data.wait()

        def combine(i, carry):
            start = pl.multiple_of(i * 16, 16)
            part = pl.ds(start, 16)
            planes = []
            for k in range(YR):
                re = mix_s[k, part, :]
                im = mix_s[k, pl.ds(pl.multiple_of(n + i * 16, 16), 16), :]
                if k > 0:
                    c = tw_ref[0, k - 1, part, :]
                    s = tw_ref[1, k - 1, part, :]
                    re, im = re * c + im * s, im * c - re * s
                planes.append((re, im))
            for k, (re, im) in enumerate(short_fft(planes, -1)):
                at = pl.ds(pl.multiple_of(k * n + start, 16), 16)
                first = jnp.where(lane < HALF, re, pltpu.roll(im, HALF, 1))
                second = jnp.where(lane < HALF, pltpu.roll(re, HALF, 1), im)
                out_ref[2 * chunk, k, part, :] = first - data_ref[2 * chunk, at, :].astype(F32)
                out_ref[2 * chunk + 1, k, part, :] = (
                    second - data_ref[2 * chunk + 1, at, :].astype(F32)
                )
            return carry

        for part in range(2):
            lax.fori_loop(part * half // 16, (part + 1) * half // 16, combine, 0)
            give(chunk, part).start()

    for chunk in range(pairs):
        for part in range(2):
            give(chunk, part).wait()


def y_forward(spec, data):
    blocks, ny, width = data.shape
    n = ny // YR
    hbm = pl.BlockSpec(memory_space=pltpu.HBM)
    out = pl.pallas_call(
        y_forward_kernel,
        in_specs=[hbm] * 4,
        out_specs=hbm,
        out_shape=jax.ShapeDtypeStruct((blocks, YR, n, width), F32),
        scratch_shapes=[
            pltpu.VMEM((blocks // 2, *spec.shape[:2], *spec.shape[3:]), F32),
            pltpu.VMEM((blocks, ny, width), BF16),
            pltpu.VMEM((4 * n, 2 * n), BF16),
            pltpu.VMEM((2, YR - 1, n, LANES), F32),
            pltpu.VMEM((blocks, YR, n, width), F32),
            pltpu.VMEM((YR, 2 * n, LANES), F32),
            pltpu.SemaphoreType.DMA((3,)),
            pltpu.SemaphoreType.DMA((blocks // 2,)),
            pltpu.SemaphoreType.DMA((blocks,)),
        ],
        compiler_params=pltpu.CompilerParams(vmem_limit_bytes=Y_GRANT),
        name="y_forward",
    )(spec, data, y_matrix(ny, True, 1.0), y_twiddle(ny))
    return out.reshape(blocks, ny, width)


def plane_chunk(planes, rows):
    chunk = max(1, 1024 // rows)
    while planes % chunk:
        chunk -= 1
    return chunk


def turn_rows(kb, planes_of, tw_ref, lanes, sign):
    out = []
    for b in range(kb):
        re, im = planes_of(b)
        if b > 0:
            c = tw_ref[0, b, :, lanes]
            s = tw_ref[1, b, :, lanes]
            if sign > 0:
                re, im = re * c - im * s, im * c + re * s
            else:
                re, im = re * c + im * s, im * c - re * s
        out.append((re, im))
    return out


def inverse_columns(gz, kb, spectra, coef_ref, tw_ref, lanes, part, re_s, im_s):
    mixed = [[None] * kb for _ in range(gz)]
    for k in range(kb):
        coef = [coef_ref[j, k, :, lanes] for j in range(3)]
        re = mix_adjoint(coef, [spectra[z][k][0] for z in range(gz)])
        im = mix_adjoint(coef, [spectra[z][k][1] for z in range(gz)])
        for z in range(gz):
            mixed[z][k] = (re[z], im[z])
    for z in range(gz):
        short = short_fft(mixed[z], 1)
        for b, (re, im) in enumerate(turn_rows(kb, lambda b: short[b], tw_ref, lanes, 1)):
            re_s[z * kb + b, part, lanes] = re
            im_s[z * kb + b, part, lanes] = im


def forward_columns(gz, kb, coef_ref, tw_ref, lanes, part, re_s, im_s):
    spectra = []
    for z in range(gz):
        rows_of = lambda b: (re_s[z * kb + b, part, lanes], im_s[z * kb + b, part, lanes])
        spectra.append(short_fft(turn_rows(kb, rows_of, tw_ref, lanes, -1), -1))
    out = [[None] * kb for _ in range(gz)]
    for k in range(kb):
        coef = [coef_ref[j, k, :, lanes] for j in range(3)]
        re = mix(coef, [spectra[z][k][0] for z in range(gz)])
        im = mix(coef, [spectra[z][k][1] for z in range(gz)])
        for z in range(gz):
            out[z][k] = (re[z], im[z])
    return out


def inverse_product(re, im, table_ref):
    ka = re.shape[1]
    high, low = split2(jnp.concatenate([re, im], axis=1))
    value = dot(high, table_ref[...])
    return value[:, :ka] + value[:, ka:] + dot(low, table_ref[:, :ka])


def forward_product(field, table_ref):
    ka = field.shape[1]
    high, low = split2(field)
    value = dot(high, table_ref[...])
    value = value[:, : 2 * ka] + value[:, 2 * ka :] + dot(low, table_ref[:, : 2 * ka])
    return value[:, :ka], value[:, ka:]


def next_plane(field_ref, p, kb):
    rows, ka = field_ref.shape[1:]
    if (p + 1) % kb:
        return field_ref[p + 1]
    lane = lax.broadcasted_iota(jnp.int32, (rows, ka), 1)
    return jnp.where(lane == ka - 1, field_ref[p], pltpu.roll(field_ref[p + 1 - kb], ka - 1, 1))


def prev_plane(field_ref, p, kb):
    rows, ka = field_ref.shape[1:]
    if p % kb:
        return field_ref[p - 1]
    lane = lax.broadcasted_iota(jnp.int32, (rows, ka), 1)
    return jnp.where(lane == 0, field_ref[p], pltpu.roll(field_ref[p + kb - 1], 1, 1))


def first_kernel(
    gz, edge_ref, field_ref, coef_ref, tw_ref, table_ref, sums_ref, spec_ref, *refs
):
    piece_refs, (re_s, im_s) = refs[:-2], refs[-2:]
    planes, rows, ka = field_ref.shape
    kb = planes // gz
    projected = forward_into(gz, field_ref, coef_ref, tw_ref, table_ref, spec_ref, re_s, im_s)
    cut(gz, edge_ref, spec_ref, piece_refs)
    row = lax.broadcasted_iota(jnp.int32, (rows, ka), 0)
    square = jnp.zeros((8, LANES), F32)
    slope = jnp.zeros((8, LANES), F32)
    for p in range(planes):
        here = field_ref[p]
        square = square + fold(here * here)
        along_x = next_plane(field_ref, p, kb) - here
        along_y = jnp.where(row == rows - 1, 0.0, pltpu.roll(here, rows - 1, 0) - here)
        terms = along_x * along_x + along_y * along_y
        if p + kb < planes:
            along_z = field_ref[p + kb] - here
            terms = terms + along_z * along_z
        slope = slope + fold(terms)
    sums_ref[0] = square
    sums_ref[1] = projected
    sums_ref[2] = slope


def columns_back(spec_ref, chunk, coef_ref, tw_ref, re_s, im_s, j, carry):
    gz, kb = spec_ref.shape[:2]
    lanes = slice(chunk * LANES, (chunk + 1) * LANES)
    part = pl.ds(pl.multiple_of(j * 8, 8), 8)
    spectra = [
        [(spec_ref[z, k, chunk, 0, part, :], spec_ref[z, k, chunk, 1, part, :]) for k in range(kb)]
        for z in range(gz)
    ]
    inverse_columns(gz, kb, spectra, coef_ref, tw_ref, lanes, part, re_s, im_s)
    return carry


def middle_kernel(
    spec_hbm, coef_ref, tw_ref, inverse_ref, forward_ref,
    d0_ref, head_ref, tail_ref, spec_ref, re_s, im_s, sems,
):
    gz, kb, chunks, _, rows, _ = spec_ref.shape
    ka = chunks * LANES
    planes = gz * kb

    def fetch(chunk):
        return pltpu.make_async_copy(
            spec_hbm.at[:, :, chunk], spec_ref.at[:, :, chunk], sems.at[chunk]
        )

    for chunk in range(chunks):
        fetch(chunk).start()
    for chunk in range(chunks):
        fetch(chunk).wait()
        lax.fori_loop(
            0, rows // 8,
            functools.partial(columns_back, spec_ref, chunk, coef_ref, tw_ref, re_s, im_s), 0,
        )

    step = plane_chunk(planes, rows)
    shape2, shape3 = (step * rows, ka), (step, rows, ka)

    def there_and_back(i, carry):
        part = pl.ds(i * step, step)
        field = inverse_product(re_s[part].reshape(shape2), im_s[part].reshape(shape2), inverse_ref)
        d0_ref[part] = field.reshape(shape3)
        re, im = forward_product(field, forward_ref)
        re_s[part] = re.reshape(shape3)
        im_s[part] = im.reshape(shape3)
        return carry

    lax.fori_loop(0, planes // step, there_and_back, 0)

    def second_columns(j, total):
        part = pl.ds(pl.multiple_of(j * 8, 8), 8)
        for chunk in range(chunks):
            lanes = slice(chunk * LANES, (chunk + 1) * LANES)
            spectra = forward_columns(gz, kb, coef_ref, tw_ref, lanes, part, re_s, im_s)
            for z in range(gz):
                for k in range(kb):
                    for p in range(2):
                        value = spectra[z][k][p]
                        spec_ref[z, k, chunk, p, part, :] = value
                        total = total + value * value
        return total

    projected = lax.fori_loop(0, rows // 8, second_columns, jnp.zeros((8, LANES), F32))
    for p in range(planes):
        head_ref[p : p + 1, :] = d0_ref[p, :1, :]
        head_ref[planes + p : planes + p + 1, :] = d0_ref[p, 1:2, :]
        for part in range(2):
            at = 2 * planes + 2 * p + part
            for chunk in range(chunks):
                lanes = slice(chunk * LANES, (chunk + 1) * LANES)
                head_ref[at : at + 1, lanes] = spec_ref[p // kb, p % kb, chunk, part, :1, :]
        tail_ref[p : p + 1, :] = d0_ref[p, rows - 1 : rows, :]

    row = lax.broadcasted_iota(jnp.int32, (rows, ka), 0)
    square = jnp.zeros((8, LANES), F32)
    slope = jnp.zeros((8, LANES), F32)
    for p in range(planes):
        here = d0_ref[p]
        square = square + fold(here * here)
        along_x = next_plane(d0_ref, p, kb) - here
        along_y = jnp.where(row == rows - 1, 0.0, pltpu.roll(here, rows - 1, 0) - here)
        terms = along_x * along_x + along_y * along_y
        if p + kb < planes:
            along_z = d0_ref[p + kb] - here
            terms = terms + along_z * along_z
        slope = slope + fold(terms)
    block = sums_block([square, projected, slope])
    for ref in (head_ref, tail_ref):
        at = ref.shape[0] - 8
        ref[at:, :] = jnp.zeros((8, ka), F32)
        ref[at:, :LANES] = block


def middle(spec, coef, nx):
    gz, kb, chunks, _, rows, _ = spec.shape
    ka = chunks * LANES
    planes = gz * kb
    vmem = pl.BlockSpec(memory_space=pltpu.VMEM)
    field = jax.ShapeDtypeStruct((planes, rows, ka), F32)
    return pl.pallas_call(
        middle_kernel,
        in_specs=[pl.BlockSpec(memory_space=pltpu.HBM)] + [vmem] * 4,
        out_specs=[vmem] * 4,
        out_shape=[
            field,
            jax.ShapeDtypeStruct((4 * planes + 8, ka), F32),
            jax.ShapeDtypeStruct((planes + 8, ka), F32),
            jax.ShapeDtypeStruct(spec.shape, F32),
        ],
        scratch_shapes=[
            pltpu.VMEM((planes, rows, ka), F32),
            pltpu.VMEM((planes, rows, ka), F32),
            pltpu.SemaphoreType.DMA((chunks,)),
        ],
        compiler_params=pltpu.CompilerParams(vmem_limit_bytes=X_GRANT),
        name="middle",
    )(
        spec, coef, x_twiddle(nx, ka), jnp.asarray(x_inverse_matrix(nx, ka)),
        x_forward_matrix(nx, ka),
    )


def normal_kernel(spec_ref, coef_ref, tw_ref, table_ref, out_ref, re_s, im_s):
    gz, kb, chunks, _, rows, _ = spec_ref.shape
    planes, ka = gz * kb, chunks * LANES

    for chunk in range(chunks):
        lax.fori_loop(
            0, rows // 8,
            functools.partial(columns_back, spec_ref, chunk, coef_ref, tw_ref, re_s, im_s), 0,
        )

    step = plane_chunk(planes, rows)
    shape = (step * rows, ka)
    for start in range(0, planes, step):
        part = slice(start, start + step)
        field = inverse_product(re_s[part].reshape(shape), im_s[part].reshape(shape), table_ref)
        out_ref[part] = field.reshape(step, rows, ka)


def normal_product(spec, coef, nx):
    gz, kb, chunks, _, rows, _ = spec.shape
    planes, ka = gz * kb, chunks * LANES
    vmem = pl.BlockSpec(memory_space=pltpu.VMEM)
    return pl.pallas_call(
        normal_kernel,
        in_specs=[vmem] * 4,
        out_specs=vmem,
        out_shape=jax.ShapeDtypeStruct((planes, rows, ka), F32),
        scratch_shapes=[pltpu.VMEM((planes, rows, ka), F32)] * 2,
        compiler_params=pltpu.CompilerParams(vmem_limit_bytes=X_GRANT),
        cost_estimate=pl.CostEstimate(
            flops=12 * planes * rows * ka * ka, bytes_accessed=12 * planes * rows * ka, transcendentals=0
        ),
        name="normal_product",
    )(spec, coef, x_twiddle(nx, ka), jnp.asarray(x_inverse_matrix(nx, ka)))


def next_normal_row(gz, next_ref, coef_ref, tw_ref, table_ref, row_s, re_s, im_s):
    planes, ka = row_s.shape
    kb = planes // gz
    for start in range(0, ka, LANES):
        lanes = slice(start, start + LANES)

        def row_of(z, k, part):
            at = 2 * planes + 2 * (z * kb + k) + part
            return jnp.broadcast_to(next_ref[at : at + 1, lanes], (8, LANES))

        spectra = [[(row_of(z, k, 0), row_of(z, k, 1)) for k in range(kb)] for z in range(gz)]
        inverse_columns(gz, kb, spectra, coef_ref, tw_ref, lanes, slice(0, 8), re_s, im_s)
    shape = (planes * 8, ka)
    field = inverse_product(re_s[...].reshape(shape), im_s[...].reshape(shape), table_ref)
    for p in range(planes):
        row_s[p : p + 1, :] = field[8 * p : 8 * p + 1, :]


def border_kernel(edge_ref, head_ref, tail_ref, next_ref, prev_ref, after_ref, out_ref):
    del after_ref
    planes = tail_ref.shape[0] - 8

    def sums_of(ref):
        return ref[ref.shape[0] - 8 :, :LANES]

    def border(after, before):
        step = after[:planes, :] - before[:planes, :]
        return fold(step * step)

    second = edge_ref[2] > 0
    below = border(head_ref, prev_ref) * jnp.where(edge_ref[0] > 0, 0.0, 1.0)
    above = border(next_ref, tail_ref) * jnp.where(edge_ref[1] > 0, 0.0, 1.0)
    other = jnp.where(second, sums_of(prev_ref), sums_of(next_ref))
    none = jnp.zeros((8, LANES), F32)
    put_copies(out_ref, sums_of(tail_ref) + other + sums_block([none, none, below + above]))


def border_sums(edge, head, tail, next_head, prev_tail, after, copies):
    vmem = pl.BlockSpec(memory_space=pltpu.VMEM)
    return pl.pallas_call(
        border_kernel,
        in_specs=[pl.BlockSpec(memory_space=pltpu.SMEM)]
        + [vmem] * 4
        + [pl.BlockSpec(memory_space=pl.ANY)],
        out_specs=vmem,
        out_shape=jax.ShapeDtypeStruct((copies, 8, LANES), F32),
        compiler_params=pltpu.CompilerParams(vmem_limit_bytes=2 * MIB),
        name="border_sums",
    )(edge, head, tail, next_head, prev_tail, after)


def second_kernel(
    gz, edge_ref, d0_ref, nd0_ref, tail_ref, prev_ref, next_ref,
    coef_ref, tw_ref, table_ref, inverse_ref, *refs,
):
    sums_refs, refs = refs[:1], refs[1:]
    d1_ref, eta_ref, out_ref, spec_ref, re_s, im_s, row_s, nrow_s, re8_s, im8_s = refs
    next_normal_row(gz, next_ref, coef_ref, tw_ref, inverse_ref, nrow_s, re8_s, im8_s)
    planes, rows, ka = d0_ref.shape
    kb = planes // gz
    eta_here = step_of(sums_refs)
    eta_ref[...] = jnp.broadcast_to(eta_here, (8, LANES))
    eta = jnp.max(eta_here)
    first = edge_ref[0] > 0
    last = edge_ref[1] > 0

    def shrink(difference):
        return jnp.clip(-eta * difference, -CLIP, CLIP)

    lane2 = lax.broadcasted_iota(jnp.int32, (kb, ka), 1)
    row2 = lax.broadcasted_iota(jnp.int32, (kb, ka), 0)
    for z in range(gz):
        part = slice(z * kb, (z + 1) * kb)
        here = next_ref[part, :]
        value = here - eta * nrow_s[part, :]
        up = pltpu.roll(here, kb - 1, 0)
        up = jnp.where(
            row2 == kb - 1, jnp.where(lane2 == ka - 1, here, pltpu.roll(up, ka - 1, 1)), up
        )
        down = pltpu.roll(here, 1, 0)
        down = jnp.where(row2 == 0, jnp.where(lane2 == 0, here, pltpu.roll(down, 1, 1)), down)
        value = value + shrink(here - down) - shrink(up - here)
        value = value + shrink(here - tail_ref[part, :]) - shrink(next_ref[planes + z * kb : planes + (z + 1) * kb, :] - here)
        if z > 0:
            value = value + shrink(here - next_ref[(z - 1) * kb : z * kb, :])
        if z + 1 < gz:
            value = value - shrink(next_ref[(z + 1) * kb : (z + 2) * kb, :] - here)
        row_s[part, :] = value

    row = lax.broadcasted_iota(jnp.int32, (rows, ka), 0)
    square = jnp.zeros((8, LANES), F32)
    for p in range(planes):
        here = d0_ref[p]
        value = here - eta * nd0_ref[p]
        if p % kb == 0:
            clipped_x = shrink(here - prev_plane(d0_ref, p, kb))
        value = value + clipped_x
        clipped_x = shrink(next_plane(d0_ref, p, kb) - here)
        value = value - clipped_x
        below = jnp.where(last, here[rows - 1 :, :], next_ref[p : p + 1, :])
        above = jnp.where(first, here[:1, :], prev_ref[p : p + 1, :])
        upper = shrink(jnp.where(row == rows - 1, below, pltpu.roll(here, rows - 1, 0)) - here)
        lower = jnp.where(row == 0, shrink(here[:1, :] - above), pltpu.roll(upper, 1, 0))
        value = value + lower - upper
        if p >= kb:
            value = value + shrink(here - d0_ref[p - kb])
        if p + kb < planes:
            value = value - shrink(d0_ref[p + kb] - here)
        d1_ref[p] = value
        square = square + fold(value * value)

    slope = jnp.zeros((8, LANES), F32)
    for p in range(planes):
        here = d1_ref[p]
        along_x = next_plane(d1_ref, p, kb) - here
        below = jnp.where(last, here[rows - 1 :, :], row_s[p : p + 1, :])
        along_y = jnp.where(row == rows - 1, below, pltpu.roll(here, rows - 1, 0)) - here
        terms = along_x * along_x + along_y * along_y
        if p + kb < planes:
            along_z = d1_ref[p + kb] - here
            terms = terms + along_z * along_z
        slope = slope + fold(terms)

    step = plane_chunk(planes, rows)

    def multiply(i, carry):
        part = pl.ds(i * step, step)
        re, im = forward_product(d1_ref[part].reshape(step * rows, ka), table_ref)
        re_s[part] = re.reshape(step, rows, ka)
        im_s[part] = im.reshape(step, rows, ka)
        return carry

    lax.fori_loop(0, planes // step, multiply, 0)

    def columns(j, total):
        part = pl.ds(pl.multiple_of(j * 8, 8), 8)
        for chunk in range(ka // LANES):
            lanes = slice(chunk * LANES, (chunk + 1) * LANES)
            spectra = forward_columns(gz, kb, coef_ref, tw_ref, lanes, part, re_s, im_s)
            for z in range(gz):
                for k in range(kb):
                    for p in range(2):
                        value = spectra[z][k][p]
                        spec_ref[z, k, chunk, p, part, :] = value
                        total = total + value * value
        return total

    projected = lax.fori_loop(0, rows // 8, columns, jnp.zeros((8, LANES), F32))
    put_copies(out_ref, sums_block([square, projected, slope]))


def second_descent(edge, sums, d0, nd0, tail, prev_tail, next_head, coef, gz, nx):
    planes, rows, ka = d0.shape
    vmem = pl.BlockSpec(memory_space=pltpu.VMEM)
    return pl.pallas_call(
        functools.partial(second_kernel, gz),
        in_specs=[pl.BlockSpec(memory_space=pltpu.SMEM)] + [vmem] * 10,
        out_specs=[vmem] * 4,
        out_shape=[
            jax.ShapeDtypeStruct((planes, rows, ka), F32),
            jax.ShapeDtypeStruct((8, LANES), F32),
            jax.ShapeDtypeStruct(sums.shape, F32),
            jax.ShapeDtypeStruct((gz, planes // gz, ka // LANES, 2, rows, LANES), F32),
        ],
        scratch_shapes=[
            pltpu.VMEM((planes, rows, ka), F32),
            pltpu.VMEM((planes, rows, ka), F32),
            pltpu.VMEM((planes, ka), F32),
            pltpu.VMEM((planes, ka), F32),
            pltpu.VMEM((planes, 8, ka), F32),
            pltpu.VMEM((planes, 8, ka), F32),
        ],
        compiler_params=pltpu.CompilerParams(vmem_limit_bytes=X_GRANT),
        name="second_descent",
    )(
        edge, d0, nd0, tail, prev_tail, next_head, coef,
        x_twiddle(nx, ka), x_forward_matrix(nx, ka), jnp.asarray(x_inverse_matrix(nx, ka)), sums,
    )


def combine_kernel(gz, eta_ref, *refs):
    sums_refs, (first_ref, second_ref, out_ref, steps_ref) = refs[:gz], refs[gz:]
    eta0 = jnp.max(eta_ref[...])
    eta1 = jnp.max(step_of(sums_refs))
    steps_ref[0] = eta_ref[...]
    steps_ref[1] = jnp.full((8, LANES), eta1, F32)
    count = out_ref.shape[0]
    start = pl.program_id(0) * count
    for i in range(count):
        out_ref[i] = -(eta0 * first_ref[start + i] + eta1 * second_ref[start + i])


def combine_spectra(eta, sums, first, second):
    gz = len(sums)
    planes, *rest = first.shape
    count = 4 if planes % 4 == 0 else 1
    vmem = pl.BlockSpec(memory_space=pltpu.VMEM)
    return pl.pallas_call(
        functools.partial(combine_kernel, gz),
        grid=(planes // count,),
        in_specs=[vmem] * (3 + gz),
        out_specs=[
            pl.BlockSpec((count, *rest), lambda i: (i, 0, 0, 0, 0)),
            pl.BlockSpec((2, 8, LANES), lambda i: (0, 0, 0)),
        ],
        out_shape=[
            jax.ShapeDtypeStruct(first.shape, F32),
            jax.ShapeDtypeStruct((2, 8, LANES), F32),
        ],
        compiler_params=pltpu.CompilerParams(vmem_limit_bytes=50 * MIB),
        name="combine_spectra",
    )(eta, *sums, first, second)


def to_core(piece, r):
    gz = lax.axis_size("gz")
    return lax.ppermute(piece, "gz", [(i, (i + r) % gz) for i in range(gz)]) if r else piece


def to_chips(parts):
    return lax.all_to_all(parts, "gy", 0, 0, tiled=True)


def to_devices(parts):
    gz, gy, *rest = parts.shape
    parts = lax.all_to_all(parts.reshape(gz * gy, *rest), ("gz", "gy"), 0, 0, tiled=True)
    return parts.reshape(gz, gy, *rest)


def everywhere(sums):
    sums = to_chips(sums)
    return [to_core(sums, r) for r in range(lax.axis_size("gz"))]


def shards(data, band_offset, interp_weight):
    gz = lax.axis_size("gz")
    gy = lax.axis_size("gy")
    devices = gz * gy
    data = data[0]
    blocks, ny, width = data.shape
    rows = ny // devices
    ka = blocks * HALF
    nx = ka * gy

    core = lax.axis_index("gz")
    flat = lax.axis_index("gy") * gz + core
    edge = jnp.stack([flat == 0, flat == devices - 1, core]).astype(jnp.int32)
    order = [(i % gz) * gy + i // gz for i in range(devices)]
    up = [(order[i + 1], order[i]) for i in range(devices - 1)]
    down = [(order[i], order[i + 1]) for i in range(devices - 1)]

    lower = band_offset < 0
    weight = interp_weight
    coef = jnp.stack(
        [
            jnp.where(lower, weight[1], weight[0]),
            jnp.where(lower, weight[0], 0.0),
            jnp.where(lower, 0.0, weight[1]),
        ]
    ).reshape(3, gy, 1, ka)
    coef = jnp.broadcast_to(coef, (3, gy, 8, ka))

    spec = to_devices(y_inverse(data, rows, gz, gy))
    d0, head, tail, first = middle(spec, coef, nx)
    next_head = lax.ppermute(head, ("gz", "gy"), up)
    prev_tail = lax.ppermute(tail, ("gz", "gy"), down)
    nd0 = normal_product(first, coef, nx)
    sums = to_chips(border_sums(edge, head, tail, next_head, prev_tail, nd0, gy))
    d1, eta, sums, second = second_descent(
        edge, sums, d0, nd0, tail, prev_tail, next_head, coef, gz, nx
    )
    sums = everywhere(sums)
    flat_shape = (devices, ka // LANES, 2, rows, LANES)
    spec, etas = combine_spectra(eta, sums, first.reshape(flat_shape), second.reshape(flat_shape))
    residual = y_forward(to_devices(spec.reshape(first.shape)), data)

    volume = -(etas[0, 0, 0] * d0 + etas[1, 0, 0] * d1)
    volume = volume.reshape(gz, gy, rows, ka).transpose(0, 2, 3, 1).reshape(gz, rows, nx)
    parts = [
        to_core(lax.dynamic_index_in_dim(volume, lax.rem(core + r, gz), 0, False), r)
        for r in range(gz)
    ]
    volume = jnp.zeros((gz, rows, nx), F32)
    for r, part in enumerate(parts):
        volume = lax.dynamic_update_index_in_dim(volume, part, lax.rem(core + gz - r, gz), 0)
    return (volume.reshape(1, gz * rows, nx), residual[None])


NX = 4096
NY = 2048
XB = 64
YB = 64
ITERS = 2
XA = 64
YA = 32
PRECISE = lax.Precision.HIGHEST


def with_halo(block, sides, width):
    for axis, dim in sides:
        count = lax.axis_size(axis)
        forward = [(i, i + 1) for i in range(count - 1)]
        backward = [(target, source) for source, target in forward]
        low = lax.ppermute(
            lax.slice_in_dim(block, block.shape[dim] - width, None, axis=dim), axis, forward
        )
        high = lax.ppermute(lax.slice_in_dim(block, 0, width, axis=dim), axis, backward)
        block = jnp.concatenate([low, block, high], axis=dim)
    return block


def from_behind(block, axis, distance):
    devices = range(lax.axis_size(axis))
    route = [(i - distance, i) for i in devices if i - distance in devices]
    return lax.ppermute(block, axis, route)


def unit_table(length):
    counter = jnp.arange(length, dtype=jnp.int32)
    phase_int = counter[:, None] * counter[None, :] % length
    angles = 2.0 * jnp.pi / length * phase_int.astype(jnp.float32)
    factor = length ** (-0.5)
    return (jnp.cos(angles) * factor, jnp.sin(angles) * factor)


def twiddle_table(row_len, col_len, period):
    phase_int = (
        jnp.arange(row_len, dtype=jnp.int32)[:, None]
        * jnp.arange(col_len, dtype=jnp.int32)[None, :]
        % period
    )
    angles = 2.0 * jnp.pi / period * phase_int.astype(jnp.float32)
    return (jnp.cos(angles), jnp.sin(angles))


def split_parts(packed):
    half_width = packed.shape[-1] // 2
    return (packed[..., :half_width], packed[..., half_width:])


def join_parts(real_part, imag_part):
    return jnp.concatenate([real_part, imag_part], axis=-1)


def complex_contract(packed, cos_table, sin_table, subscripts, conj_sign):
    cos_out = jnp.einsum(subscripts, packed, cos_table, precision=PRECISE)
    sin_out = jnp.einsum(subscripts, packed, sin_table, precision=PRECISE)
    cos_re, cos_im = split_parts(cos_out)
    sin_re, sin_im = split_parts(sin_out)
    return join_parts(cos_re - conj_sign * sin_im, cos_im + conj_sign * sin_re)


def rotate(packed, cos_table, sin_table, conj_sign):
    real_part, imag_part = split_parts(packed)
    return join_parts(
        real_part * cos_table - conj_sign * imag_part * sin_table,
        imag_part * cos_table + conj_sign * real_part * sin_table,
    )


def forward_x(volume):
    slices, row_count = (volume.shape[0], volume.shape[1])
    cos_a, sin_a = unit_table(XA)
    cos_b, sin_b = unit_table(XB)
    first_table = jnp.concatenate([cos_a, -sin_a], axis=1)
    grid_view = volume.reshape(slices, row_count, XA, XB)
    mixing = jnp.einsum("zyab,am->zybm", grid_view, first_table, precision=PRECISE)
    tw_cos, tw_sin = twiddle_table(XB, XA, NX)
    mixing = rotate(mixing, tw_cos, tw_sin, -1.0)
    return complex_contract(mixing, cos_b, sin_b, "zybm,bl->zlym", -1.0)


def inverse_x(packed):
    slices, row_count = (packed.shape[0], packed.shape[2])
    cos_a, sin_a = unit_table(XA)
    cos_b, sin_b = unit_table(XB)
    mixing = complex_contract(packed, cos_b, sin_b, "zlym,lb->zybm", 1.0)
    tw_cos, tw_sin = twiddle_table(XB, XA, NX)
    mixing = rotate(mixing, tw_cos, tw_sin, 1.0)
    last_table = jnp.concatenate([cos_a, -sin_a], axis=0)
    grid_view = jnp.einsum("zybm,ma->zyab", mixing, last_table, precision=PRECISE)
    return grid_view.reshape(slices, row_count, NX)


def forward_y(packed):
    slices, blocks, width = (packed.shape[0], packed.shape[1], packed.shape[3])
    cos_a, sin_a = unit_table(YA)
    cos_b, sin_b = unit_table(YB)
    grid_view = packed.reshape(slices, blocks, YA, YB, width)
    mixing = complex_contract(grid_view, cos_a, sin_a, "zjcdm,ck->zjkdm", -1.0)
    tw_cos, tw_sin = twiddle_table(YA, YB, NY)
    mixing = rotate(mixing, tw_cos[:, :, None], tw_sin[:, :, None], -1.0)
    result = complex_contract(mixing, cos_b, sin_b, "zjkdm,dl->zjlkm", -1.0)
    return result.reshape(slices, blocks, NY, width)


def inverse_y(packed):
    slices, blocks, width = (packed.shape[0], packed.shape[1], packed.shape[3])
    cos_a, sin_a = unit_table(YA)
    cos_b, sin_b = unit_table(YB)
    grid_view = packed.reshape(slices, blocks, YB, YA, width)
    mixing = complex_contract(grid_view, cos_b, sin_b, "zjlkm,ld->zjkdm", 1.0)
    tw_cos, tw_sin = twiddle_table(YA, YB, NY)
    mixing = rotate(mixing, tw_cos[:, :, None], tw_sin[:, :, None], 1.0)
    result = complex_contract(mixing, cos_a, sin_a, "zjkdm,kc->zjcdm", 1.0)
    return result.reshape(slices, blocks, NY, width)


def tilt_coefficients(band_offset, interp_weight, first_block, blocks):
    offsets = lax.dynamic_slice_in_dim(band_offset.reshape(XB, XA), first_block, blocks, 0)
    weights = lax.dynamic_slice_in_dim(interp_weight.reshape(2, XB, XA), first_block, blocks, 1)
    lower_tap = (jnp.concatenate([offsets, offsets], axis=1) < 0)[:, None, :]
    first_weight = jnp.concatenate([weights[0], weights[0]], axis=1)[:, None, :]
    second_weight = jnp.concatenate([weights[1], weights[1]], axis=1)[:, None, :]
    return (lower_tap, first_weight, second_weight)


def tilt(field_in, coefficients, adjoint):
    lower_tap, first_weight, second_weight = coefficients
    padded = with_halo(field_in, (("gz", 0),), 1)
    below_rim = padded[:-2]
    middle = padded[1:-1]
    above_rim = padded[2:]
    if adjoint:
        return jnp.where(
            lower_tap,
            first_weight * above_rim + second_weight * middle,
            first_weight * middle + second_weight * below_rim,
        )
    return jnp.where(
        lower_tap,
        first_weight * below_rim + second_weight * middle,
        first_weight * middle + second_weight * above_rim,
    )


def to_pencil(slab_part):
    return lax.all_to_all(slab_part, "gy", split_axis=1, concat_axis=2, tiled=True)


def to_slab(pencil_part):
    return lax.all_to_all(pencil_part, "gy", split_axis=2, concat_axis=1, tiled=True)


def back_project(packed, pencil_coef):
    return inverse_x(to_slab(inverse_y(tilt(packed, pencil_coef, True))))


def edge_masks(slices, row_count):
    z_global = lax.axis_index("gz") * slices + jnp.arange(slices, dtype=jnp.int32)
    y_global = lax.axis_index("gy") * row_count + jnp.arange(row_count, dtype=jnp.int32)
    keep_z = (z_global < slices * lax.axis_size("gz") - 1).astype(jnp.float32)[:, None, None]
    keep_y = (y_global < row_count * lax.axis_size("gy") - 1).astype(jnp.float32)[None, :, None]
    return (keep_z, keep_y)


def forward_diff(field_in, keep_z, keep_y):
    slices, row_count = (field_in.shape[0], field_in.shape[1])
    next_z = from_behind(field_in, "gz", -1)
    next_y = from_behind(field_in[:, :1], "gy", -1)
    along_z = (jnp.concatenate([field_in[1:], next_z], axis=0) - field_in) * keep_z
    along_y = (jnp.concatenate([field_in[:, 1:], next_y], axis=1) - field_in) * keep_y
    zero_col = jnp.zeros((slices, row_count, 1), jnp.float32)
    along_x = jnp.concatenate([field_in[:, :, 1:] - field_in[:, :, :-1], zero_col], axis=2)
    return jnp.stack([along_z, along_y, along_x])


def transpose_diff(components, keep_z, keep_y):
    slices, row_count = (components.shape[1], components.shape[2])
    zero_col = jnp.zeros((slices, row_count, 1), jnp.float32)
    comp_z = components[0] * keep_z
    comp_y = components[1] * keep_y
    comp_x = jnp.concatenate([components[2][:, :, :-1], zero_col], axis=2)
    prev_z = from_behind(comp_z, "gz", 1)
    prev_y = from_behind(comp_y[:, -1:], "gy", 1)
    result = jnp.concatenate([prev_z, comp_z[:-1]], axis=0) - comp_z
    result = result + jnp.concatenate([prev_y, comp_y[:, :-1]], axis=1) - comp_y
    result = result + jnp.concatenate([zero_col, comp_x[:, :, :-1]], axis=2) - comp_x
    return result


def plain_shards(data, band_offset, interp_weight):
    slices = data.shape[0]
    blocks = data.shape[1]
    width = data.shape[3]
    row_count = NY // lax.axis_size("gy")
    slab_coef = tilt_coefficients(band_offset, interp_weight, 0, XB)
    pencil_coef = tilt_coefficients(
        band_offset, interp_weight, lax.axis_index("gy") * blocks, blocks
    )
    keep_z, keep_y = edge_masks(slices, row_count)
    measured = data.astype(jnp.float32)
    volume = jnp.zeros((slices, row_count, NX), jnp.float32)
    grad_volume = jnp.zeros((3, slices, row_count, NX), jnp.float32)
    split_var = grad_volume
    dual_var = grad_volume
    data_back = back_project(measured, pencil_coef)
    normal_part = jnp.zeros_like(volume)
    tilted = jnp.zeros((slices, XB, row_count, width), jnp.float32)
    for iteration in range(ITERS):
        data_grad = normal_part - data_back
        if iteration > 0:
            tv_gap = grad_volume - split_var + dual_var / PENALTY
            descent = data_grad + PENALTY * transpose_diff(tv_gap, keep_z, keep_y)
        else:
            descent = data_grad
        slope_field = forward_diff(descent, keep_z, keep_y)
        projected = tilt(forward_x(descent), slab_coef, False)
        line_totals = lax.psum(
            (
                jnp.sum(descent * descent),
                jnp.sum(projected * projected),
                jnp.sum(slope_field * slope_field),
            ),
            ("gz", "gy"),
        )
        step_length = line_totals[0] / (line_totals[1] + PENALTY * line_totals[2])
        volume = volume - step_length * descent
        grad_volume = grad_volume - step_length * slope_field
        tilted = tilted - step_length * projected
        if iteration + 1 < ITERS:
            normal_part = normal_part - step_length * inverse_x(tilt(projected, slab_coef, True))
        if iteration + 1 < ITERS:
            shifted = grad_volume + dual_var / PENALTY
            split_var = shifted - jnp.clip(shifted, -TV_WEIGHT / PENALTY, TV_WEIGHT / PENALTY)
            dual_var = PENALTY * (grad_volume - split_var)
    residual = forward_y(to_pencil(tilted)) - measured
    return (volume, residual)


def tiles_fit(mesh, ny, blocks):
    rows = ny // (mesh.shape["gz"] * mesh.shape["gy"])
    return mesh.shape["gz"] == 2 and rows % 16 == 0 and mesh.shape["gy"] % YR == 0 and blocks // mesh.shape["gy"] % 2 == 0


def solution(mesh):
    in_specs = (P("gz", "gy", None, None), P(), P())
    out_specs = (P("gz", "gy", None), P("gz", "gy", None, None))

    def run(data, band_offset, interp_weight):
        body = shards if tiles_fit(mesh, data.shape[2], data.shape[1]) else plain_shards
        call = jax.shard_map(
            body, mesh=mesh, in_specs=in_specs, out_specs=out_specs, check_vma=False
        )
        return call(data, band_offset, interp_weight)

    return run
```

```python
import functools

import jax
import jax.numpy as jnp
import numpy as np
from jax import lax
from jax.experimental import pallas as pl
from jax.experimental.pallas import tpu as pltpu
from jax.sharding import PartitionSpec as P

PENALTY = 0.5
TV_WEIGHT = 0.25
CLIP = TV_WEIGHT / PENALTY
HALF = 64
YR = 8
LANES = 128
F32 = jnp.float32
BF16 = jnp.bfloat16
MIB = 1024 * 1024
Y_GRANT = 56 * MIB
X_GRANT = 20 * MIB


def dft_parts(length, scale):
    index = np.arange(length)
    angles = 2.0 * np.pi / length * (index[:, None] * index[None, :] % length)
    return np.cos(angles) * scale, np.sin(angles) * scale


def host_parts(table):
    table = table.astype(np.float32)
    high = table.astype(BF16)
    low = (table - high.astype(np.float32)).astype(BF16)
    return high, low


def y_matrix(ny, forward, sign):
    n = ny // YR
    cos, sin = dft_parts(n, sign * ny**-0.5)
    if forward:
        table = np.block([[cos, sin], [-sin, cos]])
    else:
        table = np.block([[cos, -sin], [sin, cos]])
    return jnp.asarray(np.concatenate(host_parts(table), axis=0))


def y_twiddle(ny):
    n = ny // YR
    angles = 2.0 * np.pi / ny * (np.arange(1, YR)[:, None] * np.arange(n)[None, :])
    table = np.stack([np.cos(angles), np.sin(angles)]).astype(np.float32)
    return jnp.asarray(np.ascontiguousarray(np.broadcast_to(table[..., None], (2, YR - 1, n, LANES))))


def x_inverse_matrix(nx, ka):
    cos, sin = dft_parts(ka, nx**-0.5)
    return np.concatenate(host_parts(np.concatenate([cos, -sin], axis=0)), axis=1)


def x_forward_matrix(nx, ka):
    cos, sin = dft_parts(ka, nx**-0.5)
    return jnp.asarray(np.concatenate(host_parts(np.concatenate([cos, -sin], axis=1)), axis=1))


def x_twiddle(nx, ka):
    kb = nx // ka
    angles = 2.0 * np.pi / nx * (np.arange(kb)[:, None] * np.arange(ka)[None, :])
    table = np.stack([np.cos(angles), np.sin(angles)]).astype(np.float32)
    return jnp.asarray(np.ascontiguousarray(np.broadcast_to(table[:, :, None], (2, kb, 8, ka))))


def short_fft(planes, sign):
    n = len(planes)
    if n == 1:
        return planes
    even = short_fft(planes[0::2], sign)
    odd = short_fft(planes[1::2], sign)
    half = n // 2
    out = [None] * n
    for k in range(half):
        er, ei = even[k]
        tr, ti = odd[k]
        if 4 * k == n:
            if sign > 0:
                out[k] = (er - ti, ei + tr)
                out[k + half] = (er + ti, ei - tr)
            else:
                out[k] = (er + ti, ei - tr)
                out[k + half] = (er - ti, ei + tr)
            continue
        if k > 0:
            c = float(np.cos(2.0 * np.pi * k / n))
            s = float(sign * np.sin(2.0 * np.pi * k / n))
            if 8 * k == n:
                tr, ti = (tr - ti, ti + tr) if sign > 0 else (tr + ti, ti - tr)
                tr, ti = tr * c, ti * c
            elif 8 * k == 3 * n:
                m = float(np.sin(2.0 * np.pi * k / n))
                tr, ti = (-(tr + ti), tr - ti) if sign > 0 else (ti - tr, -(tr + ti))
                tr, ti = tr * m, ti * m
            else:
                tr, ti = tr * c - ti * s, ti * c + tr * s
        out[k] = (er + tr, ei + ti)
        out[k + half] = (er - tr, ei - ti)
    return out


def split2(x):
    high = x.astype(BF16)
    return high, (x - high.astype(F32)).astype(BF16)


def dot(a, b):
    return jnp.dot(a, b, preferred_element_type=F32)


def fold(x):
    rows, lanes = x.shape
    x = jnp.sum(x.reshape(rows // 8, 8, lanes), axis=0)
    total = x[:, :LANES]
    for i in range(1, lanes // LANES):
        total = total + x[:, i * LANES : (i + 1) * LANES]
    return total


def full_sum(x):
    return jnp.sum(jnp.sum(x, axis=0, keepdims=True), axis=1, keepdims=True)


def step_of(sums_refs):
    total = sum(jnp.sum(sums_ref[...], axis=0) for sums_ref in sums_refs)
    parts = jnp.sum(total, axis=1, keepdims=True)
    return parts[0:1] / (parts[1:2] + PENALTY * parts[2:3])


def sums_block(values):
    rows = [jnp.sum(v, axis=0, keepdims=True) for v in values]
    index = lax.broadcasted_iota(jnp.int32, (8, LANES), 0)
    block = jnp.zeros((8, LANES), F32)
    for i, row in enumerate(rows):
        block = jnp.where(index == i, jnp.broadcast_to(row, (8, LANES)), block)
    return block


def put_copies(out_ref, block):
    for i in range(out_ref.shape[0]):
        out_ref[i] = block


def mix_adjoint(coef, planes):
    own, below, above = coef
    out = []
    for z in range(len(planes)):
        value = own * planes[z]
        if z + 1 < len(planes):
            value = value + below * planes[z + 1]
        if z > 0:
            value = value + above * planes[z - 1]
        out.append(value)
    return out


def mix(coef, planes):
    own, below, above = coef
    out = []
    for z in range(len(planes)):
        value = own * planes[z]
        if z > 0:
            value = value + below * planes[z - 1]
        if z + 1 < len(planes):
            value = value + above * planes[z + 1]
        out.append(value)
    return out


def y_inverse_kernel(
    data_hbm, table_hbm, tw_hbm, out_hbm,
    data_ref, table_ref, tw_ref, out_ref, re_s, im_s, mix_s, sems, out_sems,
):
    blocks, ny, _ = data_ref.shape
    n = ny // YR
    gz, _, _, _, rows, _ = out_ref.shape
    lane = lax.broadcasted_iota(jnp.int32, (n, LANES), 1)
    pairs = blocks // 2

    def fetch(chunk):
        part = pl.ds(2 * chunk, 2)
        return pltpu.make_async_copy(data_hbm.at[part], data_ref.at[part], sems.at[2 + chunk])

    def give(chunk, core):
        at = (core, slice(None), chunk)
        return pltpu.make_async_copy(out_ref.at[at], out_hbm.at[at], out_sems.at[chunk * gz + core])

    fetch_table = pltpu.make_async_copy(table_hbm, table_ref, sems.at[0])
    fetch_tw = pltpu.make_async_copy(tw_hbm, tw_ref, sems.at[1])
    fetch(0).start()
    fetch_table.start()
    fetch_tw.start()
    for chunk in range(1, pairs):
        fetch(chunk).start()

    for chunk in range(pairs):
        fetch(chunk).wait()

        def unpack(i, carry):
            part = pl.ds(pl.multiple_of(i * n, n), n)
            first = data_ref[2 * chunk, part, :].astype(F32)
            second = data_ref[2 * chunk + 1, part, :].astype(F32)
            re_s[part, :] = jnp.where(lane < HALF, first, pltpu.roll(second, HALF, 1))
            im_s[part, :] = jnp.where(lane < HALF, pltpu.roll(first, HALF, 1), second)
            return carry

        lax.fori_loop(0, YR, unpack, 0)
        if chunk == 0:
            fetch_table.wait()

        for k in range(0, YR, 2):
            pieces = [
                jnp.concatenate([s[pl.ds(k + d, n, stride=YR), :] for d in range(2)], axis=1)
                for s in (re_s, im_s)
            ]
            both = dot(table_ref[...], jnp.concatenate(pieces, axis=0).astype(BF16))
            both = both[: 2 * n] + both[2 * n :]
            for d in range(2):
                mix_s[k + d] = both[:, d * LANES : (d + 1) * LANES]

        if chunk == 0:
            fetch_tw.wait()

        tiles = rows // 8
        for core in range(gz):

            def combine(i, carry):
                y2 = ((i // tiles) * gz + core) * rows + lax.rem(i, tiles) * 8
                part = pl.ds(pl.multiple_of(y2, 8), 8)
                planes = []
                for k in range(YR):
                    re = mix_s[k, part, :]
                    im = mix_s[k, pl.ds(pl.multiple_of(n + y2, 8), 8), :]
                    if k > 0:
                        c = tw_ref[0, k - 1, part, :]
                        s = tw_ref[1, k - 1, part, :]
                        re, im = re * c - im * s, im * c + re * s
                    planes.append((re, im))
                at = pl.ds(pl.multiple_of(lax.rem(i, tiles) * 8, 8), 8)
                for k, (re, im) in enumerate(short_fft(planes, 1)):
                    to = k * (n // (gz * rows)) + i // tiles
                    out_ref[core, to, chunk, 0, at, :] = re
                    out_ref[core, to, chunk, 1, at, :] = im
                return carry

            lax.fori_loop(0, n // gz // 8, combine, 0, unroll=2)
            give(chunk, core).start()

    for chunk in range(pairs):
        for core in range(gz):
            give(chunk, core).wait()


def y_inverse(data, rows, gz, gy):
    blocks, ny, width = data.shape
    n = ny // YR
    shape = (gz, gy, blocks // 2, 2, rows, LANES)
    hbm = pl.BlockSpec(memory_space=pltpu.HBM)
    return pl.pallas_call(
        y_inverse_kernel,
        in_specs=[hbm] * 3,
        out_specs=hbm,
        out_shape=jax.ShapeDtypeStruct(shape, F32),
        scratch_shapes=[
            pltpu.VMEM((blocks, ny, width), BF16),
            pltpu.VMEM((4 * n, 2 * n), BF16),
            pltpu.VMEM((2, YR - 1, n, LANES), F32),
            pltpu.VMEM(shape, F32),
            pltpu.VMEM((ny, LANES), F32),
            pltpu.VMEM((ny, LANES), F32),
            pltpu.VMEM((YR, 2 * n, LANES), F32),
            pltpu.SemaphoreType.DMA((2 + blocks // 2,)),
            pltpu.SemaphoreType.DMA((blocks // 2 * gz,)),
        ],
        compiler_params=pltpu.CompilerParams(vmem_limit_bytes=Y_GRANT),
        name="y_inverse",
    )(data, y_matrix(ny, False, -1.0), y_twiddle(ny))


def y_forward_kernel(
    spec_hbm, data_hbm, table_hbm, tw_hbm, out_hbm,
    spec_ref, data_ref, table_ref, tw_ref, out_ref, mix_s, sems, spec_sems, out_sems,
):
    blocks, ny, _ = data_ref.shape
    n = ny // YR
    _, gz, gy, _, rows, _ = spec_ref.shape
    pairs = blocks // 2
    half = n // 2

    def fetch(chunk):
        return pltpu.make_async_copy(
            spec_hbm.at[:, :, chunk], spec_ref.at[chunk], spec_sems.at[chunk]
        )

    def give(chunk, part):
        at = (pl.ds(2 * chunk, 2), slice(None), pl.ds(part * half, half))
        return pltpu.make_async_copy(out_ref.at[at], out_hbm.at[at], out_sems.at[2 * chunk + part])

    fetch_table = pltpu.make_async_copy(table_hbm, table_ref, sems.at[0])
    fetch_tw = pltpu.make_async_copy(tw_hbm, tw_ref, sems.at[1])
    fetch_data = pltpu.make_async_copy(data_hbm, data_ref, sems.at[2])
    fetch(0).start()
    fetch_table.start()
    fetch_tw.start()
    fetch_data.start()
    for chunk in range(1, pairs):
        fetch(chunk).start()

    def rows_of(chunk, p, k):
        part = pl.ds(k, rows // YR, stride=YR)
        return jnp.concatenate(
            [spec_ref[chunk, core, i, p, part, :] for i in range(gy) for core in range(gz)], axis=0
        )

    lane = lax.broadcasted_iota(jnp.int32, (16, LANES), 1)
    for chunk in range(pairs):
        fetch(chunk).wait()

        if chunk == 0:
            fetch_table.wait()

        for k in range(0, YR, 2):
            pieces = [
                jnp.concatenate([rows_of(chunk, p, k + d) for d in range(2)], axis=1)
                for p in range(2)
            ]
            high, low = split2(jnp.concatenate(pieces, axis=0))
            both = dot(table_ref[...], high)
            both = both[: 2 * n] + both[2 * n :] + dot(table_ref[: 2 * n], low)
            for d in range(2):
                mix_s[k + d] = both[:, d * LANES : (d + 1) * LANES]
        if chunk == 0:
            fetch_tw.wait()
            fetch_data.wait()

        def combine(i, carry):
            start = pl.multiple_of(i * 16, 16)
            part = pl.ds(start, 16)
            planes = []
            for k in range(YR):
                re = mix_s[k, part, :]
                im = mix_s[k, pl.ds(pl.multiple_of(n + i * 16, 16), 16), :]
                if k > 0:
                    c = tw_ref[0, k - 1, part, :]
                    s = tw_ref[1, k - 1, part, :]
                    re, im = re * c + im * s, im * c - re * s
                planes.append((re, im))
            for k, (re, im) in enumerate(short_fft(planes, -1)):
                at = pl.ds(pl.multiple_of(k * n + start, 16), 16)
                first = jnp.where(lane < HALF, re, pltpu.roll(im, HALF, 1))
                second = jnp.where(lane < HALF, pltpu.roll(re, HALF, 1), im)
                out_ref[2 * chunk, k, part, :] = first - data_ref[2 * chunk, at, :].astype(F32)
                out_ref[2 * chunk + 1, k, part, :] = (
                    second - data_ref[2 * chunk + 1, at, :].astype(F32)
                )
            return carry

        for part in range(2):
            lax.fori_loop(part * half // 16, (part + 1) * half // 16, combine, 0)
            give(chunk, part).start()

    for chunk in range(pairs):
        for part in range(2):
            give(chunk, part).wait()


def y_forward(spec, data):
    blocks, ny, width = data.shape
    n = ny // YR
    hbm = pl.BlockSpec(memory_space=pltpu.HBM)
    out = pl.pallas_call(
        y_forward_kernel,
        in_specs=[hbm] * 4,
        out_specs=hbm,
        out_shape=jax.ShapeDtypeStruct((blocks, YR, n, width), F32),
        scratch_shapes=[
            pltpu.VMEM((blocks // 2, *spec.shape[:2], *spec.shape[3:]), F32),
            pltpu.VMEM((blocks, ny, width), BF16),
            pltpu.VMEM((4 * n, 2 * n), BF16),
            pltpu.VMEM((2, YR - 1, n, LANES), F32),
            pltpu.VMEM((blocks, YR, n, width), F32),
            pltpu.VMEM((YR, 2 * n, LANES), F32),
            pltpu.SemaphoreType.DMA((3,)),
            pltpu.SemaphoreType.DMA((blocks // 2,)),
            pltpu.SemaphoreType.DMA((blocks,)),
        ],
        compiler_params=pltpu.CompilerParams(vmem_limit_bytes=Y_GRANT),
        name="y_forward",
    )(spec, data, y_matrix(ny, True, 1.0), y_twiddle(ny))
    return out.reshape(blocks, ny, width)


def plane_chunk(planes, rows):
    chunk = max(1, 1024 // rows)
    while planes % chunk:
        chunk -= 1
    return chunk


def turn_rows(kb, planes_of, tw_ref, lanes, sign):
    out = []
    for b in range(kb):
        re, im = planes_of(b)
        if b > 0:
            c = tw_ref[0, b, :, lanes]
            s = tw_ref[1, b, :, lanes]
            if sign > 0:
                re, im = re * c - im * s, im * c + re * s
            else:
                re, im = re * c + im * s, im * c - re * s
        out.append((re, im))
    return out


def inverse_columns(gz, kb, spectra, coef_ref, tw_ref, lanes, part, re_s, im_s):
    mixed = [[None] * kb for _ in range(gz)]
    for k in range(kb):
        coef = [coef_ref[j, k, :, lanes] for j in range(3)]
        re = mix_adjoint(coef, [spectra[z][k][0] for z in range(gz)])
        im = mix_adjoint(coef, [spectra[z][k][1] for z in range(gz)])
        for z in range(gz):
            mixed[z][k] = (re[z], im[z])
    for z in range(gz):
        short = short_fft(mixed[z], 1)
        for b, (re, im) in enumerate(turn_rows(kb, lambda b: short[b], tw_ref, lanes, 1)):
            re_s[z * kb + b, part, lanes] = re
            im_s[z * kb + b, part, lanes] = im


def forward_columns(gz, kb, coef_ref, tw_ref, lanes, part, re_s, im_s):
    spectra = []
    for z in range(gz):
        rows_of = lambda b: (re_s[z * kb + b, part, lanes], im_s[z * kb + b, part, lanes])
        spectra.append(short_fft(turn_rows(kb, rows_of, tw_ref, lanes, -1), -1))
    out = [[None] * kb for _ in range(gz)]
    for k in range(kb):
        coef = [coef_ref[j, k, :, lanes] for j in range(3)]
        re = mix(coef, [spectra[z][k][0] for z in range(gz)])
        im = mix(coef, [spectra[z][k][1] for z in range(gz)])
        for z in range(gz):
            out[z][k] = (re[z], im[z])
    return out


def inverse_product(re, im, table_ref):
    ka = re.shape[1]
    high, low = split2(jnp.concatenate([re, im], axis=1))
    value = dot(high, table_ref[...])
    return value[:, :ka] + value[:, ka:] + dot(low, table_ref[:, :ka])


def forward_product(field, table_ref):
    ka = field.shape[1]
    high, low = split2(field)
    value = dot(high, table_ref[...])
    value = value[:, : 2 * ka] + value[:, 2 * ka :] + dot(low, table_ref[:, : 2 * ka])
    return value[:, :ka], value[:, ka:]


def next_plane(field_ref, p, kb):
    rows, ka = field_ref.shape[1:]
    if (p + 1) % kb:
        return field_ref[p + 1]
    lane = lax.broadcasted_iota(jnp.int32, (rows, ka), 1)
    return jnp.where(lane == ka - 1, field_ref[p], pltpu.roll(field_ref[p + 1 - kb], ka - 1, 1))


def prev_plane(field_ref, p, kb):
    rows, ka = field_ref.shape[1:]
    if p % kb:
        return field_ref[p - 1]
    lane = lax.broadcasted_iota(jnp.int32, (rows, ka), 1)
    return jnp.where(lane == 0, field_ref[p], pltpu.roll(field_ref[p + kb - 1], 1, 1))


def first_kernel(
    gz, edge_ref, field_ref, coef_ref, tw_ref, table_ref, sums_ref, spec_ref, *refs
):
    piece_refs, (re_s, im_s) = refs[:-2], refs[-2:]
    planes, rows, ka = field_ref.shape
    kb = planes // gz
    projected = forward_into(gz, field_ref, coef_ref, tw_ref, table_ref, spec_ref, re_s, im_s)
    cut(gz, edge_ref, spec_ref, piece_refs)
    row = lax.broadcasted_iota(jnp.int32, (rows, ka), 0)
    square = jnp.zeros((8, LANES), F32)
    slope = jnp.zeros((8, LANES), F32)
    for p in range(planes):
        here = field_ref[p]
        square = square + fold(here * here)
        along_x = next_plane(field_ref, p, kb) - here
        along_y = jnp.where(row == rows - 1, 0.0, pltpu.roll(here, rows - 1, 0) - here)
        terms = along_x * along_x + along_y * along_y
        if p + kb < planes:
            along_z = field_ref[p + kb] - here
            terms = terms + along_z * along_z
        slope = slope + fold(terms)
    sums_ref[0] = square
    sums_ref[1] = projected
    sums_ref[2] = slope


def columns_back(spec_ref, chunk, coef_ref, tw_ref, re_s, im_s, j, carry):
    gz, kb = spec_ref.shape[:2]
    lanes = slice(chunk * LANES, (chunk + 1) * LANES)
    part = pl.ds(pl.multiple_of(j * 8, 8), 8)
    spectra = [
        [(spec_ref[z, k, chunk, 0, part, :], spec_ref[z, k, chunk, 1, part, :]) for k in range(kb)]
        for z in range(gz)
    ]
    inverse_columns(gz, kb, spectra, coef_ref, tw_ref, lanes, part, re_s, im_s)
    return carry


def middle_kernel(
    spec_hbm, coef_ref, tw_ref, inverse_ref, forward_ref,
    d0_ref, head_ref, tail_ref, spec_ref, re_s, im_s, sems,
):
    gz, kb, chunks, _, rows, _ = spec_ref.shape
    ka = chunks * LANES
    planes = gz * kb

    def fetch(chunk, z):
        return pltpu.make_async_copy(
            spec_hbm.at[z, :, chunk], spec_ref.at[z, :, chunk], sems.at[chunk * gz + z]
        )

    for chunk in range(chunks):
        for z in range(gz):
            fetch(chunk, z).start()
    for chunk in range(chunks):
        for z in range(gz):
            fetch(chunk, z).wait()
        lax.fori_loop(
            0, rows // 8,
            functools.partial(columns_back, spec_ref, chunk, coef_ref, tw_ref, re_s, im_s), 0,
        )

    step = plane_chunk(planes, rows)
    shape2, shape3 = (step * rows, ka), (step, rows, ka)

    def there_and_back(i, carry):
        part = pl.ds(i * step, step)
        field = inverse_product(re_s[part].reshape(shape2), im_s[part].reshape(shape2), inverse_ref)
        d0_ref[part] = field.reshape(shape3)
        re, im = forward_product(field, forward_ref)
        re_s[part] = re.reshape(shape3)
        im_s[part] = im.reshape(shape3)
        return carry

    lax.fori_loop(0, planes // step, there_and_back, 0)

    def second_columns(j, total):
        part = pl.ds(pl.multiple_of(j * 8, 8), 8)
        for chunk in range(chunks):
            lanes = slice(chunk * LANES, (chunk + 1) * LANES)
            spectra = forward_columns(gz, kb, coef_ref, tw_ref, lanes, part, re_s, im_s)
            for z in range(gz):
                for k in range(kb):
                    for p in range(2):
                        value = spectra[z][k][p]
                        spec_ref[z, k, chunk, p, part, :] = value
                        total = total + value * value
        return total

    projected = lax.fori_loop(0, rows // 8, second_columns, jnp.zeros((8, LANES), F32))
    for p in range(planes):
        head_ref[p : p + 1, :] = d0_ref[p, :1, :]
        head_ref[planes + p : planes + p + 1, :] = d0_ref[p, 1:2, :]
        for part in range(2):
            at = 2 * planes + 2 * p + part
            for chunk in range(chunks):
                lanes = slice(chunk * LANES, (chunk + 1) * LANES)
                head_ref[at : at + 1, lanes] = spec_ref[p // kb, p % kb, chunk, part, :1, :]
        tail_ref[p : p + 1, :] = d0_ref[p, rows - 1 : rows, :]

    row = lax.broadcasted_iota(jnp.int32, (rows, ka), 0)
    square = jnp.zeros((8, LANES), F32)
    slope = jnp.zeros((8, LANES), F32)
    for p in range(planes):
        here = d0_ref[p]
        square = square + fold(here * here)
        along_x = next_plane(d0_ref, p, kb) - here
        along_y = jnp.where(row == rows - 1, 0.0, pltpu.roll(here, rows - 1, 0) - here)
        terms = along_x * along_x + along_y * along_y
        if p + kb < planes:
            along_z = d0_ref[p + kb] - here
            terms = terms + along_z * along_z
        slope = slope + fold(terms)
    block = sums_block([square, projected, slope])
    for ref in (head_ref, tail_ref):
        at = ref.shape[0] - 8
        ref[at:, :] = jnp.zeros((8, ka), F32)
        ref[at:, :LANES] = block


def middle(spec, coef, nx):
    gz, kb, chunks, _, rows, _ = spec.shape
    ka = chunks * LANES
    planes = gz * kb
    vmem = pl.BlockSpec(memory_space=pltpu.VMEM)
    field = jax.ShapeDtypeStruct((planes, rows, ka), F32)
    return pl.pallas_call(
        middle_kernel,
        in_specs=[pl.BlockSpec(memory_space=pltpu.HBM)] + [vmem] * 4,
        out_specs=[vmem] * 4,
        out_shape=[
            field,
            jax.ShapeDtypeStruct((4 * planes + 8, ka), F32),
            jax.ShapeDtypeStruct((planes + 8, ka), F32),
            jax.ShapeDtypeStruct(spec.shape, F32),
        ],
        scratch_shapes=[
            pltpu.VMEM((planes, rows, ka), F32),
            pltpu.VMEM((planes, rows, ka), F32),
            pltpu.SemaphoreType.DMA((chunks * gz,)),
        ],
        compiler_params=pltpu.CompilerParams(vmem_limit_bytes=X_GRANT),
        name="middle",
    )(
        spec, coef, x_twiddle(nx, ka), jnp.asarray(x_inverse_matrix(nx, ka)),
        x_forward_matrix(nx, ka),
    )


def normal_kernel(spec_ref, coef_ref, tw_ref, table_ref, out_ref, re_s, im_s):
    gz, kb, chunks, _, rows, _ = spec_ref.shape
    planes, ka = gz * kb, chunks * LANES

    for chunk in range(chunks):
        lax.fori_loop(
            0, rows // 8,
            functools.partial(columns_back, spec_ref, chunk, coef_ref, tw_ref, re_s, im_s), 0,
        )

    step = plane_chunk(planes, rows)
    shape = (step * rows, ka)
    for start in range(0, planes, step):
        part = slice(start, start + step)
        field = inverse_product(re_s[part].reshape(shape), im_s[part].reshape(shape), table_ref)
        out_ref[part] = field.reshape(step, rows, ka)


def normal_product(spec, coef, nx):
    gz, kb, chunks, _, rows, _ = spec.shape
    planes, ka = gz * kb, chunks * LANES
    vmem = pl.BlockSpec(memory_space=pltpu.VMEM)
    return pl.pallas_call(
        normal_kernel,
        in_specs=[vmem] * 4,
        out_specs=vmem,
        out_shape=jax.ShapeDtypeStruct((planes, rows, ka), F32),
        scratch_shapes=[pltpu.VMEM((planes, rows, ka), F32)] * 2,
        compiler_params=pltpu.CompilerParams(vmem_limit_bytes=X_GRANT),
        cost_estimate=pl.CostEstimate(
            flops=12 * planes * rows * ka * ka, bytes_accessed=12 * planes * rows * ka, transcendentals=0
        ),
        name="normal_product",
    )(spec, coef, x_twiddle(nx, ka), jnp.asarray(x_inverse_matrix(nx, ka)))


def next_normal_row(gz, next_ref, coef_ref, tw_ref, table_ref, row_s, re_s, im_s):
    planes, ka = row_s.shape
    kb = planes // gz
    for start in range(0, ka, LANES):
        lanes = slice(start, start + LANES)

        def row_of(z, k, part):
            at = 2 * planes + 2 * (z * kb + k) + part
            return jnp.broadcast_to(next_ref[at : at + 1, lanes], (8, LANES))

        spectra = [[(row_of(z, k, 0), row_of(z, k, 1)) for k in range(kb)] for z in range(gz)]
        inverse_columns(gz, kb, spectra, coef_ref, tw_ref, lanes, slice(0, 8), re_s, im_s)
    shape = (planes * 8, ka)
    field = inverse_product(re_s[...].reshape(shape), im_s[...].reshape(shape), table_ref)
    for p in range(planes):
        row_s[p : p + 1, :] = field[8 * p : 8 * p + 1, :]


def border_kernel(edge_ref, head_ref, tail_ref, next_ref, prev_ref, after_ref, out_ref):
    del after_ref
    planes = tail_ref.shape[0] - 8

    def sums_of(ref):
        return ref[ref.shape[0] - 8 :, :LANES]

    def border(after, before):
        step = after[:planes, :] - before[:planes, :]
        return fold(step * step)

    second = edge_ref[2] > 0
    below = border(head_ref, prev_ref) * jnp.where(edge_ref[0] > 0, 0.0, 1.0)
    above = border(next_ref, tail_ref) * jnp.where(edge_ref[1] > 0, 0.0, 1.0)
    other = jnp.where(second, sums_of(prev_ref), sums_of(next_ref))
    none = jnp.zeros((8, LANES), F32)
    put_copies(out_ref, sums_of(tail_ref) + other + sums_block([none, none, below + above]))


def border_sums(edge, head, tail, next_head, prev_tail, after, copies):
    vmem = pl.BlockSpec(memory_space=pltpu.VMEM)
    return pl.pallas_call(
        border_kernel,
        in_specs=[pl.BlockSpec(memory_space=pltpu.SMEM)]
        + [vmem] * 4
        + [pl.BlockSpec(memory_space=pl.ANY)],
        out_specs=vmem,
        out_shape=jax.ShapeDtypeStruct((copies, 8, LANES), F32),
        compiler_params=pltpu.CompilerParams(vmem_limit_bytes=2 * MIB),
        name="border_sums",
    )(edge, head, tail, next_head, prev_tail, after)


def second_kernel(
    gz, edge_ref, d0_ref, nd0_ref, tail_ref, prev_ref, next_ref,
    coef_ref, tw_ref, table_ref, inverse_ref, *refs,
):
    sums_refs, refs = refs[:1], refs[1:]
    d1_ref, eta_ref, out_ref, spec_ref, re_s, im_s, row_s, nrow_s, re8_s, im8_s = refs
    next_normal_row(gz, next_ref, coef_ref, tw_ref, inverse_ref, nrow_s, re8_s, im8_s)
    planes, rows, ka = d0_ref.shape
    kb = planes // gz
    eta_here = step_of(sums_refs)
    eta_ref[...] = jnp.broadcast_to(eta_here, (8, LANES))
    eta = jnp.max(eta_here)
    first = edge_ref[0] > 0
    last = edge_ref[1] > 0

    def shrink(difference):
        return jnp.clip(-eta * difference, -CLIP, CLIP)

    lane2 = lax.broadcasted_iota(jnp.int32, (kb, ka), 1)
    row2 = lax.broadcasted_iota(jnp.int32, (kb, ka), 0)
    for z in range(gz):
        part = slice(z * kb, (z + 1) * kb)
        here = next_ref[part, :]
        value = here - eta * nrow_s[part, :]
        up = pltpu.roll(here, kb - 1, 0)
        up = jnp.where(
            row2 == kb - 1, jnp.where(lane2 == ka - 1, here, pltpu.roll(up, ka - 1, 1)), up
        )
        down = pltpu.roll(here, 1, 0)
        down = jnp.where(row2 == 0, jnp.where(lane2 == 0, here, pltpu.roll(down, 1, 1)), down)
        value = value + shrink(here - down) - shrink(up - here)
        value = value + shrink(here - tail_ref[part, :]) - shrink(next_ref[planes + z * kb : planes + (z + 1) * kb, :] - here)
        if z > 0:
            value = value + shrink(here - next_ref[(z - 1) * kb : z * kb, :])
        if z + 1 < gz:
            value = value - shrink(next_ref[(z + 1) * kb : (z + 2) * kb, :] - here)
        row_s[part, :] = value

    row = lax.broadcasted_iota(jnp.int32, (rows, ka), 0)
    square = jnp.zeros((8, LANES), F32)
    for p in range(planes):
        here = d0_ref[p]
        value = here - eta * nd0_ref[p]
        if p % kb == 0:
            clipped_x = shrink(here - prev_plane(d0_ref, p, kb))
        value = value + clipped_x
        clipped_x = shrink(next_plane(d0_ref, p, kb) - here)
        value = value - clipped_x
        below = jnp.where(last, here[rows - 1 :, :], next_ref[p : p + 1, :])
        above = jnp.where(first, here[:1, :], prev_ref[p : p + 1, :])
        upper = shrink(jnp.where(row == rows - 1, below, pltpu.roll(here, rows - 1, 0)) - here)
        lower = jnp.where(row == 0, shrink(here[:1, :] - above), pltpu.roll(upper, 1, 0))
        value = value + lower - upper
        if p >= kb:
            value = value + shrink(here - d0_ref[p - kb])
        if p + kb < planes:
            value = value - shrink(d0_ref[p + kb] - here)
        d1_ref[p] = value
        square = square + fold(value * value)

    slope = jnp.zeros((8, LANES), F32)
    for p in range(planes):
        here = d1_ref[p]
        along_x = next_plane(d1_ref, p, kb) - here
        below = jnp.where(last, here[rows - 1 :, :], row_s[p : p + 1, :])
        along_y = jnp.where(row == rows - 1, below, pltpu.roll(here, rows - 1, 0)) - here
        terms = along_x * along_x + along_y * along_y
        if p + kb < planes:
            along_z = d1_ref[p + kb] - here
            terms = terms + along_z * along_z
        slope = slope + fold(terms)

    step = plane_chunk(planes, rows)

    def multiply(i, carry):
        part = pl.ds(i * step, step)
        re, im = forward_product(d1_ref[part].reshape(step * rows, ka), table_ref)
        re_s[part] = re.reshape(step, rows, ka)
        im_s[part] = im.reshape(step, rows, ka)
        return carry

    lax.fori_loop(0, planes // step, multiply, 0)

    def columns(j, total):
        part = pl.ds(pl.multiple_of(j * 8, 8), 8)
        for chunk in range(ka // LANES):
            lanes = slice(chunk * LANES, (chunk + 1) * LANES)
            spectra = forward_columns(gz, kb, coef_ref, tw_ref, lanes, part, re_s, im_s)
            for z in range(gz):
                for k in range(kb):
                    for p in range(2):
                        value = spectra[z][k][p]
                        spec_ref[z, k, chunk, p, part, :] = value
                        total = total + value * value
        return total

    projected = lax.fori_loop(0, rows // 8, columns, jnp.zeros((8, LANES), F32))
    put_copies(out_ref, sums_block([square, projected, slope]))


def second_descent(edge, sums, d0, nd0, tail, prev_tail, next_head, coef, gz, nx):
    planes, rows, ka = d0.shape
    vmem = pl.BlockSpec(memory_space=pltpu.VMEM)
    return pl.pallas_call(
        functools.partial(second_kernel, gz),
        in_specs=[pl.BlockSpec(memory_space=pltpu.SMEM)] + [vmem] * 10,
        out_specs=[vmem] * 4,
        out_shape=[
            jax.ShapeDtypeStruct((planes, rows, ka), F32),
            jax.ShapeDtypeStruct((8, LANES), F32),
            jax.ShapeDtypeStruct(sums.shape, F32),
            jax.ShapeDtypeStruct((gz, planes // gz, ka // LANES, 2, rows, LANES), F32),
        ],
        scratch_shapes=[
            pltpu.VMEM((planes, rows, ka), F32),
            pltpu.VMEM((planes, rows, ka), F32),
            pltpu.VMEM((planes, ka), F32),
            pltpu.VMEM((planes, ka), F32),
            pltpu.VMEM((planes, 8, ka), F32),
            pltpu.VMEM((planes, 8, ka), F32),
        ],
        compiler_params=pltpu.CompilerParams(vmem_limit_bytes=X_GRANT),
        name="second_descent",
    )(
        edge, d0, nd0, tail, prev_tail, next_head, coef,
        x_twiddle(nx, ka), x_forward_matrix(nx, ka), jnp.asarray(x_inverse_matrix(nx, ka)), sums,
    )


def combine_kernel(gz, eta_ref, *refs):
    sums_refs, (first_ref, second_ref, out_ref, steps_ref) = refs[:gz], refs[gz:]
    eta0 = jnp.max(eta_ref[...])
    eta1 = jnp.max(step_of(sums_refs))
    steps_ref[0] = eta_ref[...]
    steps_ref[1] = jnp.full((8, LANES), eta1, F32)
    count = out_ref.shape[0]
    start = pl.program_id(0) * count
    for i in range(count):
        out_ref[i] = -(eta0 * first_ref[start + i] + eta1 * second_ref[start + i])


def combine_spectra(eta, sums, first, second):
    gz = len(sums)
    planes, *rest = first.shape
    count = 4 if planes % 4 == 0 else 1
    vmem = pl.BlockSpec(memory_space=pltpu.VMEM)
    return pl.pallas_call(
        functools.partial(combine_kernel, gz),
        grid=(planes // count,),
        in_specs=[vmem] * (3 + gz),
        out_specs=[
            pl.BlockSpec((count, *rest), lambda i: (i, 0, 0, 0, 0)),
            pl.BlockSpec((2, 8, LANES), lambda i: (0, 0, 0)),
        ],
        out_shape=[
            jax.ShapeDtypeStruct(first.shape, F32),
            jax.ShapeDtypeStruct((2, 8, LANES), F32),
        ],
        compiler_params=pltpu.CompilerParams(vmem_limit_bytes=6 * MIB),
        name="combine_spectra",
    )(eta, *sums, first, second)


def to_core(piece, r):
    gz = lax.axis_size("gz")
    return lax.ppermute(piece, "gz", [(i, (i + r) % gz) for i in range(gz)]) if r else piece


def to_chips(parts):
    return lax.all_to_all(parts, "gy", 0, 0, tiled=True)


def to_devices(parts):
    gz, gy, *rest = parts.shape
    parts = lax.all_to_all(parts.reshape(gz * gy, *rest), ("gz", "gy"), 0, 0, tiled=True)
    return parts.reshape(gz, gy, *rest)


def everywhere(sums):
    sums = to_chips(sums)
    return [to_core(sums, r) for r in range(lax.axis_size("gz"))]


def shards(data, band_offset, interp_weight):
    gz = lax.axis_size("gz")
    gy = lax.axis_size("gy")
    devices = gz * gy
    data = data[0]
    blocks, ny, width = data.shape
    rows = ny // devices
    ka = blocks * HALF
    nx = ka * gy

    core = lax.axis_index("gz")
    flat = lax.axis_index("gy") * gz + core
    edge = jnp.stack([flat == 0, flat == devices - 1, core]).astype(jnp.int32)
    order = [(i % gz) * gy + i // gz for i in range(devices)]
    up = [(order[i + 1], order[i]) for i in range(devices - 1)]
    down = [(order[i], order[i + 1]) for i in range(devices - 1)]

    lower = band_offset < 0
    weight = interp_weight
    coef = jnp.stack(
        [
            jnp.where(lower, weight[1], weight[0]),
            jnp.where(lower, weight[0], 0.0),
            jnp.where(lower, 0.0, weight[1]),
        ]
    ).reshape(3, gy, 1, ka)
    coef = jnp.broadcast_to(coef, (3, gy, 8, ka))

    spec = to_devices(y_inverse(data, rows, gz, gy))
    d0, head, tail, first = middle(spec, coef, nx)
    next_head = lax.ppermute(head, ("gz", "gy"), up)
    prev_tail = lax.ppermute(tail, ("gz", "gy"), down)
    nd0 = normal_product(first, coef, nx)
    sums = to_chips(border_sums(edge, head, tail, next_head, prev_tail, nd0, gy))
    d1, eta, sums, second = second_descent(
        edge, sums, d0, nd0, tail, prev_tail, next_head, coef, gz, nx
    )
    sums = everywhere(sums)
    flat_shape = (devices, ka // LANES, 2, rows, LANES)
    spec, etas = combine_spectra(eta, sums, first.reshape(flat_shape), second.reshape(flat_shape))
    residual = y_forward(to_devices(spec.reshape(first.shape)), data)

    volume = -(etas[0, 0, 0] * d0 + etas[1, 0, 0] * d1)
    volume = volume.reshape(gz, gy, rows, ka).transpose(0, 2, 3, 1).reshape(gz, rows, nx)
    parts = [
        to_core(lax.dynamic_index_in_dim(volume, lax.rem(core + r, gz), 0, False), r)
        for r in range(gz)
    ]
    volume = jnp.zeros((gz, rows, nx), F32)
    for r, part in enumerate(parts):
        volume = lax.dynamic_update_index_in_dim(volume, part, lax.rem(core + gz - r, gz), 0)
    return (volume.reshape(1, gz * rows, nx), residual[None])


NX = 4096
NY = 2048
XB = 64
YB = 64
ITERS = 2
XA = 64
YA = 32
PRECISE = lax.Precision.HIGHEST


def with_halo(block, sides, width):
    for axis, dim in sides:
        count = lax.axis_size(axis)
        forward = [(i, i + 1) for i in range(count - 1)]
        backward = [(target, source) for source, target in forward]
        low = lax.ppermute(
            lax.slice_in_dim(block, block.shape[dim] - width, None, axis=dim), axis, forward
        )
        high = lax.ppermute(lax.slice_in_dim(block, 0, width, axis=dim), axis, backward)
        block = jnp.concatenate([low, block, high], axis=dim)
    return block


def from_behind(block, axis, distance):
    devices = range(lax.axis_size(axis))
    route = [(i - distance, i) for i in devices if i - distance in devices]
    return lax.ppermute(block, axis, route)


def unit_table(length):
    counter = jnp.arange(length, dtype=jnp.int32)
    phase_int = counter[:, None] * counter[None, :] % length
    angles = 2.0 * jnp.pi / length * phase_int.astype(jnp.float32)
    factor = length ** (-0.5)
    return (jnp.cos(angles) * factor, jnp.sin(angles) * factor)


def twiddle_table(row_len, col_len, period):
    phase_int = (
        jnp.arange(row_len, dtype=jnp.int32)[:, None]
        * jnp.arange(col_len, dtype=jnp.int32)[None, :]
        % period
    )
    angles = 2.0 * jnp.pi / period * phase_int.astype(jnp.float32)
    return (jnp.cos(angles), jnp.sin(angles))


def split_parts(packed):
    half_width = packed.shape[-1] // 2
    return (packed[..., :half_width], packed[..., half_width:])


def join_parts(real_part, imag_part):
    return jnp.concatenate([real_part, imag_part], axis=-1)


def complex_contract(packed, cos_table, sin_table, subscripts, conj_sign):
    cos_out = jnp.einsum(subscripts, packed, cos_table, precision=PRECISE)
    sin_out = jnp.einsum(subscripts, packed, sin_table, precision=PRECISE)
    cos_re, cos_im = split_parts(cos_out)
    sin_re, sin_im = split_parts(sin_out)
    return join_parts(cos_re - conj_sign * sin_im, cos_im + conj_sign * sin_re)


def rotate(packed, cos_table, sin_table, conj_sign):
    real_part, imag_part = split_parts(packed)
    return join_parts(
        real_part * cos_table - conj_sign * imag_part * sin_table,
        imag_part * cos_table + conj_sign * real_part * sin_table,
    )


def forward_x(volume):
    slices, row_count = (volume.shape[0], volume.shape[1])
    cos_a, sin_a = unit_table(XA)
    cos_b, sin_b = unit_table(XB)
    first_table = jnp.concatenate([cos_a, -sin_a], axis=1)
    grid_view = volume.reshape(slices, row_count, XA, XB)
    mixing = jnp.einsum("zyab,am->zybm", grid_view, first_table, precision=PRECISE)
    tw_cos, tw_sin = twiddle_table(XB, XA, NX)
    mixing = rotate(mixing, tw_cos, tw_sin, -1.0)
    return complex_contract(mixing, cos_b, sin_b, "zybm,bl->zlym", -1.0)


def inverse_x(packed):
    slices, row_count = (packed.shape[0], packed.shape[2])
    cos_a, sin_a = unit_table(XA)
    cos_b, sin_b = unit_table(XB)
    mixing = complex_contract(packed, cos_b, sin_b, "zlym,lb->zybm", 1.0)
    tw_cos, tw_sin = twiddle_table(XB, XA, NX)
    mixing = rotate(mixing, tw_cos, tw_sin, 1.0)
    last_table = jnp.concatenate([cos_a, -sin_a], axis=0)
    grid_view = jnp.einsum("zybm,ma->zyab", mixing, last_table, precision=PRECISE)
    return grid_view.reshape(slices, row_count, NX)


def forward_y(packed):
    slices, blocks, width = (packed.shape[0], packed.shape[1], packed.shape[3])
    cos_a, sin_a = unit_table(YA)
    cos_b, sin_b = unit_table(YB)
    grid_view = packed.reshape(slices, blocks, YA, YB, width)
    mixing = complex_contract(grid_view, cos_a, sin_a, "zjcdm,ck->zjkdm", -1.0)
    tw_cos, tw_sin = twiddle_table(YA, YB, NY)
    mixing = rotate(mixing, tw_cos[:, :, None], tw_sin[:, :, None], -1.0)
    result = complex_contract(mixing, cos_b, sin_b, "zjkdm,dl->zjlkm", -1.0)
    return result.reshape(slices, blocks, NY, width)


def inverse_y(packed):
    slices, blocks, width = (packed.shape[0], packed.shape[1], packed.shape[3])
    cos_a, sin_a = unit_table(YA)
    cos_b, sin_b = unit_table(YB)
    grid_view = packed.reshape(slices, blocks, YB, YA, width)
    mixing = complex_contract(grid_view, cos_b, sin_b, "zjlkm,ld->zjkdm", 1.0)
    tw_cos, tw_sin = twiddle_table(YA, YB, NY)
    mixing = rotate(mixing, tw_cos[:, :, None], tw_sin[:, :, None], 1.0)
    result = complex_contract(mixing, cos_a, sin_a, "zjkdm,kc->zjcdm", 1.0)
    return result.reshape(slices, blocks, NY, width)


def tilt_coefficients(band_offset, interp_weight, first_block, blocks):
    offsets = lax.dynamic_slice_in_dim(band_offset.reshape(XB, XA), first_block, blocks, 0)
    weights = lax.dynamic_slice_in_dim(interp_weight.reshape(2, XB, XA), first_block, blocks, 1)
    lower_tap = (jnp.concatenate([offsets, offsets], axis=1) < 0)[:, None, :]
    first_weight = jnp.concatenate([weights[0], weights[0]], axis=1)[:, None, :]
    second_weight = jnp.concatenate([weights[1], weights[1]], axis=1)[:, None, :]
    return (lower_tap, first_weight, second_weight)


def tilt(field_in, coefficients, adjoint):
    lower_tap, first_weight, second_weight = coefficients
    padded = with_halo(field_in, (("gz", 0),), 1)
    below_rim = padded[:-2]
    middle = padded[1:-1]
    above_rim = padded[2:]
    if adjoint:
        return jnp.where(
            lower_tap,
            first_weight * above_rim + second_weight * middle,
            first_weight * middle + second_weight * below_rim,
        )
    return jnp.where(
        lower_tap,
        first_weight * below_rim + second_weight * middle,
        first_weight * middle + second_weight * above_rim,
    )


def to_pencil(slab_part):
    return lax.all_to_all(slab_part, "gy", split_axis=1, concat_axis=2, tiled=True)


def to_slab(pencil_part):
    return lax.all_to_all(pencil_part, "gy", split_axis=2, concat_axis=1, tiled=True)


def back_project(packed, pencil_coef):
    return inverse_x(to_slab(inverse_y(tilt(packed, pencil_coef, True))))


def edge_masks(slices, row_count):
    z_global = lax.axis_index("gz") * slices + jnp.arange(slices, dtype=jnp.int32)
    y_global = lax.axis_index("gy") * row_count + jnp.arange(row_count, dtype=jnp.int32)
    keep_z = (z_global < slices * lax.axis_size("gz") - 1).astype(jnp.float32)[:, None, None]
    keep_y = (y_global < row_count * lax.axis_size("gy") - 1).astype(jnp.float32)[None, :, None]
    return (keep_z, keep_y)


def forward_diff(field_in, keep_z, keep_y):
    slices, row_count = (field_in.shape[0], field_in.shape[1])
    next_z = from_behind(field_in, "gz", -1)
    next_y = from_behind(field_in[:, :1], "gy", -1)
    along_z = (jnp.concatenate([field_in[1:], next_z], axis=0) - field_in) * keep_z
    along_y = (jnp.concatenate([field_in[:, 1:], next_y], axis=1) - field_in) * keep_y
    zero_col = jnp.zeros((slices, row_count, 1), jnp.float32)
    along_x = jnp.concatenate([field_in[:, :, 1:] - field_in[:, :, :-1], zero_col], axis=2)
    return jnp.stack([along_z, along_y, along_x])


def transpose_diff(components, keep_z, keep_y):
    slices, row_count = (components.shape[1], components.shape[2])
    zero_col = jnp.zeros((slices, row_count, 1), jnp.float32)
    comp_z = components[0] * keep_z
    comp_y = components[1] * keep_y
    comp_x = jnp.concatenate([components[2][:, :, :-1], zero_col], axis=2)
    prev_z = from_behind(comp_z, "gz", 1)
    prev_y = from_behind(comp_y[:, -1:], "gy", 1)
    result = jnp.concatenate([prev_z, comp_z[:-1]], axis=0) - comp_z
    result = result + jnp.concatenate([prev_y, comp_y[:, :-1]], axis=1) - comp_y
    result = result + jnp.concatenate([zero_col, comp_x[:, :, :-1]], axis=2) - comp_x
    return result


def plain_shards(data, band_offset, interp_weight):
    slices = data.shape[0]
    blocks = data.shape[1]
    width = data.shape[3]
    row_count = NY // lax.axis_size("gy")
    slab_coef = tilt_coefficients(band_offset, interp_weight, 0, XB)
    pencil_coef = tilt_coefficients(
        band_offset, interp_weight, lax.axis_index("gy") * blocks, blocks
    )
    keep_z, keep_y = edge_masks(slices, row_count)
    measured = data.astype(jnp.float32)
    volume = jnp.zeros((slices, row_count, NX), jnp.float32)
    grad_volume = jnp.zeros((3, slices, row_count, NX), jnp.float32)
    split_var = grad_volume
    dual_var = grad_volume
    data_back = back_project(measured, pencil_coef)
    normal_part = jnp.zeros_like(volume)
    tilted = jnp.zeros((slices, XB, row_count, width), jnp.float32)
    for iteration in range(ITERS):
        data_grad = normal_part - data_back
        if iteration > 0:
            tv_gap = grad_volume - split_var + dual_var / PENALTY
            descent = data_grad + PENALTY * transpose_diff(tv_gap, keep_z, keep_y)
        else:
            descent = data_grad
        slope_field = forward_diff(descent, keep_z, keep_y)
        projected = tilt(forward_x(descent), slab_coef, False)
        line_totals = lax.psum(
            (
                jnp.sum(descent * descent),
                jnp.sum(projected * projected),
                jnp.sum(slope_field * slope_field),
            ),
            ("gz", "gy"),
        )
        step_length = line_totals[0] / (line_totals[1] + PENALTY * line_totals[2])
        volume = volume - step_length * descent
        grad_volume = grad_volume - step_length * slope_field
        tilted = tilted - step_length * projected
        if iteration + 1 < ITERS:
            normal_part = normal_part - step_length * inverse_x(tilt(projected, slab_coef, True))
        if iteration + 1 < ITERS:
            shifted = grad_volume + dual_var / PENALTY
            split_var = shifted - jnp.clip(shifted, -TV_WEIGHT / PENALTY, TV_WEIGHT / PENALTY)
            dual_var = PENALTY * (grad_volume - split_var)
    residual = forward_y(to_pencil(tilted)) - measured
    return (volume, residual)


def tiles_fit(mesh, ny, blocks):
    rows = ny // (mesh.shape["gz"] * mesh.shape["gy"])
    return mesh.shape["gz"] == 2 and rows % 16 == 0 and mesh.shape["gy"] % YR == 0 and blocks // mesh.shape["gy"] % 2 == 0


def solution(mesh):
    in_specs = (P("gz", "gy", None, None), P(), P())
    out_specs = (P("gz", "gy", None), P("gz", "gy", None, None))

    def run(data, band_offset, interp_weight):
        body = shards if tiles_fit(mesh, data.shape[2], data.shape[1]) else plain_shards
        call = jax.shard_map(
            body, mesh=mesh, in_specs=in_specs, out_specs=out_specs, check_vma=False
        )
        return call(data, band_offset, interp_weight)

    return run
```
